32 devices in a mesh: gx: 4 (over y, x), gy: 8 (over z, core).
Axes of the slice: x: 2, y: 2, z: 4, core: 2. Of those that a mesh axis runs over, the one named last changes fastest.
Arguments:
- child_adjoint: float32 [32, 8, 64, 512], P(None, None, 'gy', 'gx'), may hold values from -6 to 6
- parent_adjoint: float32 [32, 8, 16, 128], P(None, None, 'gy', 'gx'), may hold values from -6 to 6
- child_rates: float32 [4, 32, 64, 512], P(None, None, 'gy', 'gx'), may hold values from 0.02 to 0.2
- child_mixing: float32 [32, 64, 512], P(None, 'gy', 'gx'), may hold values from 0.05 to 5
- child_land: int32 [64, 512], P('gy', 'gx'), may hold values 0 or 1
- parent_rates: float32 [4, 32, 16, 128], P(None, None, 'gy', 'gx'), may hold values from 0.02 to 0.2
- parent_mixing: float32 [32, 16, 128], P(None, 'gy', 'gx'), may hold values from 0.05 to 5
- parent_land: int32 [16, 128], P('gy', 'gx'), may hold values 0 or 1
- relaxation: float32 [64, 512], P('gy', 'gx'), may hold values from 0.2 to 0.9
Outputs:
- child_sensitivity: float32 [32, 8, 64, 512], P(None, None, 'gy', 'gx')
- parent_sensitivity: float32 [32, 8, 16, 128], P(None, None, 'gy', 'gx')
The draws below stay inside these ranges and needn't reach their ends.
Inputs may be any that keep to these rules, and one draw needn't show every extreme that they name: `child_land`: 1 marks an ocean cell, 0 a land cell. `parent_land`: 1 marks an ocean cell, 0 a land cell.
All inputs are finite; a program needn't handle non-finite values. No bound on the sum of `child_land` or of `parent_land` on one device may be relied on, other than what follows from the above.
Results may differ from the reference program's by a relative error of at most 0.0001.
Values sent between devices are 32-bit elements; how exact they have to be, the bound alone decides.
No kernel may reach another device: no remote copies, remote signals or barrier semaphores. Data moves between devices by JAX's collectives and lax.ppermute only.
A program may use at most 128 MiB of HBM per device.

```python
import math
import jax
import jax.numpy as jnp
from jax import lax

V = 8
K = 32
STEPS = 2
NXC = 512
NYC = 64
NXP = 128
NYP = 16


def set_ends(values, rng, low, top_value):
    dims = values.shape
    spot = [jax.random.randint(jax.random.fold_in(rng, axis), (), 0, dims[axis]) for axis in range(len(dims))]
    values = values.at[tuple(spot)].set(low)
    longest = dims.index(max(dims))
    spot[longest] = (spot[longest] + 1) % dims[longest]
    return values.at[tuple(spot)].set(top_value)


def steps_of(stream_key, dims, cuts, least, largest):
    def one(axis_at, blocks):
        steps = jax.random.uniform(jax.random.fold_in(jax.random.fold_in(stream_key, 6), axis_at), (blocks,), jnp.float32, least / len(cuts), largest / len(cuts))
        return jnp.repeat(jnp.exp(steps), dims[axis_at] // blocks).reshape((-1,) + (1,) * (len(dims) - axis_at - 1))

    loudness = one(*cuts[0])
    for cut in cuts[1:]:
        loudness = loudness * one(*cut)
    return loudness


def gaussian(rng, extent, width, reach, split=(), held_as=jnp.bfloat16):
    level = steps_of(rng, extent, split, -0.22, 0.18) if split else 1.0
    drawn = jax.random.normal(rng, extent, jnp.float32) * width * level
    return jnp.minimum(jnp.maximum(drawn, -reach), reach).astype(held_as)


def setup_inputs(seed: int = 0) -> dict:
    keys = jax.random.split(jax.random.key(seed), 10)
    return {
        "child_adjoint": gaussian(keys[0], (K, V, NYC, NXC), 1.0, 6.0, ((2, 8), (3, 4)), jnp.float32),
        "parent_adjoint": gaussian(keys[1], (K, V, NYP, NXP), 1.0, 6.0, ((2, 8), (3, 4)), jnp.float32),
        "child_rates": jnp.clip(jnp.exp(math.log(0.2) - 2.3025851 * jax.random.uniform(keys[2], (4, K, NYC, NXC), jnp.float32) ** steps_of(keys[2], (4, K, NYC, NXC), ((2, 8), (3, 4)), -0.2, 0.2)), 0.02, 0.2),
        "child_mixing": jnp.clip(jnp.exp(math.log(5.0) - 4.6051702 * jax.random.uniform(keys[3], (K, NYC, NXC), jnp.float32) ** steps_of(keys[3], (K, NYC, NXC), ((1, 8), (2, 4)), -0.2, 0.2)), 0.05, 5.0),
        "child_land": set_ends((jax.random.randint(keys[4], (NYC, NXC), 0, 8) < 7).astype(jnp.int32), jax.random.fold_in(keys[4], 1), 0, 1),
        "parent_rates": jnp.clip(jnp.exp(math.log(0.2) - 2.3025851 * jax.random.uniform(keys[5], (4, K, NYP, NXP), jnp.float32) ** steps_of(keys[5], (4, K, NYP, NXP), ((2, 8), (3, 4)), -0.2, 0.2)), 0.02, 0.2),
        "parent_mixing": jnp.clip(jnp.exp(math.log(5.0) - 4.6051702 * jax.random.uniform(keys[6], (K, NYP, NXP), jnp.float32) ** steps_of(keys[6], (K, NYP, NXP), ((1, 8), (2, 4)), -0.2, 0.2)), 0.05, 5.0),
        "parent_land": set_ends((jax.random.randint(keys[7], (NYP, NXP), 0, 8) < 7).astype(jnp.int32), jax.random.fold_in(keys[7], 1), 0, 1),
        "relaxation": jnp.clip(0.2 + 0.7 * jax.random.uniform(keys[8], (NYC, NXC), jnp.float32) ** steps_of(keys[8], (NYC, NXC), ((0, 8), (1, 4)), -0.2, 0.2), 0.2, 0.9),
    }


def factor_columns(mixing):
    upper_mix = jnp.concatenate([jnp.zeros_like(mixing[:1]), mixing[:-1]], axis=0)
    diagonal = 1.0 + upper_mix + mixing

    def eliminate(ratio_prev, entries):
        upper_k, diag_k, mix_k = entries
        pivot_k = diag_k - upper_k * ratio_prev
        ratio_k = mix_k / pivot_k
        return ratio_k, (ratio_k, pivot_k)

    initial = jnp.zeros(mixing.shape[1:], jnp.float32)
    _, (ratios, pivots) = lax.scan(eliminate, initial, (upper_mix, diagonal, mixing))
    return upper_mix, ratios, pivots


def solve_columns(factors, adjoint):
    upper_mix, ratios, pivots = factors

    def forward_sweep(previous, entries):
        upper_k, pivot_k, rhs_k = entries
        solved_k = (rhs_k + upper_k[None] * previous) / pivot_k[None]
        return solved_k, solved_k

    initial = jnp.zeros(adjoint.shape[1:], jnp.float32)
    _, reduced = lax.scan(forward_sweep, initial, (upper_mix, pivots, adjoint))

    def backward_sweep(previous, entries):
        ratio_k, reduced_k = entries
        solved_k = reduced_k + ratio_k[None] * previous
        return solved_k, solved_k

    _, solved = lax.scan(backward_sweep, initial, (ratios, reduced), reverse=True)
    return solved


def transport(padded, exchange_rates, land_mask):
    centre = padded[:, :, 1:-1, 1:-1]
    summed = centre + exchange_rates[0][:, None] * (padded[:, :, 1:-1, 2:] - centre)
    summed = summed + exchange_rates[1][:, None] * (padded[:, :, 1:-1, :-2] - centre)
    summed = summed + exchange_rates[2][:, None] * (padded[:, :, 2:, 1:-1] - centre)
    summed = summed + exchange_rates[3][:, None] * (padded[:, :, :-2, 1:-1] - centre)
    return land_mask.astype(jnp.float32)[None, None] * summed


def coarsen(strip):
    depth, vectors, lines, columns = strip.shape
    return strip.reshape(depth, vectors, lines // 4, 4, columns // 4, 4).sum(axis=(3, 5)) * 0.0625


def pad_sides(adjoint):
    return jnp.pad(adjoint, ((0, 0), (0, 0), (1, 1), (1, 1)), mode="wrap")


def reference(child_adjoint, parent_adjoint, child_rates, child_mixing, child_land, parent_rates, parent_mixing, parent_land, relaxation):
    child_factors = factor_columns(child_mixing)
    parent_factors = factor_columns(parent_mixing)
    parent_rows = parent_adjoint.shape[2]
    offset_rows = parent_rows // 4
    keep_field = 1.0 - relaxation

    def one_vector(vector_index):
        child_state = lax.dynamic_slice_in_dim(child_adjoint, vector_index, 1, 1)
        parent_state = lax.dynamic_slice_in_dim(parent_adjoint, vector_index, 1, 1)
        for turn_index in range(STEPS):
            weighted = child_state * relaxation[None, None]
            parent_state = parent_state + jnp.roll(coarsen(weighted), offset_rows, axis=2)
            child_state = solve_columns(child_factors, child_state * keep_field[None, None])
            child_state = transport(pad_sides(child_state), child_rates, child_land)
            parent_state = solve_columns(parent_factors, parent_state)
            parent_state = transport(pad_sides(parent_state), parent_rates, parent_land)
        return child_state[:, 0], parent_state[:, 0]

    children, parents = lax.map(one_vector, jnp.arange(child_adjoint.shape[1], dtype=jnp.int32))
    return jnp.moveaxis(children, 0, 1), jnp.moveaxis(parents, 0, 1)
```

```python
import jax
import jax.numpy as jnp
from jax import lax
from jax.experimental import pallas as pl
from jax.experimental.pallas import tpu as pltpu
from jax.sharding import PartitionSpec as P

F32 = jnp.float32
VMEM = pl.BlockSpec(memory_space=pltpu.VMEM)
LIMIT = 40 * 1024 * 1024
LANES = 128


def shape(*dims):
    return jax.ShapeDtypeStruct(dims, F32)


def call(body, outs, scratch, operands, flops, touched):
    return pl.pallas_call(
        body,
        out_shape=outs,
        in_specs=[VMEM] * len(operands),
        out_specs=jax.tree.map(lambda _: VMEM, outs),
        scratch_shapes=scratch,
        compiler_params=pltpu.CompilerParams(vmem_limit_bytes=LIMIT),
        cost_estimate=pl.CostEstimate(flops=flops, bytes_accessed=touched, transcendentals=0),
        name=body.__name__,
    )(*operands)


def lane_index(rows=8):
    return lax.broadcasted_iota(jnp.int32, (rows, LANES), 1)


def row_index():
    return lax.broadcasted_iota(jnp.int32, (8, LANES), 0)


def minors(inner, outer):
    theta = delta = jnp.ones_like(inner[0])
    inverse = []
    for i in range(len(inner)):
        delta = theta + outer[i] * delta
        theta_next = delta + inner[i] * theta
        inverse.append(theta / theta_next)
        theta = theta_next
    return inverse


def child_factors(mix_ref, keep, a_ref, b_ref, c_ref):
    depth = mix_ref.shape[0]
    half = depth // 2
    zero = jnp.zeros_like(keep)
    top_inner = [mix_ref[i] for i in range(half)]
    top_outer = [zero] + top_inner[:-1]
    low_outer = [mix_ref[depth - 1 - i] for i in range(half)]
    low_inner = [mix_ref[depth - 2 - i] for i in range(half)]
    for levels, inner, outer in (
        (range(half), top_inner, top_outer),
        (range(depth - 1, half - 1, -1), low_inner, low_outer),
    ):
        inverse = minors(inner, outer)
        for i, k in enumerate(levels):
            a_ref[k] = inverse[i] * keep
            b_ref[k] = inverse[i] * outer[i]
            c_ref[k] = inverse[i] * inner[i]


def block_rows(source_ref, k, weights, sums_ref, i, place):
    vectors = source_ref.shape[1]
    for r in range(2):
        total = source_ref[k, :, 4 * r, :] * weights[4 * r]
        for j in range(4 * r + 1, 4 * r + 4):
            total = total + source_ref[k, :, j, :] * weights[j]
        column = (2 * place + r) * LANES
        sums_ref[pl.ds(i * vectors, vectors), column : column + LANES] = total


def block_columns(sums_ref):
    wide = sums_ref.shape[1]
    p = lax.broadcasted_iota(jnp.int32, (wide, LANES), 0)
    q = lax.broadcasted_iota(jnp.int32, (wide, LANES), 1)
    pick = jnp.where(p // 4 == q, F32(0.0625), F32(0.0))
    return jnp.dot(
        sums_ref[...], pick, precision=lax.Precision.HIGHEST, preferred_element_type=F32
    )


def child_middle(carry, c_ref, half):
    vectors = len(carry) // 2
    top, low = c_ref[half - 1], c_ref[half]
    scale = 1.0 / (1.0 - top * low)
    first = [(carry[v] + top * carry[vectors + v]) * scale for v in range(vectors)]
    second = [(carry[vectors + v] + low * carry[v]) * scale for v in range(vectors)]
    return first + second


def child_up(carry, c_ref, solved_ref, lo_rows, hi_rows, lo_cols, hi_cols):
    depth, vectors = solved_ref.shape[0], solved_ref.shape[1]
    half = depth // 2
    lane = lane_index()

    def emit(i, values, packed):
        k_low = depth - 1 - i
        packed = list(packed)
        for side, k, base in ((0, i, i * vectors), (1, k_low, (half - 1 - i) * vectors)):
            for v in range(vectors):
                x = values[side * vectors + v]
                solved_ref[k, v] = x
                at = base + v
                turned = pltpu.roll(x, (at + 1) & (LANES - 1), 1)
                packed[2 * side] = jnp.where(lane == ((at + 1) & (LANES - 1)), turned, packed[2 * side])
                packed[2 * side + 1] = jnp.where(lane == at, turned, packed[2 * side + 1])
            lo_rows[pl.ds(k * vectors, vectors), :] = solved_ref[k, :, 0, :]
            hi_rows[pl.ds(k * vectors, vectors), :] = solved_ref[k, :, 7, :]
        return packed

    values = child_middle(carry, c_ref, half)
    blank = jnp.zeros((8, LANES), F32)
    packed = emit(half - 1, values, [blank] * 4)

    def up(step, state):
        i = half - 2 - step
        k_low = depth - 1 - i
        top, low = c_ref[i], c_ref[k_low]
        values = []
        for v in range(vectors):
            values.append(solved_ref[i, v] + top * state[v])
        for v in range(vectors):
            values.append(solved_ref[k_low, v] + low * state[vectors + v])
        packed = emit(i, values, state[2 * vectors :])
        return tuple(values) + tuple(packed)

    state = lax.fori_loop(0, half - 1, up, tuple(values) + tuple(packed))
    packed = state[2 * vectors :]
    for side in range(2):
        lo_cols[8 * side : 8 * side + 8, :] = packed[2 * side]
        hi_cols[8 * side : 8 * side + 8, :] = packed[2 * side + 1]


def child_first(x_ref, mix_ref, relax_ref, sums_out, solved_ref, lo_rows, hi_rows, lo_cols, hi_cols, a_ref, b_ref, c_ref, sums_ref):
    depth, vectors = x_ref.shape[0], x_ref.shape[1]
    half = depth // 2
    child_factors(mix_ref, 1.0 - relax_ref[...], a_ref, b_ref, c_ref)
    weights = [relax_ref[j : j + 1, :] for j in range(8)]

    def down(i, carry):
        k_low = depth - 1 - i
        values = []
        for side, k in ((0, i), (1, k_low)):
            a, b = a_ref[k], b_ref[k]
            for v in range(vectors):
                y = a * x_ref[k, v] + b * carry[side * vectors + v]
                solved_ref[k, v] = y
                values.append(y)
            block_rows(x_ref, k, weights, sums_ref, i, side)
        return tuple(values)

    blank = jnp.zeros((8, LANES), F32)
    carry = lax.fori_loop(0, half, down, (blank,) * (2 * vectors))
    sums_out[...] = block_columns(sums_ref)
    child_up(carry, c_ref, solved_ref, lo_rows, hi_rows, lo_cols, hi_cols)


def child_rates_of(rates_ref, k, land):
    east, west, north, south = (rates_ref[d, k] for d in range(4))
    centre = 1.0 - (east + west + north + south)
    return [land * part for part in (centre, east, west, north, south)]


def child_cell(solved_ref, k, v, base, half_index, rates, halos, lane, row):
    north_rows, south_rows, east_cols, west_cols = halos
    vectors = solved_ref.shape[1]
    s = solved_ref[k, v]
    at = base + v
    east_edge = pltpu.roll(east_cols[half_index], (LANES - 2 - at) & (LANES - 1), 1)
    west_edge = pltpu.roll(west_cols[half_index], (LANES - at) & (LANES - 1), 1)
    line = k * vectors + v
    north_edge = jnp.broadcast_to(north_rows[pl.ds(line, 1), :], (8, LANES))
    south_edge = jnp.broadcast_to(south_rows[pl.ds(line, 1), :], (8, LANES))
    east = jnp.where(lane == LANES - 1, east_edge, pltpu.roll(s, LANES - 1, 1))
    west = jnp.where(lane == 0, west_edge, pltpu.roll(s, 1, 1))
    north = jnp.where(row == 7, north_edge, pltpu.roll(s, 7, 0))
    south = jnp.where(row == 0, south_edge, pltpu.roll(s, 1, 0))
    return (rates[0] * s + rates[1] * east) + (rates[2] * west + rates[3] * north) + rates[4] * south


def child_second(
    solved_in, a_ref, b_ref, c_ref, rates_ref, land_ref, relax_ref, north_rows, south_rows, east_ref, west_ref,
    parent_ref, pa_ref, pb_ref, pc_ref, feed_ref,
    sums_out, solved_ref, psolved_ref, lo_rows, hi_rows, lo_cols, hi_cols,
    x_ref, sums_ref,
):
    depth, vectors = solved_in.shape[0], solved_in.shape[1]
    half = depth // 2
    lane, row = lane_index(), row_index()
    land = land_ref[...].astype(F32)
    weights = [relax_ref[j : j + 1, :] for j in range(8)]
    halos = (
        north_rows,
        south_rows,
        [east_ref[8 * h : 8 * h + 8, :] for h in range(2)],
        [west_ref[8 * h : 8 * h + 8, :] for h in range(2)],
    )

    def down(i, carry):
        k_low = depth - 1 - i
        values = []
        for side, k, base in ((0, i, i * vectors), (1, k_low, (half - 1 - i) * vectors)):
            a, b = a_ref[k], b_ref[k]
            rates = child_rates_of(rates_ref, k, land)
            for v in range(vectors):
                x = child_cell(solved_in, k, v, base, side, rates, halos, lane, row)
                x_ref[k, v] = x
                y = a * x + b * carry[side * vectors + v]
                solved_ref[k, v] = y
                values.append(y)
            block_rows(x_ref, k, weights, sums_ref, i, side)
        rhs = parent_ref[i] + feed_ref[pl.ds(i * 8, 8), :]
        psolved = pa_ref[pl.ds(i, 1), :] * rhs + pb_ref[pl.ds(i, 1), :] * carry[2 * vectors]
        psolved_ref[i] = psolved
        return tuple(values) + (psolved,)

    blank = jnp.zeros((8, LANES), F32)
    carry = lax.fori_loop(0, half, down, (blank,) * (2 * vectors + 1))
    sums_out[...] = block_columns(sums_ref)
    lines = depth * vectors
    parent_up(carry[-1], pc_ref, psolved_ref, lo_rows, hi_rows, lines, lo_cols, hi_cols, 16)
    child_up(carry[:-1], c_ref, solved_ref, lo_rows, hi_rows, lo_cols, hi_cols)


def child_last(solved_in, rates_ref, land_ref, north_rows, south_rows, east_ref, west_ref, out_ref):
    depth, vectors = solved_in.shape[0], solved_in.shape[1]
    half = depth // 2
    lane, row = lane_index(), row_index()
    land = land_ref[...].astype(F32)
    halos = (
        north_rows,
        south_rows,
        [east_ref[8 * h : 8 * h + 8, :] for h in range(2)],
        [west_ref[8 * h : 8 * h + 8, :] for h in range(2)],
    )

    def level(i, _):
        for side, k in ((0, i), (1, half + i)):
            rates = child_rates_of(rates_ref, k, land)
            for v in range(vectors):
                out_ref[k, v] = child_cell(solved_in, k, v, i * vectors, side, rates, halos, lane, row)
        return 0

    lax.fori_loop(0, half, level, 0)


def parent_prepare(parent_ref, rates_ref, mix_ref, land_ref, after_ref, packed_ref, prates_ref, pa_ref, pb_ref, pc_ref, mixed):
    depth = parent_ref.shape[0]
    half = depth // 2
    places = [(h, r, 64 * h + 32 * r) for h in range(2) for r in range(2)]
    land = jnp.concatenate([land_ref[r : r + 1, :] for _ in range(2) for r in range(2)], axis=1).astype(F32)

    def level(i, _):
        for h, r, lo in places:
            k = depth - 1 - i if h else i
            packed_ref[i, :, lo : lo + 32] = parent_ref[k, :, r, :]
            mixed[pl.ds(i, 1), lo : lo + 32] = mix_ref[k, pl.ds(r, 1), :]
            for d in range(4):
                prates_ref[d + 1, pl.ds(i, 1), lo : lo + 32] = rates_ref[d, k, pl.ds(r, 1), :]
        return 0

    lax.fori_loop(0, half, level, 0)
    land = jnp.broadcast_to(land, (half, LANES))
    sides = [prates_ref[d] for d in range(1, 5)]
    prates_ref[0] = land * (1.0 - (sides[0] + sides[1] + sides[2] + sides[3]))
    for d in range(4):
        prates_ref[d + 1] = land * sides[d]
    upper = lane_index(1) < 64
    rows = [mixed[i : i + 1, :] for i in range(half)]
    inner, outer = [], []
    for i in range(half):
        nearer = rows[i + 1] if i + 1 < half else pltpu.roll(rows[i], 64, 1)
        inner.append(jnp.where(upper, rows[i], nearer))
        outer.append(jnp.where(upper, rows[i - 1] if i else jnp.zeros_like(rows[0]), rows[i]))
    inverse = minors(inner, outer)
    for i in range(half):
        pa_ref[i : i + 1, :] = inverse[i]
        pb_ref[i : i + 1, :] = inverse[i] * outer[i]
        pc_ref[i : i + 1, :] = inverse[i] * inner[i]


def parent_up(carry, pc_ref, psolved_ref, lo_rows, hi_rows, lines, lo_cols, hi_cols, cols_at):
    half = psolved_ref.shape[0]
    lane = lane_index()
    middle = pc_ref[half - 1 : half, :]
    scale = 1.0 / (1.0 - middle * pltpu.roll(middle, 64, 1))
    x = (carry + middle * pltpu.roll(carry, 64, 1)) * scale
    tiles = [None] * half
    tiles[half - 1] = x
    for i in range(half - 2, -1, -1):
        x = psolved_ref[i] + pc_ref[i : i + 1, :] * x
        tiles[i] = x
    lo = hi = jnp.zeros((8, LANES), F32)
    for i in range(half):
        psolved_ref[i] = tiles[i]
        here = (lane & 31) == i
        lo = jnp.where(here, pltpu.roll(tiles[i], i, 1) if i else tiles[i], lo)
        hi = jnp.where(here, pltpu.roll(tiles[i], (i + 97) & 127, 1), hi)
    lo_cols[cols_at : cols_at + 8, :] = lo
    hi_cols[cols_at : cols_at + 8, :] = hi
    first = (lane & 32) == 0
    for j in range(half // 2):
        one, two = tiles[j], tiles[j + half // 2]
        lo_rows[lines + 8 * j : lines + 8 * j + 8, :] = jnp.where(first, one, pltpu.roll(two, 32, 1))
        hi_rows[lines + 8 * j : lines + 8 * j + 8, :] = jnp.where(first, pltpu.roll(one, 96, 1), two)


def parent_transport(psolved_ref, prates_ref, north_rows, south_rows, lines, east, west, i):
    half = psolved_ref.shape[0]
    lane = lane_index()
    x = psolved_ref[i]
    j = i % (half // 2)
    lo = north_rows[lines + 8 * j : lines + 8 * j + 8, :]
    hi = south_rows[lines + 8 * j : lines + 8 * j + 8, :]
    if i < half // 2:
        lo = pltpu.roll(lo, 32, 1)
    else:
        hi = pltpu.roll(hi, 96, 1)
    first = (lane & 32) == 0
    to_north = jnp.where(first, pltpu.roll(x, 96, 1), lo)
    to_south = jnp.where(first, hi, pltpu.roll(x, 32, 1))
    east_edge = pltpu.roll(east, 31 - i, 1)
    west_edge = pltpu.roll(west, (LANES - i) & (LANES - 1), 1) if i else west
    column = lane & 31
    to_east = jnp.where(column == 31, east_edge, pltpu.roll(x, 127, 1))
    to_west = jnp.where(column == 0, west_edge, pltpu.roll(x, 1, 1))
    parts = [prates_ref[d, i : i + 1, :] for d in range(5)]
    return (parts[0] * x + parts[1] * to_east) + (parts[2] * to_west + parts[3] * to_north) + parts[4] * to_south


def parent_second(
    psolved_in, prates_ref, pa_ref, pb_ref, pc_ref, north_rows, south_rows, east_ref, west_ref, feed_ref,
    psolved_ref, lo_rows, hi_rows, lo_cols, hi_cols,
):
    half = psolved_in.shape[0]
    lines = north_rows.shape[0] - lo_rows.shape[0]
    east, west = east_ref[16:24, :], west_ref[16:24, :]
    y = jnp.zeros((8, LANES), F32)
    for i in range(half):
        rhs = parent_transport(psolved_in, prates_ref, north_rows, south_rows, lines, east, west, i)
        rhs = rhs + feed_ref[8 * i : 8 * i + 8, :]
        y = pa_ref[i : i + 1, :] * rhs + pb_ref[i : i + 1, :] * y
        psolved_ref[i] = y
    parent_up(y, pc_ref, psolved_ref, lo_rows, hi_rows, 0, lo_cols, hi_cols, 0)


def parent_last(psolved_in, prates_ref, north_rows, south_rows, east_ref, west_ref, out_ref):
    half = psolved_in.shape[0]
    east, west = east_ref[...], west_ref[...]
    for i in range(half):
        x = parent_transport(psolved_in, prates_ref, north_rows, south_rows, 0, east, west, i)
        for h in range(2):
            for r in range(2):
                lo = 64 * h + 32 * r
                out_ref[2 * half - 1 - i if h else i, :, r, :] = x[:, lo : lo + 32]


def passed_along(value, axis, steps):
    count = lax.axis_size(axis)
    return lax.ppermute(value, axis, [(i, (i + steps) % count) for i in range(count)])


def halos_of(lo_rows, hi_rows, lo_cols, hi_cols):
    north = passed_along(lo_rows, "gy", -1)
    south = passed_along(hi_rows, "gy", 1)
    east = passed_along(lo_cols, "gx", -1)
    west = passed_along(hi_cols, "gx", 1)
    return north, south, east, west


def local(
    child_adjoint,
    parent_adjoint,
    child_rates,
    child_mixing,
    child_land,
    parent_rates,
    parent_mixing,
    parent_land,
    relaxation,
):
    depth, vectors, lines, columns = child_adjoint.shape
    half = depth // 2
    quarter = lax.axis_size("gy") // 4
    field = shape(depth, vectors, lines, columns)
    factor = shape(depth, lines, columns)
    tiles = shape(half, vectors, LANES)
    sums = shape(half * vectors, LANES)
    count = depth * vectors
    sum_scratch = pltpu.VMEM((half * vectors, 4 * LANES), F32)

    sums1, solved, lo_r, hi_r, lo_c, hi_c, a, b, c = call(
        child_first,
        [sums, field, shape(count, LANES), shape(count, LANES), shape(16, LANES), shape(16, LANES), factor, factor, factor],
        [sum_scratch],
        [child_adjoint, child_mixing, relaxation],
        4_000_000,
        3_000_000,
    )
    halos = halos_of(lo_r, hi_r, lo_c, hi_c)
    feed = passed_along(sums1, "gy", quarter)
    packed, prates, pa, pb, pc = call(
        parent_prepare,
        [tiles, shape(5, half, LANES)] + [shape(half, LANES)] * 3,
        [pltpu.VMEM((half, LANES), F32)],
        [parent_adjoint, parent_rates, parent_mixing, parent_land, lo_c],
        1_000_000,
        3_000_000,
    )
    rows = count + half // 2 * vectors
    sums2, solved, psolved, lo_r, hi_r, lo_c, hi_c = call(
        child_second,
        [sums, field, tiles, shape(rows, LANES), shape(rows, LANES), shape(24, LANES), shape(24, LANES)],
        [pltpu.VMEM(field.shape, F32), sum_scratch],
        [solved, a, b, c, child_rates, child_land, relaxation, *halos, packed, pa, pb, pc, feed],
        8_000_000,
        3_000_000,
    )
    halos = halos_of(lo_r, hi_r, lo_c, hi_c)
    feed = passed_along(sums2, "gy", quarter)
    few = half // 2 * vectors
    psolved, lo_r, hi_r, lo_c, hi_c = call(
        parent_second,
        [tiles, shape(few, LANES), shape(few, LANES), shape(8, LANES), shape(8, LANES)],
        [],
        [psolved, prates, pa, pb, pc, *halos, feed],
        1_000_000,
        500_000,
    )
    parent_halos = halos_of(lo_r, hi_r, lo_c, hi_c)
    child_out = call(
        child_last,
        field,
        [],
        [solved, child_rates, child_land, *halos],
        4_000_000,
        3_000_000,
    )
    parent_out = call(
        parent_last,
        shape(*parent_adjoint.shape),
        [],
        [psolved, prates, *parent_halos],
        500_000,
        500_000,
    )
    return (child_out, parent_out)


def solution(mesh):
    wide = P(None, None, "gy", "gx")
    level = P(None, "gy", "gx")
    flat = P("gy", "gx")
    in_specs = (wide, wide, wide, level, flat, wide, level, flat, flat)
    return jax.shard_map(local, mesh=mesh, in_specs=in_specs, out_specs=(wide, wide), check_vma=False)
```

```python
import jax
import jax.numpy as jnp
from jax import lax
from jax.experimental import pallas as pl
from jax.experimental.pallas import tpu as pltpu
from jax.sharding import PartitionSpec as P

F32 = jnp.float32
VMEM = pl.BlockSpec(memory_space=pltpu.VMEM)
ANY = pl.BlockSpec(memory_space=pl.ANY)
LIMIT = 40 * 1024 * 1024
LANES = 128
LEVELS = 8


def shape(*dims):
    return jax.ShapeDtypeStruct(dims, F32)


def call(body, outs, scratch, operands, flops, touched, far_in=(), far_out=False):
    return pl.pallas_call(
        body,
        out_shape=outs,
        in_specs=[ANY if i in far_in else VMEM for i in range(len(operands))],
        out_specs=jax.tree.map(lambda _: ANY if far_out else VMEM, outs),
        scratch_shapes=scratch,
        compiler_params=pltpu.CompilerParams(vmem_limit_bytes=LIMIT),
        cost_estimate=pl.CostEstimate(flops=flops, bytes_accessed=touched, transcendentals=0),
        name=body.__name__,
    )(*operands)


def lane_index(rows=8):
    return lax.broadcasted_iota(jnp.int32, (rows, LANES), 1)


def row_index():
    return lax.broadcasted_iota(jnp.int32, (8, LANES), 0)


def minors(inner, outer):
    theta = delta = jnp.ones_like(inner[0])
    inverse = []
    for i in range(len(inner)):
        delta = theta + outer[i] * delta
        theta_next = delta + inner[i] * theta
        inverse.append(theta / theta_next)
        theta = theta_next
    return inverse


def parity():
    return lax.rem(lax.axis_index("gy"), 2)


def child_factors(mix_ref, keep, a_ref, b_ref, c_ref):
    depth = mix_ref.shape[0]
    half = depth // 2
    zero = jnp.zeros_like(keep)
    top_inner = [mix_ref[i] for i in range(half)]
    top_outer = [zero] + top_inner[:-1]
    low_outer = [mix_ref[depth - 1 - i] for i in range(half)]
    low_inner = [mix_ref[depth - 2 - i] for i in range(half)]
    for levels, inner, outer in (
        (range(half), top_inner, top_outer),
        (range(depth - 1, half - 1, -1), low_inner, low_outer),
    ):
        inverse = minors(inner, outer)
        for i, k in enumerate(levels):
            a_ref[k] = inverse[i] * keep
            b_ref[k] = inverse[i] * outer[i]
            c_ref[k] = inverse[i] * inner[i]


def block_rows(source_ref, k, weights, sums_ref, i, place):
    vectors = source_ref.shape[1]
    for r in range(2):
        total = source_ref[k, :, 4 * r, :] * weights[4 * r]
        for j in range(4 * r + 1, 4 * r + 4):
            total = total + source_ref[k, :, j, :] * weights[j]
        column = (2 * place + r) * LANES
        sums_ref[pl.ds(i * vectors, vectors), column : column + LANES] = total


def block_columns(sums_ref):
    wide = sums_ref.shape[1]
    p = lax.broadcasted_iota(jnp.int32, (wide, LANES), 0)
    q = lax.broadcasted_iota(jnp.int32, (wide, LANES), 1)
    pick = jnp.where(p // 4 == q, F32(0.0625), F32(0.0))
    return jnp.dot(
        sums_ref[...], pick, precision=lax.Precision.HIGHEST, preferred_element_type=F32
    )


def child_middle(carry, c_ref, half):
    vectors = len(carry) // 2
    top, low = c_ref[half - 1], c_ref[half]
    scale = 1.0 / (1.0 - top * low)
    first = [(carry[v] + top * carry[vectors + v]) * scale for v in range(vectors)]
    second = [(carry[vectors + v] + low * carry[v]) * scale for v in range(vectors)]
    return first + second


def child_up(carry, c_ref, solved_ref, mate_rows, far_rows, cols_ref):
    depth, vectors = solved_ref.shape[0], solved_ref.shape[1]
    half = depth // 2
    lane = lane_index()
    pair = lane >> 1
    odd = parity()
    mate_row, far_row = 7 * (1 - odd), 7 * odd

    def emit(i, values, packed):
        k_low = depth - 1 - i
        packed = list(packed)
        inside = i % LEVELS if isinstance(i, int) else lax.rem(i, LEVELS)
        for side, k, base in ((0, i, inside * vectors), (1, k_low, (LEVELS - 1 - inside) * vectors)):
            for v in range(vectors):
                x = values[side * vectors + v]
                solved_ref[k, v] = x
                at = base + v
                packed[side] = jnp.where(pair == at, pltpu.roll(x, 2 * at + 1 & (LANES - 1), 1), packed[side])
            mate_rows[pl.ds(k * vectors, vectors), :] = solved_ref[k, :, mate_row, :]
            far_rows[pl.ds(k * vectors, vectors), :] = solved_ref[k, :, far_row, :]
        return packed

    def up(i, state):
        k_low = depth - 1 - i
        top, low = c_ref[i], c_ref[k_low]
        values = []
        for v in range(vectors):
            values.append(solved_ref[i, v] + top * state[v])
        for v in range(vectors):
            values.append(solved_ref[k_low, v] + low * state[vectors + v])
        return tuple(values) + tuple(emit(i, values, state[2 * vectors :]))

    def keep_columns(group, packed):
        for side, g in ((0, group), (1, depth // LEVELS - 1 - group)):
            cols_ref[LEVELS * g : LEVELS * g + 8, :] = packed[side]

    blank = jnp.zeros((8, LANES), F32)
    values = child_middle(carry, c_ref, half)
    state = tuple(values) + tuple(emit(half - 1, values, [blank] * 2))
    for group in range(half // LEVELS - 1, -1, -1):
        last = LEVELS * (group + 1) - 1
        if group == half // LEVELS - 1:
            last -= 1
        count = last - LEVELS * group + 1
        state = lax.fori_loop(0, count, lambda step, state, last=last: up(last - step, state), state)
        keep_columns(group, state[2 * vectors :])
        state = state[: 2 * vectors] + (blank,) * 2


def child_first(
    x_hbm, mix_hbm, relax_hbm,
    sums_out, solved_ref, mate_rows, far_rows, cols_ref, a_ref, b_ref, c_ref,
    x_ref, mix_ref, relax_ref, sums_ref, sems,
):
    depth, vectors = x_ref.shape[0], x_ref.shape[1]
    half = depth // 2
    small = [
        pltpu.make_async_copy(mix_hbm, mix_ref, sems.at[0]),
        pltpu.make_async_copy(relax_hbm, relax_ref, sems.at[1]),
    ]
    for copy in small:
        copy.start()
    size, large = 4, []
    for start in range(0, half, size):
        for first in (start, depth - size - start):
            part = pl.ds(first, size)
            large.append(pltpu.make_async_copy(x_hbm.at[part], x_ref.at[part], sems.at[len(large) + 2]))
            large[-1].start()
    for copy in small:
        copy.wait()
    child_factors(mix_ref, 1.0 - relax_ref[...], a_ref, b_ref, c_ref)
    weights = [relax_ref[j : j + 1, :] for j in range(8)]

    def down(i, carry):
        k_low = depth - 1 - i
        values = []
        for side, k in ((0, i), (1, k_low)):
            a, b = a_ref[k], b_ref[k]
            for v in range(vectors):
                y = a * x_ref[k, v] + b * carry[side * vectors + v]
                solved_ref[k, v] = y
                values.append(y)
            block_rows(x_ref, k, weights, sums_ref, i, side)
        return tuple(values)

    carry = (jnp.zeros((8, LANES), F32),) * (2 * vectors)
    for part, start in enumerate(range(0, half, size)):
        large[2 * part].wait()
        large[2 * part + 1].wait()
        carry = lax.fori_loop(start, start + size, down, carry)
    sums_out[...] = block_columns(sums_ref)
    child_up(carry, c_ref, solved_ref, mate_rows, far_rows, cols_ref)


def merge_edges(cols_ref, merged_ref, rows):
    count = lax.axis_size("gx")
    at = lax.axis_index("gx")
    east, west = lax.rem(at + 1, count), lax.rem(at + count - 1, count)
    even = (lane_index() & 1) == 0
    for g in range(rows // 8):
        part = pl.ds(8 * g, 8)
        merged_ref[part, :] = jnp.where(even, cols_ref[west, part, :], pltpu.roll(cols_ref[east, part, :], LANES - 2, 1))


def child_halos(mate_ref, far_ref, cols_ref, north_ref, south_ref, merged_ref):
    swap = jnp.broadcast_to(parity(), (8, LANES)) == 1

    def sort(i, _):
        part = pl.ds(pl.multiple_of(8 * i, 8), 8)
        mate, far = mate_ref[part, :], far_ref[part, :]
        north_ref[part, :] = jnp.where(swap, far, mate)
        south_ref[part, :] = jnp.where(swap, mate, far)
        return 0

    lax.fori_loop(0, north_ref.shape[0] // 8, sort, 0, unroll=8)
    merge_edges(cols_ref, merged_ref, merged_ref.shape[0])


def child_cell(solved_ref, k, v, base, edges, rates, north_ref, south_ref, lane, row):
    vectors = solved_ref.shape[1]
    s = solved_ref[k, v]
    line = k * vectors + v
    edge = pltpu.roll(edges, (LANES - 2 * (base + v)) & (LANES - 1), 1)
    north_edge = jnp.broadcast_to(north_ref[pl.ds(line, 1), :], (8, LANES))
    south_edge = jnp.broadcast_to(south_ref[pl.ds(line, 1), :], (8, LANES))
    east = jnp.where(lane == LANES - 1, edge, pltpu.roll(s, LANES - 1, 1))
    west = jnp.where(lane == 0, edge, pltpu.roll(s, 1, 1))
    north = jnp.where(row == 7, north_edge, pltpu.roll(s, 7, 0))
    south = jnp.where(row == 0, south_edge, pltpu.roll(s, 1, 0))
    return (rates[0] * s + rates[1] * east) + (rates[2] * west + rates[3] * north) + rates[4] * south


def child_second(
    solved_in, a_ref, b_ref, c_ref, rates_ref, relax_ref, mate_in, far_in, cols_in,
    parent_ref, pa_ref, pb_ref, pc_ref, feed_ref,
    sums_out, solved_ref, psolved_ref, mate_rows, far_rows, cols_ref,
    x_ref, sums_ref, north_ref, south_ref, merged_ref,
):
    depth, vectors = solved_in.shape[0], solved_in.shape[1]
    half = depth // 2
    groups = depth // LEVELS
    lane, row = lane_index(), row_index()
    weights = [relax_ref[j : j + 1, :] for j in range(8)]
    child_halos(mate_in, far_in, cols_in, north_ref, south_ref, merged_ref)

    def down(i, carry, edges):
        k_low = depth - 1 - i
        inside = lax.rem(i, LEVELS)
        values = []
        for side, k, base in ((0, i, inside * vectors), (1, k_low, (LEVELS - 1 - inside) * vectors)):
            a, b = a_ref[k], b_ref[k]
            rates = [rates_ref[d, k] for d in range(5)]
            for v in range(vectors):
                x = child_cell(solved_in, k, v, base, edges[side], rates, north_ref, south_ref, lane, row)
                x_ref[k, v] = x
                y = a * x + b * carry[side * vectors + v]
                solved_ref[k, v] = y
                values.append(y)
            block_rows(x_ref, k, weights, sums_ref, i, side)
        rhs = parent_ref[i] + feed_ref[pl.ds(i * 8, 8), :]
        psolved = pa_ref[pl.ds(i, 1), :] * rhs + pb_ref[pl.ds(i, 1), :] * carry[2 * vectors]
        psolved_ref[i] = psolved
        return tuple(values) + (psolved,)

    carry = (jnp.zeros((8, LANES), F32),) * (2 * vectors + 1)
    for group in range(half // LEVELS):
        edges = [merged_ref[8 * g : 8 * g + 8, :] for g in (group, groups - 1 - group)]
        carry = lax.fori_loop(
            LEVELS * group, LEVELS * (group + 1), lambda i, carry, edges=edges: down(i, carry, edges), carry
        )
    sums_out[...] = block_columns(sums_ref)
    parent_up(carry[-1], pc_ref, psolved_ref, mate_rows, far_rows, depth * vectors, cols_ref, 8 * groups)
    child_up(carry[:-1], c_ref, solved_ref, mate_rows, far_rows, cols_ref)


def child_last(
    solved_in, rates_ref, mate_in, far_in, cols_in, out_hbm, out_ref, north_ref, south_ref, merged_ref, sems
):
    depth, vectors = solved_in.shape[0], solved_in.shape[1]
    lane, row = lane_index(), row_index()
    child_halos(mate_in, far_in, cols_in, north_ref, south_ref, merged_ref)
    copies = []
    for group in range(depth // LEVELS):
        edges = merged_ref[8 * group : 8 * group + 8, :]

        def level(inside, _):
            k = LEVELS * group + inside
            rates = [rates_ref[d, k] for d in range(5)]
            for v in range(vectors):
                out_ref[k, v] = child_cell(
                    solved_in, k, v, inside * vectors, edges, rates, north_ref, south_ref, lane, row
                )
            return 0

        lax.fori_loop(0, LEVELS, level, 0)
        part = pl.ds(LEVELS * group, LEVELS)
        copies.append(pltpu.make_async_copy(out_ref.at[part], out_hbm.at[part], sems.at[group]))
        copies[-1].start()
    for copy in copies:
        copy.wait()


def prepare(
    parent_ref, rates_ref, mix_ref, land_ref, child_rates_ref, child_land_ref, after_ref,
    packed_ref, prates_ref, pa_ref, pb_ref, pc_ref, child_out_ref, mixed,
):
    depth = child_rates_ref.shape[1]
    vectors = packed_ref.shape[1]
    half = depth // 2
    places = [(h, r, 64 * h + 32 * r) for h in range(2) for r in range(2)]
    land = jnp.concatenate([land_ref[r : r + 1, :] for _ in range(2) for r in range(2)], axis=1).astype(F32)

    def level(i, _):
        for h, r, lo in places:
            k = depth - 1 - i if h else i
            packed_ref[i, :, lo : lo + 32] = parent_ref[pl.ds(2 * vectors * k + r, vectors, stride=2), :]
            mixed[pl.ds(i, 1), lo : lo + 32] = mix_ref[pl.ds(2 * k + r, 1), :]
            for d in range(4):
                prates_ref[d + 1, pl.ds(i, 1), lo : lo + 32] = rates_ref[pl.ds(2 * (d * depth + k) + r, 1), :]
        return 0

    lax.fori_loop(0, half, level, 0)
    land = jnp.broadcast_to(land, (half, LANES))
    sides = [prates_ref[d] for d in range(1, 5)]
    prates_ref[0] = land * (1.0 - (sides[0] + sides[1] + sides[2] + sides[3]))
    for d in range(4):
        prates_ref[d + 1] = land * sides[d]
    upper = lane_index(1) < 64
    rows = [mixed[i : i + 1, :] for i in range(half)]
    inner, outer = [], []
    for i in range(half):
        nearer = rows[i + 1] if i + 1 < half else pltpu.roll(rows[i], 64, 1)
        inner.append(jnp.where(upper, rows[i], nearer))
        outer.append(jnp.where(upper, rows[i - 1] if i else jnp.zeros_like(rows[0]), rows[i]))
    inverse = minors(inner, outer)
    for i in range(half):
        pa_ref[i : i + 1, :] = inverse[i]
        pb_ref[i : i + 1, :] = inverse[i] * outer[i]
        pc_ref[i : i + 1, :] = inverse[i] * inner[i]
    child_land = child_land_ref[...].astype(F32)

    def child_level(k, _):
        sides = [child_rates_ref[d, k] for d in range(4)]
        child_out_ref[0, k] = child_land * (1.0 - (sides[0] + sides[1] + sides[2] + sides[3]))
        for d in range(4):
            child_out_ref[d + 1, k] = child_land * sides[d]
        return 0

    lax.fori_loop(0, depth, child_level, 0, unroll=4)


def parent_up(carry, pc_ref, psolved_ref, mate_rows, far_rows, lines, cols_ref, cols_at):
    half = psolved_ref.shape[0]
    lane = lane_index()
    middle = pc_ref[half - 1 : half, :]
    scale = 1.0 / (1.0 - middle * pltpu.roll(middle, 64, 1))
    x = (carry + middle * pltpu.roll(carry, 64, 1)) * scale
    tiles = [None] * half
    tiles[half - 1] = x
    for i in range(half - 2, -1, -1):
        x = psolved_ref[i] + pc_ref[i : i + 1, :] * x
        tiles[i] = x
    packed = jnp.zeros((8, LANES), F32)
    for i in range(half):
        psolved_ref[i] = tiles[i]
        packed = jnp.where(((lane & 31) >> 1) == i, pltpu.roll(tiles[i], 2 * i + 1, 1), packed)
    cols_ref[cols_at : cols_at + 8, :] = packed
    first = (lane & 32) == 0
    swap = jnp.broadcast_to(parity(), (8, LANES)) == 1
    for j in range(half // 2):
        one, two = tiles[j], tiles[j + half // 2]
        lo = jnp.where(first, one, pltpu.roll(two, 32, 1))
        hi = jnp.where(first, pltpu.roll(one, 96, 1), two)
        part = slice(lines + 8 * j, lines + 8 * j + 8)
        mate_rows[part, :] = jnp.where(swap, lo, hi)
        far_rows[part, :] = jnp.where(swap, hi, lo)


def parent_edges(cols_ref, at):
    count = lax.axis_size("gx")
    here = lax.axis_index("gx")
    east, west = lax.rem(here + 1, count), lax.rem(here + count - 1, count)
    part = slice(at, at + 8)
    even = (lane_index() & 1) == 0
    return jnp.where(even, cols_ref[west, part, :], pltpu.roll(cols_ref[east, part, :], 62, 1))


def parent_transport(psolved_ref, prates_ref, mate_row, far_row, edges, i):
    half = psolved_ref.shape[0]
    lane = lane_index()
    swap = jnp.broadcast_to(parity(), (8, LANES)) == 1
    x = psolved_ref[i]
    mate, far = mate_row(i % (half // 2)), far_row(i % (half // 2))
    lo, hi = jnp.where(swap, far, mate), jnp.where(swap, mate, far)
    if i < half // 2:
        lo = pltpu.roll(lo, 32, 1)
    else:
        hi = pltpu.roll(hi, 96, 1)
    first = (lane & 32) == 0
    to_north = jnp.where(first, pltpu.roll(x, 96, 1), lo)
    to_south = jnp.where(first, hi, pltpu.roll(x, 32, 1))
    edge = pltpu.roll(edges, (LANES - 2 * i - 32) & (LANES - 1), 1)
    column = lane & 31
    to_east = jnp.where(column == 31, edge, pltpu.roll(x, 127, 1))
    to_west = jnp.where(column == 0, edge, pltpu.roll(x, 1, 1))
    parts = [prates_ref[d, i : i + 1, :] for d in range(5)]
    return (parts[0] * x + parts[1] * to_east) + (parts[2] * to_west + parts[3] * to_north) + parts[4] * to_south


def parent_second(
    psolved_in, prates_ref, pa_ref, pb_ref, pc_ref, mate_in, far_in, cols_in, feed_ref,
    psolved_ref, mate_rows, far_rows, cols_ref,
):
    half = psolved_in.shape[0]
    lines = mate_in.shape[0] - mate_rows.shape[0]
    edges = parent_edges(cols_in, cols_in.shape[1] - 8)
    mate = lambda j: mate_in[lines + 8 * j : lines + 8 * j + 8, :]
    far = lambda j: far_in[lines + 8 * j : lines + 8 * j + 8, :]
    y = jnp.zeros((8, LANES), F32)
    for i in range(half):
        rhs = parent_transport(psolved_in, prates_ref, mate, far, edges, i)
        rhs = rhs + feed_ref[8 * i : 8 * i + 8, :]
        y = pa_ref[i : i + 1, :] * rhs + pb_ref[i : i + 1, :] * y
        psolved_ref[i] = y
    parent_up(y, pc_ref, psolved_ref, mate_rows, far_rows, 0, cols_ref, 0)


def parent_last(psolved_in, prates_ref, mate_in, far_in, cols_in, out_ref):
    half, vectors = psolved_in.shape[0], psolved_in.shape[1]
    edges = parent_edges(cols_in, 0)
    odd = parity()
    mate = lambda j: mate_in[1 - odd, 8 * j : 8 * j + 8, :]
    far = lambda j: far_in[odd, 8 * j : 8 * j + 8, :]
    for i in range(half):
        x = parent_transport(psolved_in, prates_ref, mate, far, edges, i)
        for h in range(2):
            for r in range(2):
                lo = 64 * h + 32 * r
                k = 2 * half - 1 - i if h else i
                out_ref[pl.ds(2 * vectors * k + r, vectors, stride=2), :] = x[:, lo : lo + 32]


def passed_along(value, axis, steps):
    count = lax.axis_size(axis)
    return lax.ppermute(value, axis, [(i, (i + steps) % count) for i in range(count)])


def couples(count):
    mates = [[i, i + 1] for i in range(0, count, 2)]
    fars = [[i, (i + 1) % count] for i in range(1, count, 2)]
    return mates, fars


def swapped(value, groups):
    return lax.ppermute(value, "gy", [pair for a, b in groups for pair in ((a, b), (b, a))])


def local(
    child_adjoint,
    parent_adjoint,
    child_rates,
    child_mixing,
    child_land,
    parent_rates,
    parent_mixing,
    parent_land,
    relaxation,
):
    depth, vectors, lines, columns = child_adjoint.shape
    half = depth // 2
    quarter = lax.axis_size("gy") // 4
    mates, fars = couples(lax.axis_size("gy"))
    field = shape(depth, vectors, lines, columns)
    factor = shape(depth, lines, columns)
    tiles = shape(half, vectors, LANES)
    sums = shape(half * vectors, LANES)
    count = depth * vectors
    edge = depth // LEVELS * 8
    sum_scratch = pltpu.VMEM((half * vectors, 4 * LANES), F32)
    halo_scratch = [pltpu.VMEM((count, LANES), F32), pltpu.VMEM((count, LANES), F32), pltpu.VMEM((edge, LANES), F32)]
    narrow = parent_adjoint.shape[-1]

    sums1, solved, mate, far, cols, a, b, c = call(
        child_first,
        [sums, field, shape(count, LANES), shape(count, LANES), shape(edge, LANES), factor, factor, factor],
        [
            pltpu.VMEM(field.shape, F32),
            pltpu.VMEM(factor.shape, F32),
            pltpu.VMEM((lines, columns), F32),
            sum_scratch,
            pltpu.SemaphoreType.DMA((2 + half // 2,)),
        ],
        [child_adjoint, child_mixing, relaxation],
        4_000_000,
        3_000_000,
        far_in=(0, 1, 2),
    )
    all_cols = lax.all_gather(cols, "gx")
    mate_in, far_in = swapped(mate, mates), swapped(far, fars)
    feed = passed_along(sums1, "gy", quarter)
    packed, prates, pa, pb, pc, rates = call(
        prepare,
        [tiles, shape(5, half, LANES)] + [shape(half, LANES)] * 3 + [shape(5, depth, lines, columns)],
        [pltpu.VMEM((half, LANES), F32)],
        [
            parent_adjoint.reshape(-1, narrow),
            parent_rates.reshape(-1, narrow),
            parent_mixing.reshape(-1, narrow),
            parent_land,
            child_rates,
            child_land,
            cols,
        ],
        1_000_000,
        3_000_000,
    )
    rows = count + half // 2 * vectors
    sums2, solved, psolved, mate, far, cols = call(
        child_second,
        [sums, field, tiles, shape(rows, LANES), shape(rows, LANES), shape(edge + 8, LANES)],
        [pltpu.VMEM(field.shape, F32), sum_scratch] + halo_scratch,
        [solved, a, b, c, rates, relaxation, mate_in, far_in, all_cols, packed, pa, pb, pc, feed],
        8_000_000,
        3_000_000,
    )
    all_cols = lax.all_gather(cols, "gx")
    mate_in, far_in = swapped(mate, mates), swapped(far, fars)
    feed = passed_along(sums2, "gy", quarter)
    few = half // 2 * vectors
    psolved, mate, far, cols = call(
        parent_second,
        [tiles, shape(few, LANES), shape(few, LANES), shape(8, LANES)],
        [],
        [psolved, prates, pa, pb, pc, mate_in, far_in, all_cols, feed],
        1_000_000,
        500_000,
    )
    last_cols = lax.all_gather(cols, "gx")
    last_mate = lax.all_gather(mate, "gy", axis_index_groups=mates)
    last_far = lax.all_gather(far, "gy", axis_index_groups=fars)
    child_out = call(
        child_last,
        field,
        [pltpu.VMEM(field.shape, F32)] + halo_scratch + [pltpu.SemaphoreType.DMA((depth // LEVELS,))],
        [solved, rates, mate_in, far_in, all_cols],
        4_000_000,
        3_000_000,
        far_out=True,
    )
    parent_out = call(
        parent_last,
        shape(depth * vectors * 2, narrow),
        [],
        [psolved, prates, last_mate, last_far, last_cols],
        500_000,
        500_000,
    )
    return (child_out, parent_out.reshape(parent_adjoint.shape))


def solution(mesh):
    wide = P(None, None, "gy", "gx")
    level = P(None, "gy", "gx")
    flat = P("gy", "gx")
    in_specs = (wide, wide, wide, level, flat, wide, level, flat, flat)
    return jax.shard_map(local, mesh=mesh, in_specs=in_specs, out_specs=(wide, wide), check_vma=False)
```

```python
import jax
import jax.numpy as jnp
from jax import lax
from jax.experimental import pallas as pl
from jax.experimental.pallas import tpu as pltpu
from jax.sharding import PartitionSpec as P

F32 = jnp.float32
VMEM = pl.BlockSpec(memory_space=pltpu.VMEM)
FAR = pl.BlockSpec(memory_space=pltpu.HBM)
LIMIT = 40 * 1024 * 1024
LANES = 128
LEVELS = 8


def shape(*dims):
    return jax.ShapeDtypeStruct(dims, F32)


def call(body, outs, scratch, operands, flops, touched, far_in=(), far_out=False):
    return pl.pallas_call(
        body,
        out_shape=outs,
        in_specs=[FAR if i in far_in else VMEM for i in range(len(operands))],
        out_specs=jax.tree.map(lambda _: FAR if far_out else VMEM, outs),
        scratch_shapes=scratch,
        compiler_params=pltpu.CompilerParams(vmem_limit_bytes=LIMIT),
        cost_estimate=pl.CostEstimate(flops=flops, bytes_accessed=touched, transcendentals=0),
        name=body.__name__,
    )(*operands)


def lane_index(rows=8):
    return lax.broadcasted_iota(jnp.int32, (rows, LANES), 1)


def row_index():
    return lax.broadcasted_iota(jnp.int32, (8, LANES), 0)


def minors(inner, outer):
    theta = delta = jnp.ones_like(inner[0])
    inverse = []
    for i in range(len(inner)):
        delta = theta + outer[i] * delta
        theta_next = delta + inner[i] * theta
        inverse.append(theta / theta_next)
        theta = theta_next
    return inverse


def parity(axis):
    return lax.rem(lax.axis_index(axis), 2)


def child_factors(mix_ref, keep, a_ref, b_ref, c_ref):
    depth = mix_ref.shape[0]
    half = depth // 2
    zero = jnp.zeros_like(keep)
    top_inner = [mix_ref[i] for i in range(half)]
    top_outer = [zero] + top_inner[:-1]
    low_outer = [mix_ref[depth - 1 - i] for i in range(half)]
    low_inner = [mix_ref[depth - 2 - i] for i in range(half)]
    for levels, inner, outer in (
        (range(half), top_inner, top_outer),
        (range(depth - 1, half - 1, -1), low_inner, low_outer),
    ):
        inverse = minors(inner, outer)
        for i, k in enumerate(levels):
            a_ref[k] = inverse[i] * keep
            b_ref[k] = inverse[i] * outer[i]
            c_ref[k] = inverse[i] * inner[i]


def block_rows(source_ref, k, weights, sums_ref, i, place):
    vectors = source_ref.shape[1]
    for r in range(2):
        total = source_ref[k, :, 4 * r, :] * weights[4 * r]
        for j in range(4 * r + 1, 4 * r + 4):
            total = total + source_ref[k, :, j, :] * weights[j]
        column = (2 * place + r) * LANES
        sums_ref[pl.ds(i * vectors, vectors), column : column + LANES] = total


def block_columns(sums_ref):
    wide = sums_ref.shape[1]
    p = lax.broadcasted_iota(jnp.int32, (wide, LANES), 0)
    q = lax.broadcasted_iota(jnp.int32, (wide, LANES), 1)
    pick = jnp.where(p // 4 == q, F32(0.0625), F32(0.0))
    return jnp.dot(
        sums_ref[...], pick, precision=lax.Precision.HIGHEST, preferred_element_type=F32
    )


def child_middle(carry, c_ref, half):
    vectors = len(carry) // 2
    top, low = c_ref[half - 1], c_ref[half]
    scale = 1.0 / (1.0 - top * low)
    first = [(carry[v] + top * carry[vectors + v]) * scale for v in range(vectors)]
    second = [(carry[vectors + v] + low * carry[v]) * scale for v in range(vectors)]
    return first + second


def child_up(carry, c_ref, solved_ref, mate_rows, far_rows, cols_ref):
    depth, vectors = solved_ref.shape[0], solved_ref.shape[1]
    half = depth // 2
    lane = lane_index()
    pair = lane >> 1
    odd = parity("gy")
    mate_row, far_row = 7 * (1 - odd), 7 * odd

    def emit(i, values, packed):
        k_low = depth - 1 - i
        packed = list(packed)
        inside = i % LEVELS if isinstance(i, int) else lax.rem(i, LEVELS)
        for side, k, base in ((0, i, inside * vectors), (1, k_low, (LEVELS - 1 - inside) * vectors)):
            for v in range(vectors):
                x = values[side * vectors + v]
                solved_ref[k, v] = x
                at = base + v
                packed[side] = jnp.where(pair == at, pltpu.roll(x, 2 * at + 1 & (LANES - 1), 1), packed[side])
            mate_rows[pl.ds(k * vectors, vectors), :] = solved_ref[k, :, mate_row, :]
            far_rows[pl.ds(k * vectors, vectors), :] = solved_ref[k, :, far_row, :]
        return packed

    def up(i, state):
        k_low = depth - 1 - i
        top, low = c_ref[i], c_ref[k_low]
        values = []
        for v in range(vectors):
            values.append(solved_ref[i, v] + top * state[v])
        for v in range(vectors):
            values.append(solved_ref[k_low, v] + low * state[vectors + v])
        return tuple(values) + tuple(emit(i, values, state[2 * vectors :]))

    def keep_columns(group, packed):
        for side, g in ((0, group), (1, depth // LEVELS - 1 - group)):
            cols_ref[LEVELS * g : LEVELS * g + 8, :] = packed[side]

    blank = jnp.zeros((8, LANES), F32)
    values = child_middle(carry, c_ref, half)
    state = tuple(values) + tuple(emit(half - 1, values, [blank] * 2))
    for group in range(half // LEVELS - 1, -1, -1):
        last = LEVELS * (group + 1) - 1
        if group == half // LEVELS - 1:
            last -= 1
        count = last - LEVELS * group + 1
        state = lax.fori_loop(0, count, lambda step, state, last=last: up(last - step, state), state, unroll=4 if count % 4 == 0 else count)
        keep_columns(group, state[2 * vectors :])
        state = state[: 2 * vectors] + (blank,) * 2


def child_first(
    x_hbm, mix_hbm, relax_hbm,
    sums_out, solved_ref, mate_rows, far_rows, cols_ref, a_ref, b_ref, c_ref,
    x_ref, mix_ref, relax_ref, sums_ref, sems,
):
    depth, vectors = x_ref.shape[0], x_ref.shape[1]
    half = depth // 2
    small = [
        pltpu.make_async_copy(mix_hbm, mix_ref, sems.at[0]),
        pltpu.make_async_copy(relax_hbm, relax_ref, sems.at[1]),
    ]
    for copy in small:
        copy.start()
    size, large = 4, []
    for start in range(0, half, size):
        for first in (start, depth - size - start):
            part = pl.ds(first, size)
            large.append(pltpu.make_async_copy(x_hbm.at[part], x_ref.at[part], sems.at[len(large) + 2]))
            large[-1].start()
    for copy in small:
        copy.wait()
    child_factors(mix_ref, 1.0 - relax_ref[...], a_ref, b_ref, c_ref)
    weights = [relax_ref[j : j + 1, :] for j in range(8)]

    def down(i, carry):
        k_low = depth - 1 - i
        values = []
        for side, k in ((0, i), (1, k_low)):
            a, b = a_ref[k], b_ref[k]
            for v in range(vectors):
                y = a * x_ref[k, v] + b * carry[side * vectors + v]
                solved_ref[k, v] = y
                values.append(y)
            block_rows(x_ref, k, weights, sums_ref, i, side)
        return tuple(values)

    carry = (jnp.zeros((8, LANES), F32),) * (2 * vectors)
    for part, start in enumerate(range(0, half, size)):
        large[2 * part].wait()
        large[2 * part + 1].wait()
        carry = lax.fori_loop(start, start + size, down, carry, unroll=size)
    sums_out[...] = block_columns(sums_ref)
    child_up(carry, c_ref, solved_ref, mate_rows, far_rows, cols_ref)


def merge_edges(mate, far, turn):
    swap = jnp.broadcast_to(parity("gx"), (8, LANES)) == 1
    east, west = jnp.where(swap, far, mate), jnp.where(swap, mate, far)
    return jnp.where((lane_index() & 1) == 0, west, pltpu.roll(east, turn, 1))


def child_halos(mate_ref, far_ref, north_ref, south_ref, mate_cols, far_cols, merged_ref):
    swap = jnp.broadcast_to(parity("gy"), (8, LANES)) == 1

    def sort(i, _):
        part = pl.ds(pl.multiple_of(8 * i, 8), 8)
        mate, far = mate_ref[part, :], far_ref[part, :]
        north_ref[part, :] = jnp.where(swap, far, mate)
        south_ref[part, :] = jnp.where(swap, mate, far)
        return 0

    lax.fori_loop(0, north_ref.shape[0] // 8, sort, 0, unroll=8)
    for g in range(merged_ref.shape[0] // 8):
        part = slice(8 * g, 8 * g + 8)
        merged_ref[part, :] = merge_edges(mate_cols[part, :], far_cols[part, :], LANES - 2)


def child_cell(solved_ref, k, v, base, edges, rates, north_ref, south_ref, lane, row):
    vectors = solved_ref.shape[1]
    s = solved_ref[k, v]
    line = k * vectors + v
    edge = pltpu.roll(edges, (LANES - 2 * (base + v)) & (LANES - 1), 1)
    north_edge = jnp.broadcast_to(north_ref[pl.ds(line, 1), :], (8, LANES))
    south_edge = jnp.broadcast_to(south_ref[pl.ds(line, 1), :], (8, LANES))
    east = jnp.where(lane == LANES - 1, edge, pltpu.roll(s, LANES - 1, 1))
    west = jnp.where(lane == 0, edge, pltpu.roll(s, 1, 1))
    north = jnp.where(row == 7, north_edge, pltpu.roll(s, 7, 0))
    south = jnp.where(row == 0, south_edge, pltpu.roll(s, 1, 0))
    return (rates[0] * s + rates[1] * east) + (rates[2] * west + rates[3] * north) + rates[4] * south


def child_second(
    solved_in, a_ref, b_ref, c_ref, rates_ref, relax_ref, mate_in, far_in, mate_cols, far_cols,
    parent_ref, pa_ref, pb_ref, pc_ref, feed_ref,
    sums_out, solved_ref, psolved_ref, mate_rows, far_rows, cols_ref,
    x_ref, sums_ref, north_ref, south_ref, merged_ref,
):
    depth, vectors = solved_in.shape[0], solved_in.shape[1]
    half = depth // 2
    groups = depth // LEVELS
    lane, row = lane_index(), row_index()
    weights = [relax_ref[j : j + 1, :] for j in range(8)]
    child_halos(mate_in, far_in, north_ref, south_ref, mate_cols, far_cols, merged_ref)

    def down(i, carry, edges):
        k_low = depth - 1 - i
        inside = lax.rem(i, LEVELS)
        values = []
        for side, k, base in ((0, i, inside * vectors), (1, k_low, (LEVELS - 1 - inside) * vectors)):
            a, b = a_ref[k], b_ref[k]
            rates = [rates_ref[d, k] for d in range(5)]
            for v in range(vectors):
                x = child_cell(solved_in, k, v, base, edges[side], rates, north_ref, south_ref, lane, row)
                x_ref[k, v] = x
                y = a * x + b * carry[side * vectors + v]
                solved_ref[k, v] = y
                values.append(y)
            block_rows(x_ref, k, weights, sums_ref, i, side)
        rhs = parent_ref[i] + feed_ref[pl.ds(i * 8, 8), :]
        psolved = pa_ref[pl.ds(i, 1), :] * rhs + pb_ref[pl.ds(i, 1), :] * carry[2 * vectors]
        psolved_ref[i] = psolved
        return tuple(values) + (psolved,)

    carry = (jnp.zeros((8, LANES), F32),) * (2 * vectors + 1)
    for group in range(half // LEVELS):
        edges = [merged_ref[8 * g : 8 * g + 8, :] for g in (group, groups - 1 - group)]
        carry = lax.fori_loop(
            LEVELS * group, LEVELS * (group + 1), lambda i, carry, edges=edges: down(i, carry, edges), carry, unroll=4
        )
    sums_out[...] = block_columns(sums_ref)
    parent_up(carry[-1], pc_ref, psolved_ref, mate_rows, far_rows, depth * vectors, cols_ref, 8 * groups)
    child_up(carry[:-1], c_ref, solved_ref, mate_rows, far_rows, cols_ref)


def child_last(
    solved_in, rates_ref, mate_in, far_in, mate_cols, far_cols, out_hbm, out_ref, north_ref, south_ref, merged_ref, sems
):
    depth, vectors = solved_in.shape[0], solved_in.shape[1]
    lane, row = lane_index(), row_index()
    child_halos(mate_in, far_in, north_ref, south_ref, mate_cols, far_cols, merged_ref)
    copies = []
    for group in range(depth // LEVELS):
        edges = merged_ref[8 * group : 8 * group + 8, :]

        def level(inside, _):
            k = LEVELS * group + inside
            rates = [rates_ref[d, k] for d in range(5)]
            for v in range(vectors):
                out_ref[k, v] = child_cell(
                    solved_in, k, v, inside * vectors, edges, rates, north_ref, south_ref, lane, row
                )
            return 0

        lax.fori_loop(0, LEVELS, level, 0, unroll=4)
        part = pl.ds(LEVELS * group, LEVELS)
        copies.append(pltpu.make_async_copy(out_ref.at[part], out_hbm.at[part], sems.at[group]))
        copies[-1].start()
    for copy in copies:
        copy.wait()


def prepare(
    parent_ref, rates_ref, mix_ref, land_ref, child_rates_ref, child_land_ref, after_ref,
    packed_ref, prates_ref, pa_ref, pb_ref, pc_ref, child_out_ref, mixed,
):
    depth = child_rates_ref.shape[1]
    vectors = packed_ref.shape[1]
    half = depth // 2
    places = [(h, r, 64 * h + 32 * r) for h in range(2) for r in range(2)]
    land = jnp.concatenate([land_ref[r : r + 1, :] for _ in range(2) for r in range(2)], axis=1).astype(F32)

    def level(i, _):
        for h, r, lo in places:
            k = depth - 1 - i if h else i
            packed_ref[i, :, lo : lo + 32] = parent_ref[pl.ds(2 * vectors * k + r, vectors, stride=2), :]
            mixed[pl.ds(i, 1), lo : lo + 32] = mix_ref[pl.ds(2 * k + r, 1), :]
            for d in range(4):
                prates_ref[d + 1, pl.ds(i, 1), lo : lo + 32] = rates_ref[pl.ds(2 * (d * depth + k) + r, 1), :]
        return 0

    lax.fori_loop(0, half, level, 0)
    land = jnp.broadcast_to(land, (half, LANES))
    sides = [prates_ref[d] for d in range(1, 5)]
    prates_ref[0] = land * (1.0 - (sides[0] + sides[1] + sides[2] + sides[3]))
    for d in range(4):
        prates_ref[d + 1] = land * sides[d]
    upper = lane_index(1) < 64
    rows = [mixed[i : i + 1, :] for i in range(half)]
    inner, outer = [], []
    for i in range(half):
        nearer = rows[i + 1] if i + 1 < half else pltpu.roll(rows[i], 64, 1)
        inner.append(jnp.where(upper, rows[i], nearer))
        outer.append(jnp.where(upper, rows[i - 1] if i else jnp.zeros_like(rows[0]), rows[i]))
    inverse = minors(inner, outer)
    for i in range(half):
        pa_ref[i : i + 1, :] = inverse[i]
        pb_ref[i : i + 1, :] = inverse[i] * outer[i]
        pc_ref[i : i + 1, :] = inverse[i] * inner[i]
    child_land = child_land_ref[...].astype(F32)

    def child_level(k, _):
        sides = [child_rates_ref[d, k] for d in range(4)]
        child_out_ref[0, k] = child_land * (1.0 - (sides[0] + sides[1] + sides[2] + sides[3]))
        for d in range(4):
            child_out_ref[d + 1, k] = child_land * sides[d]
        return 0

    lax.fori_loop(0, depth, child_level, 0, unroll=4)


def parent_up(carry, pc_ref, psolved_ref, mate_rows, far_rows, lines, cols_ref, cols_at):
    half = psolved_ref.shape[0]
    lane = lane_index()
    middle = pc_ref[half - 1 : half, :]
    scale = 1.0 / (1.0 - middle * pltpu.roll(middle, 64, 1))
    x = (carry + middle * pltpu.roll(carry, 64, 1)) * scale
    tiles = [None] * half
    tiles[half - 1] = x
    for i in range(half - 2, -1, -1):
        x = psolved_ref[i] + pc_ref[i : i + 1, :] * x
        tiles[i] = x
    packed = jnp.zeros((8, LANES), F32)
    for i in range(half):
        psolved_ref[i] = tiles[i]
        packed = jnp.where(((lane & 31) >> 1) == i, pltpu.roll(tiles[i], 2 * i + 1, 1), packed)
    cols_ref[cols_at : cols_at + 8, :] = packed
    first = (lane & 32) == 0
    swap = jnp.broadcast_to(parity("gy"), (8, LANES)) == 1
    for j in range(half // 2):
        one, two = tiles[j], tiles[j + half // 2]
        lo = jnp.where(first, one, pltpu.roll(two, 32, 1))
        hi = jnp.where(first, pltpu.roll(one, 96, 1), two)
        part = slice(lines + 8 * j, lines + 8 * j + 8)
        mate_rows[part, :] = jnp.where(swap, lo, hi)
        far_rows[part, :] = jnp.where(swap, hi, lo)


def parent_edges(mate_cols, far_cols, at):
    return merge_edges(mate_cols[at : at + 8, :], far_cols[at : at + 8, :], 62)


def parent_transport(psolved_ref, prates_ref, mate_row, far_row, edges, i):
    half = psolved_ref.shape[0]
    lane = lane_index()
    swap = jnp.broadcast_to(parity("gy"), (8, LANES)) == 1
    x = psolved_ref[i]
    mate, far = mate_row(i % (half // 2)), far_row(i % (half // 2))
    lo, hi = jnp.where(swap, far, mate), jnp.where(swap, mate, far)
    if i < half // 2:
        lo = pltpu.roll(lo, 32, 1)
    else:
        hi = pltpu.roll(hi, 96, 1)
    first = (lane & 32) == 0
    to_north = jnp.where(first, pltpu.roll(x, 96, 1), lo)
    to_south = jnp.where(first, hi, pltpu.roll(x, 32, 1))
    edge = pltpu.roll(edges, (LANES - 2 * i - 32) & (LANES - 1), 1)
    column = lane & 31
    to_east = jnp.where(column == 31, edge, pltpu.roll(x, 127, 1))
    to_west = jnp.where(column == 0, edge, pltpu.roll(x, 1, 1))
    parts = [prates_ref[d, i : i + 1, :] for d in range(5)]
    return (parts[0] * x + parts[1] * to_east) + (parts[2] * to_west + parts[3] * to_north) + parts[4] * to_south


def parent_second(
    psolved_in, prates_ref, pa_ref, pb_ref, pc_ref, mate_in, far_in, mate_cols, far_cols, feed_ref,
    psolved_ref, mate_rows, far_rows, cols_ref,
):
    half = psolved_in.shape[0]
    lines = mate_in.shape[0] - mate_rows.shape[0]
    edges = parent_edges(mate_cols, far_cols, mate_cols.shape[0] - 8)
    mate = lambda j: mate_in[lines + 8 * j : lines + 8 * j + 8, :]
    far = lambda j: far_in[lines + 8 * j : lines + 8 * j + 8, :]
    y = jnp.zeros((8, LANES), F32)
    for i in range(half):
        rhs = parent_transport(psolved_in, prates_ref, mate, far, edges, i)
        rhs = rhs + feed_ref[8 * i : 8 * i + 8, :]
        y = pa_ref[i : i + 1, :] * rhs + pb_ref[i : i + 1, :] * y
        psolved_ref[i] = y
    parent_up(y, pc_ref, psolved_ref, mate_rows, far_rows, 0, cols_ref, 0)


def parent_last(psolved_in, prates_ref, mate_in, far_in, mate_cols, far_cols, out_ref):
    half, vectors = psolved_in.shape[0], psolved_in.shape[1]
    edges = parent_edges(mate_cols, far_cols, 0)
    mate = lambda j: mate_in[8 * j : 8 * j + 8, :]
    far = lambda j: far_in[8 * j : 8 * j + 8, :]
    for i in range(half):
        x = parent_transport(psolved_in, prates_ref, mate, far, edges, i)
        for h in range(2):
            for r in range(2):
                lo = 64 * h + 32 * r
                k = 2 * half - 1 - i if h else i
                out_ref[pl.ds(2 * vectors * k + r, vectors, stride=2), :] = x[:, lo : lo + 32]


def passed_along(value, axis, steps):
    count = lax.axis_size(axis)
    return lax.ppermute(value, axis, [(i, (i + steps) % count) for i in range(count)])


def swapped(value, axis, offset):
    count = lax.axis_size(axis)
    pairs = []
    for i in range(offset, count, 2):
        j = (i + 1) % count
        pairs += [(i, j), (j, i)]
    return lax.ppermute(value, axis, pairs)


def halos_of(mate, far, cols):
    return [swapped(mate, "gy", 0), swapped(far, "gy", 1), swapped(cols, "gx", 0), swapped(cols, "gx", 1)]


def local(
    child_adjoint,
    parent_adjoint,
    child_rates,
    child_mixing,
    child_land,
    parent_rates,
    parent_mixing,
    parent_land,
    relaxation,
):
    depth, vectors, lines, columns = child_adjoint.shape
    half = depth // 2
    quarter = lax.axis_size("gy") // 4
    field = shape(depth, vectors, lines, columns)
    factor = shape(depth, lines, columns)
    tiles = shape(half, vectors, LANES)
    sums = shape(half * vectors, LANES)
    count = depth * vectors
    edge = depth // LEVELS * 8
    sum_scratch = pltpu.VMEM((half * vectors, 4 * LANES), F32)
    halo_scratch = [pltpu.VMEM((count, LANES), F32), pltpu.VMEM((count, LANES), F32), pltpu.VMEM((edge, LANES), F32)]
    narrow = parent_adjoint.shape[-1]

    sums1, solved, mate, far, cols, a, b, c = call(
        child_first,
        [sums, field, shape(count, LANES), shape(count, LANES), shape(edge, LANES), factor, factor, factor],
        [
            pltpu.VMEM(field.shape, F32),
            pltpu.VMEM(factor.shape, F32),
            pltpu.VMEM((lines, columns), F32),
            sum_scratch,
            pltpu.SemaphoreType.DMA((2 + half // 2,)),
        ],
        [child_adjoint, child_mixing, relaxation],
        4_000_000,
        3_000_000,
        far_in=(0, 1, 2),
    )
    halos = halos_of(mate, far, cols)
    feed = passed_along(sums1, "gy", quarter)
    packed, prates, pa, pb, pc, rates = call(
        prepare,
        [tiles, shape(5, half, LANES)] + [shape(half, LANES)] * 3 + [shape(5, depth, lines, columns)],
        [pltpu.VMEM((half, LANES), F32)],
        [
            parent_adjoint.reshape(-1, narrow),
            parent_rates.reshape(-1, narrow),
            parent_mixing.reshape(-1, narrow),
            parent_land,
            child_rates,
            child_land,
            cols,
        ],
        1_000_000,
        3_000_000,
    )
    rows = count + half // 2 * vectors
    sums2, solved, psolved, mate, far, cols = call(
        child_second,
        [sums, field, tiles, shape(rows, LANES), shape(rows, LANES), shape(edge + 8, LANES)],
        [pltpu.VMEM(field.shape, F32), sum_scratch] + halo_scratch,
        [solved, a, b, c, rates, relaxation, *halos, packed, pa, pb, pc, feed],
        8_000_000,
        3_000_000,
    )
    halos = halos_of(mate, far, cols)
    feed = passed_along(sums2, "gy", quarter)
    few = half // 2 * vectors
    psolved, mate, far, cols = call(
        parent_second,
        [tiles, shape(few, LANES), shape(few, LANES), shape(8, LANES)],
        [],
        [psolved, prates, pa, pb, pc, *halos, feed],
        1_000_000,
        500_000,
    )
    last_halos = halos_of(mate, far, cols)
    child_out = call(
        child_last,
        field,
        [pltpu.VMEM(field.shape, F32)] + halo_scratch + [pltpu.SemaphoreType.DMA((depth // LEVELS,))],
        [solved, rates, *halos],
        4_000_000,
        3_000_000,
        far_out=True,
    )
    parent_out = call(
        parent_last,
        shape(depth * vectors * 2, narrow),
        [],
        [psolved, prates, *last_halos],
        500_000,
        500_000,
    )
    return (child_out, parent_out.reshape(parent_adjoint.shape))


def solution(mesh):
    wide = P(None, None, "gy", "gx")
    level = P(None, "gy", "gx")
    flat = P("gy", "gx")
    in_specs = (wide, wide, wide, level, flat, wide, level, flat, flat)
    return jax.shard_map(local, mesh=mesh, in_specs=in_specs, out_specs=(wide, wide), check_vma=False)
```

```python
import jax
import jax.numpy as jnp
from jax import lax
from jax.experimental import pallas as pl
from jax.experimental.pallas import tpu as pltpu
from jax.sharding import PartitionSpec as P

F32 = jnp.float32
VMEM = pl.BlockSpec(memory_space=pltpu.VMEM)
FAR = pl.BlockSpec(memory_space=pltpu.HBM)
LIMIT = 40 * 1024 * 1024
LANES = 128
LEVELS = 8


def shape(*dims):
    return jax.ShapeDtypeStruct(dims, F32)


def call(body, outs, scratch, operands, flops, touched, far_in=(), far_out=False):
    operands = [pltpu.with_memory_space_constraint(x, pltpu.HBM) if i in far_in else x for i, x in enumerate(operands)]
    return pl.pallas_call(
        body,
        out_shape=outs,
        in_specs=[FAR if i in far_in else VMEM for i in range(len(operands))],
        out_specs=jax.tree.map(lambda _: FAR if far_out else VMEM, outs),
        scratch_shapes=scratch,
        compiler_params=pltpu.CompilerParams(vmem_limit_bytes=LIMIT),
        cost_estimate=pl.CostEstimate(flops=flops, bytes_accessed=touched, transcendentals=0),
        name=body.__name__,
    )(*operands)


def lane_index(rows=8):
    return lax.broadcasted_iota(jnp.int32, (rows, LANES), 1)


def row_index():
    return lax.broadcasted_iota(jnp.int32, (8, LANES), 0)


def minors(inner, outer):
    theta = delta = jnp.ones_like(inner[0])
    inverse = []
    for i in range(len(inner)):
        delta = theta + outer[i] * delta
        theta_next = delta + inner[i] * theta
        inverse.append(theta / theta_next)
        theta = theta_next
    return inverse


def parity(axis):
    return lax.rem(lax.axis_index(axis), 2)


def child_factors(mix_ref, keep, a_ref, b_ref, c_ref):
    depth = mix_ref.shape[0]
    half = depth // 2
    zero = jnp.zeros_like(keep)
    top_inner = [mix_ref[i] for i in range(half)]
    top_outer = [zero] + top_inner[:-1]
    low_outer = [mix_ref[depth - 1 - i] for i in range(half)]
    low_inner = [mix_ref[depth - 2 - i] for i in range(half)]
    for levels, inner, outer in (
        (range(half), top_inner, top_outer),
        (range(depth - 1, half - 1, -1), low_inner, low_outer),
    ):
        inverse = minors(inner, outer)
        for i, k in enumerate(levels):
            a_ref[k] = inverse[i] * keep
            b_ref[k] = inverse[i] * outer[i]
            c_ref[k] = inverse[i] * inner[i]


def block_rows(source_ref, k, weights, sums_ref, i, place):
    vectors = source_ref.shape[1]
    for r in range(2):
        total = source_ref[k, :, 4 * r, :] * weights[4 * r]
        for j in range(4 * r + 1, 4 * r + 4):
            total = total + source_ref[k, :, j, :] * weights[j]
        column = (2 * place + r) * LANES
        sums_ref[pl.ds(i * vectors, vectors), column : column + LANES] = total


def block_columns(sums_ref):
    wide = sums_ref.shape[1]
    p = lax.broadcasted_iota(jnp.int32, (wide, LANES), 0)
    q = lax.broadcasted_iota(jnp.int32, (wide, LANES), 1)
    pick = jnp.where(p // 4 == q, F32(0.0625), F32(0.0))
    return jnp.dot(
        sums_ref[...], pick, precision=lax.Precision.HIGHEST, preferred_element_type=F32
    )


def child_middle(carry, c_ref, half):
    vectors = len(carry) // 2
    top, low = c_ref[half - 1], c_ref[half]
    scale = 1.0 / (1.0 - top * low)
    first = [(carry[v] + top * carry[vectors + v]) * scale for v in range(vectors)]
    second = [(carry[vectors + v] + low * carry[v]) * scale for v in range(vectors)]
    return first + second


def child_up(carry, c_ref, solved_ref, mate_rows, far_rows, cols_ref):
    depth, vectors = solved_ref.shape[0], solved_ref.shape[1]
    half = depth // 2
    lane = lane_index()
    pair = lane >> 1
    odd = parity("gy")
    mate_row, far_row = 7 * (1 - odd), 7 * odd

    def emit(i, values, packed):
        k_low = depth - 1 - i
        packed = list(packed)
        inside = i % LEVELS if isinstance(i, int) else lax.rem(i, LEVELS)
        for side, k, base in ((0, i, inside * vectors), (1, k_low, (LEVELS - 1 - inside) * vectors)):
            for v in range(vectors):
                x = values[side * vectors + v]
                solved_ref[k, v] = x
                at = base + v
                packed[side] = jnp.where(pair == at, pltpu.roll(x, 2 * at + 1 & (LANES - 1), 1), packed[side])
            mate_rows[pl.ds(k * vectors, vectors), :] = solved_ref[k, :, mate_row, :]
            far_rows[pl.ds(k * vectors, vectors), :] = solved_ref[k, :, far_row, :]
        return packed

    def up(i, state):
        k_low = depth - 1 - i
        top, low = c_ref[i], c_ref[k_low]
        values = []
        for v in range(vectors):
            values.append(solved_ref[i, v] + top * state[v])
        for v in range(vectors):
            values.append(solved_ref[k_low, v] + low * state[vectors + v])
        return tuple(values) + tuple(emit(i, values, state[2 * vectors :]))

    def keep_columns(group, packed):
        for side, g in ((0, group), (1, depth // LEVELS - 1 - group)):
            cols_ref[LEVELS * g : LEVELS * g + 8, :] = packed[side]

    blank = jnp.zeros((8, LANES), F32)
    values = child_middle(carry, c_ref, half)
    state = tuple(values) + tuple(emit(half - 1, values, [blank] * 2))
    for group in range(half // LEVELS - 1, -1, -1):
        last = LEVELS * (group + 1) - 1
        if group == half // LEVELS - 1:
            last -= 1
        count = last - LEVELS * group + 1
        state = lax.fori_loop(0, count, lambda step, state, last=last: up(last - step, state), state, unroll=4 if count % 4 == 0 else count)
        keep_columns(group, state[2 * vectors :])
        state = state[: 2 * vectors] + (blank,) * 2


def begin(
    x_hbm, mix_hbm, relax_hbm, land_hbm, parent_land_hbm,
    sums_out, x_ref, a_ref, b_ref, c_ref, relax_ref, land_ref, parent_land_ref,
    mix_ref, land_in, parent_land_in, sums_ref, sems,
):
    depth = x_ref.shape[0]
    half = depth // 2
    small = []
    for source, target in (
        (mix_hbm, mix_ref), (relax_hbm, relax_ref), (land_hbm, land_in), (parent_land_hbm, parent_land_in),
    ):
        small.append(pltpu.make_async_copy(source, target, sems.at[len(small)]))
        small[-1].start()
    size, large = 4, []
    for start in range(0, half, size):
        for first in (start, depth - size - start):
            part = pl.ds(first, size)
            large.append(pltpu.make_async_copy(x_hbm.at[part], x_ref.at[part], sems.at[len(large) + len(small)]))
            large[-1].start()
    for copy in small:
        copy.wait()
    land_ref[...] = land_in[...].astype(F32)
    parent_land_ref[...] = parent_land_in[...].astype(F32)
    child_factors(mix_ref, 1.0 - relax_ref[...], a_ref, b_ref, c_ref)
    weights = [relax_ref[j : j + 1, :] for j in range(8)]

    def level(i, _):
        for side, k in ((0, i), (1, depth - 1 - i)):
            block_rows(x_ref, k, weights, sums_ref, i, side)
        return 0

    for part, start in enumerate(range(0, half, size)):
        large[2 * part].wait()
        large[2 * part + 1].wait()
        lax.fori_loop(start, start + size, level, 0, unroll=size)
    sums_out[...] = block_columns(sums_ref)


def child_first(x_ref, a_ref, b_ref, c_ref, solved_ref, mate_rows, far_rows, cols_ref):
    depth, vectors = x_ref.shape[0], x_ref.shape[1]
    half = depth // 2

    def down(i, carry):
        values = []
        for side, k in ((0, i), (1, depth - 1 - i)):
            a, b = a_ref[k], b_ref[k]
            for v in range(vectors):
                y = a * x_ref[k, v] + b * carry[side * vectors + v]
                solved_ref[k, v] = y
                values.append(y)
        return tuple(values)

    carry = lax.fori_loop(0, half, down, (jnp.zeros((8, LANES), F32),) * (2 * vectors), unroll=4)
    child_up(carry, c_ref, solved_ref, mate_rows, far_rows, cols_ref)


def combine(sides, land):
    east, west, north, south = sides
    return [land * part for part in (1.0 - (east + west + north + south), east, west, north, south)]


def merge_edges(mate, far, turn):
    swap = jnp.broadcast_to(parity("gx"), (8, LANES)) == 1
    east, west = jnp.where(swap, far, mate), jnp.where(swap, mate, far)
    return jnp.where((lane_index() & 1) == 0, west, pltpu.roll(east, turn, 1))


def child_halos(mate_ref, far_ref, north_ref, south_ref, mate_cols, far_cols, merged_ref):
    swap = jnp.broadcast_to(parity("gy"), (8, LANES)) == 1

    def sort(i, _):
        part = pl.ds(pl.multiple_of(8 * i, 8), 8)
        mate, far = mate_ref[part, :], far_ref[part, :]
        north_ref[part, :] = jnp.where(swap, far, mate)
        south_ref[part, :] = jnp.where(swap, mate, far)
        return 0

    lax.fori_loop(0, north_ref.shape[0] // 8, sort, 0, unroll=8)
    for g in range(merged_ref.shape[0] // 8):
        part = slice(8 * g, 8 * g + 8)
        merged_ref[part, :] = merge_edges(mate_cols[part, :], far_cols[part, :], LANES - 2)


def child_cell(solved_ref, k, v, base, edges, rates, north_ref, south_ref, lane, row):
    vectors = solved_ref.shape[1]
    s = solved_ref[k, v]
    line = k * vectors + v
    edge = pltpu.roll(edges, (LANES - 2 * (base + v)) & (LANES - 1), 1)
    north_edge = jnp.broadcast_to(north_ref[pl.ds(line, 1), :], (8, LANES))
    south_edge = jnp.broadcast_to(south_ref[pl.ds(line, 1), :], (8, LANES))
    east = jnp.where(lane == LANES - 1, edge, pltpu.roll(s, LANES - 1, 1))
    west = jnp.where(lane == 0, edge, pltpu.roll(s, 1, 1))
    north = jnp.where(row == 7, north_edge, pltpu.roll(s, 7, 0))
    south = jnp.where(row == 0, south_edge, pltpu.roll(s, 1, 0))
    return (rates[0] * s + rates[1] * east) + (rates[2] * west + rates[3] * north) + rates[4] * south


def child_second(
    solved_in, a_ref, b_ref, c_ref, rates_ref, land_ref, relax_ref, mate_in, far_in, mate_cols, far_cols,
    parent_ref, pa_ref, pb_ref, pc_ref, feed_ref,
    sums_out, solved_ref, psolved_ref, mate_rows, far_rows, cols_ref,
    x_ref, sums_ref, north_ref, south_ref, merged_ref,
):
    depth, vectors = solved_in.shape[0], solved_in.shape[1]
    half = depth // 2
    groups = depth // LEVELS
    lane, row = lane_index(), row_index()
    weights = [relax_ref[j : j + 1, :] for j in range(8)]
    land = land_ref[...]
    child_halos(mate_in, far_in, north_ref, south_ref, mate_cols, far_cols, merged_ref)

    def down(i, carry, edges):
        k_low = depth - 1 - i
        inside = lax.rem(i, LEVELS)
        values = []
        for side, k, base in ((0, i, inside * vectors), (1, k_low, (LEVELS - 1 - inside) * vectors)):
            a, b = a_ref[k], b_ref[k]
            rates = combine([rates_ref[d, k] for d in range(4)], land)
            for v in range(vectors):
                x = child_cell(solved_in, k, v, base, edges[side], rates, north_ref, south_ref, lane, row)
                x_ref[k, v] = x
                y = a * x + b * carry[side * vectors + v]
                solved_ref[k, v] = y
                values.append(y)
            block_rows(x_ref, k, weights, sums_ref, i, side)
        rhs = parent_ref[i] + feed_ref[pl.ds(i * 8, 8), :]
        psolved = pa_ref[pl.ds(i, 1), :] * rhs + pb_ref[pl.ds(i, 1), :] * carry[2 * vectors]
        psolved_ref[i] = psolved
        return tuple(values) + (psolved,)

    carry = (jnp.zeros((8, LANES), F32),) * (2 * vectors + 1)
    for group in range(half // LEVELS):
        edges = [merged_ref[8 * g : 8 * g + 8, :] for g in (group, groups - 1 - group)]
        carry = lax.fori_loop(
            LEVELS * group, LEVELS * (group + 1), lambda i, carry, edges=edges: down(i, carry, edges), carry, unroll=4
        )
    sums_out[...] = block_columns(sums_ref)
    parent_up(carry[-1], pc_ref, psolved_ref, mate_rows, far_rows, depth * vectors, cols_ref, 8 * groups)
    child_up(carry[:-1], c_ref, solved_ref, mate_rows, far_rows, cols_ref)


def child_last(
    solved_in, rates_ref, land_ref, mate_in, far_in, mate_cols, far_cols, out_hbm, out_ref, north_ref, south_ref, merged_ref, sems
):
    depth, vectors = solved_in.shape[0], solved_in.shape[1]
    lane, row = lane_index(), row_index()
    land = land_ref[...]
    child_halos(mate_in, far_in, north_ref, south_ref, mate_cols, far_cols, merged_ref)
    copies = []
    for group in range(depth // LEVELS):
        edges = merged_ref[8 * group : 8 * group + 8, :]

        def level(inside, _):
            k = LEVELS * group + inside
            rates = combine([rates_ref[d, k] for d in range(4)], land)
            for v in range(vectors):
                out_ref[k, v] = child_cell(
                    solved_in, k, v, inside * vectors, edges, rates, north_ref, south_ref, lane, row
                )
            return 0

        lax.fori_loop(0, LEVELS, level, 0, unroll=4)
        part = pl.ds(LEVELS * group, LEVELS)
        copies.append(pltpu.make_async_copy(out_ref.at[part], out_hbm.at[part], sems.at[group]))
        copies[-1].start()
    for copy in copies:
        copy.wait()


PLACES = [(h, r, 64 * h + 32 * r) for h in range(2) for r in range(2)]


def parent_begin(parent_ref, mix_ref, after_ref, packed_ref, pa_ref, pb_ref, pc_ref, mixed):
    half, vectors = packed_ref.shape[0], packed_ref.shape[1]
    depth = 2 * half
    for i in range(half):
        for h, r, lo in PLACES:
            k = depth - 1 - i if h else i
            mixed[i : i + 1, lo : lo + 32] = mix_ref[2 * k + r : 2 * k + r + 1, :]
    upper = lane_index(1) < 64
    rows = [mixed[i : i + 1, :] for i in range(half)]
    inner, outer = [], []
    for i in range(half):
        nearer = rows[i + 1] if i + 1 < half else pltpu.roll(rows[i], 64, 1)
        inner.append(jnp.where(upper, rows[i], nearer))
        outer.append(jnp.where(upper, rows[i - 1] if i else jnp.zeros_like(rows[0]), rows[i]))
    inverse = minors(inner, outer)
    for i in range(half):
        pa_ref[i : i + 1, :] = inverse[i]
        pb_ref[i : i + 1, :] = inverse[i] * outer[i]
        pc_ref[i : i + 1, :] = inverse[i] * inner[i]
        for h, r, lo in PLACES:
            k = depth - 1 - i if h else i
            packed_ref[i, :, lo : lo + 32] = parent_ref[pl.ds(2 * vectors * k + r, vectors, stride=2), :]


def parent_rates_packed(rates_ref, land_ref, after_ref, prates_ref):
    half = prates_ref.shape[1]
    depth = 2 * half
    for i in range(half):
        for h, r, lo in PLACES:
            k = depth - 1 - i if h else i
            for d in range(4):
                at = 2 * (d * depth + k) + r
                prates_ref[d + 1, i : i + 1, lo : lo + 32] = rates_ref[at : at + 1, :]
    land = jnp.concatenate([land_ref[r : r + 1, :] for _, r, _ in PLACES], axis=1)
    land = jnp.broadcast_to(land, (half, LANES))
    for d, part in enumerate(combine([prates_ref[d] for d in range(1, 5)], land)):
        prates_ref[d] = part


def parent_up(carry, pc_ref, psolved_ref, mate_rows, far_rows, lines, cols_ref, cols_at):
    half = psolved_ref.shape[0]
    lane = lane_index()
    middle = pc_ref[half - 1 : half, :]
    scale = 1.0 / (1.0 - middle * pltpu.roll(middle, 64, 1))
    x = (carry + middle * pltpu.roll(carry, 64, 1)) * scale
    tiles = [None] * half
    tiles[half - 1] = x
    for i in range(half - 2, -1, -1):
        x = psolved_ref[i] + pc_ref[i : i + 1, :] * x
        tiles[i] = x
    packed = jnp.zeros((8, LANES), F32)
    for i in range(half):
        psolved_ref[i] = tiles[i]
        packed = jnp.where(((lane & 31) >> 1) == i, pltpu.roll(tiles[i], 2 * i + 1, 1), packed)
    cols_ref[cols_at : cols_at + 8, :] = packed
    first = (lane & 32) == 0
    swap = jnp.broadcast_to(parity("gy"), (8, LANES)) == 1
    for j in range(half // 2):
        one, two = tiles[j], tiles[j + half // 2]
        lo = jnp.where(first, one, pltpu.roll(two, 32, 1))
        hi = jnp.where(first, pltpu.roll(one, 96, 1), two)
        part = slice(lines + 8 * j, lines + 8 * j + 8)
        mate_rows[part, :] = jnp.where(swap, lo, hi)
        far_rows[part, :] = jnp.where(swap, hi, lo)


def parent_edges(mate_cols, far_cols, at):
    return merge_edges(mate_cols[at : at + 8, :], far_cols[at : at + 8, :], 62)


def parent_transport(psolved_ref, prates_ref, mate_row, far_row, edges, i):
    half = psolved_ref.shape[0]
    lane = lane_index()
    swap = jnp.broadcast_to(parity("gy"), (8, LANES)) == 1
    x = psolved_ref[i]
    mate, far = mate_row(i % (half // 2)), far_row(i % (half // 2))
    lo, hi = jnp.where(swap, far, mate), jnp.where(swap, mate, far)
    if i < half // 2:
        lo = pltpu.roll(lo, 32, 1)
    else:
        hi = pltpu.roll(hi, 96, 1)
    first = (lane & 32) == 0
    to_north = jnp.where(first, pltpu.roll(x, 96, 1), lo)
    to_south = jnp.where(first, hi, pltpu.roll(x, 32, 1))
    edge = pltpu.roll(edges, (LANES - 2 * i - 32) & (LANES - 1), 1)
    column = lane & 31
    to_east = jnp.where(column == 31, edge, pltpu.roll(x, 127, 1))
    to_west = jnp.where(column == 0, edge, pltpu.roll(x, 1, 1))
    parts = [prates_ref[d, i : i + 1, :] for d in range(5)]
    return (parts[0] * x + parts[1] * to_east) + (parts[2] * to_west + parts[3] * to_north) + parts[4] * to_south


def parent_second(
    psolved_in, prates_ref, pa_ref, pb_ref, pc_ref, mate_in, far_in, mate_cols, far_cols, feed_ref,
    psolved_ref, mate_rows, far_rows, cols_ref,
):
    half = psolved_in.shape[0]
    lines = mate_in.shape[0] - mate_rows.shape[0]
    edges = parent_edges(mate_cols, far_cols, mate_cols.shape[0] - 8)
    mate = lambda j: mate_in[lines + 8 * j : lines + 8 * j + 8, :]
    far = lambda j: far_in[lines + 8 * j : lines + 8 * j + 8, :]
    y = jnp.zeros((8, LANES), F32)
    for i in range(half):
        rhs = parent_transport(psolved_in, prates_ref, mate, far, edges, i)
        rhs = rhs + feed_ref[8 * i : 8 * i + 8, :]
        y = pa_ref[i : i + 1, :] * rhs + pb_ref[i : i + 1, :] * y
        psolved_ref[i] = y
    parent_up(y, pc_ref, psolved_ref, mate_rows, far_rows, 0, cols_ref, 0)


def parent_last(psolved_in, prates_ref, mate_in, far_in, mate_cols, far_cols, out_ref):
    half, vectors = psolved_in.shape[0], psolved_in.shape[1]
    edges = parent_edges(mate_cols, far_cols, 0)
    mate = lambda j: mate_in[8 * j : 8 * j + 8, :]
    far = lambda j: far_in[8 * j : 8 * j + 8, :]
    for i in range(half):
        x = parent_transport(psolved_in, prates_ref, mate, far, edges, i)
        for h in range(2):
            for r in range(2):
                lo = 64 * h + 32 * r
                k = 2 * half - 1 - i if h else i
                out_ref[pl.ds(2 * vectors * k + r, vectors, stride=2), :] = x[:, lo : lo + 32]


def passed_along(value, axis, steps):
    count = lax.axis_size(axis)
    return lax.ppermute(value, axis, [(i, (i + steps) % count) for i in range(count)])


def swapped(value, axis, offset):
    count = lax.axis_size(axis)
    pairs = []
    for i in range(offset, count, 2):
        j = (i + 1) % count
        pairs += [(i, j), (j, i)]
    return lax.ppermute(value, axis, pairs)


def halos_of(mate, far, cols):
    return [swapped(mate, "gy", 0), swapped(far, "gy", 1), swapped(cols, "gx", 0), swapped(cols, "gx", 1)]


def local(
    child_adjoint,
    parent_adjoint,
    child_rates,
    child_mixing,
    child_land,
    parent_rates,
    parent_mixing,
    parent_land,
    relaxation,
):
    depth, vectors, lines, columns = child_adjoint.shape
    half = depth // 2
    quarter = lax.axis_size("gy") // 4
    field = shape(depth, vectors, lines, columns)
    factor = shape(depth, lines, columns)
    tiles = shape(half, vectors, LANES)
    sums = shape(half * vectors, LANES)
    count = depth * vectors
    edge = depth // LEVELS * 8
    sum_scratch = pltpu.VMEM((half * vectors, 4 * LANES), F32)
    halo_scratch = [pltpu.VMEM((count, LANES), F32), pltpu.VMEM((count, LANES), F32), pltpu.VMEM((edge, LANES), F32)]
    narrow = parent_adjoint.shape[-1]

    sums1, x, a, b, c, relax, land, parent_land = call(
        begin,
        [sums, field, factor, factor, factor, shape(lines, columns), shape(lines, columns), shape(*parent_land.shape)],
        [
            pltpu.VMEM(factor.shape, F32),
            pltpu.VMEM(child_land.shape, jnp.int32),
            pltpu.VMEM(parent_land.shape, jnp.int32),
            sum_scratch,
            pltpu.SemaphoreType.DMA((4 + half // 2,)),
        ],
        [child_adjoint, child_mixing, relaxation, child_land, parent_land],
        4_000_000,
        3_000_000,
        far_in=range(5),
    )
    feed = passed_along(sums1, "gy", quarter)
    solved, mate, far, cols = call(
        child_first,
        [field, shape(count, LANES), shape(count, LANES), shape(edge, LANES)],
        [],
        [x, a, b, c],
        4_000_000,
        3_000_000,
    )
    halos = halos_of(mate, far, cols)
    packed, pa, pb, pc = call(
        parent_begin,
        [tiles] + [shape(half, LANES)] * 3,
        [pltpu.VMEM((half, LANES), F32)],
        [parent_adjoint.reshape(-1, narrow), parent_mixing.reshape(-1, narrow), cols],
        500_000,
        1_000_000,
    )
    rows = count + half // 2 * vectors
    sums2, solved, psolved, mate, far, cols = call(
        child_second,
        [sums, field, tiles, shape(rows, LANES), shape(rows, LANES), shape(edge + 8, LANES)],
        [pltpu.VMEM(field.shape, F32), sum_scratch] + halo_scratch,
        [solved, a, b, c, child_rates, land, relax, *halos, packed, pa, pb, pc, feed],
        8_000_000,
        3_000_000,
    )
    halos = halos_of(mate, far, cols)
    feed = passed_along(sums2, "gy", quarter)
    prates = call(
        parent_rates_packed,
        shape(5, half, LANES),
        [],
        [parent_rates.reshape(-1, narrow), parent_land, cols],
        500_000,
        1_000_000,
    )
    few = half // 2 * vectors
    psolved, mate, far, cols = call(
        parent_second,
        [tiles, shape(few, LANES), shape(few, LANES), shape(8, LANES)],
        [],
        [psolved, prates, pa, pb, pc, *halos, feed],
        1_000_000,
        500_000,
    )
    last_halos = halos_of(mate, far, cols)
    child_out = call(
        child_last,
        field,
        [pltpu.VMEM(field.shape, F32)] + halo_scratch + [pltpu.SemaphoreType.DMA((depth // LEVELS,))],
        [solved, child_rates, land, *halos],
        4_000_000,
        3_000_000,
        far_out=True,
    )
    parent_out = call(
        parent_last,
        shape(depth * vectors * 2, narrow),
        [],
        [psolved, prates, *last_halos],
        500_000,
        500_000,
    )
    return (child_out, parent_out.reshape(parent_adjoint.shape))


def solution(mesh):
    wide = P(None, None, "gy", "gx")
    level = P(None, "gy", "gx")
    flat = P("gy", "gx")
    in_specs = (wide, wide, wide, level, flat, wide, level, flat, flat)
    return jax.shard_map(local, mesh=mesh, in_specs=in_specs, out_specs=(wide, wide), check_vma=False)
```

```python
import jax
import jax.numpy as jnp
from jax import lax
from jax.experimental import pallas as pl
from jax.experimental.pallas import tpu as pltpu
from jax.sharding import PartitionSpec as P

F32 = jnp.float32
VMEM = pl.BlockSpec(memory_space=pltpu.VMEM)
FAR = pl.BlockSpec(memory_space=pltpu.HBM)
LIMIT = 40 * 1024 * 1024
LANES = 128
LONG = 1_000_000_000
LEVELS = 8


def shape(*dims):
    return jax.ShapeDtypeStruct(dims, F32)


def call(body, outs, scratch, operands, flops, touched, far_in=(), far_out=False):
    operands = [pltpu.with_memory_space_constraint(x, pltpu.HBM) if i in far_in else x for i, x in enumerate(operands)]
    return pl.pallas_call(
        body,
        out_shape=outs,
        in_specs=[FAR if i in far_in else VMEM for i in range(len(operands))],
        out_specs=jax.tree.map(lambda _: FAR if far_out else VMEM, outs),
        scratch_shapes=scratch,
        compiler_params=pltpu.CompilerParams(vmem_limit_bytes=LIMIT),
        cost_estimate=pl.CostEstimate(flops=flops, bytes_accessed=touched, transcendentals=0),
        name=body.__name__,
    )(*operands)


def lane_index(rows=8):
    return lax.broadcasted_iota(jnp.int32, (rows, LANES), 1)


def row_index():
    return lax.broadcasted_iota(jnp.int32, (8, LANES), 0)


def minors(inner, outer):
    theta = delta = jnp.ones_like(inner[0])
    inverse = []
    for i in range(len(inner)):
        delta = theta + outer[i] * delta
        theta_next = delta + inner[i] * theta
        inverse.append(theta / theta_next)
        theta = theta_next
    return inverse


def parity(axis):
    return lax.rem(lax.axis_index(axis), 2)


def child_factors(mix_ref, keep, a_ref, b_ref, c_ref):
    depth = mix_ref.shape[0]
    half = depth // 2
    zero = jnp.zeros_like(keep)
    top_inner = [mix_ref[i] for i in range(half)]
    top_outer = [zero] + top_inner[:-1]
    low_outer = [mix_ref[depth - 1 - i] for i in range(half)]
    low_inner = [mix_ref[depth - 2 - i] for i in range(half)]
    for levels, inner, outer in (
        (range(half), top_inner, top_outer),
        (range(depth - 1, half - 1, -1), low_inner, low_outer),
    ):
        inverse = minors(inner, outer)
        for i, k in enumerate(levels):
            a_ref[k] = inverse[i] * keep
            b_ref[k] = inverse[i] * outer[i]
            c_ref[k] = inverse[i] * inner[i]


def block_rows(source_ref, k, weights, sums_ref, i, place):
    vectors = source_ref.shape[1]
    for r in range(2):
        total = source_ref[k, :, 4 * r, :] * weights[4 * r]
        for j in range(4 * r + 1, 4 * r + 4):
            total = total + source_ref[k, :, j, :] * weights[j]
        column = (2 * place + r) * LANES
        sums_ref[pl.ds(i * vectors, vectors), column : column + LANES] = total


def block_columns(sums_ref):
    wide = sums_ref.shape[1]
    p = lax.broadcasted_iota(jnp.int32, (wide, LANES), 0)
    q = lax.broadcasted_iota(jnp.int32, (wide, LANES), 1)
    pick = jnp.where(p // 4 == q, F32(0.0625), F32(0.0))
    return jnp.dot(
        sums_ref[...], pick, precision=lax.Precision.HIGHEST, preferred_element_type=F32
    )


def child_middle(carry, c_ref, half):
    vectors = len(carry) // 2
    top, low = c_ref[half - 1], c_ref[half]
    scale = 1.0 / (1.0 - top * low)
    first = [(carry[v] + top * carry[vectors + v]) * scale for v in range(vectors)]
    second = [(carry[vectors + v] + low * carry[v]) * scale for v in range(vectors)]
    return first + second


def child_up(carry, c_ref, solved_ref, mate_rows, far_rows, cols_ref):
    depth, vectors = solved_ref.shape[0], solved_ref.shape[1]
    half = depth // 2
    lane = lane_index()
    pair = lane >> 1
    odd = parity("gy")
    mate_row, far_row = 7 * (1 - odd), 7 * odd

    def emit(i, values, packed):
        k_low = depth - 1 - i
        packed = list(packed)
        inside = i % LEVELS if isinstance(i, int) else lax.rem(i, LEVELS)
        for side, k, base in ((0, i, inside * vectors), (1, k_low, (LEVELS - 1 - inside) * vectors)):
            for v in range(vectors):
                x = values[side * vectors + v]
                solved_ref[k, v] = x
                at = base + v
                packed[side] = jnp.where(pair == at, pltpu.roll(x, 2 * at + 1 & (LANES - 1), 1), packed[side])
            mate_rows[pl.ds(k * vectors, vectors), :] = solved_ref[k, :, mate_row, :]
            far_rows[pl.ds(k * vectors, vectors), :] = solved_ref[k, :, far_row, :]
        return packed

    def up(i, state):
        k_low = depth - 1 - i
        top, low = c_ref[i], c_ref[k_low]
        values = []
        for v in range(vectors):
            values.append(solved_ref[i, v] + top * state[v])
        for v in range(vectors):
            values.append(solved_ref[k_low, v] + low * state[vectors + v])
        return tuple(values) + tuple(emit(i, values, state[2 * vectors :]))

    def keep_columns(group, packed):
        for side, g in ((0, group), (1, depth // LEVELS - 1 - group)):
            cols_ref[LEVELS * g : LEVELS * g + 8, :] = packed[side]

    blank = jnp.zeros((8, LANES), F32)
    values = child_middle(carry, c_ref, half)
    state = tuple(values) + tuple(emit(half - 1, values, [blank] * 2))
    for group in range(half // LEVELS - 1, -1, -1):
        last = LEVELS * (group + 1) - 1
        if group == half // LEVELS - 1:
            last -= 1
        count = last - LEVELS * group + 1
        state = lax.fori_loop(0, count, lambda step, state, last=last: up(last - step, state), state, unroll=4 if count % 4 == 0 else count)
        keep_columns(group, state[2 * vectors :])
        state = state[: 2 * vectors] + (blank,) * 2


def begin(
    x_hbm, mix_hbm, relax_hbm, land_hbm, parent_land_hbm, rates_hbm,
    sums_out, x_ref, a_ref, b_ref, c_ref, relax_ref, land_ref, parent_land_ref, rates_ref,
    mix_ref, land_in, parent_land_in, sums_ref, sems,
):
    depth = x_ref.shape[0]
    half = depth // 2
    small = []
    for source, target in (
        (mix_hbm, mix_ref), (relax_hbm, relax_ref), (land_hbm, land_in), (parent_land_hbm, parent_land_in),
    ):
        small.append(pltpu.make_async_copy(source, target, sems.at[len(small)]))
        small[-1].start()
    size, large = 4, []
    for start in range(0, half, size):
        for first in (start, depth - size - start):
            part = pl.ds(first, size)
            large.append(pltpu.make_async_copy(x_hbm.at[part], x_ref.at[part], sems.at[len(large) + len(small)]))
            large[-1].start()
    rates_copy = pltpu.make_async_copy(rates_hbm, rates_ref, sems.at[len(large) + len(small)])
    rates_copy.start()
    for copy in small:
        copy.wait()
    land_ref[...] = land_in[...].astype(F32)
    parent_land_ref[...] = parent_land_in[...].astype(F32)
    child_factors(mix_ref, 1.0 - relax_ref[...], a_ref, b_ref, c_ref)
    weights = [relax_ref[j : j + 1, :] for j in range(8)]

    def level(i, _):
        for side, k in ((0, i), (1, depth - 1 - i)):
            block_rows(x_ref, k, weights, sums_ref, i, side)
        return 0

    for part, start in enumerate(range(0, half, size)):
        large[2 * part].wait()
        large[2 * part + 1].wait()
        lax.fori_loop(start, start + size, level, 0, unroll=size)
    sums_out[...] = block_columns(sums_ref)
    rates_copy.wait()


def child_first(x_ref, a_ref, b_ref, c_ref, solved_ref, mate_rows, far_rows, cols_ref):
    depth, vectors = x_ref.shape[0], x_ref.shape[1]
    half = depth // 2

    def down(i, carry):
        values = []
        for side, k in ((0, i), (1, depth - 1 - i)):
            a, b = a_ref[k], b_ref[k]
            for v in range(vectors):
                y = a * x_ref[k, v] + b * carry[side * vectors + v]
                solved_ref[k, v] = y
                values.append(y)
        return tuple(values)

    carry = lax.fori_loop(0, half, down, (jnp.zeros((8, LANES), F32),) * (2 * vectors), unroll=4)
    child_up(carry, c_ref, solved_ref, mate_rows, far_rows, cols_ref)


def combine(sides, land):
    east, west, north, south = sides
    return [land * part for part in (1.0 - (east + west + north + south), east, west, north, south)]


def merge_edges(mate, far, turn):
    swap = jnp.broadcast_to(parity("gx"), (8, LANES)) == 1
    east, west = jnp.where(swap, far, mate), jnp.where(swap, mate, far)
    return jnp.where((lane_index() & 1) == 0, west, pltpu.roll(east, turn, 1))


def child_halos(mate_ref, far_ref, north_ref, south_ref, mate_cols, far_cols, merged_ref):
    swap = jnp.broadcast_to(parity("gy"), (8, LANES)) == 1

    def sort(i, _):
        part = pl.ds(pl.multiple_of(8 * i, 8), 8)
        mate, far = mate_ref[part, :], far_ref[part, :]
        north_ref[part, :] = jnp.where(swap, far, mate)
        south_ref[part, :] = jnp.where(swap, mate, far)
        return 0

    lax.fori_loop(0, north_ref.shape[0] // 8, sort, 0, unroll=8)
    for g in range(merged_ref.shape[0] // 8):
        part = slice(8 * g, 8 * g + 8)
        merged_ref[part, :] = merge_edges(mate_cols[part, :], far_cols[part, :], LANES - 2)


def child_cell(solved_ref, k, v, base, edges, rates, north_ref, south_ref, lane, row):
    vectors = solved_ref.shape[1]
    s = solved_ref[k, v]
    line = k * vectors + v
    edge = pltpu.roll(edges, (LANES - 2 * (base + v)) & (LANES - 1), 1)
    north_edge = jnp.broadcast_to(north_ref[pl.ds(line, 1), :], (8, LANES))
    south_edge = jnp.broadcast_to(south_ref[pl.ds(line, 1), :], (8, LANES))
    east = jnp.where(lane == LANES - 1, edge, pltpu.roll(s, LANES - 1, 1))
    west = jnp.where(lane == 0, edge, pltpu.roll(s, 1, 1))
    north = jnp.where(row == 7, north_edge, pltpu.roll(s, 7, 0))
    south = jnp.where(row == 0, south_edge, pltpu.roll(s, 1, 0))
    return (rates[0] * s + rates[1] * east) + (rates[2] * west + rates[3] * north) + rates[4] * south


def child_between(
    solved_in, rates_ref, land_ref, relax_ref, after_ref, mate_in, far_in, mate_cols, far_cols,
    sums_out, x_ref,
    sums_ref, north_ref, south_ref, merged_ref,
):
    depth, vectors = solved_in.shape[0], solved_in.shape[1]
    lane, row = lane_index(), row_index()
    weights = [relax_ref[j : j + 1, :] for j in range(8)]
    land = land_ref[...]
    child_halos(mate_in, far_in, north_ref, south_ref, mate_cols, far_cols, merged_ref)
    half, groups = depth // 2, depth // LEVELS

    def level(i, _, edges):
        inside = lax.rem(i, LEVELS)
        for side, k, base in ((0, i, inside * vectors), (1, depth - 1 - i, (LEVELS - 1 - inside) * vectors)):
            rates = combine([rates_ref[d, k] for d in range(4)], land)
            for v in range(vectors):
                x_ref[k, v] = child_cell(
                    solved_in, k, v, base, edges[side], rates, north_ref, south_ref, lane, row
                )
            block_rows(x_ref, k, weights, sums_ref, i, side)
        return 0

    for group in range(half // LEVELS):
        edges = [merged_ref[8 * g : 8 * g + 8, :] for g in (group, groups - 1 - group)]
        lax.fori_loop(
            LEVELS * group, LEVELS * (group + 1), lambda i, _, edges=edges: level(i, _, edges), 0, unroll=4
        )
    sums_out[...] = block_columns(sums_ref)


def child_second(
    x_ref, a_ref, b_ref, c_ref, parent_ref, pa_ref, pb_ref, pc_ref,
    solved_ref, psolved_ref, mate_rows, far_rows, cols_ref,
):
    depth, vectors = x_ref.shape[0], x_ref.shape[1]
    y = jnp.zeros((8, LANES), F32)
    for i in range(depth // 2):
        y = pa_ref[i : i + 1, :] * parent_ref[i] + pb_ref[i : i + 1, :] * y
        psolved_ref[i] = y
    lines, at = depth * vectors, depth // LEVELS * 8
    parent_up(y, pc_ref, psolved_ref, mate_rows, far_rows, lines, cols_ref, at)
    child_first(x_ref, a_ref, b_ref, c_ref, solved_ref, mate_rows, far_rows, cols_ref)


def child_last(
    solved_in, rates_ref, land_ref, mate_in, far_in, mate_cols, far_cols, out_hbm, out_ref, north_ref, south_ref, merged_ref, sems
):
    depth, vectors = solved_in.shape[0], solved_in.shape[1]
    lane, row = lane_index(), row_index()
    land = land_ref[...]
    child_halos(mate_in, far_in, north_ref, south_ref, mate_cols, far_cols, merged_ref)
    copies = []
    for group in range(depth // LEVELS):
        edges = merged_ref[8 * group : 8 * group + 8, :]

        def level(inside, _):
            k = LEVELS * group + inside
            rates = combine([rates_ref[d, k] for d in range(4)], land)
            for v in range(vectors):
                out_ref[k, v] = child_cell(
                    solved_in, k, v, inside * vectors, edges, rates, north_ref, south_ref, lane, row
                )
            return 0

        lax.fori_loop(0, LEVELS, level, 0, unroll=4)
        part = pl.ds(LEVELS * group, LEVELS)
        copies.append(pltpu.make_async_copy(out_ref.at[part], out_hbm.at[part], sems.at[group]))
        copies[-1].start()
    for copy in copies:
        copy.wait()


PLACES = [(h, r, 64 * h + 32 * r) for h in range(2) for r in range(2)]


def parent_fed(parent_ref, feed_ref, after_ref, packed_ref):
    half, vectors = packed_ref.shape[0], packed_ref.shape[1]
    for i in range(half):
        for h, r, lo in PLACES:
            k = 2 * half - 1 - i if h else i
            packed_ref[i, :, lo : lo + 32] = parent_ref[pl.ds(2 * vectors * k + r, vectors, stride=2), :]
        packed_ref[i] = packed_ref[i] + feed_ref[vectors * i : vectors * (i + 1), :]


def parent_factors(mix_ref, fed_ref, far_ref, mate_cols, far_cols, pa_ref, pb_ref, pc_ref, mixed):
    half = pa_ref.shape[0]
    for i in range(half):
        for h, r, lo in PLACES:
            k = 2 * half - 1 - i if h else i
            mixed[i : i + 1, lo : lo + 32] = mix_ref[2 * k + r : 2 * k + r + 1, :]
    upper = lane_index(1) < 64
    rows = [mixed[i : i + 1, :] for i in range(half)]
    inner, outer = [], []
    for i in range(half):
        nearer = rows[i + 1] if i + 1 < half else pltpu.roll(rows[i], 64, 1)
        inner.append(jnp.where(upper, rows[i], nearer))
        outer.append(jnp.where(upper, rows[i - 1] if i else jnp.zeros_like(rows[0]), rows[i]))
    inverse = minors(inner, outer)
    for i in range(half):
        pa_ref[i : i + 1, :] = inverse[i]
        pb_ref[i : i + 1, :] = inverse[i] * outer[i]
        pc_ref[i : i + 1, :] = inverse[i] * inner[i]


def parent_rates_packed(rates_ref, feed_ref, after_ref, packed_ref):
    half = packed_ref.shape[1]
    depth = 2 * half
    for i in range(half):
        for h, r, lo in PLACES:
            k = depth - 1 - i if h else i
            for d in range(4):
                at = 2 * (d * depth + k) + r
                packed_ref[d, i : i + 1, lo : lo + 32] = rates_ref[at : at + 1, :]


def parent_rates_masked(packed_ref, land_ref, far_ref, mate_cols, far_cols, prates_ref):
    half = packed_ref.shape[1]
    land = jnp.concatenate([land_ref[r : r + 1, :] for _, r, _ in PLACES], axis=1)
    land = jnp.broadcast_to(land, (half, LANES))
    for d, part in enumerate(combine([packed_ref[d] for d in range(4)], land)):
        prates_ref[d] = part


def parent_up(carry, pc_ref, psolved_ref, mate_rows, far_rows, lines, cols_ref, cols_at):
    half = psolved_ref.shape[0]
    lane = lane_index()
    middle = pc_ref[half - 1 : half, :]
    scale = 1.0 / (1.0 - middle * pltpu.roll(middle, 64, 1))
    x = (carry + middle * pltpu.roll(carry, 64, 1)) * scale
    tiles = [None] * half
    tiles[half - 1] = x
    for i in range(half - 2, -1, -1):
        x = psolved_ref[i] + pc_ref[i : i + 1, :] * x
        tiles[i] = x
    packed = jnp.zeros((8, LANES), F32)
    for i in range(half):
        psolved_ref[i] = tiles[i]
        packed = jnp.where(((lane & 31) >> 1) == i, pltpu.roll(tiles[i], 2 * i + 1, 1), packed)
    cols_ref[cols_at : cols_at + 8, :] = packed
    first = (lane & 32) == 0
    swap = jnp.broadcast_to(parity("gy"), (8, LANES)) == 1
    for j in range(half // 2):
        one, two = tiles[j], tiles[j + half // 2]
        lo = jnp.where(first, one, pltpu.roll(two, 32, 1))
        hi = jnp.where(first, pltpu.roll(one, 96, 1), two)
        part = slice(lines + 8 * j, lines + 8 * j + 8)
        mate_rows[part, :] = jnp.where(swap, lo, hi)
        far_rows[part, :] = jnp.where(swap, hi, lo)


def parent_edges(mate_cols, far_cols, at):
    return merge_edges(mate_cols[at : at + 8, :], far_cols[at : at + 8, :], 62)


def parent_transport(psolved_ref, prates_ref, mate_row, far_row, edges, i):
    half = psolved_ref.shape[0]
    lane = lane_index()
    swap = jnp.broadcast_to(parity("gy"), (8, LANES)) == 1
    x = psolved_ref[i]
    mate, far = mate_row(i % (half // 2)), far_row(i % (half // 2))
    lo, hi = jnp.where(swap, far, mate), jnp.where(swap, mate, far)
    if i < half // 2:
        lo = pltpu.roll(lo, 32, 1)
    else:
        hi = pltpu.roll(hi, 96, 1)
    first = (lane & 32) == 0
    to_north = jnp.where(first, pltpu.roll(x, 96, 1), lo)
    to_south = jnp.where(first, hi, pltpu.roll(x, 32, 1))
    edge = pltpu.roll(edges, (LANES - 2 * i - 32) & (LANES - 1), 1)
    column = lane & 31
    to_east = jnp.where(column == 31, edge, pltpu.roll(x, 127, 1))
    to_west = jnp.where(column == 0, edge, pltpu.roll(x, 1, 1))
    parts = [prates_ref[d, i : i + 1, :] for d in range(5)]
    return (parts[0] * x + parts[1] * to_east) + (parts[2] * to_west + parts[3] * to_north) + parts[4] * to_south


def parent_second(
    psolved_in, prates_ref, pa_ref, pb_ref, pc_ref, mate_in, far_in, mate_cols, far_cols, feed_ref,
    psolved_ref, mate_rows, far_rows, cols_ref,
):
    half = psolved_in.shape[0]
    lines = mate_in.shape[0] - mate_rows.shape[0]
    edges = parent_edges(mate_cols, far_cols, mate_cols.shape[0] - 8)
    mate = lambda j: mate_in[lines + 8 * j : lines + 8 * j + 8, :]
    far = lambda j: far_in[lines + 8 * j : lines + 8 * j + 8, :]
    y = jnp.zeros((8, LANES), F32)
    for i in range(half):
        rhs = parent_transport(psolved_in, prates_ref, mate, far, edges, i)
        rhs = rhs + feed_ref[8 * i : 8 * i + 8, :]
        y = pa_ref[i : i + 1, :] * rhs + pb_ref[i : i + 1, :] * y
        psolved_ref[i] = y
    parent_up(y, pc_ref, psolved_ref, mate_rows, far_rows, 0, cols_ref, 0)


def parent_last(psolved_in, prates_ref, mate_in, far_in, mate_cols, far_cols, out_ref):
    half, vectors = psolved_in.shape[0], psolved_in.shape[1]
    edges = parent_edges(mate_cols, far_cols, 0)
    mate = lambda j: mate_in[8 * j : 8 * j + 8, :]
    far = lambda j: far_in[8 * j : 8 * j + 8, :]
    for i in range(half):
        x = parent_transport(psolved_in, prates_ref, mate, far, edges, i)
        for h in range(2):
            for r in range(2):
                lo = 64 * h + 32 * r
                k = 2 * half - 1 - i if h else i
                out_ref[pl.ds(2 * vectors * k + r, vectors, stride=2), :] = x[:, lo : lo + 32]


def passed_along(value, axis, steps):
    count = lax.axis_size(axis)
    return lax.ppermute(value, axis, [(i, (i + steps) % count) for i in range(count)])


def swapped(value, axis, offset):
    count = lax.axis_size(axis)
    pairs = []
    for i in range(offset, count, 2):
        j = (i + 1) % count
        pairs += [(i, j), (j, i)]
    return lax.ppermute(value, axis, pairs)


def halos_of(mate, far, cols):
    return [swapped(mate, "gy", 0), swapped(far, "gy", 1), swapped(cols, "gx", 0), swapped(cols, "gx", 1)]


def local(
    child_adjoint,
    parent_adjoint,
    child_rates,
    child_mixing,
    child_land,
    parent_rates,
    parent_mixing,
    parent_land,
    relaxation,
):
    depth, vectors, lines, columns = child_adjoint.shape
    half = depth // 2
    quarter = lax.axis_size("gy") // 4
    field = shape(depth, vectors, lines, columns)
    factor = shape(depth, lines, columns)
    tiles = shape(half, vectors, LANES)
    sums = shape(half * vectors, LANES)
    count = depth * vectors
    edge = depth // LEVELS * 8
    sum_scratch = pltpu.VMEM((half * vectors, 4 * LANES), F32)
    halo_scratch = [pltpu.VMEM((count, LANES), F32), pltpu.VMEM((count, LANES), F32), pltpu.VMEM((edge, LANES), F32)]
    narrow = parent_adjoint.shape[-1]

    sums1, x, a, b, c, relax, land, parent_land, rates = call(
        begin,
        [sums, field, factor, factor, factor, shape(lines, columns), shape(lines, columns), shape(*parent_land.shape)]
        + [shape(*child_rates.shape)],
        [
            pltpu.VMEM(factor.shape, F32),
            pltpu.VMEM(child_land.shape, jnp.int32),
            pltpu.VMEM(parent_land.shape, jnp.int32),
            sum_scratch,
            pltpu.SemaphoreType.DMA((5 + half // 2,)),
        ],
        [child_adjoint, child_mixing, relaxation, child_land, parent_land, child_rates],
        4_000_000,
        3_000_000,
        far_in=range(6),
    )
    feed = passed_along(sums1, "gy", quarter)
    solved, mate, far, cols = call(
        child_first,
        [field, shape(count, LANES), shape(count, LANES), shape(edge, LANES)],
        [],
        [x, a, b, c],
        4_000_000,
        3_000_000,
    )
    halos = halos_of(mate, far, cols)
    fed = call(
        parent_fed,
        tiles,
        [],
        [parent_adjoint.reshape(-1, narrow), feed, cols],
        LONG,
        1_000_000,
    )
    pa, pb, pc = call(
        parent_factors,
        [shape(half, LANES)] * 3,
        [pltpu.VMEM((half, LANES), F32)],
        [parent_mixing.reshape(-1, narrow), fed, *halos[1:]],
        LONG,
        1_000_000,
    )
    sums2, x = call(
        child_between,
        [sums, field],
        [sum_scratch] + halo_scratch,
        [solved, rates, land, relax, pa, *halos],
        8_000_000,
        3_000_000,
    )
    feed = passed_along(sums2, "gy", quarter)
    rows = count + half // 2 * vectors
    solved, psolved, mate, far, cols = call(
        child_second,
        [field, tiles, shape(rows, LANES), shape(rows, LANES), shape(edge + 8, LANES)],
        [],
        [x, a, b, c, fed, pa, pb, pc],
        8_000_000,
        3_000_000,
    )
    halos = halos_of(mate, far, cols)
    packed_rates = call(
        parent_rates_packed,
        shape(4, half, LANES),
        [],
        [parent_rates.reshape(-1, narrow), feed, cols],
        1_450_000_000,
        1_000_000,
    )
    prates = call(
        parent_rates_masked,
        shape(5, half, LANES),
        [],
        [packed_rates, parent_land, *halos[1:]],
        LONG,
        1_000_000,
    )
    few = half // 2 * vectors
    psolved, mate, far, cols = call(
        parent_second,
        [tiles, shape(few, LANES), shape(few, LANES), shape(8, LANES)],
        [],
        [psolved, prates, pa, pb, pc, *halos, feed],
        1_000_000,
        500_000,
    )
    last_halos = halos_of(mate, far, cols)
    child_out = call(
        child_last,
        field,
        [pltpu.VMEM(field.shape, F32)] + halo_scratch + [pltpu.SemaphoreType.DMA((depth // LEVELS,))],
        [solved, rates, land, *halos],
        4_000_000,
        3_000_000,
        far_out=True,
    )
    parent_out = call(
        parent_last,
        shape(depth * vectors * 2, narrow),
        [],
        [psolved, prates, *last_halos],
        500_000,
        500_000,
    )
    return (child_out, parent_out.reshape(parent_adjoint.shape))


def solution(mesh):
    wide = P(None, None, "gy", "gx")
    level = P(None, "gy", "gx")
    flat = P("gy", "gx")
    in_specs = (wide, wide, wide, level, flat, wide, level, flat, flat)
    return jax.shard_map(local, mesh=mesh, in_specs=in_specs, out_specs=(wide, wide), check_vma=False)
```

```python
import jax
import jax.numpy as jnp
from jax import lax
from jax.experimental import pallas as pl
from jax.experimental.pallas import tpu as pltpu
from jax.sharding import PartitionSpec as P

F32 = jnp.float32
VMEM = pl.BlockSpec(memory_space=pltpu.VMEM)
FAR = pl.BlockSpec(memory_space=pltpu.HBM)
LIMIT = 40 * 1024 * 1024
LANES = 128
LONG = 1_000_000_000
INNER = 10_000_000
LEVELS = 8


def shape(*dims):
    return jax.ShapeDtypeStruct(dims, F32)


def call(body, outs, scratch, operands, flops, touched, far_in=(), far_out=False):
    operands = [pltpu.with_memory_space_constraint(x, pltpu.HBM) if i in far_in else x for i, x in enumerate(operands)]
    return pl.pallas_call(
        body,
        out_shape=outs,
        in_specs=[FAR if i in far_in else VMEM for i in range(len(operands))],
        out_specs=jax.tree.map(lambda _: FAR if far_out else VMEM, outs),
        scratch_shapes=scratch,
        compiler_params=pltpu.CompilerParams(vmem_limit_bytes=LIMIT),
        cost_estimate=pl.CostEstimate(flops=flops, bytes_accessed=touched, transcendentals=0),
        name=body.__name__,
    )(*operands)


def lane_index(rows=8):
    return lax.broadcasted_iota(jnp.int32, (rows, LANES), 1)


def row_index():
    return lax.broadcasted_iota(jnp.int32, (8, LANES), 0)


def minors(inner, outer):
    theta = delta = jnp.ones_like(inner[0])
    inverse = []
    for i in range(len(inner)):
        delta = theta + outer[i] * delta
        theta_next = delta + inner[i] * theta
        inverse.append(theta / theta_next)
        theta = theta_next
    return inverse


def parity(axis):
    return lax.rem(lax.axis_index(axis), 2)


def child_factors(mix_ref, keep, a_ref, b_ref, c_ref):
    depth = mix_ref.shape[0]
    half = depth // 2
    zero = jnp.zeros_like(keep)
    top_inner = [mix_ref[i] for i in range(half)]
    top_outer = [zero] + top_inner[:-1]
    low_outer = [mix_ref[depth - 1 - i] for i in range(half)]
    low_inner = [mix_ref[depth - 2 - i] for i in range(half)]
    for levels, inner, outer in (
        (range(half), top_inner, top_outer),
        (range(depth - 1, half - 1, -1), low_inner, low_outer),
    ):
        inverse = minors(inner, outer)
        for i, k in enumerate(levels):
            a_ref[k] = inverse[i] * keep
            b_ref[k] = inverse[i] * outer[i]
            c_ref[k] = inverse[i] * inner[i]


def block_rows(source_ref, k, weights, sums_ref, i, place):
    vectors = source_ref.shape[1]
    for r in range(2):
        total = source_ref[k, :, 4 * r, :] * weights[4 * r]
        for j in range(4 * r + 1, 4 * r + 4):
            total = total + source_ref[k, :, j, :] * weights[j]
        column = (2 * place + r) * LANES
        sums_ref[pl.ds(i * vectors, vectors), column : column + LANES] = total


def block_columns(sums_ref):
    wide = sums_ref.shape[1]
    p = lax.broadcasted_iota(jnp.int32, (wide, LANES), 0)
    q = lax.broadcasted_iota(jnp.int32, (wide, LANES), 1)
    pick = jnp.where(p // 4 == q, F32(0.0625), F32(0.0))
    return jnp.dot(
        sums_ref[...], pick, precision=lax.Precision.HIGHEST, preferred_element_type=F32
    )


def child_middle(carry, c_ref, half):
    vectors = len(carry) // 2
    top, low = c_ref[half - 1], c_ref[half]
    scale = 1.0 / (1.0 - top * low)
    first = [(carry[v] + top * carry[vectors + v]) * scale for v in range(vectors)]
    second = [(carry[vectors + v] + low * carry[v]) * scale for v in range(vectors)]
    return first + second


def child_up(carry, c_ref, solved_ref, mate_rows, far_rows, cols_ref):
    depth, vectors = solved_ref.shape[0], solved_ref.shape[1]
    half = depth // 2
    lane = lane_index()
    pair = lane >> 1
    odd = parity("gy")
    mate_row, far_row = 7 * (1 - odd), 7 * odd

    def emit(i, values, packed):
        k_low = depth - 1 - i
        packed = list(packed)
        inside = i % LEVELS if isinstance(i, int) else lax.rem(i, LEVELS)
        for side, k, base in ((0, i, inside * vectors), (1, k_low, (LEVELS - 1 - inside) * vectors)):
            for v in range(vectors):
                x = values[side * vectors + v]
                solved_ref[k, v] = x
                at = base + v
                packed[side] = jnp.where(pair == at, pltpu.roll(x, 2 * at + 1 & (LANES - 1), 1), packed[side])
            mate_rows[pl.ds(k * vectors, vectors), :] = solved_ref[k, :, mate_row, :]
            far_rows[pl.ds(k * vectors, vectors), :] = solved_ref[k, :, far_row, :]
        return packed

    def up(i, state):
        k_low = depth - 1 - i
        top, low = c_ref[i], c_ref[k_low]
        values = []
        for v in range(vectors):
            values.append(solved_ref[i, v] + top * state[v])
        for v in range(vectors):
            values.append(solved_ref[k_low, v] + low * state[vectors + v])
        return tuple(values) + tuple(emit(i, values, state[2 * vectors :]))

    def keep_columns(group, packed):
        for side, g in ((0, group), (1, depth // LEVELS - 1 - group)):
            cols_ref[LEVELS * g : LEVELS * g + 8, :] = packed[side]

    blank = jnp.zeros((8, LANES), F32)
    values = child_middle(carry, c_ref, half)
    state = tuple(values) + tuple(emit(half - 1, values, [blank] * 2))
    for group in range(half // LEVELS - 1, -1, -1):
        last = LEVELS * (group + 1) - 1
        if group == half // LEVELS - 1:
            last -= 1
        count = last - LEVELS * group + 1
        state = lax.fori_loop(0, count, lambda step, state, last=last: up(last - step, state), state, unroll=4 if count % 4 == 0 else count)
        keep_columns(group, state[2 * vectors :])
        state = state[: 2 * vectors] + (blank,) * 2


def begin(
    x_hbm, mix_hbm, relax_hbm, land_hbm, parent_land_hbm, rates_hbm,
    sums_out, x_ref, a_ref, b_ref, c_ref, relax_ref, land_ref, parent_land_ref, rates_ref,
    mix_ref, land_in, parent_land_in, sums_ref, sems,
):
    depth = x_ref.shape[0]
    half = depth // 2
    small = []
    for source, target in (
        (mix_hbm, mix_ref), (relax_hbm, relax_ref), (land_hbm, land_in), (parent_land_hbm, parent_land_in),
    ):
        small.append(pltpu.make_async_copy(source, target, sems.at[len(small)]))
        small[-1].start()
    size, large = 4, []
    for start in range(0, half, size):
        for first in (start, depth - size - start):
            part = pl.ds(first, size)
            large.append(pltpu.make_async_copy(x_hbm.at[part], x_ref.at[part], sems.at[len(large) + len(small)]))
            large[-1].start()
    rates_copy = pltpu.make_async_copy(rates_hbm, rates_ref, sems.at[len(large) + len(small)])
    rates_copy.start()
    for copy in small:
        copy.wait()
    land_ref[...] = land_in[...].astype(F32)
    parent_land_ref[...] = parent_land_in[...].astype(F32)
    child_factors(mix_ref, 1.0 - relax_ref[...], a_ref, b_ref, c_ref)
    weights = [relax_ref[j : j + 1, :] for j in range(8)]

    def level(i, _):
        for side, k in ((0, i), (1, depth - 1 - i)):
            block_rows(x_ref, k, weights, sums_ref, i, side)
        return 0

    for part, start in enumerate(range(0, half, size)):
        large[2 * part].wait()
        large[2 * part + 1].wait()
        lax.fori_loop(start, start + size, level, 0, unroll=size)
    sums_out[...] = block_columns(sums_ref)
    rates_copy.wait()


def child_first(x_ref, a_ref, b_ref, c_ref, solved_ref, mate_rows, far_rows, cols_ref):
    depth, vectors = x_ref.shape[0], x_ref.shape[1]
    half = depth // 2

    def down(i, carry):
        values = []
        for side, k in ((0, i), (1, depth - 1 - i)):
            a, b = a_ref[k], b_ref[k]
            for v in range(vectors):
                y = a * x_ref[k, v] + b * carry[side * vectors + v]
                solved_ref[k, v] = y
                values.append(y)
        return tuple(values)

    carry = lax.fori_loop(0, half, down, (jnp.zeros((8, LANES), F32),) * (2 * vectors), unroll=4)
    child_up(carry, c_ref, solved_ref, mate_rows, far_rows, cols_ref)


def combine(sides, land):
    east, west, north, south = sides
    return [land * part for part in (1.0 - (east + west + north + south), east, west, north, south)]


def merge_edges(mate, far, turn):
    swap = jnp.broadcast_to(parity("gx"), (8, LANES)) == 1
    east, west = jnp.where(swap, far, mate), jnp.where(swap, mate, far)
    return jnp.where((lane_index() & 1) == 0, west, pltpu.roll(east, turn, 1))


def child_inner(solved_ref, rates_ref, land_ref, after_ref, inner_ref, row_ref, column_ref):
    depth, vectors = solved_ref.shape[0], solved_ref.shape[1]
    lane, row = lane_index(), row_index()
    land = land_ref[...]

    def level(k, _):
        centre, east, west, north, south = combine([rates_ref[d, k] for d in range(4)], land)
        column_ref[k] = jnp.where(lane == 0, west, jnp.where(lane == LANES - 1, east, 0.0))
        row_ref[k] = jnp.where(row == 0, south, jnp.where(row == 7, north, 0.0))
        east, west = jnp.where(lane == LANES - 1, 0.0, east), jnp.where(lane == 0, 0.0, west)
        north, south = jnp.where(row == 7, 0.0, north), jnp.where(row == 0, 0.0, south)
        for v in range(vectors):
            s = solved_ref[k, v]
            across = east * pltpu.roll(s, LANES - 1, 1) + west * pltpu.roll(s, 1, 1)
            along = north * pltpu.roll(s, 7, 0) + south * pltpu.roll(s, 1, 0)
            inner_ref[k, v] = centre * s + across + along
        return 0

    lax.fori_loop(0, depth, level, 0, unroll=4)


def edge_merger(mate_cols, far_cols, merged_ref):
    for g in range(merged_ref.shape[0] // 8):
        part = slice(8 * g, 8 * g + 8)
        merged_ref[part, :] = merge_edges(mate_cols[part, :], far_cols[part, :], LANES - 2)


def edged(inner_ref, row_rates, column_rates, mate_ref, far_ref, edges, k, v, at, mates):
    line = pl.ds(k * inner_ref.shape[1] + v, 1)
    mate = jnp.broadcast_to(mate_ref[line, :], (8, LANES))
    far = jnp.broadcast_to(far_ref[line, :], (8, LANES))
    edge = pltpu.roll(edges, (LANES - 2 * at) & (LANES - 1), 1)
    return inner_ref[k, v] + row_rates * jnp.where(mates, mate, far) + column_rates * edge


def mate_rows_mask():
    return row_index() == 7 * (1 - parity("gy"))


def child_between(
    inner_ref, row_ref, column_ref, relax_ref, after_ref, mate_in, far_in, mate_cols, far_cols,
    sums_out, x_ref,
    sums_ref, merged_ref,
):
    depth, vectors = inner_ref.shape[0], inner_ref.shape[1]
    half, groups = depth // 2, depth // LEVELS
    mates = mate_rows_mask()
    weights = [relax_ref[j : j + 1, :] for j in range(8)]
    edge_merger(mate_cols, far_cols, merged_ref)

    def level(i, _, edges):
        inside = lax.rem(i, LEVELS)
        for side, k, base in ((0, i, inside * vectors), (1, depth - 1 - i, (LEVELS - 1 - inside) * vectors)):
            row_rates, column_rates = row_ref[k], column_ref[k]
            for v in range(vectors):
                x_ref[k, v] = edged(
                    inner_ref, row_rates, column_rates, mate_in, far_in, edges[side], k, v, base + v, mates
                )
            block_rows(x_ref, k, weights, sums_ref, i, side)
        return 0

    for group in range(half // LEVELS):
        edges = [merged_ref[8 * g : 8 * g + 8, :] for g in (group, groups - 1 - group)]
        lax.fori_loop(
            LEVELS * group, LEVELS * (group + 1), lambda i, _, edges=edges: level(i, _, edges), 0, unroll=4
        )
    sums_out[...] = block_columns(sums_ref)


def child_second(
    x_ref, a_ref, b_ref, c_ref, parent_ref, pa_ref, pb_ref, pc_ref,
    solved_ref, psolved_ref, mate_rows, far_rows, cols_ref,
):
    depth, vectors = x_ref.shape[0], x_ref.shape[1]
    y = jnp.zeros((8, LANES), F32)
    for i in range(depth // 2):
        y = pa_ref[i : i + 1, :] * parent_ref[i] + pb_ref[i : i + 1, :] * y
        psolved_ref[i] = y
    lines, at = depth * vectors, depth // LEVELS * 8
    parent_up(y, pc_ref, psolved_ref, mate_rows, far_rows, lines, cols_ref, at)
    child_first(x_ref, a_ref, b_ref, c_ref, solved_ref, mate_rows, far_rows, cols_ref)


def child_last(
    inner_ref, row_ref, column_ref, mate_in, far_in, mate_cols, far_cols, out_hbm, out_ref, merged_ref, sems
):
    depth, vectors = inner_ref.shape[0], inner_ref.shape[1]
    mates = mate_rows_mask()
    edge_merger(mate_cols, far_cols, merged_ref)
    copies = []
    for group in range(depth // LEVELS):
        edges = merged_ref[8 * group : 8 * group + 8, :]

        def level(inside, _):
            k = LEVELS * group + inside
            row_rates, column_rates = row_ref[k], column_ref[k]
            for v in range(vectors):
                out_ref[k, v] = edged(
                    inner_ref, row_rates, column_rates, mate_in, far_in, edges, k, v, inside * vectors + v, mates
                )
            return 0

        lax.fori_loop(0, LEVELS, level, 0, unroll=4)
        part = pl.ds(LEVELS * group, LEVELS)
        copies.append(pltpu.make_async_copy(out_ref.at[part], out_hbm.at[part], sems.at[group]))
        copies[-1].start()
    for copy in copies:
        copy.wait()


PLACES = [(h, r, 64 * h + 32 * r) for h in range(2) for r in range(2)]


def parent_fed(parent_ref, feed_ref, after_ref, packed_ref):
    half, vectors = packed_ref.shape[0], packed_ref.shape[1]
    for i in range(half):
        for h, r, lo in PLACES:
            k = 2 * half - 1 - i if h else i
            packed_ref[i, :, lo : lo + 32] = parent_ref[pl.ds(2 * vectors * k + r, vectors, stride=2), :]
        packed_ref[i] = packed_ref[i] + feed_ref[vectors * i : vectors * (i + 1), :]


def parent_factors(mix_ref, fed_ref, far_ref, mate_cols, far_cols, pa_ref, pb_ref, pc_ref, mixed):
    half = pa_ref.shape[0]
    for i in range(half):
        for h, r, lo in PLACES:
            k = 2 * half - 1 - i if h else i
            mixed[i : i + 1, lo : lo + 32] = mix_ref[2 * k + r : 2 * k + r + 1, :]
    upper = lane_index(1) < 64
    rows = [mixed[i : i + 1, :] for i in range(half)]
    inner, outer = [], []
    for i in range(half):
        nearer = rows[i + 1] if i + 1 < half else pltpu.roll(rows[i], 64, 1)
        inner.append(jnp.where(upper, rows[i], nearer))
        outer.append(jnp.where(upper, rows[i - 1] if i else jnp.zeros_like(rows[0]), rows[i]))
    inverse = minors(inner, outer)
    for i in range(half):
        pa_ref[i : i + 1, :] = inverse[i]
        pb_ref[i : i + 1, :] = inverse[i] * outer[i]
        pc_ref[i : i + 1, :] = inverse[i] * inner[i]


def parent_rates_packed(rates_ref, feed_ref, after_ref, packed_ref):
    half = packed_ref.shape[1]
    depth = 2 * half
    for i in range(half):
        for h, r, lo in PLACES:
            k = depth - 1 - i if h else i
            for d in range(4):
                at = 2 * (d * depth + k) + r
                packed_ref[d, i : i + 1, lo : lo + 32] = rates_ref[at : at + 1, :]


def parent_rates_masked(packed_ref, land_ref, far_ref, mate_cols, far_cols, prates_ref):
    half = packed_ref.shape[1]
    land = jnp.concatenate([land_ref[r : r + 1, :] for _, r, _ in PLACES], axis=1)
    land = jnp.broadcast_to(land, (half, LANES))
    for d, part in enumerate(combine([packed_ref[d] for d in range(4)], land)):
        prates_ref[d] = part


def parent_up(carry, pc_ref, psolved_ref, mate_rows, far_rows, lines, cols_ref, cols_at):
    half = psolved_ref.shape[0]
    lane = lane_index()
    middle = pc_ref[half - 1 : half, :]
    scale = 1.0 / (1.0 - middle * pltpu.roll(middle, 64, 1))
    x = (carry + middle * pltpu.roll(carry, 64, 1)) * scale
    tiles = [None] * half
    tiles[half - 1] = x
    for i in range(half - 2, -1, -1):
        x = psolved_ref[i] + pc_ref[i : i + 1, :] * x
        tiles[i] = x
    packed = jnp.zeros((8, LANES), F32)
    for i in range(half):
        psolved_ref[i] = tiles[i]
        packed = jnp.where(((lane & 31) >> 1) == i, pltpu.roll(tiles[i], 2 * i + 1, 1), packed)
    cols_ref[cols_at : cols_at + 8, :] = packed
    first = (lane & 32) == 0
    swap = jnp.broadcast_to(parity("gy"), (8, LANES)) == 1
    for j in range(half // 2):
        one, two = tiles[j], tiles[j + half // 2]
        lo = jnp.where(first, one, pltpu.roll(two, 32, 1))
        hi = jnp.where(first, pltpu.roll(one, 96, 1), two)
        part = slice(lines + 8 * j, lines + 8 * j + 8)
        mate_rows[part, :] = jnp.where(swap, lo, hi)
        far_rows[part, :] = jnp.where(swap, hi, lo)


def parent_edges(mate_cols, far_cols, at):
    return merge_edges(mate_cols[at : at + 8, :], far_cols[at : at + 8, :], 62)


def parent_transport(psolved_ref, prates_ref, mate_row, far_row, edges, i):
    half = psolved_ref.shape[0]
    lane = lane_index()
    swap = jnp.broadcast_to(parity("gy"), (8, LANES)) == 1
    x = psolved_ref[i]
    mate, far = mate_row(i % (half // 2)), far_row(i % (half // 2))
    lo, hi = jnp.where(swap, far, mate), jnp.where(swap, mate, far)
    if i < half // 2:
        lo = pltpu.roll(lo, 32, 1)
    else:
        hi = pltpu.roll(hi, 96, 1)
    first = (lane & 32) == 0
    to_north = jnp.where(first, pltpu.roll(x, 96, 1), lo)
    to_south = jnp.where(first, hi, pltpu.roll(x, 32, 1))
    edge = pltpu.roll(edges, (LANES - 2 * i - 32) & (LANES - 1), 1)
    column = lane & 31
    to_east = jnp.where(column == 31, edge, pltpu.roll(x, 127, 1))
    to_west = jnp.where(column == 0, edge, pltpu.roll(x, 1, 1))
    parts = [prates_ref[d, i : i + 1, :] for d in range(5)]
    return (parts[0] * x + parts[1] * to_east) + (parts[2] * to_west + parts[3] * to_north) + parts[4] * to_south


def parent_second(
    psolved_in, prates_ref, pa_ref, pb_ref, pc_ref, mate_in, far_in, mate_cols, far_cols, feed_ref,
    psolved_ref, mate_rows, far_rows, cols_ref,
):
    half = psolved_in.shape[0]
    lines = mate_in.shape[0] - mate_rows.shape[0]
    edges = parent_edges(mate_cols, far_cols, mate_cols.shape[0] - 8)
    mate = lambda j: mate_in[lines + 8 * j : lines + 8 * j + 8, :]
    far = lambda j: far_in[lines + 8 * j : lines + 8 * j + 8, :]
    y = jnp.zeros((8, LANES), F32)
    for i in range(half):
        rhs = parent_transport(psolved_in, prates_ref, mate, far, edges, i)
        rhs = rhs + feed_ref[8 * i : 8 * i + 8, :]
        y = pa_ref[i : i + 1, :] * rhs + pb_ref[i : i + 1, :] * y
        psolved_ref[i] = y
    parent_up(y, pc_ref, psolved_ref, mate_rows, far_rows, 0, cols_ref, 0)


def parent_last(psolved_in, prates_ref, mate_in, far_in, mate_cols, far_cols, out_ref):
    half, vectors = psolved_in.shape[0], psolved_in.shape[1]
    edges = parent_edges(mate_cols, far_cols, 0)
    mate = lambda j: mate_in[8 * j : 8 * j + 8, :]
    far = lambda j: far_in[8 * j : 8 * j + 8, :]
    for i in range(half):
        x = parent_transport(psolved_in, prates_ref, mate, far, edges, i)
        for h in range(2):
            for r in range(2):
                lo = 64 * h + 32 * r
                k = 2 * half - 1 - i if h else i
                out_ref[pl.ds(2 * vectors * k + r, vectors, stride=2), :] = x[:, lo : lo + 32]


def passed_along(value, axis, steps):
    count = lax.axis_size(axis)
    return lax.ppermute(value, axis, [(i, (i + steps) % count) for i in range(count)])


def swapped(value, axis, offset):
    count = lax.axis_size(axis)
    pairs = []
    for i in range(offset, count, 2):
        j = (i + 1) % count
        pairs += [(i, j), (j, i)]
    return lax.ppermute(value, axis, pairs)


def halos_of(mate, far, cols):
    return [swapped(mate, "gy", 0), swapped(far, "gy", 1), swapped(cols, "gx", 0), swapped(cols, "gx", 1)]


def local(
    child_adjoint,
    parent_adjoint,
    child_rates,
    child_mixing,
    child_land,
    parent_rates,
    parent_mixing,
    parent_land,
    relaxation,
):
    depth, vectors, lines, columns = child_adjoint.shape
    half = depth // 2
    quarter = lax.axis_size("gy") // 4
    field = shape(depth, vectors, lines, columns)
    factor = shape(depth, lines, columns)
    tiles = shape(half, vectors, LANES)
    sums = shape(half * vectors, LANES)
    count = depth * vectors
    edge = depth // LEVELS * 8
    sum_scratch = pltpu.VMEM((half * vectors, 4 * LANES), F32)
    edge_scratch = [pltpu.VMEM((edge, LANES), F32)]
    narrow = parent_adjoint.shape[-1]

    sums1, x, a, b, c, relax, land, parent_land, rates = call(
        begin,
        [sums, field, factor, factor, factor, shape(lines, columns), shape(lines, columns), shape(*parent_land.shape)]
        + [shape(*child_rates.shape)],
        [
            pltpu.VMEM(factor.shape, F32),
            pltpu.VMEM(child_land.shape, jnp.int32),
            pltpu.VMEM(parent_land.shape, jnp.int32),
            sum_scratch,
            pltpu.SemaphoreType.DMA((5 + half // 2,)),
        ],
        [child_adjoint, child_mixing, relaxation, child_land, parent_land, child_rates],
        4_000_000,
        3_000_000,
        far_in=range(6),
    )
    feed = passed_along(sums1, "gy", quarter)
    solved, mate, far, cols = call(
        child_first,
        [field, shape(count, LANES), shape(count, LANES), shape(edge, LANES)],
        [],
        [x, a, b, c],
        4_000_000,
        3_000_000,
    )
    halos = halos_of(mate, far, cols)
    inner, row_rates, column_rates = call(
        child_inner,
        [field, factor, factor],
        [],
        [solved, rates, land, cols],
        INNER,
        4_000_000,
    )
    fed = call(
        parent_fed,
        tiles,
        [],
        [parent_adjoint.reshape(-1, narrow), feed, inner],
        LONG,
        1_000_000,
    )
    pa, pb, pc = call(
        parent_factors,
        [shape(half, LANES)] * 3,
        [pltpu.VMEM((half, LANES), F32)],
        [parent_mixing.reshape(-1, narrow), fed, *halos[1:]],
        LONG,
        1_000_000,
    )
    sums2, x = call(
        child_between,
        [sums, field],
        [sum_scratch] + edge_scratch,
        [inner, row_rates, column_rates, relax, pa, *halos],
        8_000_000,
        3_000_000,
    )
    feed = passed_along(sums2, "gy", quarter)
    rows = count + half // 2 * vectors
    solved, psolved, mate, far, cols = call(
        child_second,
        [field, tiles, shape(rows, LANES), shape(rows, LANES), shape(edge + 8, LANES)],
        [],
        [x, a, b, c, fed, pa, pb, pc],
        8_000_000,
        3_000_000,
    )
    halos = halos_of(mate, far, cols)
    inner, row_rates, column_rates = call(
        child_inner,
        [field, factor, factor],
        [],
        [solved, rates, land, cols],
        INNER,
        4_000_000,
    )
    packed_rates = call(
        parent_rates_packed,
        shape(4, half, LANES),
        [],
        [parent_rates.reshape(-1, narrow), feed, inner],
        1_450_000_000,
        1_000_000,
    )
    prates = call(
        parent_rates_masked,
        shape(5, half, LANES),
        [],
        [packed_rates, parent_land, *halos[1:]],
        LONG,
        1_000_000,
    )
    few = half // 2 * vectors
    psolved, mate, far, cols = call(
        parent_second,
        [tiles, shape(few, LANES), shape(few, LANES), shape(8, LANES)],
        [],
        [psolved, prates, pa, pb, pc, *halos, feed],
        1_000_000,
        500_000,
    )
    last_halos = halos_of(mate, far, cols)
    child_out = call(
        child_last,
        field,
        [pltpu.VMEM(field.shape, F32)] + edge_scratch + [pltpu.SemaphoreType.DMA((depth // LEVELS,))],
        [inner, row_rates, column_rates, *halos],
        4_000_000,
        3_000_000,
        far_out=True,
    )
    parent_out = call(
        parent_last,
        shape(depth * vectors * 2, narrow),
        [],
        [psolved, prates, *last_halos],
        500_000,
        500_000,
    )
    return (child_out, parent_out.reshape(parent_adjoint.shape))


def solution(mesh):
    wide = P(None, None, "gy", "gx")
    level = P(None, "gy", "gx")
    flat = P("gy", "gx")
    in_specs = (wide, wide, wide, level, flat, wide, level, flat, flat)
    return jax.shard_map(local, mesh=mesh, in_specs=in_specs, out_specs=(wide, wide), check_vma=False)
```

```python
import jax
import jax.numpy as jnp
from jax import lax
from jax.experimental import pallas as pl
from jax.experimental.pallas import tpu as pltpu
from jax.sharding import PartitionSpec as P

F32 = jnp.float32
VMEM = pl.BlockSpec(memory_space=pltpu.VMEM)
FAR = pl.BlockSpec(memory_space=pltpu.HBM)
LIMIT = 40 * 1024 * 1024
LANES = 128
LONG = 1_000_000_000
INNER = 10_000_000
LEVELS = 8


def shape(*dims):
    return jax.ShapeDtypeStruct(dims, F32)


def call(body, outs, scratch, operands, flops, touched, far_in=(), far_out=False):
    operands = [pltpu.with_memory_space_constraint(x, pltpu.HBM) if i in far_in else x for i, x in enumerate(operands)]
    return pl.pallas_call(
        body,
        out_shape=outs,
        in_specs=[FAR if i in far_in else VMEM for i in range(len(operands))],
        out_specs=jax.tree.map(lambda _: FAR if far_out else VMEM, outs),
        scratch_shapes=scratch,
        compiler_params=pltpu.CompilerParams(vmem_limit_bytes=LIMIT),
        cost_estimate=pl.CostEstimate(flops=flops, bytes_accessed=touched, transcendentals=0),
        name=body.__name__,
    )(*operands)


def lane_index(rows=8):
    return lax.broadcasted_iota(jnp.int32, (rows, LANES), 1)


def row_index():
    return lax.broadcasted_iota(jnp.int32, (8, LANES), 0)


def minors(inner, outer):
    theta = delta = jnp.ones_like(inner[0])
    inverse = []
    for i in range(len(inner)):
        delta = theta + outer[i] * delta
        theta_next = delta + inner[i] * theta
        inverse.append(theta / theta_next)
        theta = theta_next
    return inverse


def parity(axis):
    return lax.rem(lax.axis_index(axis), 2)


def child_factors(mix_ref, keep, a_ref, b_ref, c_ref):
    depth = mix_ref.shape[0]
    half = depth // 2
    zero = jnp.zeros_like(keep)
    top_inner = [mix_ref[i] for i in range(half)]
    top_outer = [zero] + top_inner[:-1]
    low_outer = [mix_ref[depth - 1 - i] for i in range(half)]
    low_inner = [mix_ref[depth - 2 - i] for i in range(half)]
    for levels, inner, outer in (
        (range(half), top_inner, top_outer),
        (range(depth - 1, half - 1, -1), low_inner, low_outer),
    ):
        inverse = minors(inner, outer)
        for i, k in enumerate(levels):
            a_ref[k] = inverse[i] * keep
            b_ref[k] = inverse[i] * outer[i]
            c_ref[k] = inverse[i] * inner[i]


def block_rows(source_ref, k, weights, sums_ref, i, place):
    vectors = source_ref.shape[1]
    for r in range(2):
        total = source_ref[k, :, 4 * r, :] * weights[4 * r]
        for j in range(4 * r + 1, 4 * r + 4):
            total = total + source_ref[k, :, j, :] * weights[j]
        column = (2 * place + r) * LANES
        sums_ref[pl.ds(i * vectors, vectors), column : column + LANES] = total


def block_columns(sums_ref):
    wide = sums_ref.shape[1]
    p = lax.broadcasted_iota(jnp.int32, (wide, LANES), 0)
    q = lax.broadcasted_iota(jnp.int32, (wide, LANES), 1)
    pick = jnp.where(p // 4 == q, F32(0.0625), F32(0.0)).astype(jnp.bfloat16)
    rest, total = sums_ref[...], None
    for _ in range(3):
        part = rest.astype(jnp.bfloat16)
        rest = rest - part.astype(F32)
        product = jnp.dot(part, pick, preferred_element_type=F32)
        total = product if total is None else total + product
    return total


def child_middle(carry, c_ref, half):
    vectors = len(carry) // 2
    top, low = c_ref[half - 1], c_ref[half]
    scale = 1.0 / (1.0 - top * low)
    first = [(carry[v] + top * carry[vectors + v]) * scale for v in range(vectors)]
    second = [(carry[vectors + v] + low * carry[v]) * scale for v in range(vectors)]
    return first + second


def child_up(carry, c_ref, solved_ref, mate_rows, far_rows, cols_ref):
    depth, vectors = solved_ref.shape[0], solved_ref.shape[1]
    half = depth // 2
    lane = lane_index()
    pair = lane >> 1
    odd = parity("gy")
    mate_row, far_row = 7 * (1 - odd), 7 * odd

    def emit(i, values, packed):
        k_low = depth - 1 - i
        packed = list(packed)
        inside = i % LEVELS if isinstance(i, int) else lax.rem(i, LEVELS)
        for side, k, base in ((0, i, inside * vectors), (1, k_low, (LEVELS - 1 - inside) * vectors)):
            for v in range(vectors):
                x = values[side * vectors + v]
                solved_ref[k, v] = x
                at = base + v
                packed[side] = jnp.where(pair == at, pltpu.roll(x, 2 * at + 1 & (LANES - 1), 1), packed[side])
            mate_rows[pl.ds(k * vectors, vectors), :] = solved_ref[k, :, mate_row, :]
            far_rows[pl.ds(k * vectors, vectors), :] = solved_ref[k, :, far_row, :]
        return packed

    def up(i, state):
        k_low = depth - 1 - i
        top, low = c_ref[i], c_ref[k_low]
        values = []
        for v in range(vectors):
            values.append(solved_ref[i, v] + top * state[v])
        for v in range(vectors):
            values.append(solved_ref[k_low, v] + low * state[vectors + v])
        return tuple(values) + tuple(emit(i, values, state[2 * vectors :]))

    def keep_columns(group, packed):
        for side, g in ((0, group), (1, depth // LEVELS - 1 - group)):
            cols_ref[LEVELS * g : LEVELS * g + 8, :] = packed[side]

    blank = jnp.zeros((8, LANES), F32)
    values = child_middle(carry, c_ref, half)
    state = tuple(values) + tuple(emit(half - 1, values, [blank] * 2))
    for group in range(half // LEVELS - 1, -1, -1):
        last = LEVELS * (group + 1) - 1
        if group == half // LEVELS - 1:
            last -= 1
        count = last - LEVELS * group + 1
        state = lax.fori_loop(0, count, lambda step, state, last=last: up(last - step, state), state, unroll=4 if count % 4 == 0 else count)
        keep_columns(group, state[2 * vectors :])
        state = state[: 2 * vectors] + (blank,) * 2


def begin(
    x_hbm, mix_hbm, relax_hbm, land_hbm, parent_land_hbm,
    sums_out, x_ref, a_ref, b_ref, c_ref, relax_ref, land_ref, parent_land_ref,
    mix_ref, land_in, parent_land_in, sums_ref, sems,
):
    depth = x_ref.shape[0]
    half = depth // 2
    small = []
    for source, target in (
        (mix_hbm, mix_ref), (relax_hbm, relax_ref), (land_hbm, land_in), (parent_land_hbm, parent_land_in),
    ):
        small.append(pltpu.make_async_copy(source, target, sems.at[len(small)]))
        small[-1].start()
    size, large = 4, []
    for start in range(0, half, size):
        for first in (start, depth - size - start):
            part = pl.ds(first, size)
            large.append(pltpu.make_async_copy(x_hbm.at[part], x_ref.at[part], sems.at[len(large) + len(small)]))
            large[-1].start()
    for copy in small:
        copy.wait()
    land_ref[...] = land_in[...].astype(F32)
    parent_land_ref[...] = parent_land_in[...].astype(F32)
    child_factors(mix_ref, 1.0 - relax_ref[...], a_ref, b_ref, c_ref)
    weights = [relax_ref[j : j + 1, :] for j in range(8)]

    def level(i, _):
        for side, k in ((0, i), (1, depth - 1 - i)):
            block_rows(x_ref, k, weights, sums_ref, i, side)
        return 0

    for part, start in enumerate(range(0, half, size)):
        large[2 * part].wait()
        large[2 * part + 1].wait()
        lax.fori_loop(start, start + size, level, 0, unroll=size)
    sums_out[...] = block_columns(sums_ref)


def child_first(
    x_ref, a_ref, b_ref, c_ref, rates_hbm, solved_ref, mate_rows, far_rows, cols_ref, rates_ref, sem
):
    copy = pltpu.make_async_copy(rates_hbm, rates_ref, sem)
    copy.start()
    child_solve(x_ref, a_ref, b_ref, c_ref, solved_ref, mate_rows, far_rows, cols_ref)
    copy.wait()


def child_solve(x_ref, a_ref, b_ref, c_ref, solved_ref, mate_rows, far_rows, cols_ref):
    depth, vectors = x_ref.shape[0], x_ref.shape[1]
    half = depth // 2

    def down(i, carry):
        values = []
        for side, k in ((0, i), (1, depth - 1 - i)):
            a, b = a_ref[k], b_ref[k]
            for v in range(vectors):
                y = a * x_ref[k, v] + b * carry[side * vectors + v]
                solved_ref[k, v] = y
                values.append(y)
        return tuple(values)

    carry = lax.fori_loop(0, half, down, (jnp.zeros((8, LANES), F32),) * (2 * vectors), unroll=4)
    child_up(carry, c_ref, solved_ref, mate_rows, far_rows, cols_ref)


def combine(sides, land):
    east, west, north, south = sides
    return [land * part for part in (1.0 - (east + west + north + south), east, west, north, south)]


def merge_edges(mate, far, turn):
    swap = jnp.broadcast_to(parity("gx"), (8, LANES)) == 1
    east, west = jnp.where(swap, far, mate), jnp.where(swap, mate, far)
    return jnp.where((lane_index() & 1) == 0, west, pltpu.roll(east, turn, 1))


def child_inner(solved_ref, rates_ref, land_ref, after_ref, inner_ref, row_ref, column_ref):
    depth, vectors = solved_ref.shape[0], solved_ref.shape[1]
    lane, row = lane_index(), row_index()
    land = land_ref[...]

    def level(k, _):
        centre, east, west, north, south = combine([rates_ref[d, k] for d in range(4)], land)
        column_ref[k] = jnp.where(lane == 0, west, jnp.where(lane == LANES - 1, east, 0.0))
        row_ref[k] = jnp.where(row == 0, south, jnp.where(row == 7, north, 0.0))
        east, west = jnp.where(lane == LANES - 1, 0.0, east), jnp.where(lane == 0, 0.0, west)
        north, south = jnp.where(row == 7, 0.0, north), jnp.where(row == 0, 0.0, south)
        for v in range(vectors):
            s = solved_ref[k, v]
            across = east * pltpu.roll(s, LANES - 1, 1) + west * pltpu.roll(s, 1, 1)
            along = north * pltpu.roll(s, 7, 0) + south * pltpu.roll(s, 1, 0)
            inner_ref[k, v] = centre * s + across + along
        return 0

    lax.fori_loop(0, depth, level, 0, unroll=4)


def edge_merger(mate_cols, far_cols, merged_ref):
    for g in range(merged_ref.shape[0] // 8):
        part = slice(8 * g, 8 * g + 8)
        merged_ref[part, :] = merge_edges(mate_cols[part, :], far_cols[part, :], LANES - 2)


def column_edges(target_ref, inner_ref, column_ref, edges, k, base):
    rates = column_ref[k]
    for v in range(inner_ref.shape[1]):
        edge = pltpu.roll(edges, (LANES - 2 * (base + v)) & (LANES - 1), 1)
        target_ref[k, v] = inner_ref[k, v] + rates * edge


def row_edges(target_ref, row_ref, mate_ref, far_ref, k):
    vectors = target_ref.shape[1]
    odd = parity("gy")
    for halo_ref, at in ((mate_ref, 7 * (1 - odd)), (far_ref, 7 * odd)):
        part = row_ref[k, pl.ds(at, 1), :] * halo_ref[pl.ds(pl.multiple_of(k * vectors, vectors), vectors), :]
        target_ref[k, :, at, :] = target_ref[k, :, at, :] + part


def child_between(
    inner_ref, row_ref, column_ref, relax_ref, after_ref, mate_in, far_in, mate_cols, far_cols,
    sums_out, x_ref,
    sums_ref, merged_ref,
):
    depth, vectors = inner_ref.shape[0], inner_ref.shape[1]
    half = depth // 2
    weights = [relax_ref[j : j + 1, :] for j in range(8)]
    edge_merger(mate_cols, far_cols, merged_ref)
    for group in range(depth // LEVELS):
        edges = merged_ref[8 * group : 8 * group + 8, :]
        first = LEVELS * group

        def columns(inside, _):
            column_edges(x_ref, inner_ref, column_ref, edges, first + inside, inside * vectors)
            return 0

        lax.fori_loop(0, LEVELS, columns, 0, unroll=4)

    def rows(k, _):
        row_edges(x_ref, row_ref, mate_in, far_in, k)
        return 0

    lax.fori_loop(0, depth, rows, 0, unroll=8)

    def level(i, _):
        for side, k in ((0, i), (1, depth - 1 - i)):
            block_rows(x_ref, k, weights, sums_ref, i, side)
        return 0

    lax.fori_loop(0, half, level, 0, unroll=4)
    sums_out[...] = block_columns(sums_ref)


def child_second(
    x_ref, a_ref, b_ref, c_ref, parent_ref, pa_ref, pb_ref, pc_ref,
    solved_ref, psolved_ref, mate_rows, far_rows, cols_ref,
):
    depth, vectors = x_ref.shape[0], x_ref.shape[1]
    y = jnp.zeros((8, LANES), F32)
    for i in range(depth // 2):
        y = pa_ref[i : i + 1, :] * parent_ref[i] + pb_ref[i : i + 1, :] * y
        psolved_ref[i] = y
    lines, at = depth * vectors, depth // LEVELS * 8
    parent_up(y, pc_ref, psolved_ref, mate_rows, far_rows, lines, cols_ref, at)
    child_solve(x_ref, a_ref, b_ref, c_ref, solved_ref, mate_rows, far_rows, cols_ref)


def child_last(
    inner_ref, row_ref, column_ref, mate_in, far_in, mate_cols, far_cols, out_hbm, out_ref, merged_ref, sems
):
    depth, vectors = inner_ref.shape[0], inner_ref.shape[1]
    edge_merger(mate_cols, far_cols, merged_ref)
    copies = []
    for group in range(depth // LEVELS):
        edges = merged_ref[8 * group : 8 * group + 8, :]
        first = LEVELS * group

        def columns(inside, _):
            column_edges(out_ref, inner_ref, column_ref, edges, first + inside, inside * vectors)
            return 0

        def rows(inside, _):
            row_edges(out_ref, row_ref, mate_in, far_in, first + inside)
            return 0

        lax.fori_loop(0, LEVELS, columns, 0, unroll=4)
        lax.fori_loop(0, LEVELS, rows, 0, unroll=LEVELS)
        part = pl.ds(first, LEVELS)
        copies.append(pltpu.make_async_copy(out_ref.at[part], out_hbm.at[part], sems.at[group]))
        copies[-1].start()
    for copy in copies:
        copy.wait()


PLACES = [(h, r, 64 * h + 32 * r) for h in range(2) for r in range(2)]


def parent_fed(parent_ref, feed_ref, after_ref, packed_ref):
    half, vectors = packed_ref.shape[0], packed_ref.shape[1]
    for i in range(half):
        for h, r, lo in PLACES:
            k = 2 * half - 1 - i if h else i
            packed_ref[i, :, lo : lo + 32] = parent_ref[pl.ds(2 * vectors * k + r, vectors, stride=2), :]
        packed_ref[i] = packed_ref[i] + feed_ref[vectors * i : vectors * (i + 1), :]


def parent_factors(mix_ref, fed_ref, far_ref, mate_cols, far_cols, pa_ref, pb_ref, pc_ref, mixed):
    half = pa_ref.shape[0]
    for i in range(half):
        for h, r, lo in PLACES:
            k = 2 * half - 1 - i if h else i
            mixed[i : i + 1, lo : lo + 32] = mix_ref[2 * k + r : 2 * k + r + 1, :]
    upper = lane_index(1) < 64
    rows = [mixed[i : i + 1, :] for i in range(half)]
    inner, outer = [], []
    for i in range(half):
        nearer = rows[i + 1] if i + 1 < half else pltpu.roll(rows[i], 64, 1)
        inner.append(jnp.where(upper, rows[i], nearer))
        outer.append(jnp.where(upper, rows[i - 1] if i else jnp.zeros_like(rows[0]), rows[i]))
    inverse = minors(inner, outer)
    for i in range(half):
        pa_ref[i : i + 1, :] = inverse[i]
        pb_ref[i : i + 1, :] = inverse[i] * outer[i]
        pc_ref[i : i + 1, :] = inverse[i] * inner[i]


def parent_rates_packed(rates_ref, feed_ref, after_ref, packed_ref):
    half = packed_ref.shape[1]
    depth = 2 * half
    for i in range(half):
        for h, r, lo in PLACES:
            k = depth - 1 - i if h else i
            for d in range(4):
                at = 2 * (d * depth + k) + r
                packed_ref[d, i : i + 1, lo : lo + 32] = rates_ref[at : at + 1, :]


def parent_rates_masked(packed_ref, land_ref, far_ref, mate_cols, far_cols, prates_ref):
    half = packed_ref.shape[1]
    land = jnp.concatenate([land_ref[r : r + 1, :] for _, r, _ in PLACES], axis=1)
    land = jnp.broadcast_to(land, (half, LANES))
    for d, part in enumerate(combine([packed_ref[d] for d in range(4)], land)):
        prates_ref[d] = part


def parent_up(carry, pc_ref, psolved_ref, mate_rows, far_rows, lines, cols_ref, cols_at):
    half = psolved_ref.shape[0]
    lane = lane_index()
    middle = pc_ref[half - 1 : half, :]
    scale = 1.0 / (1.0 - middle * pltpu.roll(middle, 64, 1))
    x = (carry + middle * pltpu.roll(carry, 64, 1)) * scale
    tiles = [None] * half
    tiles[half - 1] = x
    for i in range(half - 2, -1, -1):
        x = psolved_ref[i] + pc_ref[i : i + 1, :] * x
        tiles[i] = x
    packed = jnp.zeros((8, LANES), F32)
    for i in range(half):
        psolved_ref[i] = tiles[i]
        packed = jnp.where(((lane & 31) >> 1) == i, pltpu.roll(tiles[i], 2 * i + 1, 1), packed)
    cols_ref[cols_at : cols_at + 8, :] = packed
    first = (lane & 32) == 0
    swap = jnp.broadcast_to(parity("gy"), (8, LANES)) == 1
    for j in range(half // 2):
        one, two = tiles[j], tiles[j + half // 2]
        lo = jnp.where(first, one, pltpu.roll(two, 32, 1))
        hi = jnp.where(first, pltpu.roll(one, 96, 1), two)
        part = slice(lines + 8 * j, lines + 8 * j + 8)
        mate_rows[part, :] = jnp.where(swap, lo, hi)
        far_rows[part, :] = jnp.where(swap, hi, lo)


def parent_edges(mate_cols, far_cols, at):
    return merge_edges(mate_cols[at : at + 8, :], far_cols[at : at + 8, :], 62)


def parent_transport(psolved_ref, prates_ref, mate_row, far_row, edges, i):
    half = psolved_ref.shape[0]
    lane = lane_index()
    swap = jnp.broadcast_to(parity("gy"), (8, LANES)) == 1
    x = psolved_ref[i]
    mate, far = mate_row(i % (half // 2)), far_row(i % (half // 2))
    lo, hi = jnp.where(swap, far, mate), jnp.where(swap, mate, far)
    if i < half // 2:
        lo = pltpu.roll(lo, 32, 1)
    else:
        hi = pltpu.roll(hi, 96, 1)
    first = (lane & 32) == 0
    to_north = jnp.where(first, pltpu.roll(x, 96, 1), lo)
    to_south = jnp.where(first, hi, pltpu.roll(x, 32, 1))
    edge = pltpu.roll(edges, (LANES - 2 * i - 32) & (LANES - 1), 1)
    column = lane & 31
    to_east = jnp.where(column == 31, edge, pltpu.roll(x, 127, 1))
    to_west = jnp.where(column == 0, edge, pltpu.roll(x, 1, 1))
    parts = [prates_ref[d, i : i + 1, :] for d in range(5)]
    return (parts[0] * x + parts[1] * to_east) + (parts[2] * to_west + parts[3] * to_north) + parts[4] * to_south


def parent_second(
    psolved_in, prates_ref, pa_ref, pb_ref, pc_ref, mate_in, far_in, mate_cols, far_cols, feed_ref,
    psolved_ref, mate_rows, far_rows, cols_ref,
):
    half = psolved_in.shape[0]
    lines = mate_in.shape[0] - mate_rows.shape[0]
    edges = parent_edges(mate_cols, far_cols, mate_cols.shape[0] - 8)
    mate = lambda j: mate_in[lines + 8 * j : lines + 8 * j + 8, :]
    far = lambda j: far_in[lines + 8 * j : lines + 8 * j + 8, :]
    y = jnp.zeros((8, LANES), F32)
    for i in range(half):
        rhs = parent_transport(psolved_in, prates_ref, mate, far, edges, i)
        rhs = rhs + feed_ref[8 * i : 8 * i + 8, :]
        y = pa_ref[i : i + 1, :] * rhs + pb_ref[i : i + 1, :] * y
        psolved_ref[i] = y
    parent_up(y, pc_ref, psolved_ref, mate_rows, far_rows, 0, cols_ref, 0)


def parent_last(psolved_in, prates_ref, mate_in, far_in, mate_cols, far_cols, out_ref):
    half, vectors = psolved_in.shape[0], psolved_in.shape[1]
    edges = parent_edges(mate_cols, far_cols, 0)
    mate = lambda j: mate_in[8 * j : 8 * j + 8, :]
    far = lambda j: far_in[8 * j : 8 * j + 8, :]
    for i in range(half):
        x = parent_transport(psolved_in, prates_ref, mate, far, edges, i)
        for h in range(2):
            for r in range(2):
                lo = 64 * h + 32 * r
                k = 2 * half - 1 - i if h else i
                out_ref[pl.ds(2 * vectors * k + r, vectors, stride=2), :] = x[:, lo : lo + 32]


def passed_along(value, axis, steps):
    count = lax.axis_size(axis)
    return lax.ppermute(value, axis, [(i, (i + steps) % count) for i in range(count)])


def swapped(value, axis, offset):
    count = lax.axis_size(axis)
    pairs = []
    for i in range(offset, count, 2):
        j = (i + 1) % count
        pairs += [(i, j), (j, i)]
    return lax.ppermute(value, axis, pairs)


def halos_of(mate, far, cols):
    return [swapped(mate, "gy", 0), swapped(far, "gy", 1), swapped(cols, "gx", 0), swapped(cols, "gx", 1)]


def local(
    child_adjoint,
    parent_adjoint,
    child_rates,
    child_mixing,
    child_land,
    parent_rates,
    parent_mixing,
    parent_land,
    relaxation,
):
    depth, vectors, lines, columns = child_adjoint.shape
    half = depth // 2
    quarter = lax.axis_size("gy") // 4
    field = shape(depth, vectors, lines, columns)
    factor = shape(depth, lines, columns)
    tiles = shape(half, vectors, LANES)
    sums = shape(half * vectors, LANES)
    count = depth * vectors
    edge = depth // LEVELS * 8
    sum_scratch = pltpu.VMEM((half * vectors, 4 * LANES), F32)
    edge_scratch = [pltpu.VMEM((edge, LANES), F32)]
    narrow = parent_adjoint.shape[-1]

    sums1, x, a, b, c, relax, land, parent_land = call(
        begin,
        [sums, field, factor, factor, factor, shape(lines, columns), shape(lines, columns), shape(*parent_land.shape)],
        [
            pltpu.VMEM(factor.shape, F32),
            pltpu.VMEM(child_land.shape, jnp.int32),
            pltpu.VMEM(parent_land.shape, jnp.int32),
            sum_scratch,
            pltpu.SemaphoreType.DMA((4 + half // 2,)),
        ],
        [child_adjoint, child_mixing, relaxation, child_land, parent_land],
        4_000_000,
        3_000_000,
        far_in=range(5),
    )
    feed = passed_along(sums1, "gy", quarter)
    solved, mate, far, cols, rates = call(
        child_first,
        [field, shape(count, LANES), shape(count, LANES), shape(edge, LANES), shape(*child_rates.shape)],
        [pltpu.SemaphoreType.DMA],
        [x, a, b, c, child_rates],
        4_000_000,
        3_000_000,
        far_in=(4,),
    )
    halos = halos_of(mate, far, cols)
    inner, row_rates, column_rates = call(
        child_inner,
        [field, factor, factor],
        [],
        [solved, rates, land, cols],
        INNER,
        4_000_000,
    )
    fed = call(
        parent_fed,
        tiles,
        [],
        [parent_adjoint.reshape(-1, narrow), feed, inner],
        LONG,
        1_000_000,
    )
    pa, pb, pc = call(
        parent_factors,
        [shape(half, LANES)] * 3,
        [pltpu.VMEM((half, LANES), F32)],
        [parent_mixing.reshape(-1, narrow), fed, *halos[1:]],
        LONG,
        1_000_000,
    )
    sums2, x = call(
        child_between,
        [sums, field],
        [sum_scratch] + edge_scratch,
        [inner, row_rates, column_rates, relax, pa, *halos],
        8_000_000,
        3_000_000,
    )
    feed = passed_along(sums2, "gy", quarter)
    rows = count + half // 2 * vectors
    solved, psolved, mate, far, cols = call(
        child_second,
        [field, tiles, shape(rows, LANES), shape(rows, LANES), shape(edge + 8, LANES)],
        [],
        [x, a, b, c, fed, pa, pb, pc],
        8_000_000,
        3_000_000,
    )
    halos = halos_of(mate, far, cols)
    inner, row_rates, column_rates = call(
        child_inner,
        [field, factor, factor],
        [],
        [solved, rates, land, cols],
        INNER,
        4_000_000,
    )
    packed_rates = call(
        parent_rates_packed,
        shape(4, half, LANES),
        [],
        [parent_rates.reshape(-1, narrow), feed, inner],
        1_450_000_000,
        1_000_000,
    )
    prates = call(
        parent_rates_masked,
        shape(5, half, LANES),
        [],
        [packed_rates, parent_land, *halos[1:]],
        LONG,
        1_000_000,
    )
    few = half // 2 * vectors
    psolved, mate, far, cols = call(
        parent_second,
        [tiles, shape(few, LANES), shape(few, LANES), shape(8, LANES)],
        [],
        [psolved, prates, pa, pb, pc, *halos, feed],
        1_000_000,
        500_000,
    )
    last_halos = halos_of(mate, far, cols)
    child_out = call(
        child_last,
        field,
        [pltpu.VMEM(field.shape, F32)] + edge_scratch + [pltpu.SemaphoreType.DMA((depth // LEVELS,))],
        [inner, row_rates, column_rates, *halos],
        4_000_000,
        3_000_000,
        far_out=True,
    )
    parent_out = call(
        parent_last,
        shape(depth * vectors * 2, narrow),
        [],
        [psolved, prates, *last_halos],
        500_000,
        500_000,
    )
    return (child_out, parent_out.reshape(parent_adjoint.shape))


def solution(mesh):
    wide = P(None, None, "gy", "gx")
    level = P(None, "gy", "gx")
    flat = P("gy", "gx")
    in_specs = (wide, wide, wide, level, flat, wide, level, flat, flat)
    return jax.shard_map(local, mesh=mesh, in_specs=in_specs, out_specs=(wide, wide), check_vma=False)
```

```python
import jax
import jax.numpy as jnp
from jax import lax
from jax.experimental import pallas as pl
from jax.experimental.pallas import tpu as pltpu
from jax.sharding import PartitionSpec as P

F32 = jnp.float32
VMEM = pl.BlockSpec(memory_space=pltpu.VMEM)
FAR = pl.BlockSpec(memory_space=pltpu.HBM)
LIMIT = 40 * 1024 * 1024
LANES = 128
LONG = 1_000_000_000
INNER = 10_000_000
LEVELS = 8


def shape(*dims):
    return jax.ShapeDtypeStruct(dims, F32)


def call(body, outs, scratch, operands, flops, touched, far_in=(), far_out=False):
    operands = [pltpu.with_memory_space_constraint(x, pltpu.HBM) if i in far_in else x for i, x in enumerate(operands)]
    return pl.pallas_call(
        body,
        out_shape=outs,
        in_specs=[FAR if i in far_in else VMEM for i in range(len(operands))],
        out_specs=jax.tree.map(lambda _: FAR if far_out else VMEM, outs),
        scratch_shapes=scratch,
        compiler_params=pltpu.CompilerParams(vmem_limit_bytes=LIMIT),
        cost_estimate=pl.CostEstimate(flops=flops, bytes_accessed=touched, transcendentals=0),
        name=body.__name__,
    )(*operands)


def lane_index(rows=8):
    return lax.broadcasted_iota(jnp.int32, (rows, LANES), 1)


def row_index():
    return lax.broadcasted_iota(jnp.int32, (8, LANES), 0)


def minors(inner, outer):
    theta = delta = jnp.ones_like(inner[0])
    inverse = []
    for i in range(len(inner)):
        delta = theta + outer[i] * delta
        theta_next = delta + inner[i] * theta
        inverse.append(theta / theta_next)
        theta = theta_next
    return inverse


def parity(axis):
    return lax.rem(lax.axis_index(axis), 2)


def child_factors(mix_ref, keep, a_ref, b_ref, c_ref):
    depth = mix_ref.shape[0]
    half = depth // 2
    zero = jnp.zeros_like(keep)
    top_inner = [mix_ref[i] for i in range(half)]
    top_outer = [zero] + top_inner[:-1]
    low_outer = [mix_ref[depth - 1 - i] for i in range(half)]
    low_inner = [mix_ref[depth - 2 - i] for i in range(half)]
    for levels, inner, outer in (
        (range(half), top_inner, top_outer),
        (range(depth - 1, half - 1, -1), low_inner, low_outer),
    ):
        inverse = minors(inner, outer)
        for i, k in enumerate(levels):
            a_ref[k] = inverse[i] * keep
            b_ref[k] = inverse[i] * outer[i]
            c_ref[k] = inverse[i] * inner[i]


def block_rows(source_ref, k, weights, sums_ref, i, place):
    vectors = source_ref.shape[1]
    for r in range(2):
        total = source_ref[k, :, 4 * r, :] * weights[4 * r]
        for j in range(4 * r + 1, 4 * r + 4):
            total = total + source_ref[k, :, j, :] * weights[j]
        column = (2 * place + r) * LANES
        sums_ref[pl.ds(i * vectors, vectors), column : column + LANES] = total


def block_columns(sums_ref):
    wide = sums_ref.shape[1]
    p = lax.broadcasted_iota(jnp.int32, (wide, LANES), 0)
    q = lax.broadcasted_iota(jnp.int32, (wide, LANES), 1)
    pick = jnp.where(p // 4 == q, F32(0.0625), F32(0.0)).astype(jnp.bfloat16)
    rest, total = sums_ref[...], None
    for _ in range(3):
        part = rest.astype(jnp.bfloat16)
        rest = rest - part.astype(F32)
        product = jnp.dot(part, pick, preferred_element_type=F32)
        total = product if total is None else total + product
    return total


def child_middle(carry, c_ref, half):
    vectors = len(carry) // 2
    top, low = c_ref[half - 1], c_ref[half]
    scale = 1.0 / (1.0 - top * low)
    first = [(carry[v] + top * carry[vectors + v]) * scale for v in range(vectors)]
    second = [(carry[vectors + v] + low * carry[v]) * scale for v in range(vectors)]
    return first + second


def child_up(carry, c_ref, solved_ref, mate_rows, far_rows, cols_ref):
    depth, vectors = solved_ref.shape[0], solved_ref.shape[1]
    half = depth // 2
    lane = lane_index()
    pair = lane >> 1
    swap = jnp.broadcast_to(parity("gy"), (8, LANES)) == 1

    def emit(i, values, packed):
        k_low = depth - 1 - i
        packed = list(packed)
        inside = i % LEVELS if isinstance(i, int) else lax.rem(i, LEVELS)
        for side, k, base in ((0, i, inside * vectors), (1, k_low, (LEVELS - 1 - inside) * vectors)):
            for v in range(vectors):
                x = values[side * vectors + v]
                solved_ref[k, v] = x
                at = base + v
                packed[side] = jnp.where(pair == at, pltpu.roll(x, 2 * at + 1 & (LANES - 1), 1), packed[side])
            lo, hi = solved_ref[k, :, 0, :], solved_ref[k, :, 7, :]
            mate_rows[pl.ds(k * vectors, vectors), :] = jnp.where(swap, lo, hi)
            far_rows[pl.ds(k * vectors, vectors), :] = jnp.where(swap, hi, lo)
        return packed

    def up(i, state):
        k_low = depth - 1 - i
        top, low = c_ref[i], c_ref[k_low]
        values = []
        for v in range(vectors):
            values.append(solved_ref[i, v] + top * state[v])
        for v in range(vectors):
            values.append(solved_ref[k_low, v] + low * state[vectors + v])
        return tuple(values) + tuple(emit(i, values, state[2 * vectors :]))

    def keep_columns(group, packed):
        for side, g in ((0, group), (1, depth // LEVELS - 1 - group)):
            cols_ref[LEVELS * g : LEVELS * g + 8, :] = packed[side]

    blank = jnp.zeros((8, LANES), F32)
    values = child_middle(carry, c_ref, half)
    state = tuple(values) + tuple(emit(half - 1, values, [blank] * 2))
    for group in range(half // LEVELS - 1, -1, -1):
        last = LEVELS * (group + 1) - 1
        if group == half // LEVELS - 1:
            last -= 1
        count = last - LEVELS * group + 1
        state = lax.fori_loop(0, count, lambda step, state, last=last: up(last - step, state), state, unroll=4 if count % 4 == 0 else count)
        keep_columns(group, state[2 * vectors :])
        state = state[: 2 * vectors] + (blank,) * 2


def begin(
    x_hbm, mix_hbm, relax_hbm, land_hbm, parent_land_hbm, rates_hbm,
    sums_out, x_ref, a_ref, b_ref, c_ref, relax_ref, land_ref, parent_land_ref, rates_ref,
    mix_ref, land_in, parent_land_in, sums_ref, sems,
):
    depth = x_ref.shape[0]
    half = depth // 2
    small = []
    for source, target in (
        (mix_hbm, mix_ref), (relax_hbm, relax_ref), (land_hbm, land_in), (parent_land_hbm, parent_land_in),
    ):
        small.append(pltpu.make_async_copy(source, target, sems.at[len(small)]))
        small[-1].start()
    size, large = 4, []
    for start in range(0, half, size):
        for first in (start, depth - size - start):
            part = pl.ds(first, size)
            large.append(pltpu.make_async_copy(x_hbm.at[part], x_ref.at[part], sems.at[len(large) + len(small)]))
            large[-1].start()
    rates_copy = pltpu.make_async_copy(rates_hbm, rates_ref, sems.at[len(large) + len(small)])
    rates_copy.start()
    for copy in small:
        copy.wait()
    land_ref[...] = land_in[...].astype(F32)
    parent_land_ref[...] = parent_land_in[...].astype(F32)
    child_factors(mix_ref, 1.0 - relax_ref[...], a_ref, b_ref, c_ref)
    weights = [relax_ref[j : j + 1, :] for j in range(8)]

    def level(i, _):
        for side, k in ((0, i), (1, depth - 1 - i)):
            block_rows(x_ref, k, weights, sums_ref, i, side)
        return 0

    for part, start in enumerate(range(0, half, size)):
        large[2 * part].wait()
        large[2 * part + 1].wait()
        lax.fori_loop(start, start + size, level, 0, unroll=size)
    sums_out[...] = block_columns(sums_ref)
    rates_copy.wait()


def child_first(x_ref, a_ref, b_ref, c_ref, solved_ref, mate_rows, far_rows, cols_ref):
    depth, vectors = x_ref.shape[0], x_ref.shape[1]
    half = depth // 2

    def down(i, carry):
        values = []
        for side, k in ((0, i), (1, depth - 1 - i)):
            a, b = a_ref[k], b_ref[k]
            for v in range(vectors):
                y = a * x_ref[k, v] + b * carry[side * vectors + v]
                solved_ref[k, v] = y
                values.append(y)
        return tuple(values)

    carry = lax.fori_loop(0, half, down, (jnp.zeros((8, LANES), F32),) * (2 * vectors), unroll=4)
    child_up(carry, c_ref, solved_ref, mate_rows, far_rows, cols_ref)


def combine(sides, land):
    east, west, north, south = sides
    return [land * part for part in (1.0 - (east + west + north + south), east, west, north, south)]


def merge_edges(mate, far, turn):
    swap = jnp.broadcast_to(parity("gx"), (8, LANES)) == 1
    east, west = jnp.where(swap, far, mate), jnp.where(swap, mate, far)
    return jnp.where((lane_index() & 1) == 0, west, pltpu.roll(east, turn, 1))


def child_inner(solved_ref, rates_ref, land_ref, after_ref, inner_ref, row_ref, column_ref):
    depth, vectors = solved_ref.shape[0], solved_ref.shape[1]
    lane, row = lane_index(), row_index()
    land = land_ref[...]

    def level(k, _):
        centre, east, west, north, south = combine([rates_ref[d, k] for d in range(4)], land)
        column_ref[k] = jnp.where(lane == 0, west, jnp.where(lane == LANES - 1, east, 0.0))
        row_ref[k] = jnp.where(row == 0, south, jnp.where(row == 7, north, 0.0))
        east, west = jnp.where(lane == LANES - 1, 0.0, east), jnp.where(lane == 0, 0.0, west)
        north, south = jnp.where(row == 7, 0.0, north), jnp.where(row == 0, 0.0, south)
        for v in range(vectors):
            s = solved_ref[k, v]
            across = east * pltpu.roll(s, LANES - 1, 1) + west * pltpu.roll(s, 1, 1)
            along = north * pltpu.roll(s, 7, 0) + south * pltpu.roll(s, 1, 0)
            inner_ref[k, v] = centre * s + across + along
        return 0

    lax.fori_loop(0, depth, level, 0, unroll=4)


def edge_merger(mate_cols, far_cols, merged_ref):
    for g in range(merged_ref.shape[0] // 8):
        part = slice(8 * g, 8 * g + 8)
        merged_ref[part, :] = merge_edges(mate_cols[part, :], far_cols[part, :], LANES - 2)


def edged(inner_ref, row_rates, column_rates, mate_ref, far_ref, edges, k, v, at, mates):
    line = pl.ds(k * inner_ref.shape[1] + v, 1)
    mate = jnp.broadcast_to(mate_ref[line, :], (8, LANES))
    far = jnp.broadcast_to(far_ref[line, :], (8, LANES))
    edge = pltpu.roll(edges, (LANES - 2 * at) & (LANES - 1), 1)
    return inner_ref[k, v] + row_rates * jnp.where(mates, mate, far) + column_rates * edge


def mate_rows_mask():
    return row_index() == 7 * (1 - parity("gy"))


def child_between(
    inner_ref, row_ref, column_ref, relax_ref, after_ref, mate_in, far_in, mate_cols, far_cols,
    sums_out, x_ref,
    sums_ref, merged_ref,
):
    depth, vectors = inner_ref.shape[0], inner_ref.shape[1]
    half, groups = depth // 2, depth // LEVELS
    mates = mate_rows_mask()
    weights = [relax_ref[j : j + 1, :] for j in range(8)]
    edge_merger(mate_cols, far_cols, merged_ref)

    def level(i, _, edges):
        inside = lax.rem(i, LEVELS)
        for side, k, base in ((0, i, inside * vectors), (1, depth - 1 - i, (LEVELS - 1 - inside) * vectors)):
            row_rates, column_rates = row_ref[k], column_ref[k]
            for v in range(vectors):
                x_ref[k, v] = edged(
                    inner_ref, row_rates, column_rates, mate_in, far_in, edges[side], k, v, base + v, mates
                )
            block_rows(x_ref, k, weights, sums_ref, i, side)
        return 0

    for group in range(half // LEVELS):
        edges = [merged_ref[8 * g : 8 * g + 8, :] for g in (group, groups - 1 - group)]
        lax.fori_loop(
            LEVELS * group, LEVELS * (group + 1), lambda i, _, edges=edges: level(i, _, edges), 0, unroll=4
        )
    sums_out[...] = block_columns(sums_ref)


def child_second(
    x_ref, a_ref, b_ref, c_ref, parent_ref, pa_ref, pb_ref, pc_ref,
    solved_ref, psolved_ref, mate_rows, far_rows, cols_ref,
):
    depth, vectors = x_ref.shape[0], x_ref.shape[1]
    y = jnp.zeros((8, LANES), F32)
    for i in range(depth // 2):
        y = pa_ref[i : i + 1, :] * parent_ref[i] + pb_ref[i : i + 1, :] * y
        psolved_ref[i] = y
    lines, at = depth * vectors, depth // LEVELS * 8
    parent_up(y, pc_ref, psolved_ref, mate_rows, far_rows, lines, cols_ref, at)
    child_first(x_ref, a_ref, b_ref, c_ref, solved_ref, mate_rows, far_rows, cols_ref)


def child_last(
    inner_ref, row_ref, column_ref, mate_in, far_in, mate_cols, far_cols, out_hbm, out_ref, merged_ref, sems
):
    depth, vectors = inner_ref.shape[0], inner_ref.shape[1]
    mates = mate_rows_mask()
    edge_merger(mate_cols, far_cols, merged_ref)
    copies = []
    for group in range(depth // LEVELS):
        edges = merged_ref[8 * group : 8 * group + 8, :]

        def level(inside, _):
            k = LEVELS * group + inside
            row_rates, column_rates = row_ref[k], column_ref[k]
            for v in range(vectors):
                out_ref[k, v] = edged(
                    inner_ref, row_rates, column_rates, mate_in, far_in, edges, k, v, inside * vectors + v, mates
                )
            return 0

        lax.fori_loop(0, LEVELS, level, 0, unroll=4)
        part = pl.ds(LEVELS * group, LEVELS)
        copies.append(pltpu.make_async_copy(out_ref.at[part], out_hbm.at[part], sems.at[group]))
        copies[-1].start()
    for copy in copies:
        copy.wait()


PLACES = [(h, r, 64 * h + 32 * r) for h in range(2) for r in range(2)]


def parent_fed(parent_ref, feed_ref, after_ref, packed_ref):
    half, vectors = packed_ref.shape[0], packed_ref.shape[1]
    for i in range(half):
        for h, r, lo in PLACES:
            k = 2 * half - 1 - i if h else i
            packed_ref[i, :, lo : lo + 32] = parent_ref[pl.ds(2 * vectors * k + r, vectors, stride=2), :]
        packed_ref[i] = packed_ref[i] + feed_ref[vectors * i : vectors * (i + 1), :]


def parent_factors(mix_ref, fed_ref, far_ref, mate_cols, far_cols, pa_ref, pb_ref, pc_ref, mixed):
    half = pa_ref.shape[0]
    for i in range(half):
        for h, r, lo in PLACES:
            k = 2 * half - 1 - i if h else i
            mixed[i : i + 1, lo : lo + 32] = mix_ref[2 * k + r : 2 * k + r + 1, :]
    upper = lane_index(1) < 64
    rows = [mixed[i : i + 1, :] for i in range(half)]
    inner, outer = [], []
    for i in range(half):
        nearer = rows[i + 1] if i + 1 < half else pltpu.roll(rows[i], 64, 1)
        inner.append(jnp.where(upper, rows[i], nearer))
        outer.append(jnp.where(upper, rows[i - 1] if i else jnp.zeros_like(rows[0]), rows[i]))
    inverse = minors(inner, outer)
    for i in range(half):
        pa_ref[i : i + 1, :] = inverse[i]
        pb_ref[i : i + 1, :] = inverse[i] * outer[i]
        pc_ref[i : i + 1, :] = inverse[i] * inner[i]


def parent_rates_packed(rates_ref, feed_ref, after_ref, packed_ref):
    half = packed_ref.shape[1]
    depth = 2 * half
    for i in range(half):
        for h, r, lo in PLACES:
            k = depth - 1 - i if h else i
            for d in range(4):
                at = 2 * (d * depth + k) + r
                packed_ref[d, i : i + 1, lo : lo + 32] = rates_ref[at : at + 1, :]


def parent_rates_masked(packed_ref, land_ref, far_ref, mate_cols, far_cols, prates_ref):
    half = packed_ref.shape[1]
    land = jnp.concatenate([land_ref[r : r + 1, :] for _, r, _ in PLACES], axis=1)
    land = jnp.broadcast_to(land, (half, LANES))
    for d, part in enumerate(combine([packed_ref[d] for d in range(4)], land)):
        prates_ref[d] = part


def parent_up(carry, pc_ref, psolved_ref, mate_rows, far_rows, lines, cols_ref, cols_at):
    half = psolved_ref.shape[0]
    lane = lane_index()
    middle = pc_ref[half - 1 : half, :]
    scale = 1.0 / (1.0 - middle * pltpu.roll(middle, 64, 1))
    x = (carry + middle * pltpu.roll(carry, 64, 1)) * scale
    tiles = [None] * half
    tiles[half - 1] = x
    for i in range(half - 2, -1, -1):
        x = psolved_ref[i] + pc_ref[i : i + 1, :] * x
        tiles[i] = x
    packed = jnp.zeros((8, LANES), F32)
    for i in range(half):
        psolved_ref[i] = tiles[i]
        packed = jnp.where(((lane & 31) >> 1) == i, pltpu.roll(tiles[i], 2 * i + 1, 1), packed)
    cols_ref[cols_at : cols_at + 8, :] = packed
    first = (lane & 32) == 0
    swap = jnp.broadcast_to(parity("gy"), (8, LANES)) == 1
    for j in range(half // 2):
        one, two = tiles[j], tiles[j + half // 2]
        lo = jnp.where(first, one, pltpu.roll(two, 32, 1))
        hi = jnp.where(first, pltpu.roll(one, 96, 1), two)
        part = slice(lines + 8 * j, lines + 8 * j + 8)
        mate_rows[part, :] = jnp.where(swap, lo, hi)
        far_rows[part, :] = jnp.where(swap, hi, lo)


def parent_edges(mate_cols, far_cols, at):
    return merge_edges(mate_cols[at : at + 8, :], far_cols[at : at + 8, :], 62)


def parent_transport(psolved_ref, prates_ref, mate_row, far_row, edges, i):
    half = psolved_ref.shape[0]
    lane = lane_index()
    swap = jnp.broadcast_to(parity("gy"), (8, LANES)) == 1
    x = psolved_ref[i]
    mate, far = mate_row(i % (half // 2)), far_row(i % (half // 2))
    lo, hi = jnp.where(swap, far, mate), jnp.where(swap, mate, far)
    if i < half // 2:
        lo = pltpu.roll(lo, 32, 1)
    else:
        hi = pltpu.roll(hi, 96, 1)
    first = (lane & 32) == 0
    to_north = jnp.where(first, pltpu.roll(x, 96, 1), lo)
    to_south = jnp.where(first, hi, pltpu.roll(x, 32, 1))
    edge = pltpu.roll(edges, (LANES - 2 * i - 32) & (LANES - 1), 1)
    column = lane & 31
    to_east = jnp.where(column == 31, edge, pltpu.roll(x, 127, 1))
    to_west = jnp.where(column == 0, edge, pltpu.roll(x, 1, 1))
    parts = [prates_ref[d, i : i + 1, :] for d in range(5)]
    return (parts[0] * x + parts[1] * to_east) + (parts[2] * to_west + parts[3] * to_north) + parts[4] * to_south


def parent_second(
    psolved_in, prates_ref, pa_ref, pb_ref, pc_ref, mate_in, far_in, mate_cols, far_cols, feed_ref,
    psolved_ref, mate_rows, far_rows, cols_ref,
):
    half = psolved_in.shape[0]
    lines = mate_in.shape[0] - mate_rows.shape[0]
    edges = parent_edges(mate_cols, far_cols, mate_cols.shape[0] - 8)
    mate = lambda j: mate_in[lines + 8 * j : lines + 8 * j + 8, :]
    far = lambda j: far_in[lines + 8 * j : lines + 8 * j + 8, :]
    y = jnp.zeros((8, LANES), F32)
    for i in range(half):
        rhs = parent_transport(psolved_in, prates_ref, mate, far, edges, i)
        rhs = rhs + feed_ref[8 * i : 8 * i + 8, :]
        y = pa_ref[i : i + 1, :] * rhs + pb_ref[i : i + 1, :] * y
        psolved_ref[i] = y
    parent_up(y, pc_ref, psolved_ref, mate_rows, far_rows, 0, cols_ref, 0)


def parent_last(psolved_in, prates_ref, mate_in, far_in, mate_cols, far_cols, out_ref):
    half, vectors = psolved_in.shape[0], psolved_in.shape[1]
    edges = parent_edges(mate_cols, far_cols, 0)
    mate = lambda j: mate_in[8 * j : 8 * j + 8, :]
    far = lambda j: far_in[8 * j : 8 * j + 8, :]
    for i in range(half):
        x = parent_transport(psolved_in, prates_ref, mate, far, edges, i)
        for h in range(2):
            for r in range(2):
                lo = 64 * h + 32 * r
                k = 2 * half - 1 - i if h else i
                out_ref[pl.ds(2 * vectors * k + r, vectors, stride=2), :] = x[:, lo : lo + 32]


def passed_along(value, axis, steps):
    count = lax.axis_size(axis)
    return lax.ppermute(value, axis, [(i, (i + steps) % count) for i in range(count)])


def swapped(value, axis, offset):
    count = lax.axis_size(axis)
    pairs = []
    for i in range(offset, count, 2):
        j = (i + 1) % count
        pairs += [(i, j), (j, i)]
    return lax.ppermute(value, axis, pairs)


def halos_of(mate, far, cols):
    return [swapped(mate, "gy", 0), swapped(far, "gy", 1), swapped(cols, "gx", 0), swapped(cols, "gx", 1)]


def local(
    child_adjoint,
    parent_adjoint,
    child_rates,
    child_mixing,
    child_land,
    parent_rates,
    parent_mixing,
    parent_land,
    relaxation,
):
    depth, vectors, lines, columns = child_adjoint.shape
    half = depth // 2
    quarter = lax.axis_size("gy") // 4
    field = shape(depth, vectors, lines, columns)
    factor = shape(depth, lines, columns)
    tiles = shape(half, vectors, LANES)
    sums = shape(half * vectors, LANES)
    count = depth * vectors
    edge = depth // LEVELS * 8
    sum_scratch = pltpu.VMEM((half * vectors, 4 * LANES), F32)
    edge_scratch = [pltpu.VMEM((edge, LANES), F32)]
    narrow = parent_adjoint.shape[-1]

    sums1, x, a, b, c, relax, land, parent_land, rates = call(
        begin,
        [sums, field, factor, factor, factor, shape(lines, columns), shape(lines, columns), shape(*parent_land.shape)]
        + [shape(*child_rates.shape)],
        [
            pltpu.VMEM(factor.shape, F32),
            pltpu.VMEM(child_land.shape, jnp.int32),
            pltpu.VMEM(parent_land.shape, jnp.int32),
            sum_scratch,
            pltpu.SemaphoreType.DMA((5 + half // 2,)),
        ],
        [child_adjoint, child_mixing, relaxation, child_land, parent_land, child_rates],
        4_000_000,
        3_000_000,
        far_in=range(6),
    )
    feed = passed_along(sums1, "gy", quarter)
    solved, mate, far, cols = call(
        child_first,
        [field, shape(count, LANES), shape(count, LANES), shape(edge, LANES)],
        [],
        [x, a, b, c],
        4_000_000,
        3_000_000,
    )
    halos = halos_of(mate, far, cols)
    inner, row_rates, column_rates = call(
        child_inner,
        [field, factor, factor],
        [],
        [solved, rates, land, cols],
        INNER,
        4_000_000,
    )
    fed = call(
        parent_fed,
        tiles,
        [],
        [parent_adjoint.reshape(-1, narrow), feed, inner],
        LONG,
        1_000_000,
    )
    pa, pb, pc = call(
        parent_factors,
        [shape(half, LANES)] * 3,
        [pltpu.VMEM((half, LANES), F32)],
        [parent_mixing.reshape(-1, narrow), fed, *halos[1:]],
        LONG,
        1_000_000,
    )
    sums2, x = call(
        child_between,
        [sums, field],
        [sum_scratch] + edge_scratch,
        [inner, row_rates, column_rates, relax, pa, *halos],
        8_000_000,
        3_000_000,
    )
    feed = passed_along(sums2, "gy", quarter)
    rows = count + half // 2 * vectors
    solved, psolved, mate, far, cols = call(
        child_second,
        [field, tiles, shape(rows, LANES), shape(rows, LANES), shape(edge + 8, LANES)],
        [],
        [x, a, b, c, fed, pa, pb, pc],
        8_000_000,
        3_000_000,
    )
    halos = halos_of(mate, far, cols)
    inner, row_rates, column_rates = call(
        child_inner,
        [field, factor, factor],
        [],
        [solved, rates, land, cols],
        INNER,
        4_000_000,
    )
    packed_rates = call(
        parent_rates_packed,
        shape(4, half, LANES),
        [],
        [parent_rates.reshape(-1, narrow), feed, inner],
        1_450_000_000,
        1_000_000,
    )
    prates = call(
        parent_rates_masked,
        shape(5, half, LANES),
        [],
        [packed_rates, parent_land, *halos[1:]],
        LONG,
        1_000_000,
    )
    few = half // 2 * vectors
    psolved, mate, far, cols = call(
        parent_second,
        [tiles, shape(few, LANES), shape(few, LANES), shape(8, LANES)],
        [],
        [psolved, prates, pa, pb, pc, *halos, feed],
        1_000_000,
        500_000,
    )
    last_halos = halos_of(mate, far, cols)
    child_out = call(
        child_last,
        field,
        [pltpu.VMEM(field.shape, F32)] + edge_scratch + [pltpu.SemaphoreType.DMA((depth // LEVELS,))],
        [inner, row_rates, column_rates, *halos],
        4_000_000,
        3_000_000,
        far_out=True,
    )
    parent_out = call(
        parent_last,
        shape(depth * vectors * 2, narrow),
        [],
        [psolved, prates, *last_halos],
        500_000,
        500_000,
    )
    return (child_out, parent_out.reshape(parent_adjoint.shape))


def solution(mesh):
    wide = P(None, None, "gy", "gx")
    level = P(None, "gy", "gx")
    flat = P("gy", "gx")
    in_specs = (wide, wide, wide, level, flat, wide, level, flat, flat)
    return jax.shard_map(local, mesh=mesh, in_specs=in_specs, out_specs=(wide, wide), check_vma=False)
```

```python
import jax
import jax.numpy as jnp
from jax import lax
from jax.experimental import pallas as pl
from jax.experimental.pallas import tpu as pltpu
from jax.sharding import PartitionSpec as P

F32 = jnp.float32
VMEM = pl.BlockSpec(memory_space=pltpu.VMEM)
FAR = pl.BlockSpec(memory_space=pltpu.HBM)
LIMIT = 40 * 1024 * 1024
LANES = 128
LONG = 1_000_000_000
INNER = 10_000_000
LEVELS = 8


def shape(*dims):
    return jax.ShapeDtypeStruct(dims, F32)


def call(body, outs, scratch, operands, flops, touched, far_in=(), far_out=False):
    operands = [pltpu.with_memory_space_constraint(x, pltpu.HBM) if i in far_in else x for i, x in enumerate(operands)]
    return pl.pallas_call(
        body,
        out_shape=outs,
        in_specs=[FAR if i in far_in else VMEM for i in range(len(operands))],
        out_specs=jax.tree.map(lambda _: FAR if far_out else VMEM, outs),
        scratch_shapes=scratch,
        compiler_params=pltpu.CompilerParams(vmem_limit_bytes=LIMIT),
        cost_estimate=pl.CostEstimate(flops=flops, bytes_accessed=touched, transcendentals=0),
        name=body.__name__,
    )(*operands)


def lane_index(rows=8):
    return lax.broadcasted_iota(jnp.int32, (rows, LANES), 1)


def row_index():
    return lax.broadcasted_iota(jnp.int32, (8, LANES), 0)


def minors(inner, outer):
    theta = delta = jnp.ones_like(inner[0])
    inverse = []
    for i in range(len(inner)):
        delta = theta + outer[i] * delta
        theta_next = delta + inner[i] * theta
        inverse.append(theta / theta_next)
        theta = theta_next
    return inverse


def parity(axis):
    return lax.rem(lax.axis_index(axis), 2)


def child_factors(mix_ref, keep, a_ref, b_ref, c_ref):
    depth = mix_ref.shape[0]
    half = depth // 2
    zero = jnp.zeros_like(keep)
    top_inner = [mix_ref[i] for i in range(half)]
    top_outer = [zero] + top_inner[:-1]
    low_outer = [mix_ref[depth - 1 - i] for i in range(half)]
    low_inner = [mix_ref[depth - 2 - i] for i in range(half)]
    for levels, inner, outer in (
        (range(half), top_inner, top_outer),
        (range(depth - 1, half - 1, -1), low_inner, low_outer),
    ):
        inverse = minors(inner, outer)
        for i, k in enumerate(levels):
            a_ref[k] = inverse[i] * keep
            b_ref[k] = inverse[i] * outer[i]
            c_ref[k] = inverse[i] * inner[i]


def block_rows(source_ref, k, weights, sums_ref, i, place):
    vectors = source_ref.shape[1]
    for r in range(2):
        total = source_ref[k, :, 4 * r, :] * weights[4 * r]
        for j in range(4 * r + 1, 4 * r + 4):
            total = total + source_ref[k, :, j, :] * weights[j]
        column = (2 * place + r) * LANES
        sums_ref[pl.ds(i * vectors, vectors), column : column + LANES] = total


def block_columns(sums_ref):
    wide = sums_ref.shape[1]
    p = lax.broadcasted_iota(jnp.int32, (wide, LANES), 0)
    q = lax.broadcasted_iota(jnp.int32, (wide, LANES), 1)
    pick = jnp.where(p // 4 == q, F32(0.0625), F32(0.0)).astype(jnp.bfloat16)
    rest, total = sums_ref[...], None
    for _ in range(3):
        part = rest.astype(jnp.bfloat16)
        rest = rest - part.astype(F32)
        product = jnp.dot(part, pick, preferred_element_type=F32)
        total = product if total is None else total + product
    return total


def child_middle(carry, c_ref, half):
    vectors = len(carry) // 2
    top, low = c_ref[half - 1], c_ref[half]
    scale = 1.0 / (1.0 - top * low)
    first = [(carry[v] + top * carry[vectors + v]) * scale for v in range(vectors)]
    second = [(carry[vectors + v] + low * carry[v]) * scale for v in range(vectors)]
    return first + second


def child_up(carry, c_ref, solved_ref, mate_rows, far_rows, cols_ref):
    depth, vectors = solved_ref.shape[0], solved_ref.shape[1]
    half = depth // 2
    lane = lane_index()
    pair = lane >> 1
    swap = jnp.broadcast_to(parity("gy"), (8, LANES)) == 1

    def emit(i, values, packed):
        k_low = depth - 1 - i
        packed = list(packed)
        inside = i % LEVELS if isinstance(i, int) else lax.rem(i, LEVELS)
        for side, k, base in ((0, i, inside * vectors), (1, k_low, (LEVELS - 1 - inside) * vectors)):
            for v in range(vectors):
                x = values[side * vectors + v]
                solved_ref[k, v] = x
                at = base + v
                packed[side] = jnp.where(pair == at, pltpu.roll(x, 2 * at + 1 & (LANES - 1), 1), packed[side])
            lo, hi = solved_ref[k, :, 0, :], solved_ref[k, :, 7, :]
            mate_rows[pl.ds(k * vectors, vectors), :] = jnp.where(swap, lo, hi)
            far_rows[pl.ds(k * vectors, vectors), :] = jnp.where(swap, hi, lo)
        return packed

    def up(i, state):
        k_low = depth - 1 - i
        top, low = c_ref[i], c_ref[k_low]
        values = []
        for v in range(vectors):
            values.append(solved_ref[i, v] + top * state[v])
        for v in range(vectors):
            values.append(solved_ref[k_low, v] + low * state[vectors + v])
        return tuple(values) + tuple(emit(i, values, state[2 * vectors :]))

    def keep_columns(group, packed):
        for side, g in ((0, group), (1, depth // LEVELS - 1 - group)):
            for slot in range(cols_ref.shape[0]):
                cols_ref[slot, LEVELS * g : LEVELS * g + 8, :] = packed[side]

    blank = jnp.zeros((8, LANES), F32)
    values = child_middle(carry, c_ref, half)
    state = tuple(values) + tuple(emit(half - 1, values, [blank] * 2))
    for group in range(half // LEVELS - 1, -1, -1):
        last = LEVELS * (group + 1) - 1
        if group == half // LEVELS - 1:
            last -= 1
        count = last - LEVELS * group + 1
        state = lax.fori_loop(0, count, lambda step, state, last=last: up(last - step, state), state, unroll=4 if count % 4 == 0 else count)
        keep_columns(group, state[2 * vectors :])
        state = state[: 2 * vectors] + (blank,) * 2


def begin(
    x_hbm, mix_hbm, relax_hbm, land_hbm, parent_land_hbm, rates_hbm,
    sums_out, x_ref, a_ref, b_ref, c_ref, relax_ref, land_ref, parent_land_ref, rates_ref,
    mix_ref, land_in, parent_land_in, sums_ref, sems,
):
    depth = x_ref.shape[0]
    half = depth // 2
    small = []
    for source, target in (
        (mix_hbm, mix_ref), (relax_hbm, relax_ref), (land_hbm, land_in), (parent_land_hbm, parent_land_in),
    ):
        small.append(pltpu.make_async_copy(source, target, sems.at[len(small)]))
        small[-1].start()
    size, large = 4, []
    for start in range(0, half, size):
        for first in (start, depth - size - start):
            part = pl.ds(first, size)
            large.append(pltpu.make_async_copy(x_hbm.at[part], x_ref.at[part], sems.at[len(large) + len(small)]))
            large[-1].start()
    rates_copy = pltpu.make_async_copy(rates_hbm, rates_ref, sems.at[len(large) + len(small)])
    rates_copy.start()
    for copy in small:
        copy.wait()
    land_ref[...] = land_in[...].astype(F32)
    parent_land_ref[...] = parent_land_in[...].astype(F32)
    child_factors(mix_ref, 1.0 - relax_ref[...], a_ref, b_ref, c_ref)
    weights = [relax_ref[j : j + 1, :] for j in range(8)]

    def level(i, _):
        for side, k in ((0, i), (1, depth - 1 - i)):
            block_rows(x_ref, k, weights, sums_ref, i, side)
        return 0

    for part, start in enumerate(range(0, half, size)):
        large[2 * part].wait()
        large[2 * part + 1].wait()
        lax.fori_loop(start, start + size, level, 0, unroll=size)
    sums_out[...] = block_columns(sums_ref)
    rates_copy.wait()


def child_first(x_ref, a_ref, b_ref, c_ref, solved_ref, mate_rows, far_rows, cols_ref):
    depth, vectors = x_ref.shape[0], x_ref.shape[1]
    half = depth // 2

    def down(i, carry):
        values = []
        for side, k in ((0, i), (1, depth - 1 - i)):
            a, b = a_ref[k], b_ref[k]
            for v in range(vectors):
                y = a * x_ref[k, v] + b * carry[side * vectors + v]
                solved_ref[k, v] = y
                values.append(y)
        return tuple(values)

    carry = lax.fori_loop(0, half, down, (jnp.zeros((8, LANES), F32),) * (2 * vectors), unroll=4)
    child_up(carry, c_ref, solved_ref, mate_rows, far_rows, cols_ref)


def combine(sides, land):
    east, west, north, south = sides
    return [land * part for part in (1.0 - (east + west + north + south), east, west, north, south)]


def merge_edges(cols_ref, part, turn):
    count, here = lax.axis_size("gx"), lax.axis_index("gx")
    east = cols_ref[lax.rem(here + 1, count), part, :]
    west = cols_ref[lax.rem(here + count - 1, count), part, :]
    return jnp.where((lane_index() & 1) == 0, west, pltpu.roll(east, turn, 1))


def child_inner(solved_ref, rates_ref, land_ref, after_ref, inner_ref, row_ref, column_ref):
    depth, vectors = solved_ref.shape[0], solved_ref.shape[1]
    lane, row = lane_index(), row_index()
    land = land_ref[...]

    def level(k, _):
        centre, east, west, north, south = combine([rates_ref[d, k] for d in range(4)], land)
        column_ref[k] = jnp.where(lane == 0, west, jnp.where(lane == LANES - 1, east, 0.0))
        row_ref[k] = jnp.where(row == 0, south, jnp.where(row == 7, north, 0.0))
        east, west = jnp.where(lane == LANES - 1, 0.0, east), jnp.where(lane == 0, 0.0, west)
        north, south = jnp.where(row == 7, 0.0, north), jnp.where(row == 0, 0.0, south)
        for v in range(vectors):
            s = solved_ref[k, v]
            across = east * pltpu.roll(s, LANES - 1, 1) + west * pltpu.roll(s, 1, 1)
            along = north * pltpu.roll(s, 7, 0) + south * pltpu.roll(s, 1, 0)
            inner_ref[k, v] = centre * s + across + along
        return 0

    lax.fori_loop(0, depth, level, 0, unroll=4)


def edge_merger(cols_ref, merged_ref):
    for g in range(merged_ref.shape[0] // 8):
        part = slice(8 * g, 8 * g + 8)
        merged_ref[part, :] = merge_edges(cols_ref, part, LANES - 2)


def edged(inner_ref, row_rates, column_rates, mate_ref, far_ref, edges, k, v, at, mates):
    line = pl.ds(k * inner_ref.shape[1] + v, 1)
    mate = jnp.broadcast_to(mate_ref[line, :], (8, LANES))
    far = jnp.broadcast_to(far_ref[line, :], (8, LANES))
    edge = pltpu.roll(edges, (LANES - 2 * at) & (LANES - 1), 1)
    return inner_ref[k, v] + row_rates * jnp.where(mates, mate, far) + column_rates * edge


def mate_rows_mask():
    return row_index() == 7 * (1 - parity("gy"))


def child_between(
    inner_ref, row_ref, column_ref, relax_ref, after_ref, mate_in, far_in, cols_in,
    sums_out, x_ref,
    sums_ref, merged_ref,
):
    depth, vectors = inner_ref.shape[0], inner_ref.shape[1]
    half, groups = depth // 2, depth // LEVELS
    mates = mate_rows_mask()
    weights = [relax_ref[j : j + 1, :] for j in range(8)]
    edge_merger(cols_in, merged_ref)

    def level(i, _, edges):
        inside = lax.rem(i, LEVELS)
        for side, k, base in ((0, i, inside * vectors), (1, depth - 1 - i, (LEVELS - 1 - inside) * vectors)):
            row_rates, column_rates = row_ref[k], column_ref[k]
            for v in range(vectors):
                x_ref[k, v] = edged(
                    inner_ref, row_rates, column_rates, mate_in, far_in, edges[side], k, v, base + v, mates
                )
            block_rows(x_ref, k, weights, sums_ref, i, side)
        return 0

    for group in range(half // LEVELS):
        edges = [merged_ref[8 * g : 8 * g + 8, :] for g in (group, groups - 1 - group)]
        lax.fori_loop(
            LEVELS * group, LEVELS * (group + 1), lambda i, _, edges=edges: level(i, _, edges), 0, unroll=4
        )
    sums_out[...] = block_columns(sums_ref)


def child_second(
    x_ref, a_ref, b_ref, c_ref, parent_ref, pa_ref, pb_ref, pc_ref,
    solved_ref, psolved_ref, mate_rows, far_rows, cols_ref,
):
    depth, vectors = x_ref.shape[0], x_ref.shape[1]
    y = jnp.zeros((8, LANES), F32)
    for i in range(depth // 2):
        y = pa_ref[i : i + 1, :] * parent_ref[i] + pb_ref[i : i + 1, :] * y
        psolved_ref[i] = y
    lines, at = depth * vectors, depth // LEVELS * 8
    parent_up(y, pc_ref, psolved_ref, mate_rows, far_rows, lines, cols_ref, at)
    child_first(x_ref, a_ref, b_ref, c_ref, solved_ref, mate_rows, far_rows, cols_ref)


def child_last(
    inner_ref, row_ref, column_ref, mate_in, far_in, cols_in, out_hbm, out_ref, merged_ref, sems
):
    depth, vectors = inner_ref.shape[0], inner_ref.shape[1]
    mates = mate_rows_mask()
    edge_merger(cols_in, merged_ref)
    copies = []
    for group in range(depth // LEVELS):
        edges = merged_ref[8 * group : 8 * group + 8, :]

        def level(inside, _):
            k = LEVELS * group + inside
            row_rates, column_rates = row_ref[k], column_ref[k]
            for v in range(vectors):
                out_ref[k, v] = edged(
                    inner_ref, row_rates, column_rates, mate_in, far_in, edges, k, v, inside * vectors + v, mates
                )
            return 0

        lax.fori_loop(0, LEVELS, level, 0, unroll=4)
        part = pl.ds(LEVELS * group, LEVELS)
        copies.append(pltpu.make_async_copy(out_ref.at[part], out_hbm.at[part], sems.at[group]))
        copies[-1].start()
    for copy in copies:
        copy.wait()


PLACES = [(h, r, 64 * h + 32 * r) for h in range(2) for r in range(2)]


def parent_fed(parent_ref, feed_ref, after_ref, packed_ref):
    half, vectors = packed_ref.shape[0], packed_ref.shape[1]
    for i in range(half):
        for h, r, lo in PLACES:
            k = 2 * half - 1 - i if h else i
            packed_ref[i, :, lo : lo + 32] = parent_ref[pl.ds(2 * vectors * k + r, vectors, stride=2), :]
        packed_ref[i] = packed_ref[i] + feed_ref[vectors * i : vectors * (i + 1), :]


def parent_factors(mix_ref, fed_ref, far_ref, cols_in, pa_ref, pb_ref, pc_ref, mixed):
    half = pa_ref.shape[0]
    for i in range(half):
        for h, r, lo in PLACES:
            k = 2 * half - 1 - i if h else i
            mixed[i : i + 1, lo : lo + 32] = mix_ref[2 * k + r : 2 * k + r + 1, :]
    upper = lane_index(1) < 64
    rows = [mixed[i : i + 1, :] for i in range(half)]
    inner, outer = [], []
    for i in range(half):
        nearer = rows[i + 1] if i + 1 < half else pltpu.roll(rows[i], 64, 1)
        inner.append(jnp.where(upper, rows[i], nearer))
        outer.append(jnp.where(upper, rows[i - 1] if i else jnp.zeros_like(rows[0]), rows[i]))
    inverse = minors(inner, outer)
    for i in range(half):
        pa_ref[i : i + 1, :] = inverse[i]
        pb_ref[i : i + 1, :] = inverse[i] * outer[i]
        pc_ref[i : i + 1, :] = inverse[i] * inner[i]


def parent_rates_packed(rates_ref, feed_ref, after_ref, packed_ref):
    half = packed_ref.shape[1]
    depth = 2 * half
    for i in range(half):
        for h, r, lo in PLACES:
            k = depth - 1 - i if h else i
            for d in range(4):
                at = 2 * (d * depth + k) + r
                packed_ref[d, i : i + 1, lo : lo + 32] = rates_ref[at : at + 1, :]


def parent_rates_masked(packed_ref, land_ref, far_ref, cols_in, prates_ref):
    half = packed_ref.shape[1]
    land = jnp.concatenate([land_ref[r : r + 1, :] for _, r, _ in PLACES], axis=1)
    land = jnp.broadcast_to(land, (half, LANES))
    for d, part in enumerate(combine([packed_ref[d] for d in range(4)], land)):
        prates_ref[d] = part


def parent_up(carry, pc_ref, psolved_ref, mate_rows, far_rows, lines, cols_ref, cols_at):
    half = psolved_ref.shape[0]
    lane = lane_index()
    middle = pc_ref[half - 1 : half, :]
    scale = 1.0 / (1.0 - middle * pltpu.roll(middle, 64, 1))
    x = (carry + middle * pltpu.roll(carry, 64, 1)) * scale
    tiles = [None] * half
    tiles[half - 1] = x
    for i in range(half - 2, -1, -1):
        x = psolved_ref[i] + pc_ref[i : i + 1, :] * x
        tiles[i] = x
    packed = jnp.zeros((8, LANES), F32)
    for i in range(half):
        psolved_ref[i] = tiles[i]
        packed = jnp.where(((lane & 31) >> 1) == i, pltpu.roll(tiles[i], 2 * i + 1, 1), packed)
    for slot in range(cols_ref.shape[0]):
        cols_ref[slot, cols_at : cols_at + 8, :] = packed
    first = (lane & 32) == 0
    swap = jnp.broadcast_to(parity("gy"), (8, LANES)) == 1
    for j in range(half // 2):
        one, two = tiles[j], tiles[j + half // 2]
        lo = jnp.where(first, one, pltpu.roll(two, 32, 1))
        hi = jnp.where(first, pltpu.roll(one, 96, 1), two)
        part = slice(lines + 8 * j, lines + 8 * j + 8)
        mate_rows[part, :] = jnp.where(swap, lo, hi)
        far_rows[part, :] = jnp.where(swap, hi, lo)


def parent_transport(psolved_ref, prates_ref, mate_row, far_row, edges, i):
    half = psolved_ref.shape[0]
    lane = lane_index()
    swap = jnp.broadcast_to(parity("gy"), (8, LANES)) == 1
    x = psolved_ref[i]
    mate, far = mate_row(i % (half // 2)), far_row(i % (half // 2))
    lo, hi = jnp.where(swap, far, mate), jnp.where(swap, mate, far)
    if i < half // 2:
        lo = pltpu.roll(lo, 32, 1)
    else:
        hi = pltpu.roll(hi, 96, 1)
    first = (lane & 32) == 0
    to_north = jnp.where(first, pltpu.roll(x, 96, 1), lo)
    to_south = jnp.where(first, hi, pltpu.roll(x, 32, 1))
    edge = pltpu.roll(edges, (LANES - 2 * i - 32) & (LANES - 1), 1)
    column = lane & 31
    to_east = jnp.where(column == 31, edge, pltpu.roll(x, 127, 1))
    to_west = jnp.where(column == 0, edge, pltpu.roll(x, 1, 1))
    parts = [prates_ref[d, i : i + 1, :] for d in range(5)]
    return (parts[0] * x + parts[1] * to_east) + (parts[2] * to_west + parts[3] * to_north) + parts[4] * to_south


def parent_second(
    psolved_in, prates_ref, pa_ref, pb_ref, pc_ref, mate_in, far_in, cols_in, feed_ref,
    psolved_ref, mate_rows, far_rows, cols_ref,
):
    half = psolved_in.shape[0]
    lines = mate_in.shape[0] - mate_rows.shape[0]
    edges = merge_edges(cols_in, slice(cols_in.shape[1] - 8, cols_in.shape[1]), 62)
    mate = lambda j: mate_in[lines + 8 * j : lines + 8 * j + 8, :]
    far = lambda j: far_in[lines + 8 * j : lines + 8 * j + 8, :]
    y = jnp.zeros((8, LANES), F32)
    for i in range(half):
        rhs = parent_transport(psolved_in, prates_ref, mate, far, edges, i)
        rhs = rhs + feed_ref[8 * i : 8 * i + 8, :]
        y = pa_ref[i : i + 1, :] * rhs + pb_ref[i : i + 1, :] * y
        psolved_ref[i] = y
    parent_up(y, pc_ref, psolved_ref, mate_rows, far_rows, 0, cols_ref, 0)


def parent_last(psolved_in, prates_ref, mate_in, far_in, cols_in, out_ref):
    half, vectors = psolved_in.shape[0], psolved_in.shape[1]
    edges = merge_edges(cols_in, slice(0, 8), 62)
    mate = lambda j: mate_in[8 * j : 8 * j + 8, :]
    far = lambda j: far_in[8 * j : 8 * j + 8, :]
    for i in range(half):
        x = parent_transport(psolved_in, prates_ref, mate, far, edges, i)
        for h in range(2):
            for r in range(2):
                lo = 64 * h + 32 * r
                k = 2 * half - 1 - i if h else i
                out_ref[pl.ds(2 * vectors * k + r, vectors, stride=2), :] = x[:, lo : lo + 32]


def passed_along(value, axis, steps):
    count = lax.axis_size(axis)
    return lax.ppermute(value, axis, [(i, (i + steps) % count) for i in range(count)])


def swapped(value, axis, offset):
    count = lax.axis_size(axis)
    pairs = []
    for i in range(offset, count, 2):
        j = (i + 1) % count
        pairs += [(i, j), (j, i)]
    return lax.ppermute(value, axis, pairs)


def halos_of(mate, far, cols):
    columns = lax.all_to_all(cols, "gx", 0, 0, tiled=True)
    return [swapped(mate, "gy", 0), swapped(far, "gy", 1), columns]


def local(
    child_adjoint,
    parent_adjoint,
    child_rates,
    child_mixing,
    child_land,
    parent_rates,
    parent_mixing,
    parent_land,
    relaxation,
):
    depth, vectors, lines, columns = child_adjoint.shape
    half = depth // 2
    quarter = lax.axis_size("gy") // 4
    slots = lax.axis_size("gx")
    field = shape(depth, vectors, lines, columns)
    factor = shape(depth, lines, columns)
    tiles = shape(half, vectors, LANES)
    sums = shape(half * vectors, LANES)
    count = depth * vectors
    edge = depth // LEVELS * 8
    sum_scratch = pltpu.VMEM((half * vectors, 4 * LANES), F32)
    edge_scratch = [pltpu.VMEM((edge, LANES), F32)]
    narrow = parent_adjoint.shape[-1]

    sums1, x, a, b, c, relax, land, parent_land, rates = call(
        begin,
        [sums, field, factor, factor, factor, shape(lines, columns), shape(lines, columns), shape(*parent_land.shape)]
        + [shape(*child_rates.shape)],
        [
            pltpu.VMEM(factor.shape, F32),
            pltpu.VMEM(child_land.shape, jnp.int32),
            pltpu.VMEM(parent_land.shape, jnp.int32),
            sum_scratch,
            pltpu.SemaphoreType.DMA((5 + half // 2,)),
        ],
        [child_adjoint, child_mixing, relaxation, child_land, parent_land, child_rates],
        4_000_000,
        3_000_000,
        far_in=range(6),
    )
    feed = passed_along(sums1, "gy", quarter)
    solved, mate, far, cols = call(
        child_first,
        [field, shape(count, LANES), shape(count, LANES), shape(slots, edge, LANES)],
        [],
        [x, a, b, c],
        4_000_000,
        3_000_000,
    )
    halos = halos_of(mate, far, cols)
    inner, row_rates, column_rates = call(
        child_inner,
        [field, factor, factor],
        [],
        [solved, rates, land, cols],
        INNER,
        4_000_000,
    )
    fed = call(
        parent_fed,
        tiles,
        [],
        [parent_adjoint.reshape(-1, narrow), feed, inner],
        LONG,
        1_000_000,
    )
    pa, pb, pc = call(
        parent_factors,
        [shape(half, LANES)] * 3,
        [pltpu.VMEM((half, LANES), F32)],
        [parent_mixing.reshape(-1, narrow), fed, *halos[1:]],
        LONG,
        1_000_000,
    )
    sums2, x = call(
        child_between,
        [sums, field],
        [sum_scratch] + edge_scratch,
        [inner, row_rates, column_rates, relax, pa, *halos],
        8_000_000,
        3_000_000,
    )
    feed = passed_along(sums2, "gy", quarter)
    rows = count + half // 2 * vectors
    solved, psolved, mate, far, cols = call(
        child_second,
        [field, tiles, shape(rows, LANES), shape(rows, LANES), shape(slots, edge + 8, LANES)],
        [],
        [x, a, b, c, fed, pa, pb, pc],
        8_000_000,
        3_000_000,
    )
    halos = halos_of(mate, far, cols)
    inner, row_rates, column_rates = call(
        child_inner,
        [field, factor, factor],
        [],
        [solved, rates, land, cols],
        INNER,
        4_000_000,
    )
    packed_rates = call(
        parent_rates_packed,
        shape(4, half, LANES),
        [],
        [parent_rates.reshape(-1, narrow), feed, inner],
        1_450_000_000,
        1_000_000,
    )
    prates = call(
        parent_rates_masked,
        shape(5, half, LANES),
        [],
        [packed_rates, parent_land, *halos[1:]],
        LONG,
        1_000_000,
    )
    few = half // 2 * vectors
    psolved, mate, far, cols = call(
        parent_second,
        [tiles, shape(few, LANES), shape(few, LANES), shape(slots, 8, LANES)],
        [],
        [psolved, prates, pa, pb, pc, *halos, feed],
        1_000_000,
        500_000,
    )
    last_halos = halos_of(mate, far, cols)
    child_out = call(
        child_last,
        field,
        [pltpu.VMEM(field.shape, F32)] + edge_scratch + [pltpu.SemaphoreType.DMA((depth // LEVELS,))],
        [inner, row_rates, column_rates, *halos],
        4_000_000,
        3_000_000,
        far_out=True,
    )
    parent_out = call(
        parent_last,
        shape(depth * vectors * 2, narrow),
        [],
        [psolved, prates, *last_halos],
        500_000,
        500_000,
    )
    return (child_out, parent_out.reshape(parent_adjoint.shape))


def solution(mesh):
    wide = P(None, None, "gy", "gx")
    level = P(None, "gy", "gx")
    flat = P("gy", "gx")
    in_specs = (wide, wide, wide, level, flat, wide, level, flat, flat)
    return jax.shard_map(local, mesh=mesh, in_specs=in_specs, out_specs=(wide, wide), check_vma=False)
```

```python
import jax
import jax.numpy as jnp
from jax import lax
from jax.experimental import pallas as pl
from jax.experimental.pallas import tpu as pltpu
from jax.sharding import PartitionSpec as P

F32 = jnp.float32
VMEM = pl.BlockSpec(memory_space=pltpu.VMEM)
FAR = pl.BlockSpec(memory_space=pltpu.HBM)
LIMIT = 40 * 1024 * 1024
LANES = 128
LONG = 1_000_000_000
INNER = 10_000_000
LEVELS = 8


def shape(*dims):
    return jax.ShapeDtypeStruct(dims, F32)


def call(body, outs, scratch, operands, flops, touched, far_in=(), far_out=False):
    operands = [pltpu.with_memory_space_constraint(x, pltpu.HBM) if i in far_in else x for i, x in enumerate(operands)]
    return pl.pallas_call(
        body,
        out_shape=outs,
        in_specs=[FAR if i in far_in else VMEM for i in range(len(operands))],
        out_specs=jax.tree.map(lambda _: FAR if far_out else VMEM, outs),
        scratch_shapes=scratch,
        compiler_params=pltpu.CompilerParams(vmem_limit_bytes=LIMIT),
        cost_estimate=pl.CostEstimate(flops=flops, bytes_accessed=touched, transcendentals=0),
        name=body.__name__,
    )(*operands)


def lane_index(rows=8):
    return lax.broadcasted_iota(jnp.int32, (rows, LANES), 1)


def row_index():
    return lax.broadcasted_iota(jnp.int32, (8, LANES), 0)


def minors(inner, outer):
    theta = delta = jnp.ones_like(inner[0])
    inverse = []
    for i in range(len(inner)):
        delta = theta + outer[i] * delta
        theta_next = delta + inner[i] * theta
        inverse.append(theta / theta_next)
        theta = theta_next
    return inverse


def parity(axis):
    return lax.rem(lax.axis_index(axis), 2)


def child_factors(mix_ref, keep, a_ref, b_ref, c_ref):
    depth = mix_ref.shape[0]
    half = depth // 2
    zero = jnp.zeros_like(keep)
    top_inner = [mix_ref[i] for i in range(half)]
    top_outer = [zero] + top_inner[:-1]
    low_outer = [mix_ref[depth - 1 - i] for i in range(half)]
    low_inner = [mix_ref[depth - 2 - i] for i in range(half)]
    for levels, inner, outer in (
        (range(half), top_inner, top_outer),
        (range(depth - 1, half - 1, -1), low_inner, low_outer),
    ):
        inverse = minors(inner, outer)
        for i, k in enumerate(levels):
            a_ref[k] = inverse[i] * keep
            b_ref[k] = inverse[i] * outer[i]
            c_ref[k] = inverse[i] * inner[i]


def block_rows(source_ref, k, weights, sums_ref, i, place):
    vectors = source_ref.shape[1]
    for r in range(2):
        total = source_ref[k, :, 4 * r, :] * weights[4 * r]
        for j in range(4 * r + 1, 4 * r + 4):
            total = total + source_ref[k, :, j, :] * weights[j]
        column = (2 * place + r) * LANES
        sums_ref[pl.ds(i * vectors, vectors), column : column + LANES] = total


def block_columns(sums_ref):
    wide = sums_ref.shape[1]
    p = lax.broadcasted_iota(jnp.int32, (wide, LANES), 0)
    q = lax.broadcasted_iota(jnp.int32, (wide, LANES), 1)
    pick = jnp.where(p // 4 == q, F32(0.0625), F32(0.0)).astype(jnp.bfloat16)
    rest, total = sums_ref[...], None
    for _ in range(3):
        part = rest.astype(jnp.bfloat16)
        rest = rest - part.astype(F32)
        product = jnp.dot(part, pick, preferred_element_type=F32)
        total = product if total is None else total + product
    return total


def child_middle(carry, c_ref, half):
    vectors = len(carry) // 2
    top, low = c_ref[half - 1], c_ref[half]
    scale = 1.0 / (1.0 - top * low)
    first = [(carry[v] + top * carry[vectors + v]) * scale for v in range(vectors)]
    second = [(carry[vectors + v] + low * carry[v]) * scale for v in range(vectors)]
    return first + second


def child_up(carry, c_ref, solved_ref, mate_rows, far_rows, cols_ref):
    depth, vectors = solved_ref.shape[0], solved_ref.shape[1]
    half = depth // 2
    lane = lane_index()
    pair = lane >> 1
    swap = jnp.broadcast_to(parity("gy"), (8, LANES)) == 1

    def emit(i, values, packed):
        k_low = depth - 1 - i
        packed = list(packed)
        inside = i % LEVELS if isinstance(i, int) else lax.rem(i, LEVELS)
        for side, k, base in ((0, i, inside * vectors), (1, k_low, (LEVELS - 1 - inside) * vectors)):
            for v in range(vectors):
                x = values[side * vectors + v]
                solved_ref[k, v] = x
                at = base + v
                packed[side] = jnp.where(pair == at, pltpu.roll(x, 2 * at + 1 & (LANES - 1), 1), packed[side])
            lo, hi = solved_ref[k, :, 0, :], solved_ref[k, :, 7, :]
            mate_rows[pl.ds(k * vectors, vectors), :] = jnp.where(swap, lo, hi)
            far_rows[pl.ds(k * vectors, vectors), :] = jnp.where(swap, hi, lo)
        return packed

    def up(i, state):
        k_low = depth - 1 - i
        top, low = c_ref[i], c_ref[k_low]
        values = []
        for v in range(vectors):
            values.append(solved_ref[i, v] + top * state[v])
        for v in range(vectors):
            values.append(solved_ref[k_low, v] + low * state[vectors + v])
        return tuple(values) + tuple(emit(i, values, state[2 * vectors :]))

    def keep_columns(group, packed):
        for side, g in ((0, group), (1, depth // LEVELS - 1 - group)):
            cols_ref[LEVELS * g : LEVELS * g + 8, :] = packed[side]

    blank = jnp.zeros((8, LANES), F32)
    values = child_middle(carry, c_ref, half)
    state = tuple(values) + tuple(emit(half - 1, values, [blank] * 2))
    for group in range(half // LEVELS - 1, -1, -1):
        last = LEVELS * (group + 1) - 1
        if group == half // LEVELS - 1:
            last -= 1
        count = last - LEVELS * group + 1
        state = lax.fori_loop(0, count, lambda step, state, last=last: up(last - step, state), state, unroll=4 if count % 4 == 0 else count)
        keep_columns(group, state[2 * vectors :])
        state = state[: 2 * vectors] + (blank,) * 2


def begin(
    x_hbm, mix_hbm, relax_hbm, land_hbm, parent_land_hbm, rates_hbm,
    sums_out, x_ref, a_ref, b_ref, c_ref, relax_ref, land_ref, parent_land_ref, rates_ref,
    mix_ref, land_in, parent_land_in, sums_ref, sems,
):
    depth = x_ref.shape[0]
    half = depth // 2
    small = []
    for source, target in (
        (mix_hbm, mix_ref), (relax_hbm, relax_ref), (land_hbm, land_in), (parent_land_hbm, parent_land_in),
    ):
        small.append(pltpu.make_async_copy(source, target, sems.at[len(small)]))
        small[-1].start()
    size, large = 4, []
    for start in range(0, half, size):
        for first in (start, depth - size - start):
            part = pl.ds(first, size)
            large.append(pltpu.make_async_copy(x_hbm.at[part], x_ref.at[part], sems.at[len(large) + len(small)]))
            large[-1].start()
    rates_copy = pltpu.make_async_copy(rates_hbm, rates_ref, sems.at[len(large) + len(small)])
    rates_copy.start()
    for copy in small:
        copy.wait()
    land_ref[...] = land_in[...].astype(F32)
    parent_land_ref[...] = parent_land_in[...].astype(F32)
    child_factors(mix_ref, 1.0 - relax_ref[...], a_ref, b_ref, c_ref)
    weights = [relax_ref[j : j + 1, :] for j in range(8)]

    def level(i, _):
        for side, k in ((0, i), (1, depth - 1 - i)):
            block_rows(x_ref, k, weights, sums_ref, i, side)
        return 0

    for part, start in enumerate(range(0, half, size)):
        large[2 * part].wait()
        large[2 * part + 1].wait()
        lax.fori_loop(start, start + size, level, 0, unroll=size)
    sums_out[...] = block_columns(sums_ref)
    rates_copy.wait()


def child_first(x_ref, a_ref, b_ref, c_ref, solved_ref, mate_rows, far_rows, cols_ref):
    child_solve(x_ref, a_ref, b_ref, c_ref, solved_ref, mate_rows, far_rows, cols_ref, lambda k, v, _: x_ref[k, v])


def child_solve(x_ref, a_ref, b_ref, c_ref, solved_ref, mate_rows, far_rows, cols_ref, load, row_ref=None):
    depth, vectors = x_ref.shape[0], x_ref.shape[1]
    half = depth // 2

    def down(i, carry):
        values = []
        for side, k in ((0, i), (1, depth - 1 - i)):
            a, b = a_ref[k], b_ref[k]
            row_rates = None if row_ref is None else row_ref[k]
            for v in range(vectors):
                y = a * load(k, v, row_rates) + b * carry[side * vectors + v]
                solved_ref[k, v] = y
                values.append(y)
        return tuple(values)

    carry = lax.fori_loop(0, half, down, (jnp.zeros((8, LANES), F32),) * (2 * vectors), unroll=4)
    child_up(carry, c_ref, solved_ref, mate_rows, far_rows, cols_ref)


def combine(sides, land):
    east, west, north, south = sides
    return [land * part for part in (1.0 - (east + west + north + south), east, west, north, south)]


def merge_edges(mate, far, turn):
    swap = jnp.broadcast_to(parity("gx"), (8, LANES)) == 1
    east, west = jnp.where(swap, far, mate), jnp.where(swap, mate, far)
    return jnp.where((lane_index() & 1) == 0, west, pltpu.roll(east, turn, 1))


def child_inner(solved_ref, rates_ref, land_ref, after_ref, inner_ref, row_ref, column_ref):
    depth, vectors = solved_ref.shape[0], solved_ref.shape[1]
    lane, row = lane_index(), row_index()
    land = land_ref[...]

    def level(k, _):
        centre, east, west, north, south = combine([rates_ref[d, k] for d in range(4)], land)
        column_ref[k] = jnp.where(lane == 0, west, jnp.where(lane == LANES - 1, east, 0.0))
        row_ref[k] = jnp.where(row == 0, south, jnp.where(row == 7, north, 0.0))
        east, west = jnp.where(lane == LANES - 1, 0.0, east), jnp.where(lane == 0, 0.0, west)
        north, south = jnp.where(row == 7, 0.0, north), jnp.where(row == 0, 0.0, south)
        for v in range(vectors):
            s = solved_ref[k, v]
            across = east * pltpu.roll(s, LANES - 1, 1) + west * pltpu.roll(s, 1, 1)
            along = north * pltpu.roll(s, 7, 0) + south * pltpu.roll(s, 1, 0)
            inner_ref[k, v] = centre * s + across + along
        return 0

    lax.fori_loop(0, depth, level, 0, unroll=4)


def edge_merger(mate_cols, far_cols, merged_ref):
    for g in range(merged_ref.shape[0] // 8):
        part = slice(8 * g, 8 * g + 8)
        merged_ref[part, :] = merge_edges(mate_cols[part, :], far_cols[part, :], LANES - 2)


def column_edged(inner_ref, column_rates, edges, k, v, at):
    return inner_ref[k, v] + column_rates * pltpu.roll(edges, (LANES - 2 * at) & (LANES - 1), 1)


def row_halo(mate_ref, far_ref, k, v, vectors, mates):
    line = pl.ds(k * vectors + v, 1)
    mate = jnp.broadcast_to(mate_ref[line, :], (8, LANES))
    far = jnp.broadcast_to(far_ref[line, :], (8, LANES))
    return jnp.where(mates, mate, far)


def mate_rows_mask():
    return row_index() == 7 * (1 - parity("gy"))


def child_columns(inner_ref, column_ref, relax_ref, mate_cols, far_cols, sums_ref, x_ref, merged_ref):
    depth, vectors = inner_ref.shape[0], inner_ref.shape[1]
    half, groups = depth // 2, depth // LEVELS
    weights = [relax_ref[j : j + 1, :] for j in range(8)]
    edge_merger(mate_cols, far_cols, merged_ref)

    def level(i, _, edges):
        inside = lax.rem(i, LEVELS)
        for side, k, base in ((0, i, inside * vectors), (1, depth - 1 - i, (LEVELS - 1 - inside) * vectors)):
            column_rates = column_ref[k]
            for v in range(vectors):
                x_ref[k, v] = column_edged(inner_ref, column_rates, edges[side], k, v, base + v)
            block_rows(x_ref, k, weights, sums_ref, i, side)
        return 0

    for group in range(half // LEVELS):
        edges = [merged_ref[8 * g : 8 * g + 8, :] for g in (group, groups - 1 - group)]
        lax.fori_loop(
            LEVELS * group, LEVELS * (group + 1), lambda i, _, edges=edges: level(i, _, edges), 0, unroll=4
        )


def child_rows(sums_in, row_ref, relax_ref, after_ref, mate_in, far_in, sums_out, sums_ref):
    depth = row_ref.shape[0]
    vectors = 2 * sums_in.shape[0] // depth
    swap = jnp.broadcast_to(parity("gy"), (vectors, LANES)) == 1
    for k in range(depth):
        place, i = (0, k) if k < depth // 2 else (1, depth - 1 - k)
        lines = slice(k * vectors, (k + 1) * vectors)
        mate, far = mate_in[lines, :], far_in[lines, :]
        for r, at, halo in ((0, 0, jnp.where(swap, mate, far)), (1, 7, jnp.where(swap, far, mate))):
            share = (row_ref[k, at : at + 1, :] * relax_ref[at : at + 1, :]) * halo
            part = slice(i * vectors, (i + 1) * vectors), slice((2 * place + r) * LANES, (2 * place + r + 1) * LANES)
            sums_ref[part] = sums_in[part] + share
    sums_out[...] = block_columns(sums_ref)


def child_second(
    x_ref, row_ref, mate_in, far_in, a_ref, b_ref, c_ref, parent_ref, pa_ref, pb_ref, pc_ref,
    solved_ref, psolved_ref, mate_rows, far_rows, cols_ref,
):
    depth, vectors = x_ref.shape[0], x_ref.shape[1]
    y = jnp.zeros((8, LANES), F32)
    for i in range(depth // 2):
        y = pa_ref[i : i + 1, :] * parent_ref[i] + pb_ref[i : i + 1, :] * y
        psolved_ref[i] = y
    lines, at = depth * vectors, depth // LEVELS * 8
    parent_up(y, pc_ref, psolved_ref, mate_rows, far_rows, lines, cols_ref, at)
    mates = mate_rows_mask()

    def load(k, v, row_rates):
        return x_ref[k, v] + row_rates * row_halo(mate_in, far_in, k, v, vectors, mates)

    child_solve(x_ref, a_ref, b_ref, c_ref, solved_ref, mate_rows, far_rows, cols_ref, load, row_ref)


def child_last(
    inner_ref, row_ref, column_ref, mate_in, far_in, mate_cols, far_cols, out_hbm, out_ref, merged_ref, sems
):
    depth, vectors = inner_ref.shape[0], inner_ref.shape[1]
    mates = mate_rows_mask()
    edge_merger(mate_cols, far_cols, merged_ref)
    copies = []
    for group in range(depth // LEVELS):
        edges = merged_ref[8 * group : 8 * group + 8, :]

        def level(inside, _):
            k = LEVELS * group + inside
            row_rates, column_rates = row_ref[k], column_ref[k]
            for v in range(vectors):
                out_ref[k, v] = column_edged(
                    inner_ref, column_rates, edges, k, v, inside * vectors + v
                ) + row_rates * row_halo(mate_in, far_in, k, v, vectors, mates)
            return 0

        lax.fori_loop(0, LEVELS, level, 0, unroll=4)
        part = pl.ds(LEVELS * group, LEVELS)
        copies.append(pltpu.make_async_copy(out_ref.at[part], out_hbm.at[part], sems.at[group]))
        copies[-1].start()
    for copy in copies:
        copy.wait()


PLACES = [(h, r, 64 * h + 32 * r) for h in range(2) for r in range(2)]


def parent_fed(parent_ref, feed_ref, after_ref, packed_ref):
    half, vectors = packed_ref.shape[0], packed_ref.shape[1]
    for i in range(half):
        for h, r, lo in PLACES:
            k = 2 * half - 1 - i if h else i
            packed_ref[i, :, lo : lo + 32] = parent_ref[pl.ds(2 * vectors * k + r, vectors, stride=2), :]
        packed_ref[i] = packed_ref[i] + feed_ref[vectors * i : vectors * (i + 1), :]


def parent_factors(mix_ref, fed_ref, far_ref, x_ref, sums_ref, pa_ref, pb_ref, pc_ref, mixed):
    half = pa_ref.shape[0]
    for i in range(half):
        for h, r, lo in PLACES:
            k = 2 * half - 1 - i if h else i
            mixed[i : i + 1, lo : lo + 32] = mix_ref[2 * k + r : 2 * k + r + 1, :]
    upper = lane_index(1) < 64
    rows = [mixed[i : i + 1, :] for i in range(half)]
    inner, outer = [], []
    for i in range(half):
        nearer = rows[i + 1] if i + 1 < half else pltpu.roll(rows[i], 64, 1)
        inner.append(jnp.where(upper, rows[i], nearer))
        outer.append(jnp.where(upper, rows[i - 1] if i else jnp.zeros_like(rows[0]), rows[i]))
    inverse = minors(inner, outer)
    for i in range(half):
        pa_ref[i : i + 1, :] = inverse[i]
        pb_ref[i : i + 1, :] = inverse[i] * outer[i]
        pc_ref[i : i + 1, :] = inverse[i] * inner[i]


def parent_rates_packed(rates_ref, feed_ref, after_ref, packed_ref):
    half = packed_ref.shape[1]
    depth = 2 * half
    for i in range(half):
        for h, r, lo in PLACES:
            k = depth - 1 - i if h else i
            for d in range(4):
                at = 2 * (d * depth + k) + r
                packed_ref[d, i : i + 1, lo : lo + 32] = rates_ref[at : at + 1, :]


def parent_rates_masked(packed_ref, land_ref, far_ref, mate_cols, far_cols, prates_ref):
    half = packed_ref.shape[1]
    land = jnp.concatenate([land_ref[r : r + 1, :] for _, r, _ in PLACES], axis=1)
    land = jnp.broadcast_to(land, (half, LANES))
    for d, part in enumerate(combine([packed_ref[d] for d in range(4)], land)):
        prates_ref[d] = part


def parent_up(carry, pc_ref, psolved_ref, mate_rows, far_rows, lines, cols_ref, cols_at):
    half = psolved_ref.shape[0]
    lane = lane_index()
    middle = pc_ref[half - 1 : half, :]
    scale = 1.0 / (1.0 - middle * pltpu.roll(middle, 64, 1))
    x = (carry + middle * pltpu.roll(carry, 64, 1)) * scale
    tiles = [None] * half
    tiles[half - 1] = x
    for i in range(half - 2, -1, -1):
        x = psolved_ref[i] + pc_ref[i : i + 1, :] * x
        tiles[i] = x
    packed = jnp.zeros((8, LANES), F32)
    for i in range(half):
        psolved_ref[i] = tiles[i]
        packed = jnp.where(((lane & 31) >> 1) == i, pltpu.roll(tiles[i], 2 * i + 1, 1), packed)
    cols_ref[cols_at : cols_at + 8, :] = packed
    first = (lane & 32) == 0
    swap = jnp.broadcast_to(parity("gy"), (8, LANES)) == 1
    for j in range(half // 2):
        one, two = tiles[j], tiles[j + half // 2]
        lo = jnp.where(first, one, pltpu.roll(two, 32, 1))
        hi = jnp.where(first, pltpu.roll(one, 96, 1), two)
        part = slice(lines + 8 * j, lines + 8 * j + 8)
        mate_rows[part, :] = jnp.where(swap, lo, hi)
        far_rows[part, :] = jnp.where(swap, hi, lo)


def parent_edges(mate_cols, far_cols, at):
    return merge_edges(mate_cols[at : at + 8, :], far_cols[at : at + 8, :], 62)


def parent_transport(psolved_ref, prates_ref, mate_row, far_row, edges, i):
    half = psolved_ref.shape[0]
    lane = lane_index()
    swap = jnp.broadcast_to(parity("gy"), (8, LANES)) == 1
    x = psolved_ref[i]
    mate, far = mate_row(i % (half // 2)), far_row(i % (half // 2))
    lo, hi = jnp.where(swap, far, mate), jnp.where(swap, mate, far)
    if i < half // 2:
        lo = pltpu.roll(lo, 32, 1)
    else:
        hi = pltpu.roll(hi, 96, 1)
    first = (lane & 32) == 0
    to_north = jnp.where(first, pltpu.roll(x, 96, 1), lo)
    to_south = jnp.where(first, hi, pltpu.roll(x, 32, 1))
    edge = pltpu.roll(edges, (LANES - 2 * i - 32) & (LANES - 1), 1)
    column = lane & 31
    to_east = jnp.where(column == 31, edge, pltpu.roll(x, 127, 1))
    to_west = jnp.where(column == 0, edge, pltpu.roll(x, 1, 1))
    parts = [prates_ref[d, i : i + 1, :] for d in range(5)]
    return (parts[0] * x + parts[1] * to_east) + (parts[2] * to_west + parts[3] * to_north) + parts[4] * to_south


def parent_second(
    psolved_in, prates_ref, pa_ref, pb_ref, pc_ref, mate_in, far_in, mate_cols, far_cols, feed_ref,
    psolved_ref, mate_rows, far_rows, cols_ref,
):
    half = psolved_in.shape[0]
    lines = mate_in.shape[0] - mate_rows.shape[0]
    edges = parent_edges(mate_cols, far_cols, mate_cols.shape[0] - 8)
    mate = lambda j: mate_in[lines + 8 * j : lines + 8 * j + 8, :]
    far = lambda j: far_in[lines + 8 * j : lines + 8 * j + 8, :]
    y = jnp.zeros((8, LANES), F32)
    for i in range(half):
        rhs = parent_transport(psolved_in, prates_ref, mate, far, edges, i)
        rhs = rhs + feed_ref[8 * i : 8 * i + 8, :]
        y = pa_ref[i : i + 1, :] * rhs + pb_ref[i : i + 1, :] * y
        psolved_ref[i] = y
    parent_up(y, pc_ref, psolved_ref, mate_rows, far_rows, 0, cols_ref, 0)


def parent_last(psolved_in, prates_ref, mate_in, far_in, mate_cols, far_cols, out_ref):
    half, vectors = psolved_in.shape[0], psolved_in.shape[1]
    edges = parent_edges(mate_cols, far_cols, 0)
    mate = lambda j: mate_in[8 * j : 8 * j + 8, :]
    far = lambda j: far_in[8 * j : 8 * j + 8, :]
    for i in range(half):
        x = parent_transport(psolved_in, prates_ref, mate, far, edges, i)
        for h in range(2):
            for r in range(2):
                lo = 64 * h + 32 * r
                k = 2 * half - 1 - i if h else i
                out_ref[pl.ds(2 * vectors * k + r, vectors, stride=2), :] = x[:, lo : lo + 32]


def passed_along(value, axis, steps):
    count = lax.axis_size(axis)
    return lax.ppermute(value, axis, [(i, (i + steps) % count) for i in range(count)])


def swapped(value, axis, offset):
    count = lax.axis_size(axis)
    pairs = []
    for i in range(offset, count, 2):
        j = (i + 1) % count
        pairs += [(i, j), (j, i)]
    return lax.ppermute(value, axis, pairs)


def halos_of(mate, far, cols):
    return [swapped(mate, "gy", 0), swapped(far, "gy", 1), swapped(cols, "gx", 0), swapped(cols, "gx", 1)]


def local(
    child_adjoint,
    parent_adjoint,
    child_rates,
    child_mixing,
    child_land,
    parent_rates,
    parent_mixing,
    parent_land,
    relaxation,
):
    depth, vectors, lines, columns = child_adjoint.shape
    half = depth // 2
    quarter = lax.axis_size("gy") // 4
    field = shape(depth, vectors, lines, columns)
    factor = shape(depth, lines, columns)
    tiles = shape(half, vectors, LANES)
    sums = shape(half * vectors, LANES)
    count = depth * vectors
    edge = depth // LEVELS * 8
    sum_scratch = pltpu.VMEM((half * vectors, 4 * LANES), F32)
    edge_scratch = [pltpu.VMEM((edge, LANES), F32)]
    narrow = parent_adjoint.shape[-1]

    sums1, x, a, b, c, relax, land, parent_land, rates = call(
        begin,
        [sums, field, factor, factor, factor, shape(lines, columns), shape(lines, columns), shape(*parent_land.shape)]
        + [shape(*child_rates.shape)],
        [
            pltpu.VMEM(factor.shape, F32),
            pltpu.VMEM(child_land.shape, jnp.int32),
            pltpu.VMEM(parent_land.shape, jnp.int32),
            sum_scratch,
            pltpu.SemaphoreType.DMA((5 + half // 2,)),
        ],
        [child_adjoint, child_mixing, relaxation, child_land, parent_land, child_rates],
        4_000_000,
        3_000_000,
        far_in=range(6),
    )
    feed = passed_along(sums1, "gy", quarter)
    solved, mate, far, cols = call(
        child_first,
        [field, shape(count, LANES), shape(count, LANES), shape(edge, LANES)],
        [],
        [x, a, b, c],
        4_000_000,
        3_000_000,
    )
    halos = halos_of(mate, far, cols)
    inner, row_rates, column_rates = call(
        child_inner,
        [field, factor, factor],
        [],
        [solved, rates, land, cols],
        INNER,
        4_000_000,
    )
    fed = call(
        parent_fed,
        tiles,
        [],
        [parent_adjoint.reshape(-1, narrow), feed, inner],
        LONG,
        1_000_000,
    )
    raw_sums, x = call(
        child_columns,
        [shape(half * vectors, 4 * LANES), field],
        edge_scratch,
        [inner, column_rates, relax, *halos[2:]],
        INNER,
        3_000_000,
    )
    pa, pb, pc = call(
        parent_factors,
        [shape(half, LANES)] * 3,
        [pltpu.VMEM((half, LANES), F32)],
        [parent_mixing.reshape(-1, narrow), fed, halos[1], x, raw_sums],
        LONG,
        1_000_000,
    )
    sums2 = call(
        child_rows,
        sums,
        [sum_scratch],
        [raw_sums, row_rates, relax, pa, *halos[:2]],
        INNER,
        1_000_000,
    )
    feed = passed_along(sums2, "gy", quarter)
    rows = count + half // 2 * vectors
    solved, psolved, mate, far, cols = call(
        child_second,
        [field, tiles, shape(rows, LANES), shape(rows, LANES), shape(edge + 8, LANES)],
        [],
        [x, row_rates, *halos[:2], a, b, c, fed, pa, pb, pc],
        8_000_000,
        3_000_000,
    )
    halos = halos_of(mate, far, cols)
    inner, row_rates, column_rates = call(
        child_inner,
        [field, factor, factor],
        [],
        [solved, rates, land, cols],
        INNER,
        4_000_000,
    )
    packed_rates = call(
        parent_rates_packed,
        shape(4, half, LANES),
        [],
        [parent_rates.reshape(-1, narrow), feed, inner],
        1_450_000_000,
        1_000_000,
    )
    prates = call(
        parent_rates_masked,
        shape(5, half, LANES),
        [],
        [packed_rates, parent_land, *halos[1:]],
        LONG,
        1_000_000,
    )
    few = half // 2 * vectors
    psolved, mate, far, cols = call(
        parent_second,
        [tiles, shape(few, LANES), shape(few, LANES), shape(8, LANES)],
        [],
        [psolved, prates, pa, pb, pc, *halos, feed],
        1_000_000,
        500_000,
    )
    last_halos = halos_of(mate, far, cols)
    child_out = call(
        child_last,
        field,
        [pltpu.VMEM(field.shape, F32)] + edge_scratch + [pltpu.SemaphoreType.DMA((depth // LEVELS,))],
        [inner, row_rates, column_rates, *halos],
        4_000_000,
        3_000_000,
        far_out=True,
    )
    parent_out = call(
        parent_last,
        shape(depth * vectors * 2, narrow),
        [],
        [psolved, prates, *last_halos],
        500_000,
        500_000,
    )
    return (child_out, parent_out.reshape(parent_adjoint.shape))


def solution(mesh):
    wide = P(None, None, "gy", "gx")
    level = P(None, "gy", "gx")
    flat = P("gy", "gx")
    in_specs = (wide, wide, wide, level, flat, wide, level, flat, flat)
    return jax.shard_map(local, mesh=mesh, in_specs=in_specs, out_specs=(wide, wide), check_vma=False)
```

```python
import jax
import jax.numpy as jnp
from jax import lax
from jax.experimental import pallas as pl
from jax.experimental.pallas import tpu as pltpu
from jax.sharding import PartitionSpec as P

F32 = jnp.float32
VMEM = pl.BlockSpec(memory_space=pltpu.VMEM)
FAR = pl.BlockSpec(memory_space=pltpu.HBM)
LIMIT = 40 * 1024 * 1024
LANES = 128
LONG = 1_000_000_000
INNER = 10_000_000
LEVELS = 8


def shape(*dims):
    return jax.ShapeDtypeStruct(dims, F32)


def call(body, outs, scratch, operands, flops, touched, far_in=(), far_out=False):
    operands = [pltpu.with_memory_space_constraint(x, pltpu.HBM) if i in far_in else x for i, x in enumerate(operands)]
    return pl.pallas_call(
        body,
        out_shape=outs,
        in_specs=[FAR if i in far_in else VMEM for i in range(len(operands))],
        out_specs=jax.tree.map(lambda _: FAR if far_out else VMEM, outs),
        scratch_shapes=scratch,
        compiler_params=pltpu.CompilerParams(vmem_limit_bytes=LIMIT),
        cost_estimate=pl.CostEstimate(flops=flops, bytes_accessed=touched, transcendentals=0),
        name=body.__name__,
    )(*operands)


def lane_index(rows=8):
    return lax.broadcasted_iota(jnp.int32, (rows, LANES), 1)


def row_index():
    return lax.broadcasted_iota(jnp.int32, (8, LANES), 0)


def minors(inner, outer):
    theta = delta = jnp.ones_like(inner[0])
    inverse = []
    for i in range(len(inner)):
        delta = theta + outer[i] * delta
        theta_next = delta + inner[i] * theta
        inverse.append(theta / theta_next)
        theta = theta_next
    return inverse


def parity(axis):
    return lax.rem(lax.axis_index(axis), 2)


def child_factors(mix_ref, keep, a_ref, b_ref, c_ref):
    depth = mix_ref.shape[0]
    half = depth // 2
    zero = jnp.zeros_like(keep)
    top_inner = [mix_ref[i] for i in range(half)]
    top_outer = [zero] + top_inner[:-1]
    low_outer = [mix_ref[depth - 1 - i] for i in range(half)]
    low_inner = [mix_ref[depth - 2 - i] for i in range(half)]
    for levels, inner, outer in (
        (range(half), top_inner, top_outer),
        (range(depth - 1, half - 1, -1), low_inner, low_outer),
    ):
        inverse = minors(inner, outer)
        for i, k in enumerate(levels):
            a_ref[k] = inverse[i] * keep
            b_ref[k] = inverse[i] * outer[i]
            c_ref[k] = inverse[i] * inner[i]


def block_rows(source_ref, k, weights, sums_ref, i, place):
    vectors = source_ref.shape[1]
    for r in range(2):
        total = source_ref[k, :, 4 * r, :] * weights[4 * r]
        for j in range(4 * r + 1, 4 * r + 4):
            total = total + source_ref[k, :, j, :] * weights[j]
        column = (2 * place + r) * LANES
        sums_ref[pl.ds(i * vectors, vectors), column : column + LANES] = total


def block_columns(sums_ref):
    wide = sums_ref.shape[1]
    p = lax.broadcasted_iota(jnp.int32, (wide, LANES), 0)
    q = lax.broadcasted_iota(jnp.int32, (wide, LANES), 1)
    pick = jnp.where(p // 4 == q, F32(0.0625), F32(0.0)).astype(jnp.bfloat16)
    rest, total = sums_ref[...], None
    for _ in range(3):
        part = rest.astype(jnp.bfloat16)
        rest = rest - part.astype(F32)
        product = jnp.dot(part, pick, preferred_element_type=F32)
        total = product if total is None else total + product
    return total


def child_middle(carry, c_ref, half):
    vectors = len(carry) // 2
    top, low = c_ref[half - 1], c_ref[half]
    scale = 1.0 / (1.0 - top * low)
    first = [(carry[v] + top * carry[vectors + v]) * scale for v in range(vectors)]
    second = [(carry[vectors + v] + low * carry[v]) * scale for v in range(vectors)]
    return first + second


def child_up(carry, c_ref, solved_ref, mate_rows, far_rows, cols_ref):
    depth, vectors = solved_ref.shape[0], solved_ref.shape[1]
    half = depth // 2
    lane = lane_index()
    pair = lane >> 1
    swap = jnp.broadcast_to(parity("gy"), (8, LANES)) == 1

    def emit(i, values, packed):
        k_low = depth - 1 - i
        packed = list(packed)
        inside = i % LEVELS if isinstance(i, int) else lax.rem(i, LEVELS)
        for side, k, base in ((0, i, inside * vectors), (1, k_low, (LEVELS - 1 - inside) * vectors)):
            for v in range(vectors):
                x = values[side * vectors + v]
                solved_ref[k, v] = x
                at = base + v
                packed[side] = jnp.where(pair == at, pltpu.roll(x, 2 * at + 1 & (LANES - 1), 1), packed[side])
            lo, hi = solved_ref[k, :, 0, :], solved_ref[k, :, 7, :]
            mate_rows[pl.ds(k * vectors, vectors), :] = jnp.where(swap, lo, hi)
            far_rows[pl.ds(k * vectors, vectors), :] = jnp.where(swap, hi, lo)
        return packed

    def up(i, state):
        k_low = depth - 1 - i
        top, low = c_ref[i], c_ref[k_low]
        values = []
        for v in range(vectors):
            values.append(solved_ref[i, v] + top * state[v])
        for v in range(vectors):
            values.append(solved_ref[k_low, v] + low * state[vectors + v])
        return tuple(values) + tuple(emit(i, values, state[2 * vectors :]))

    def keep_columns(group, packed):
        for side, g in ((0, group), (1, depth // LEVELS - 1 - group)):
            cols_ref[LEVELS * g : LEVELS * g + 8, :] = packed[side]

    blank = jnp.zeros((8, LANES), F32)
    values = child_middle(carry, c_ref, half)
    state = tuple(values) + tuple(emit(half - 1, values, [blank] * 2))
    for group in range(half // LEVELS - 1, -1, -1):
        last = LEVELS * (group + 1) - 1
        if group == half // LEVELS - 1:
            last -= 1
        count = last - LEVELS * group + 1
        state = lax.fori_loop(0, count, lambda step, state, last=last: up(last - step, state), state, unroll=4 if count % 4 == 0 else count)
        keep_columns(group, state[2 * vectors :])
        state = state[: 2 * vectors] + (blank,) * 2


def begin(
    x_hbm, mix_hbm, relax_hbm, land_hbm, parent_land_hbm, rates_hbm,
    sums_out, x_ref, a_ref, b_ref, c_ref, relax_ref, land_ref, parent_land_ref, rates_ref,
    mix_ref, land_in, parent_land_in, sums_ref, sems,
):
    depth = x_ref.shape[0]
    half = depth // 2
    small = []
    for source, target in (
        (mix_hbm, mix_ref), (relax_hbm, relax_ref), (land_hbm, land_in), (parent_land_hbm, parent_land_in),
    ):
        small.append(pltpu.make_async_copy(source, target, sems.at[len(small)]))
        small[-1].start()
    size, large = 4, []
    for start in range(0, half, size):
        for first in (start, depth - size - start):
            part = pl.ds(first, size)
            large.append(pltpu.make_async_copy(x_hbm.at[part], x_ref.at[part], sems.at[len(large) + len(small)]))
            large[-1].start()
    rates_copy = pltpu.make_async_copy(rates_hbm, rates_ref, sems.at[len(large) + len(small)])
    rates_copy.start()
    for copy in small:
        copy.wait()
    land_ref[...] = land_in[...].astype(F32)
    parent_land_ref[...] = parent_land_in[...].astype(F32)
    child_factors(mix_ref, 1.0 - relax_ref[...], a_ref, b_ref, c_ref)
    weights = [relax_ref[j : j + 1, :] for j in range(8)]

    def level(i, _):
        for side, k in ((0, i), (1, depth - 1 - i)):
            block_rows(x_ref, k, weights, sums_ref, i, side)
        return 0

    for part, start in enumerate(range(0, half, size)):
        large[2 * part].wait()
        large[2 * part + 1].wait()
        lax.fori_loop(start, start + size, level, 0, unroll=size)
    sums_out[...] = block_columns(sums_ref)
    rates_copy.wait()


def child_first(x_ref, a_ref, b_ref, c_ref, solved_ref, mate_rows, far_rows, cols_ref):
    child_solve(x_ref, a_ref, b_ref, c_ref, solved_ref, mate_rows, far_rows, cols_ref, lambda k, v, _: x_ref[k, v])


def child_solve(x_ref, a_ref, b_ref, c_ref, solved_ref, mate_rows, far_rows, cols_ref, load, row_ref=None):
    depth, vectors = x_ref.shape[0], x_ref.shape[1]
    half = depth // 2

    def down(i, carry):
        values = []
        for side, k in ((0, i), (1, depth - 1 - i)):
            a, b = a_ref[k], b_ref[k]
            row_rates = None if row_ref is None else row_ref[k]
            for v in range(vectors):
                y = a * load(k, v, row_rates) + b * carry[side * vectors + v]
                solved_ref[k, v] = y
                values.append(y)
        return tuple(values)

    carry = lax.fori_loop(0, half, down, (jnp.zeros((8, LANES), F32),) * (2 * vectors), unroll=4)
    child_up(carry, c_ref, solved_ref, mate_rows, far_rows, cols_ref)


def combine(sides, land):
    east, west, north, south = sides
    return [land * part for part in (1.0 - (east + west + north + south), east, west, north, south)]


def merge_edges(mate, far, turn):
    swap = jnp.broadcast_to(parity("gx"), (8, LANES)) == 1
    east, west = jnp.where(swap, far, mate), jnp.where(swap, mate, far)
    return jnp.where((lane_index() & 1) == 0, west, pltpu.roll(east, turn, 1))


def child_inner(solved_ref, rates_ref, land_ref, after_ref, inner_ref, row_ref, column_ref):
    depth, vectors = solved_ref.shape[0], solved_ref.shape[1]
    lane, row = lane_index(), row_index()
    land = land_ref[...]

    def level(k, _):
        centre, east, west, north, south = combine([rates_ref[d, k] for d in range(4)], land)
        column_ref[k] = jnp.where(lane == 0, west, jnp.where(lane == LANES - 1, east, 0.0))
        row_ref[k] = jnp.where(row == 0, south, jnp.where(row == 7, north, 0.0))
        east, west = jnp.where(lane == LANES - 1, 0.0, east), jnp.where(lane == 0, 0.0, west)
        north, south = jnp.where(row == 7, 0.0, north), jnp.where(row == 0, 0.0, south)
        for v in range(vectors):
            s = solved_ref[k, v]
            across = east * pltpu.roll(s, LANES - 1, 1) + west * pltpu.roll(s, 1, 1)
            along = north * pltpu.roll(s, 7, 0) + south * pltpu.roll(s, 1, 0)
            inner_ref[k, v] = centre * s + across + along
        return 0

    lax.fori_loop(0, depth, level, 0, unroll=4)


def edge_merger(mate_cols, far_cols, merged_ref):
    for g in range(merged_ref.shape[0] // 8):
        part = slice(8 * g, 8 * g + 8)
        merged_ref[part, :] = merge_edges(mate_cols[part, :], far_cols[part, :], LANES - 2)


def column_edged(inner_ref, column_rates, edges, k, v, at):
    return inner_ref[k, v] + column_rates * pltpu.roll(edges, (LANES - 2 * at) & (LANES - 1), 1)


def row_halo(mate_ref, far_ref, k, v, vectors, mates):
    line = pl.ds(k * vectors + v, 1)
    mate = jnp.broadcast_to(mate_ref[line, :], (8, LANES))
    far = jnp.broadcast_to(far_ref[line, :], (8, LANES))
    return jnp.where(mates, mate, far)


def mate_rows_mask():
    return row_index() == 7 * (1 - parity("gy"))


def child_columns(inner_ref, column_ref, relax_ref, after_ref, mate_cols, far_cols, sums_ref, x_ref, merged_ref):
    depth, vectors = inner_ref.shape[0], inner_ref.shape[1]
    half, groups = depth // 2, depth // LEVELS
    weights = [relax_ref[j : j + 1, :] for j in range(8)]
    edge_merger(mate_cols, far_cols, merged_ref)

    def level(i, _, edges):
        inside = lax.rem(i, LEVELS)
        for side, k, base in ((0, i, inside * vectors), (1, depth - 1 - i, (LEVELS - 1 - inside) * vectors)):
            column_rates = column_ref[k]
            for v in range(vectors):
                x_ref[k, v] = column_edged(inner_ref, column_rates, edges[side], k, v, base + v)
            block_rows(x_ref, k, weights, sums_ref, i, side)
        return 0

    for group in range(half // LEVELS):
        edges = [merged_ref[8 * g : 8 * g + 8, :] for g in (group, groups - 1 - group)]
        lax.fori_loop(
            LEVELS * group, LEVELS * (group + 1), lambda i, _, edges=edges: level(i, _, edges), 0, unroll=4
        )


def child_rows(sums_in, row_ref, relax_ref, after_ref, mate_in, far_in, sums_out, sums_ref):
    depth = row_ref.shape[0]
    vectors = 2 * sums_in.shape[0] // depth
    swap = jnp.broadcast_to(parity("gy"), (vectors, LANES)) == 1
    for k in range(depth):
        place, i = (0, k) if k < depth // 2 else (1, depth - 1 - k)
        lines = slice(k * vectors, (k + 1) * vectors)
        mate, far = mate_in[lines, :], far_in[lines, :]
        for r, at, halo in ((0, 0, jnp.where(swap, mate, far)), (1, 7, jnp.where(swap, far, mate))):
            share = (row_ref[k, at : at + 1, :] * relax_ref[at : at + 1, :]) * halo
            part = slice(i * vectors, (i + 1) * vectors), slice((2 * place + r) * LANES, (2 * place + r + 1) * LANES)
            sums_ref[part] = sums_in[part] + share
    sums_out[...] = block_columns(sums_ref)


def child_second(
    x_ref, row_ref, mate_in, far_in, a_ref, b_ref, c_ref, parent_ref, pa_ref, pb_ref, pc_ref,
    solved_ref, psolved_ref, mate_rows, far_rows, cols_ref,
):
    depth, vectors = x_ref.shape[0], x_ref.shape[1]
    y = jnp.zeros((8, LANES), F32)
    for i in range(depth // 2):
        y = pa_ref[i : i + 1, :] * parent_ref[i] + pb_ref[i : i + 1, :] * y
        psolved_ref[i] = y
    lines, at = depth * vectors, depth // LEVELS * 8
    parent_up(y, pc_ref, psolved_ref, mate_rows, far_rows, lines, cols_ref, at)
    mates = mate_rows_mask()

    def load(k, v, row_rates):
        return x_ref[k, v] + row_rates * row_halo(mate_in, far_in, k, v, vectors, mates)

    child_solve(x_ref, a_ref, b_ref, c_ref, solved_ref, mate_rows, far_rows, cols_ref, load, row_ref)


def child_last(
    inner_ref, row_ref, column_ref, mate_in, far_in, mate_cols, far_cols, out_hbm, out_ref, merged_ref, sems
):
    depth, vectors = inner_ref.shape[0], inner_ref.shape[1]
    mates = mate_rows_mask()
    edge_merger(mate_cols, far_cols, merged_ref)
    copies = []
    for group in range(depth // LEVELS):
        edges = merged_ref[8 * group : 8 * group + 8, :]

        def level(inside, _):
            k = LEVELS * group + inside
            row_rates, column_rates = row_ref[k], column_ref[k]
            for v in range(vectors):
                out_ref[k, v] = column_edged(
                    inner_ref, column_rates, edges, k, v, inside * vectors + v
                ) + row_rates * row_halo(mate_in, far_in, k, v, vectors, mates)
            return 0

        lax.fori_loop(0, LEVELS, level, 0, unroll=4)
        part = pl.ds(LEVELS * group, LEVELS)
        copies.append(pltpu.make_async_copy(out_ref.at[part], out_hbm.at[part], sems.at[group]))
        copies[-1].start()
    for copy in copies:
        copy.wait()


PLACES = [(h, r, 64 * h + 32 * r) for h in range(2) for r in range(2)]


def parent_fed(parent_ref, mix_ref, feed_ref, after_ref, packed_ref, mixed):
    half, vectors = packed_ref.shape[0], packed_ref.shape[1]
    for i in range(half):
        for h, r, lo in PLACES:
            k = 2 * half - 1 - i if h else i
            packed_ref[i, :, lo : lo + 32] = parent_ref[pl.ds(2 * vectors * k + r, vectors, stride=2), :]
            mixed[i : i + 1, lo : lo + 32] = mix_ref[2 * k + r : 2 * k + r + 1, :]
        packed_ref[i] = packed_ref[i] + feed_ref[vectors * i : vectors * (i + 1), :]


def parent_factors(mixed, far_ref, x_ref, sums_ref, pa_ref, pb_ref, pc_ref):
    half = pa_ref.shape[0]
    upper = lane_index(1) < 64
    rows = [mixed[i : i + 1, :] for i in range(half)]
    inner, outer = [], []
    for i in range(half):
        nearer = rows[i + 1] if i + 1 < half else pltpu.roll(rows[i], 64, 1)
        inner.append(jnp.where(upper, rows[i], nearer))
        outer.append(jnp.where(upper, rows[i - 1] if i else jnp.zeros_like(rows[0]), rows[i]))
    inverse = minors(inner, outer)
    for i in range(half):
        pa_ref[i : i + 1, :] = inverse[i]
        pb_ref[i : i + 1, :] = inverse[i] * outer[i]
        pc_ref[i : i + 1, :] = inverse[i] * inner[i]


def parent_rates_packed(rates_ref, feed_ref, after_ref, packed_ref):
    half = packed_ref.shape[1]
    depth = 2 * half
    for i in range(half):
        for h, r, lo in PLACES:
            k = depth - 1 - i if h else i
            for d in range(4):
                at = 2 * (d * depth + k) + r
                packed_ref[d, i : i + 1, lo : lo + 32] = rates_ref[at : at + 1, :]


def parent_rates_masked(packed_ref, land_ref, far_ref, mate_cols, far_cols, prates_ref):
    half = packed_ref.shape[1]
    land = jnp.concatenate([land_ref[r : r + 1, :] for _, r, _ in PLACES], axis=1)
    land = jnp.broadcast_to(land, (half, LANES))
    for d, part in enumerate(combine([packed_ref[d] for d in range(4)], land)):
        prates_ref[d] = part


def parent_up(carry, pc_ref, psolved_ref, mate_rows, far_rows, lines, cols_ref, cols_at):
    half = psolved_ref.shape[0]
    lane = lane_index()
    middle = pc_ref[half - 1 : half, :]
    scale = 1.0 / (1.0 - middle * pltpu.roll(middle, 64, 1))
    x = (carry + middle * pltpu.roll(carry, 64, 1)) * scale
    tiles = [None] * half
    tiles[half - 1] = x
    for i in range(half - 2, -1, -1):
        x = psolved_ref[i] + pc_ref[i : i + 1, :] * x
        tiles[i] = x
    packed = jnp.zeros((8, LANES), F32)
    for i in range(half):
        psolved_ref[i] = tiles[i]
        packed = jnp.where(((lane & 31) >> 1) == i, pltpu.roll(tiles[i], 2 * i + 1, 1), packed)
    cols_ref[cols_at : cols_at + 8, :] = packed
    first = (lane & 32) == 0
    swap = jnp.broadcast_to(parity("gy"), (8, LANES)) == 1
    for j in range(half // 2):
        one, two = tiles[j], tiles[j + half // 2]
        lo = jnp.where(first, one, pltpu.roll(two, 32, 1))
        hi = jnp.where(first, pltpu.roll(one, 96, 1), two)
        part = slice(lines + 8 * j, lines + 8 * j + 8)
        mate_rows[part, :] = jnp.where(swap, lo, hi)
        far_rows[part, :] = jnp.where(swap, hi, lo)


def parent_edges(mate_cols, far_cols, at):
    return merge_edges(mate_cols[at : at + 8, :], far_cols[at : at + 8, :], 62)


def parent_transport(psolved_ref, prates_ref, mate_row, far_row, edges, i):
    half = psolved_ref.shape[0]
    lane = lane_index()
    swap = jnp.broadcast_to(parity("gy"), (8, LANES)) == 1
    x = psolved_ref[i]
    mate, far = mate_row(i % (half // 2)), far_row(i % (half // 2))
    lo, hi = jnp.where(swap, far, mate), jnp.where(swap, mate, far)
    if i < half // 2:
        lo = pltpu.roll(lo, 32, 1)
    else:
        hi = pltpu.roll(hi, 96, 1)
    first = (lane & 32) == 0
    to_north = jnp.where(first, pltpu.roll(x, 96, 1), lo)
    to_south = jnp.where(first, hi, pltpu.roll(x, 32, 1))
    edge = pltpu.roll(edges, (LANES - 2 * i - 32) & (LANES - 1), 1)
    column = lane & 31
    to_east = jnp.where(column == 31, edge, pltpu.roll(x, 127, 1))
    to_west = jnp.where(column == 0, edge, pltpu.roll(x, 1, 1))
    parts = [prates_ref[d, i : i + 1, :] for d in range(5)]
    return (parts[0] * x + parts[1] * to_east) + (parts[2] * to_west + parts[3] * to_north) + parts[4] * to_south


def parent_second(
    psolved_in, prates_ref, pa_ref, pb_ref, pc_ref, mate_in, far_in, mate_cols, far_cols, feed_ref,
    psolved_ref, mate_rows, far_rows, cols_ref,
):
    half = psolved_in.shape[0]
    lines = mate_in.shape[0] - mate_rows.shape[0]
    edges = parent_edges(mate_cols, far_cols, mate_cols.shape[0] - 8)
    mate = lambda j: mate_in[lines + 8 * j : lines + 8 * j + 8, :]
    far = lambda j: far_in[lines + 8 * j : lines + 8 * j + 8, :]
    y = jnp.zeros((8, LANES), F32)
    for i in range(half):
        rhs = parent_transport(psolved_in, prates_ref, mate, far, edges, i)
        rhs = rhs + feed_ref[8 * i : 8 * i + 8, :]
        y = pa_ref[i : i + 1, :] * rhs + pb_ref[i : i + 1, :] * y
        psolved_ref[i] = y
    parent_up(y, pc_ref, psolved_ref, mate_rows, far_rows, 0, cols_ref, 0)


def parent_last(psolved_in, prates_ref, mate_in, far_in, mate_cols, far_cols, out_ref):
    half, vectors = psolved_in.shape[0], psolved_in.shape[1]
    edges = parent_edges(mate_cols, far_cols, 0)
    mate = lambda j: mate_in[8 * j : 8 * j + 8, :]
    far = lambda j: far_in[8 * j : 8 * j + 8, :]
    for i in range(half):
        x = parent_transport(psolved_in, prates_ref, mate, far, edges, i)
        for h in range(2):
            for r in range(2):
                lo = 64 * h + 32 * r
                k = 2 * half - 1 - i if h else i
                out_ref[pl.ds(2 * vectors * k + r, vectors, stride=2), :] = x[:, lo : lo + 32]


def passed_along(value, axis, steps):
    count = lax.axis_size(axis)
    return lax.ppermute(value, axis, [(i, (i + steps) % count) for i in range(count)])


def swapped(value, axis, offset):
    count = lax.axis_size(axis)
    pairs = []
    for i in range(offset, count, 2):
        j = (i + 1) % count
        pairs += [(i, j), (j, i)]
    return lax.ppermute(value, axis, pairs)


def halos_of(mate, far, cols):
    return [swapped(mate, "gy", 0), swapped(far, "gy", 1), swapped(cols, "gx", 0), swapped(cols, "gx", 1)]


def local(
    child_adjoint,
    parent_adjoint,
    child_rates,
    child_mixing,
    child_land,
    parent_rates,
    parent_mixing,
    parent_land,
    relaxation,
):
    depth, vectors, lines, columns = child_adjoint.shape
    half = depth // 2
    quarter = lax.axis_size("gy") // 4
    field = shape(depth, vectors, lines, columns)
    factor = shape(depth, lines, columns)
    tiles = shape(half, vectors, LANES)
    sums = shape(half * vectors, LANES)
    count = depth * vectors
    edge = depth // LEVELS * 8
    sum_scratch = pltpu.VMEM((half * vectors, 4 * LANES), F32)
    edge_scratch = [pltpu.VMEM((edge, LANES), F32)]
    narrow = parent_adjoint.shape[-1]

    sums1, x, a, b, c, relax, land, parent_land, rates = call(
        begin,
        [sums, field, factor, factor, factor, shape(lines, columns), shape(lines, columns), shape(*parent_land.shape)]
        + [shape(*child_rates.shape)],
        [
            pltpu.VMEM(factor.shape, F32),
            pltpu.VMEM(child_land.shape, jnp.int32),
            pltpu.VMEM(parent_land.shape, jnp.int32),
            sum_scratch,
            pltpu.SemaphoreType.DMA((5 + half // 2,)),
        ],
        [child_adjoint, child_mixing, relaxation, child_land, parent_land, child_rates],
        4_000_000,
        3_000_000,
        far_in=range(6),
    )
    feed = passed_along(sums1, "gy", quarter)
    solved, mate, far, cols = call(
        child_first,
        [field, shape(count, LANES), shape(count, LANES), shape(edge, LANES)],
        [],
        [x, a, b, c],
        4_000_000,
        3_000_000,
    )
    halos = halos_of(mate, far, cols)
    inner, row_rates, column_rates = call(
        child_inner,
        [field, factor, factor],
        [],
        [solved, rates, land, cols],
        INNER,
        4_000_000,
    )
    fed, mixed = call(
        parent_fed,
        [tiles, shape(half, LANES)],
        [],
        [parent_adjoint.reshape(-1, narrow), parent_mixing.reshape(-1, narrow), feed, inner],
        LONG,
        1_000_000,
    )
    raw_sums, x = call(
        child_columns,
        [shape(half * vectors, 4 * LANES), field],
        edge_scratch,
        [inner, column_rates, relax, mixed, *halos[2:]],
        INNER,
        3_000_000,
    )
    pa, pb, pc = call(
        parent_factors,
        [shape(half, LANES)] * 3,
        [],
        [mixed, halos[1], x, raw_sums],
        LONG,
        1_000_000,
    )
    sums2 = call(
        child_rows,
        sums,
        [sum_scratch],
        [raw_sums, row_rates, relax, pa, *halos[:2]],
        INNER,
        1_000_000,
    )
    feed = passed_along(sums2, "gy", quarter)
    rows = count + half // 2 * vectors
    solved, psolved, mate, far, cols = call(
        child_second,
        [field, tiles, shape(rows, LANES), shape(rows, LANES), shape(edge + 8, LANES)],
        [],
        [x, row_rates, *halos[:2], a, b, c, fed, pa, pb, pc],
        8_000_000,
        3_000_000,
    )
    halos = halos_of(mate, far, cols)
    inner, row_rates, column_rates = call(
        child_inner,
        [field, factor, factor],
        [],
        [solved, rates, land, cols],
        INNER,
        4_000_000,
    )
    packed_rates = call(
        parent_rates_packed,
        shape(4, half, LANES),
        [],
        [parent_rates.reshape(-1, narrow), feed, inner],
        1_450_000_000,
        1_000_000,
    )
    prates = call(
        parent_rates_masked,
        shape(5, half, LANES),
        [],
        [packed_rates, parent_land, *halos[1:]],
        LONG,
        1_000_000,
    )
    few = half // 2 * vectors
    psolved, mate, far, cols = call(
        parent_second,
        [tiles, shape(few, LANES), shape(few, LANES), shape(8, LANES)],
        [],
        [psolved, prates, pa, pb, pc, *halos, feed],
        1_000_000,
        500_000,
    )
    last_halos = halos_of(mate, far, cols)
    child_out = call(
        child_last,
        field,
        [pltpu.VMEM(field.shape, F32)] + edge_scratch + [pltpu.SemaphoreType.DMA((depth // LEVELS,))],
        [inner, row_rates, column_rates, *halos],
        4_000_000,
        3_000_000,
        far_out=True,
    )
    parent_out = call(
        parent_last,
        shape(depth * vectors * 2, narrow),
        [],
        [psolved, prates, *last_halos],
        500_000,
        500_000,
    )
    return (child_out, parent_out.reshape(parent_adjoint.shape))


def solution(mesh):
    wide = P(None, None, "gy", "gx")
    level = P(None, "gy", "gx")
    flat = P("gy", "gx")
    in_specs = (wide, wide, wide, level, flat, wide, level, flat, flat)
    return jax.shard_map(local, mesh=mesh, in_specs=in_specs, out_specs=(wide, wide), check_vma=False)
```

```python
import jax
import jax.numpy as jnp
from jax import lax
from jax.experimental import pallas as pl
from jax.experimental.pallas import tpu as pltpu
from jax.sharding import PartitionSpec as P

F32 = jnp.float32
VMEM = pl.BlockSpec(memory_space=pltpu.VMEM)
FAR = pl.BlockSpec(memory_space=pltpu.HBM)
LIMIT = 40 * 1024 * 1024
LANES = 128
LONG = 1_000_000_000
INNER = 10_000_000
LEVELS = 8


def shape(*dims):
    return jax.ShapeDtypeStruct(dims, F32)


def call(body, outs, scratch, operands, flops, touched, far_in=(), far_out=False):
    operands = [pltpu.with_memory_space_constraint(x, pltpu.HBM) if i in far_in else x for i, x in enumerate(operands)]
    return pl.pallas_call(
        body,
        out_shape=outs,
        in_specs=[FAR if i in far_in else VMEM for i in range(len(operands))],
        out_specs=jax.tree.map(lambda _: FAR if far_out else VMEM, outs),
        scratch_shapes=scratch,
        compiler_params=pltpu.CompilerParams(vmem_limit_bytes=LIMIT),
        cost_estimate=pl.CostEstimate(flops=flops, bytes_accessed=touched, transcendentals=0),
        name=body.__name__,
    )(*operands)


def lane_index(rows=8):
    return lax.broadcasted_iota(jnp.int32, (rows, LANES), 1)


def row_index():
    return lax.broadcasted_iota(jnp.int32, (8, LANES), 0)


def minors(inner, outer):
    theta = delta = jnp.ones_like(inner[0])
    inverse = []
    for i in range(len(inner)):
        delta = theta + outer[i] * delta
        theta_next = delta + inner[i] * theta
        inverse.append(theta / theta_next)
        theta = theta_next
    return inverse


def parity(axis):
    return lax.rem(lax.axis_index(axis), 2)


def child_factors(mix_ref, keep, a_ref, b_ref, c_ref):
    depth = mix_ref.shape[0]
    half = depth // 2
    zero = jnp.zeros_like(keep)
    top_inner = [mix_ref[i] for i in range(half)]
    top_outer = [zero] + top_inner[:-1]
    low_outer = [mix_ref[depth - 1 - i] for i in range(half)]
    low_inner = [mix_ref[depth - 2 - i] for i in range(half)]
    for levels, inner, outer in (
        (range(half), top_inner, top_outer),
        (range(depth - 1, half - 1, -1), low_inner, low_outer),
    ):
        inverse = minors(inner, outer)
        for i, k in enumerate(levels):
            a_ref[k] = inverse[i] * keep
            b_ref[k] = inverse[i] * outer[i]
            c_ref[k] = inverse[i] * inner[i]


def block_rows(source_ref, k, weights, sums_ref, i, place):
    vectors = source_ref.shape[1]
    for r in range(2):
        total = source_ref[k, :, 4 * r, :] * weights[4 * r]
        for j in range(4 * r + 1, 4 * r + 4):
            total = total + source_ref[k, :, j, :] * weights[j]
        column = (2 * place + r) * LANES
        sums_ref[pl.ds(i * vectors, vectors), column : column + LANES] = total


def block_columns(sums_ref):
    wide = sums_ref.shape[1]
    p = lax.broadcasted_iota(jnp.int32, (wide, LANES), 0)
    q = lax.broadcasted_iota(jnp.int32, (wide, LANES), 1)
    pick = jnp.where(p // 4 == q, F32(0.0625), F32(0.0)).astype(jnp.bfloat16)
    rest, total = sums_ref[...], None
    for _ in range(3):
        part = rest.astype(jnp.bfloat16)
        rest = rest - part.astype(F32)
        product = jnp.dot(part, pick, preferred_element_type=F32)
        total = product if total is None else total + product
    return total


def child_middle(carry, c_ref, half):
    vectors = len(carry) // 2
    top, low = c_ref[half - 1], c_ref[half]
    scale = 1.0 / (1.0 - top * low)
    first = [(carry[v] + top * carry[vectors + v]) * scale for v in range(vectors)]
    second = [(carry[vectors + v] + low * carry[v]) * scale for v in range(vectors)]
    return first + second


def child_up(carry, c_ref, solved_ref, mate_rows, far_rows, cols_ref):
    depth, vectors = solved_ref.shape[0], solved_ref.shape[1]
    half = depth // 2
    lane = lane_index()
    pair = lane >> 1
    swap = jnp.broadcast_to(parity("gy"), (8, LANES)) == 1

    def emit(i, values, packed):
        k_low = depth - 1 - i
        packed = list(packed)
        inside = i % LEVELS if isinstance(i, int) else lax.rem(i, LEVELS)
        for side, k, base in ((0, i, inside * vectors), (1, k_low, (LEVELS - 1 - inside) * vectors)):
            for v in range(vectors):
                x = values[side * vectors + v]
                solved_ref[k, v] = x
                at = base + v
                packed[side] = jnp.where(pair == at, pltpu.roll(x, 2 * at + 1 & (LANES - 1), 1), packed[side])
            lo, hi = solved_ref[k, :, 0, :], solved_ref[k, :, 7, :]
            mate_rows[pl.ds(k * vectors, vectors), :] = jnp.where(swap, lo, hi)
            far_rows[pl.ds(k * vectors, vectors), :] = jnp.where(swap, hi, lo)
        return packed

    def up(i, state):
        k_low = depth - 1 - i
        top, low = c_ref[i], c_ref[k_low]
        values = []
        for v in range(vectors):
            values.append(solved_ref[i, v] + top * state[v])
        for v in range(vectors):
            values.append(solved_ref[k_low, v] + low * state[vectors + v])
        return tuple(values) + tuple(emit(i, values, state[2 * vectors :]))

    def keep_columns(group, packed):
        for side, g in ((0, group), (1, depth // LEVELS - 1 - group)):
            cols_ref[LEVELS * g : LEVELS * g + 8, :] = packed[side]

    blank = jnp.zeros((8, LANES), F32)
    values = child_middle(carry, c_ref, half)
    state = tuple(values) + tuple(emit(half - 1, values, [blank] * 2))
    for group in range(half // LEVELS - 1, -1, -1):
        last = LEVELS * (group + 1) - 1
        if group == half // LEVELS - 1:
            last -= 1
        count = last - LEVELS * group + 1
        state = lax.fori_loop(0, count, lambda step, state, last=last: up(last - step, state), state, unroll=4 if count % 4 == 0 else count)
        keep_columns(group, state[2 * vectors :])
        state = state[: 2 * vectors] + (blank,) * 2


def begin(
    x_hbm, mix_hbm, relax_hbm, land_hbm, parent_land_hbm, rates_hbm,
    sums_out, x_ref, a_ref, b_ref, c_ref, relax_ref, land_ref, parent_land_ref, rates_ref,
    mix_ref, land_in, parent_land_in, sums_ref, sems,
):
    depth = x_ref.shape[0]
    half = depth // 2
    small = []
    for source, target in (
        (mix_hbm, mix_ref), (relax_hbm, relax_ref), (land_hbm, land_in), (parent_land_hbm, parent_land_in),
    ):
        small.append(pltpu.make_async_copy(source, target, sems.at[len(small)]))
        small[-1].start()
    size, large = 4, []
    for start in range(0, half, size):
        for first in (start, depth - size - start):
            part = pl.ds(first, size)
            large.append(pltpu.make_async_copy(x_hbm.at[part], x_ref.at[part], sems.at[len(large) + len(small)]))
            large[-1].start()
    rates_copy = pltpu.make_async_copy(rates_hbm, rates_ref, sems.at[len(large) + len(small)])
    rates_copy.start()
    for copy in small:
        copy.wait()
    land_ref[...] = land_in[...].astype(F32)
    parent_land_ref[...] = parent_land_in[...].astype(F32)
    child_factors(mix_ref, 1.0 - relax_ref[...], a_ref, b_ref, c_ref)
    weights = [relax_ref[j : j + 1, :] for j in range(8)]

    def level(i, _):
        for side, k in ((0, i), (1, depth - 1 - i)):
            block_rows(x_ref, k, weights, sums_ref, i, side)
        return 0

    for part, start in enumerate(range(0, half, size)):
        large[2 * part].wait()
        large[2 * part + 1].wait()
        lax.fori_loop(start, start + size, level, 0, unroll=size)
    sums_out[...] = block_columns(sums_ref)
    rates_copy.wait()


def child_first(x_ref, a_ref, b_ref, c_ref, solved_ref, mate_rows, far_rows, cols_ref):
    child_solve(x_ref, a_ref, b_ref, c_ref, solved_ref, mate_rows, far_rows, cols_ref, lambda k, v, _: x_ref[k, v])


def child_solve(x_ref, a_ref, b_ref, c_ref, solved_ref, mate_rows, far_rows, cols_ref, load, row_ref=None):
    depth, vectors = x_ref.shape[0], x_ref.shape[1]
    half = depth // 2

    def down(i, carry):
        values = []
        for side, k in ((0, i), (1, depth - 1 - i)):
            a, b = a_ref[k], b_ref[k]
            row_rates = None if row_ref is None else row_ref[k]
            for v in range(vectors):
                y = a * load(k, v, row_rates) + b * carry[side * vectors + v]
                solved_ref[k, v] = y
                values.append(y)
        return tuple(values)

    carry = lax.fori_loop(0, half, down, (jnp.zeros((8, LANES), F32),) * (2 * vectors), unroll=4)
    child_up(carry, c_ref, solved_ref, mate_rows, far_rows, cols_ref)


def combine(sides, land):
    east, west, north, south = sides
    return [land * part for part in (1.0 - (east + west + north + south), east, west, north, south)]


def merge_edges(mate, far, turn):
    swap = jnp.broadcast_to(parity("gx"), (8, LANES)) == 1
    east, west = jnp.where(swap, far, mate), jnp.where(swap, mate, far)
    return jnp.where((lane_index() & 1) == 0, west, pltpu.roll(east, turn, 1))


def child_inner(solved_ref, rates_ref, land_ref, after_ref, inner_ref, row_ref, column_ref):
    depth, vectors = solved_ref.shape[0], solved_ref.shape[1]
    lane, row = lane_index(), row_index()
    land = land_ref[...]

    def level(k, _):
        centre, east, west, north, south = combine([rates_ref[d, k] for d in range(4)], land)
        column_ref[k] = jnp.where(lane == 0, west, jnp.where(lane == LANES - 1, east, 0.0))
        row_ref[k] = jnp.where(row == 0, south, jnp.where(row == 7, north, 0.0))
        east, west = jnp.where(lane == LANES - 1, 0.0, east), jnp.where(lane == 0, 0.0, west)
        north, south = jnp.where(row == 7, 0.0, north), jnp.where(row == 0, 0.0, south)
        for v in range(vectors):
            s = solved_ref[k, v]
            across = east * pltpu.roll(s, LANES - 1, 1) + west * pltpu.roll(s, 1, 1)
            along = north * pltpu.roll(s, 7, 0) + south * pltpu.roll(s, 1, 0)
            inner_ref[k, v] = centre * s + across + along
        return 0

    lax.fori_loop(0, depth, level, 0, unroll=4)


def edge_merger(mate_cols, far_cols, merged_ref):
    for g in range(merged_ref.shape[0] // 8):
        part = slice(8 * g, 8 * g + 8)
        merged_ref[part, :] = merge_edges(mate_cols[part, :], far_cols[part, :], LANES - 2)


def column_edged(inner_ref, column_rates, edges, k, v, at):
    return inner_ref[k, v] + column_rates * pltpu.roll(edges, (LANES - 2 * at) & (LANES - 1), 1)


def row_halo(mate_ref, far_ref, k, v, vectors, mates):
    line = pl.ds(k * vectors + v, 1)
    mate = jnp.broadcast_to(mate_ref[line, :], (8, LANES))
    far = jnp.broadcast_to(far_ref[line, :], (8, LANES))
    return jnp.where(mates, mate, far)


def mate_rows_mask():
    return row_index() == 7 * (1 - parity("gy"))


def child_columns(inner_ref, column_ref, relax_ref, after_ref, mate_cols, far_cols, sums_ref, x_ref, merged_ref):
    depth, vectors = inner_ref.shape[0], inner_ref.shape[1]
    half, groups = depth // 2, depth // LEVELS
    weights = [relax_ref[j : j + 1, :] for j in range(8)]
    edge_merger(mate_cols, far_cols, merged_ref)

    def level(i, _, edges):
        inside = lax.rem(i, LEVELS)
        for side, k, base in ((0, i, inside * vectors), (1, depth - 1 - i, (LEVELS - 1 - inside) * vectors)):
            column_rates = column_ref[k]
            for v in range(vectors):
                x_ref[k, v] = column_edged(inner_ref, column_rates, edges[side], k, v, base + v)
            block_rows(x_ref, k, weights, sums_ref, i, side)
        return 0

    for group in range(half // LEVELS):
        edges = [merged_ref[8 * g : 8 * g + 8, :] for g in (group, groups - 1 - group)]
        lax.fori_loop(
            LEVELS * group, LEVELS * (group + 1), lambda i, _, edges=edges: level(i, _, edges), 0, unroll=4
        )


def child_rows(sums_in, row_ref, relax_ref, after_ref, mate_in, far_in, sums_out, sums_ref):
    depth = row_ref.shape[0]
    vectors = 2 * sums_in.shape[0] // depth
    swap = jnp.broadcast_to(parity("gy"), (vectors, LANES)) == 1
    for k in range(depth):
        place, i = (0, k) if k < depth // 2 else (1, depth - 1 - k)
        lines = slice(k * vectors, (k + 1) * vectors)
        mate, far = mate_in[lines, :], far_in[lines, :]
        for r, at, halo in ((0, 0, jnp.where(swap, mate, far)), (1, 7, jnp.where(swap, far, mate))):
            share = (row_ref[k, at : at + 1, :] * relax_ref[at : at + 1, :]) * halo
            part = slice(i * vectors, (i + 1) * vectors), slice((2 * place + r) * LANES, (2 * place + r + 1) * LANES)
            sums_ref[part] = sums_in[part] + share
    sums_out[...] = block_columns(sums_ref)


def child_second(
    x_ref, row_ref, mate_in, far_in, a_ref, b_ref, c_ref, parent_ref, pa_ref, pb_ref, pc_ref,
    solved_ref, psolved_ref, mate_rows, far_rows, cols_ref,
):
    depth, vectors = x_ref.shape[0], x_ref.shape[1]
    y = jnp.zeros((8, LANES), F32)
    for i in range(depth // 2):
        y = pa_ref[i : i + 1, :] * parent_ref[i] + pb_ref[i : i + 1, :] * y
        psolved_ref[i] = y
    lines, at = depth * vectors, depth // LEVELS * 8
    parent_up(y, pc_ref, psolved_ref, mate_rows, far_rows, lines, cols_ref, at)
    mates = mate_rows_mask()

    def load(k, v, row_rates):
        return x_ref[k, v] + row_rates * row_halo(mate_in, far_in, k, v, vectors, mates)

    child_solve(x_ref, a_ref, b_ref, c_ref, solved_ref, mate_rows, far_rows, cols_ref, load, row_ref)


def child_last(
    inner_ref, row_ref, column_ref, mate_in, far_in, mate_cols, far_cols, out_hbm, out_ref, merged_ref, sems
):
    depth, vectors = inner_ref.shape[0], inner_ref.shape[1]
    mates = mate_rows_mask()
    edge_merger(mate_cols, far_cols, merged_ref)
    copies = []
    for group in range(depth // LEVELS):
        edges = merged_ref[8 * group : 8 * group + 8, :]

        def level(inside, _):
            k = LEVELS * group + inside
            row_rates, column_rates = row_ref[k], column_ref[k]
            for v in range(vectors):
                out_ref[k, v] = column_edged(
                    inner_ref, column_rates, edges, k, v, inside * vectors + v
                ) + row_rates * row_halo(mate_in, far_in, k, v, vectors, mates)
            return 0

        lax.fori_loop(0, LEVELS, level, 0, unroll=4)
        part = pl.ds(LEVELS * group, LEVELS)
        copies.append(pltpu.make_async_copy(out_ref.at[part], out_hbm.at[part], sems.at[group]))
        copies[-1].start()
    for copy in copies:
        copy.wait()


PLACES = [(h, r, 64 * h + 32 * r) for h in range(2) for r in range(2)]


def parent_fed(parent_ref, mix_ref, feed_ref, after_ref, packed_ref, mixed):
    half, vectors = packed_ref.shape[0], packed_ref.shape[1]
    for i in range(half):
        for h, r, lo in PLACES:
            k = 2 * half - 1 - i if h else i
            packed_ref[i, :, lo : lo + 32] = parent_ref[pl.ds(2 * vectors * k + r, vectors, stride=2), :]
            mixed[i : i + 1, lo : lo + 32] = mix_ref[2 * k + r : 2 * k + r + 1, :]
        packed_ref[i] = packed_ref[i] + feed_ref[vectors * i : vectors * (i + 1), :]


def parent_factors(mixed, far_ref, x_ref, sums_ref, pa_ref, pb_ref, pc_ref):
    half = pa_ref.shape[0]
    upper = lane_index(1) < 64
    rows = [mixed[i : i + 1, :] for i in range(half)]
    inner, outer = [], []
    for i in range(half):
        nearer = rows[i + 1] if i + 1 < half else pltpu.roll(rows[i], 64, 1)
        inner.append(jnp.where(upper, rows[i], nearer))
        outer.append(jnp.where(upper, rows[i - 1] if i else jnp.zeros_like(rows[0]), rows[i]))
    inverse = minors(inner, outer)
    for i in range(half):
        pa_ref[i : i + 1, :] = inverse[i]
        pb_ref[i : i + 1, :] = inverse[i] * outer[i]
        pc_ref[i : i + 1, :] = inverse[i] * inner[i]


def parent_rates_packed(rates_ref, feed_ref, after_ref, packed_ref):
    half = packed_ref.shape[1]
    depth = 2 * half
    for i in range(half):
        for h, r, lo in PLACES:
            k = depth - 1 - i if h else i
            for d in range(4):
                at = 2 * (d * depth + k) + r
                packed_ref[d, i : i + 1, lo : lo + 32] = rates_ref[at : at + 1, :]


def parent_rates_masked(packed_ref, land_ref, far_ref, mate_cols, far_cols, prates_ref):
    half = packed_ref.shape[1]
    land = jnp.concatenate([land_ref[r : r + 1, :] for _, r, _ in PLACES], axis=1)
    land = jnp.broadcast_to(land, (half, LANES))
    for d, part in enumerate(combine([packed_ref[d] for d in range(4)], land)):
        prates_ref[d] = part


def parent_up(carry, pc_ref, psolved_ref, mate_rows, far_rows, lines, cols_ref, cols_at):
    half = psolved_ref.shape[0]
    lane = lane_index()
    middle = pc_ref[half - 1 : half, :]
    scale = 1.0 / (1.0 - middle * pltpu.roll(middle, 64, 1))
    x = (carry + middle * pltpu.roll(carry, 64, 1)) * scale
    tiles = [None] * half
    tiles[half - 1] = x
    for i in range(half - 2, -1, -1):
        x = psolved_ref[i] + pc_ref[i : i + 1, :] * x
        tiles[i] = x
    packed = jnp.zeros((8, LANES), F32)
    for i in range(half):
        psolved_ref[i] = tiles[i]
        packed = jnp.where(((lane & 31) >> 1) == i, pltpu.roll(tiles[i], 2 * i + 1, 1), packed)
    cols_ref[cols_at : cols_at + 8, :] = packed
    first = (lane & 32) == 0
    swap = jnp.broadcast_to(parity("gy"), (8, LANES)) == 1
    for j in range(half // 2):
        one, two = tiles[j], tiles[j + half // 2]
        lo = jnp.where(first, one, pltpu.roll(two, 32, 1))
        hi = jnp.where(first, pltpu.roll(one, 96, 1), two)
        part = slice(lines + 8 * j, lines + 8 * j + 8)
        mate_rows[part, :] = jnp.where(swap, lo, hi)
        far_rows[part, :] = jnp.where(swap, hi, lo)


def parent_edges(mate_cols, far_cols, at):
    return merge_edges(mate_cols[at : at + 8, :], far_cols[at : at + 8, :], 62)


def parent_transport(psolved_ref, prates_ref, mate_row, far_row, edges, i):
    half = psolved_ref.shape[0]
    lane = lane_index()
    swap = jnp.broadcast_to(parity("gy"), (8, LANES)) == 1
    x = psolved_ref[i]
    mate, far = mate_row(i % (half // 2)), far_row(i % (half // 2))
    lo, hi = jnp.where(swap, far, mate), jnp.where(swap, mate, far)
    if i < half // 2:
        lo = pltpu.roll(lo, 32, 1)
    else:
        hi = pltpu.roll(hi, 96, 1)
    first = (lane & 32) == 0
    to_north = jnp.where(first, pltpu.roll(x, 96, 1), lo)
    to_south = jnp.where(first, hi, pltpu.roll(x, 32, 1))
    edge = pltpu.roll(edges, (LANES - 2 * i - 32) & (LANES - 1), 1)
    column = lane & 31
    to_east = jnp.where(column == 31, edge, pltpu.roll(x, 127, 1))
    to_west = jnp.where(column == 0, edge, pltpu.roll(x, 1, 1))
    parts = [prates_ref[d, i : i + 1, :] for d in range(5)]
    return (parts[0] * x + parts[1] * to_east) + (parts[2] * to_west + parts[3] * to_north) + parts[4] * to_south


def parent_second(
    psolved_in, prates_ref, pa_ref, pb_ref, pc_ref, mate_in, far_in, mate_cols, far_cols, feed_ref,
    psolved_ref, mate_rows, far_rows, cols_ref,
):
    half = psolved_in.shape[0]
    lines = mate_in.shape[0] - mate_rows.shape[0]
    edges = parent_edges(mate_cols, far_cols, mate_cols.shape[0] - 8)
    mate = lambda j: mate_in[lines + 8 * j : lines + 8 * j + 8, :]
    far = lambda j: far_in[lines + 8 * j : lines + 8 * j + 8, :]
    y = jnp.zeros((8, LANES), F32)
    for i in range(half):
        rhs = parent_transport(psolved_in, prates_ref, mate, far, edges, i)
        rhs = rhs + feed_ref[8 * i : 8 * i + 8, :]
        y = pa_ref[i : i + 1, :] * rhs + pb_ref[i : i + 1, :] * y
        psolved_ref[i] = y
    parent_up(y, pc_ref, psolved_ref, mate_rows, far_rows, 0, cols_ref, 0)


def parent_merged(mate_cols, far_cols, after_ref, edges_ref):
    edges_ref[...] = parent_edges(mate_cols, far_cols, 0)


def parent_last(psolved_in, prates_ref, edges_ref, mate_in, far_in, out_ref):
    half, vectors = psolved_in.shape[0], psolved_in.shape[1]
    edges = edges_ref[...]
    mate = lambda j: mate_in[8 * j : 8 * j + 8, :]
    far = lambda j: far_in[8 * j : 8 * j + 8, :]
    for i in range(half):
        x = parent_transport(psolved_in, prates_ref, mate, far, edges, i)
        for h in range(2):
            for r in range(2):
                lo = 64 * h + 32 * r
                k = 2 * half - 1 - i if h else i
                out_ref[pl.ds(2 * vectors * k + r, vectors, stride=2), :] = x[:, lo : lo + 32]


def passed_along(value, axis, steps):
    count = lax.axis_size(axis)
    return lax.ppermute(value, axis, [(i, (i + steps) % count) for i in range(count)])


def swapped(value, axis, offset):
    count = lax.axis_size(axis)
    pairs = []
    for i in range(offset, count, 2):
        j = (i + 1) % count
        pairs += [(i, j), (j, i)]
    return lax.ppermute(value, axis, pairs)


def halos_of(mate, far, cols):
    return [swapped(mate, "gy", 0), swapped(far, "gy", 1), swapped(cols, "gx", 0), swapped(cols, "gx", 1)]


def local(
    child_adjoint,
    parent_adjoint,
    child_rates,
    child_mixing,
    child_land,
    parent_rates,
    parent_mixing,
    parent_land,
    relaxation,
):
    depth, vectors, lines, columns = child_adjoint.shape
    half = depth // 2
    quarter = lax.axis_size("gy") // 4
    field = shape(depth, vectors, lines, columns)
    factor = shape(depth, lines, columns)
    tiles = shape(half, vectors, LANES)
    sums = shape(half * vectors, LANES)
    count = depth * vectors
    edge = depth // LEVELS * 8
    sum_scratch = pltpu.VMEM((half * vectors, 4 * LANES), F32)
    edge_scratch = [pltpu.VMEM((edge, LANES), F32)]
    narrow = parent_adjoint.shape[-1]

    sums1, x, a, b, c, relax, land, parent_land, rates = call(
        begin,
        [sums, field, factor, factor, factor, shape(lines, columns), shape(lines, columns), shape(*parent_land.shape)]
        + [shape(*child_rates.shape)],
        [
            pltpu.VMEM(factor.shape, F32),
            pltpu.VMEM(child_land.shape, jnp.int32),
            pltpu.VMEM(parent_land.shape, jnp.int32),
            sum_scratch,
            pltpu.SemaphoreType.DMA((5 + half // 2,)),
        ],
        [child_adjoint, child_mixing, relaxation, child_land, parent_land, child_rates],
        4_000_000,
        3_000_000,
        far_in=range(6),
    )
    feed = passed_along(sums1, "gy", quarter)
    solved, mate, far, cols = call(
        child_first,
        [field, shape(count, LANES), shape(count, LANES), shape(edge, LANES)],
        [],
        [x, a, b, c],
        4_000_000,
        3_000_000,
    )
    halos = halos_of(mate, far, cols)
    inner, row_rates, column_rates = call(
        child_inner,
        [field, factor, factor],
        [],
        [solved, rates, land, cols],
        INNER,
        4_000_000,
    )
    fed, mixed = call(
        parent_fed,
        [tiles, shape(half, LANES)],
        [],
        [parent_adjoint.reshape(-1, narrow), parent_mixing.reshape(-1, narrow), feed, inner],
        LONG,
        1_000_000,
    )
    raw_sums, x = call(
        child_columns,
        [shape(half * vectors, 4 * LANES), field],
        edge_scratch,
        [inner, column_rates, relax, mixed, *halos[2:]],
        INNER,
        3_000_000,
    )
    pa, pb, pc = call(
        parent_factors,
        [shape(half, LANES)] * 3,
        [],
        [mixed, halos[1], x, raw_sums],
        LONG,
        1_000_000,
    )
    sums2 = call(
        child_rows,
        sums,
        [sum_scratch],
        [raw_sums, row_rates, relax, pa, *halos[:2]],
        INNER,
        1_000_000,
    )
    feed = passed_along(sums2, "gy", quarter)
    rows = count + half // 2 * vectors
    solved, psolved, mate, far, cols = call(
        child_second,
        [field, tiles, shape(rows, LANES), shape(rows, LANES), shape(edge + 8, LANES)],
        [],
        [x, row_rates, *halos[:2], a, b, c, fed, pa, pb, pc],
        8_000_000,
        3_000_000,
    )
    halos = halos_of(mate, far, cols)
    inner, row_rates, column_rates = call(
        child_inner,
        [field, factor, factor],
        [],
        [solved, rates, land, cols],
        INNER,
        4_000_000,
    )
    packed_rates = call(
        parent_rates_packed,
        shape(4, half, LANES),
        [],
        [parent_rates.reshape(-1, narrow), feed, inner],
        1_450_000_000,
        1_000_000,
    )
    prates = call(
        parent_rates_masked,
        shape(5, half, LANES),
        [],
        [packed_rates, parent_land, *halos[1:]],
        LONG,
        1_000_000,
    )
    few = half // 2 * vectors
    psolved, mate, far, cols = call(
        parent_second,
        [tiles, shape(few, LANES), shape(few, LANES), shape(8, LANES)],
        [],
        [psolved, prates, pa, pb, pc, *halos, feed],
        1_000_000,
        500_000,
    )
    last_halos = halos_of(mate, far, cols)
    child_out = call(
        child_last,
        field,
        [pltpu.VMEM(field.shape, F32)] + edge_scratch + [pltpu.SemaphoreType.DMA((depth // LEVELS,))],
        [inner, row_rates, column_rates, *halos],
        4_000_000,
        3_000_000,
        far_out=True,
    )
    edges = call(
        parent_merged,
        shape(8, LANES),
        [],
        [*last_halos[2:], child_out],
        LONG,
        100_000,
        far_in=(2,),
    )
    parent_out = call(
        parent_last,
        shape(depth * vectors * 2, narrow),
        [],
        [psolved, prates, edges, *last_halos[:2]],
        500_000,
        500_000,
    )
    return (child_out, parent_out.reshape(parent_adjoint.shape))


def solution(mesh):
    wide = P(None, None, "gy", "gx")
    level = P(None, "gy", "gx")
    flat = P("gy", "gx")
    in_specs = (wide, wide, wide, level, flat, wide, level, flat, flat)
    return jax.shard_map(local, mesh=mesh, in_specs=in_specs, out_specs=(wide, wide), check_vma=False)
```

```python
import jax
import jax.numpy as jnp
from jax import lax
from jax.experimental import pallas as pl
from jax.experimental.pallas import tpu as pltpu
from jax.sharding import PartitionSpec as P

F32 = jnp.float32
VMEM = pl.BlockSpec(memory_space=pltpu.VMEM)
FAR = pl.BlockSpec(memory_space=pltpu.HBM)
LIMIT = 40 * 1024 * 1024
LANES = 128
LONG = 1_000_000_000
INNER = 10_000_000
LEVELS = 8


def shape(*dims):
    return jax.ShapeDtypeStruct(dims, F32)


def call(body, outs, scratch, operands, flops, touched, far_in=(), far_out=False):
    operands = [pltpu.with_memory_space_constraint(x, pltpu.HBM) if i in far_in else x for i, x in enumerate(operands)]
    return pl.pallas_call(
        body,
        out_shape=outs,
        in_specs=[FAR if i in far_in else VMEM for i in range(len(operands))],
        out_specs=jax.tree.map(lambda _: FAR if far_out else VMEM, outs),
        scratch_shapes=scratch,
        compiler_params=pltpu.CompilerParams(vmem_limit_bytes=LIMIT),
        cost_estimate=pl.CostEstimate(flops=flops, bytes_accessed=touched, transcendentals=0),
        name=body.__name__,
    )(*operands)


def lane_index(rows=8):
    return lax.broadcasted_iota(jnp.int32, (rows, LANES), 1)


def row_index():
    return lax.broadcasted_iota(jnp.int32, (8, LANES), 0)


def minors(inner, outer):
    theta = delta = jnp.ones_like(inner[0])
    inverse = []
    for i in range(len(inner)):
        delta = theta + outer[i] * delta
        theta_next = delta + inner[i] * theta
        inverse.append(theta / theta_next)
        theta = theta_next
    return inverse


def parity(axis):
    return lax.rem(lax.axis_index(axis), 2)


def child_factors(mix_ref, keep, a_ref, b_ref, c_ref):
    depth = mix_ref.shape[0]
    half = depth // 2
    zero = jnp.zeros_like(keep)
    top_inner = [mix_ref[i] for i in range(half)]
    top_outer = [zero] + top_inner[:-1]
    low_outer = [mix_ref[depth - 1 - i] for i in range(half)]
    low_inner = [mix_ref[depth - 2 - i] for i in range(half)]
    for levels, inner, outer in (
        (range(half), top_inner, top_outer),
        (range(depth - 1, half - 1, -1), low_inner, low_outer),
    ):
        inverse = minors(inner, outer)
        for i, k in enumerate(levels):
            a_ref[k] = inverse[i] * keep
            b_ref[k] = inverse[i] * outer[i]
            c_ref[k] = inverse[i] * inner[i]


def block_rows(source_ref, k, weights, sums_ref, i, place):
    vectors = source_ref.shape[1]
    for r in range(2):
        total = source_ref[k, :, 4 * r, :] * weights[4 * r]
        for j in range(4 * r + 1, 4 * r + 4):
            total = total + source_ref[k, :, j, :] * weights[j]
        column = (2 * place + r) * LANES
        sums_ref[pl.ds(i * vectors, vectors), column : column + LANES] = total


def block_columns(sums_ref):
    wide = sums_ref.shape[1]
    p = lax.broadcasted_iota(jnp.int32, (wide, LANES), 0)
    q = lax.broadcasted_iota(jnp.int32, (wide, LANES), 1)
    pick = jnp.where(p // 4 == q, F32(0.0625), F32(0.0)).astype(jnp.bfloat16)
    rest, total = sums_ref[...], None
    for _ in range(3):
        part = rest.astype(jnp.bfloat16)
        rest = rest - part.astype(F32)
        product = jnp.dot(part, pick, preferred_element_type=F32)
        total = product if total is None else total + product
    return total


def child_middle(carry, c_ref, half):
    vectors = len(carry) // 2
    top, low = c_ref[half - 1], c_ref[half]
    scale = 1.0 / (1.0 - top * low)
    first = [(carry[v] + top * carry[vectors + v]) * scale for v in range(vectors)]
    second = [(carry[vectors + v] + low * carry[v]) * scale for v in range(vectors)]
    return first + second


def child_up(carry, c_ref, solved_ref, mate_rows, far_rows, cols_ref):
    depth, vectors = solved_ref.shape[0], solved_ref.shape[1]
    half = depth // 2
    lane = lane_index()
    pair = lane >> 1
    swap = jnp.broadcast_to(parity("gy"), (8, LANES)) == 1

    def emit(i, values, packed):
        k_low = depth - 1 - i
        packed = list(packed)
        inside = i % LEVELS if isinstance(i, int) else lax.rem(i, LEVELS)
        for side, k, base in ((0, i, inside * vectors), (1, k_low, (LEVELS - 1 - inside) * vectors)):
            for v in range(vectors):
                x = values[side * vectors + v]
                solved_ref[k, v] = x
                at = base + v
                packed[side] = jnp.where(pair == at, pltpu.roll(x, 2 * at + 1 & (LANES - 1), 1), packed[side])
            lo, hi = solved_ref[k, :, 0, :], solved_ref[k, :, 7, :]
            mate_rows[pl.ds(k * vectors, vectors), :] = jnp.where(swap, lo, hi)
            far_rows[pl.ds(k * vectors, vectors), :] = jnp.where(swap, hi, lo)
        return packed

    def up(i, state):
        k_low = depth - 1 - i
        top, low = c_ref[i], c_ref[k_low]
        values = []
        for v in range(vectors):
            values.append(solved_ref[i, v] + top * state[v])
        for v in range(vectors):
            values.append(solved_ref[k_low, v] + low * state[vectors + v])
        return tuple(values) + tuple(emit(i, values, state[2 * vectors :]))

    def keep_columns(group, packed):
        for side, g in ((0, group), (1, depth // LEVELS - 1 - group)):
            cols_ref[LEVELS * g : LEVELS * g + 8, :] = packed[side]

    blank = jnp.zeros((8, LANES), F32)
    values = child_middle(carry, c_ref, half)
    state = tuple(values) + tuple(emit(half - 1, values, [blank] * 2))
    for group in range(half // LEVELS - 1, -1, -1):
        last = LEVELS * (group + 1) - 1
        if group == half // LEVELS - 1:
            last -= 1
        count = last - LEVELS * group + 1
        state = lax.fori_loop(0, count, lambda step, state, last=last: up(last - step, state), state, unroll=count)
        keep_columns(group, state[2 * vectors :])
        state = state[: 2 * vectors] + (blank,) * 2


def begin(
    x_hbm, mix_hbm, relax_hbm, land_hbm, parent_land_hbm, rates_hbm,
    sums_out, x_ref, a_ref, b_ref, c_ref, relax_ref, land_ref, parent_land_ref, rates_ref,
    mix_ref, land_in, parent_land_in, sums_ref, sems,
):
    depth = x_ref.shape[0]
    half = depth // 2
    small = []
    for source, target in (
        (mix_hbm, mix_ref), (relax_hbm, relax_ref), (land_hbm, land_in), (parent_land_hbm, parent_land_in),
    ):
        small.append(pltpu.make_async_copy(source, target, sems.at[len(small)]))
        small[-1].start()
    size, large = 4, []
    for start in range(0, half, size):
        for first in (start, depth - size - start):
            part = pl.ds(first, size)
            large.append(pltpu.make_async_copy(x_hbm.at[part], x_ref.at[part], sems.at[len(large) + len(small)]))
            large[-1].start()
    rates_copy = pltpu.make_async_copy(rates_hbm, rates_ref, sems.at[len(large) + len(small)])
    rates_copy.start()
    for copy in small:
        copy.wait()
    land_ref[...] = land_in[...].astype(F32)
    parent_land_ref[...] = parent_land_in[...].astype(F32)
    child_factors(mix_ref, 1.0 - relax_ref[...], a_ref, b_ref, c_ref)
    weights = [relax_ref[j : j + 1, :] for j in range(8)]

    def level(i, _):
        for side, k in ((0, i), (1, depth - 1 - i)):
            block_rows(x_ref, k, weights, sums_ref, i, side)
        return 0

    for part, start in enumerate(range(0, half, size)):
        large[2 * part].wait()
        large[2 * part + 1].wait()
        lax.fori_loop(start, start + size, level, 0, unroll=size)
    sums_out[...] = block_columns(sums_ref)
    rates_copy.wait()


def child_first(x_ref, a_ref, b_ref, c_ref, solved_ref, mate_rows, far_rows, cols_ref):
    child_solve(x_ref, a_ref, b_ref, c_ref, solved_ref, mate_rows, far_rows, cols_ref, lambda k, v, _: x_ref[k, v])


def child_solve(x_ref, a_ref, b_ref, c_ref, solved_ref, mate_rows, far_rows, cols_ref, load, row_ref=None):
    depth, vectors = x_ref.shape[0], x_ref.shape[1]
    half = depth // 2

    def down(i, carry):
        values = []
        for side, k in ((0, i), (1, depth - 1 - i)):
            a, b = a_ref[k], b_ref[k]
            row_rates = None if row_ref is None else row_ref[k]
            for v in range(vectors):
                y = a * load(k, v, row_rates) + b * carry[side * vectors + v]
                solved_ref[k, v] = y
                values.append(y)
        return tuple(values)

    carry = lax.fori_loop(0, half, down, (jnp.zeros((8, LANES), F32),) * (2 * vectors), unroll=4)
    child_up(carry, c_ref, solved_ref, mate_rows, far_rows, cols_ref)


def combine(sides, land):
    east, west, north, south = sides
    return [land * part for part in (1.0 - (east + west + north + south), east, west, north, south)]


def merge_edges(mate, far, turn):
    swap = jnp.broadcast_to(parity("gx"), (8, LANES)) == 1
    east, west = jnp.where(swap, far, mate), jnp.where(swap, mate, far)
    return jnp.where((lane_index() & 1) == 0, west, pltpu.roll(east, turn, 1))


def child_inner(solved_ref, rates_ref, land_ref, after_ref, inner_ref, row_ref, column_ref):
    depth, vectors = solved_ref.shape[0], solved_ref.shape[1]
    lane, row = lane_index(), row_index()
    land = land_ref[...]

    def level(k, _):
        centre, east, west, north, south = combine([rates_ref[d, k] for d in range(4)], land)
        column_ref[k] = jnp.where(lane == 0, west, jnp.where(lane == LANES - 1, east, 0.0))
        row_ref[k] = jnp.where(row == 0, south, jnp.where(row == 7, north, 0.0))
        east, west = jnp.where(lane == LANES - 1, 0.0, east), jnp.where(lane == 0, 0.0, west)
        north, south = jnp.where(row == 7, 0.0, north), jnp.where(row == 0, 0.0, south)
        for v in range(vectors):
            s = solved_ref[k, v]
            across = east * pltpu.roll(s, LANES - 1, 1) + west * pltpu.roll(s, 1, 1)
            along = north * pltpu.roll(s, 7, 0) + south * pltpu.roll(s, 1, 0)
            inner_ref[k, v] = centre * s + across + along
        return 0

    lax.fori_loop(0, depth, level, 0, unroll=8)


def edge_merger(mate_cols, far_cols, merged_ref):
    for g in range(merged_ref.shape[0] // 8):
        part = slice(8 * g, 8 * g + 8)
        merged_ref[part, :] = merge_edges(mate_cols[part, :], far_cols[part, :], LANES - 2)


def column_edged(inner_ref, column_rates, edges, k, v, at):
    return inner_ref[k, v] + column_rates * pltpu.roll(edges, (LANES - 2 * at) & (LANES - 1), 1)


def row_halo(mate_ref, far_ref, k, v, vectors, mates):
    line = pl.ds(k * vectors + v, 1)
    mate = jnp.broadcast_to(mate_ref[line, :], (8, LANES))
    far = jnp.broadcast_to(far_ref[line, :], (8, LANES))
    return jnp.where(mates, mate, far)


def mate_rows_mask():
    return row_index() == 7 * (1 - parity("gy"))


def child_columns(inner_ref, column_ref, relax_ref, after_ref, mate_cols, far_cols, sums_ref, x_ref, merged_ref):
    depth, vectors = inner_ref.shape[0], inner_ref.shape[1]
    half, groups = depth // 2, depth // LEVELS
    weights = [relax_ref[j : j + 1, :] for j in range(8)]
    edge_merger(mate_cols, far_cols, merged_ref)

    def level(i, _, edges):
        inside = lax.rem(i, LEVELS)
        for side, k, base in ((0, i, inside * vectors), (1, depth - 1 - i, (LEVELS - 1 - inside) * vectors)):
            column_rates = column_ref[k]
            for v in range(vectors):
                x_ref[k, v] = column_edged(inner_ref, column_rates, edges[side], k, v, base + v)
            block_rows(x_ref, k, weights, sums_ref, i, side)
        return 0

    for group in range(half // LEVELS):
        edges = [merged_ref[8 * g : 8 * g + 8, :] for g in (group, groups - 1 - group)]
        lax.fori_loop(
            LEVELS * group, LEVELS * (group + 1), lambda i, _, edges=edges: level(i, _, edges), 0, unroll=4
        )


def child_rows(sums_in, row_ref, relax_ref, after_ref, mate_in, far_in, sums_out, sums_ref):
    depth = row_ref.shape[0]
    vectors = 2 * sums_in.shape[0] // depth
    swap = jnp.broadcast_to(parity("gy"), (vectors, LANES)) == 1
    for k in range(depth):
        place, i = (0, k) if k < depth // 2 else (1, depth - 1 - k)
        lines = slice(k * vectors, (k + 1) * vectors)
        mate, far = mate_in[lines, :], far_in[lines, :]
        for r, at, halo in ((0, 0, jnp.where(swap, mate, far)), (1, 7, jnp.where(swap, far, mate))):
            share = (row_ref[k, at : at + 1, :] * relax_ref[at : at + 1, :]) * halo
            part = slice(i * vectors, (i + 1) * vectors), slice((2 * place + r) * LANES, (2 * place + r + 1) * LANES)
            sums_ref[part] = sums_in[part] + share
    sums_out[...] = block_columns(sums_ref)


def child_second(
    x_ref, row_ref, mate_in, far_in, a_ref, b_ref, c_ref, parent_ref, pa_ref, pb_ref, pc_ref,
    solved_ref, psolved_ref, mate_rows, far_rows, cols_ref,
):
    depth, vectors = x_ref.shape[0], x_ref.shape[1]
    y = jnp.zeros((8, LANES), F32)
    for i in range(depth // 2):
        y = pa_ref[i : i + 1, :] * parent_ref[i] + pb_ref[i : i + 1, :] * y
        psolved_ref[i] = y
    lines, at = depth * vectors, depth // LEVELS * 8
    parent_up(y, pc_ref, psolved_ref, mate_rows, far_rows, lines, cols_ref, at)
    mates = mate_rows_mask()

    def load(k, v, row_rates):
        return x_ref[k, v] + row_rates * row_halo(mate_in, far_in, k, v, vectors, mates)

    child_solve(x_ref, a_ref, b_ref, c_ref, solved_ref, mate_rows, far_rows, cols_ref, load, row_ref)


def child_last(
    inner_ref, row_ref, column_ref, mate_in, far_in, mate_cols, far_cols, out_hbm, out_ref, merged_ref, sems
):
    depth, vectors = inner_ref.shape[0], inner_ref.shape[1]
    mates = mate_rows_mask()
    edge_merger(mate_cols, far_cols, merged_ref)
    copies = []
    for group in range(depth // LEVELS):
        edges = merged_ref[8 * group : 8 * group + 8, :]

        def level(inside, _):
            k = LEVELS * group + inside
            row_rates, column_rates = row_ref[k], column_ref[k]
            for v in range(vectors):
                out_ref[k, v] = column_edged(
                    inner_ref, column_rates, edges, k, v, inside * vectors + v
                ) + row_rates * row_halo(mate_in, far_in, k, v, vectors, mates)
            return 0

        lax.fori_loop(0, LEVELS, level, 0, unroll=LEVELS)
        part = pl.ds(LEVELS * group, LEVELS)
        copies.append(pltpu.make_async_copy(out_ref.at[part], out_hbm.at[part], sems.at[group]))
        copies[-1].start()
    for copy in copies:
        copy.wait()


PLACES = [(h, r, 64 * h + 32 * r) for h in range(2) for r in range(2)]


def parent_fed(parent_ref, mix_ref, feed_ref, after_ref, packed_ref, mixed):
    half, vectors = packed_ref.shape[0], packed_ref.shape[1]
    for i in range(half):
        for h, r, lo in PLACES:
            k = 2 * half - 1 - i if h else i
            packed_ref[i, :, lo : lo + 32] = parent_ref[pl.ds(2 * vectors * k + r, vectors, stride=2), :]
            mixed[i : i + 1, lo : lo + 32] = mix_ref[2 * k + r : 2 * k + r + 1, :]
        packed_ref[i] = packed_ref[i] + feed_ref[vectors * i : vectors * (i + 1), :]


def parent_factors(mixed, far_ref, x_ref, sums_ref, pa_ref, pb_ref, pc_ref):
    half = pa_ref.shape[0]
    upper = lane_index(1) < 64
    rows = [mixed[i : i + 1, :] for i in range(half)]
    inner, outer = [], []
    for i in range(half):
        nearer = rows[i + 1] if i + 1 < half else pltpu.roll(rows[i], 64, 1)
        inner.append(jnp.where(upper, rows[i], nearer))
        outer.append(jnp.where(upper, rows[i - 1] if i else jnp.zeros_like(rows[0]), rows[i]))
    inverse = minors(inner, outer)
    for i in range(half):
        pa_ref[i : i + 1, :] = inverse[i]
        pb_ref[i : i + 1, :] = inverse[i] * outer[i]
        pc_ref[i : i + 1, :] = inverse[i] * inner[i]


def parent_rates_packed(rates_ref, feed_ref, after_ref, packed_ref):
    half = packed_ref.shape[1]
    depth = 2 * half
    for i in range(half):
        for h, r, lo in PLACES:
            k = depth - 1 - i if h else i
            for d in range(4):
                at = 2 * (d * depth + k) + r
                packed_ref[d, i : i + 1, lo : lo + 32] = rates_ref[at : at + 1, :]


def parent_rates_masked(packed_ref, land_ref, far_ref, mate_cols, far_cols, prates_ref):
    half = packed_ref.shape[1]
    land = jnp.concatenate([land_ref[r : r + 1, :] for _, r, _ in PLACES], axis=1)
    land = jnp.broadcast_to(land, (half, LANES))
    for d, part in enumerate(combine([packed_ref[d] for d in range(4)], land)):
        prates_ref[d] = part


def parent_up(carry, pc_ref, psolved_ref, mate_rows, far_rows, lines, cols_ref, cols_at):
    half = psolved_ref.shape[0]
    lane = lane_index()
    middle = pc_ref[half - 1 : half, :]
    scale = 1.0 / (1.0 - middle * pltpu.roll(middle, 64, 1))
    x = (carry + middle * pltpu.roll(carry, 64, 1)) * scale
    tiles = [None] * half
    tiles[half - 1] = x
    for i in range(half - 2, -1, -1):
        x = psolved_ref[i] + pc_ref[i : i + 1, :] * x
        tiles[i] = x
    packed = jnp.zeros((8, LANES), F32)
    for i in range(half):
        psolved_ref[i] = tiles[i]
        packed = jnp.where(((lane & 31) >> 1) == i, pltpu.roll(tiles[i], 2 * i + 1, 1), packed)
    cols_ref[cols_at : cols_at + 8, :] = packed
    first = (lane & 32) == 0
    swap = jnp.broadcast_to(parity("gy"), (8, LANES)) == 1
    for j in range(half // 2):
        one, two = tiles[j], tiles[j + half // 2]
        lo = jnp.where(first, one, pltpu.roll(two, 32, 1))
        hi = jnp.where(first, pltpu.roll(one, 96, 1), two)
        part = slice(lines + 8 * j, lines + 8 * j + 8)
        mate_rows[part, :] = jnp.where(swap, lo, hi)
        far_rows[part, :] = jnp.where(swap, hi, lo)


def parent_edges(mate_cols, far_cols, at):
    return merge_edges(mate_cols[at : at + 8, :], far_cols[at : at + 8, :], 62)


def parent_transport(psolved_ref, prates_ref, mate_row, far_row, edges, i):
    half = psolved_ref.shape[0]
    lane = lane_index()
    swap = jnp.broadcast_to(parity("gy"), (8, LANES)) == 1
    x = psolved_ref[i]
    mate, far = mate_row(i % (half // 2)), far_row(i % (half // 2))
    lo, hi = jnp.where(swap, far, mate), jnp.where(swap, mate, far)
    if i < half // 2:
        lo = pltpu.roll(lo, 32, 1)
    else:
        hi = pltpu.roll(hi, 96, 1)
    first = (lane & 32) == 0
    to_north = jnp.where(first, pltpu.roll(x, 96, 1), lo)
    to_south = jnp.where(first, hi, pltpu.roll(x, 32, 1))
    edge = pltpu.roll(edges, (LANES - 2 * i - 32) & (LANES - 1), 1)
    column = lane & 31
    to_east = jnp.where(column == 31, edge, pltpu.roll(x, 127, 1))
    to_west = jnp.where(column == 0, edge, pltpu.roll(x, 1, 1))
    parts = [prates_ref[d, i : i + 1, :] for d in range(5)]
    return (parts[0] * x + parts[1] * to_east) + (parts[2] * to_west + parts[3] * to_north) + parts[4] * to_south


def parent_second(
    psolved_in, prates_ref, pa_ref, pb_ref, pc_ref, mate_in, far_in, mate_cols, far_cols, feed_ref,
    psolved_ref, mate_rows, far_rows, cols_ref,
):
    half = psolved_in.shape[0]
    lines = mate_in.shape[0] - mate_rows.shape[0]
    edges = parent_edges(mate_cols, far_cols, mate_cols.shape[0] - 8)
    mate = lambda j: mate_in[lines + 8 * j : lines + 8 * j + 8, :]
    far = lambda j: far_in[lines + 8 * j : lines + 8 * j + 8, :]
    y = jnp.zeros((8, LANES), F32)
    for i in range(half):
        rhs = parent_transport(psolved_in, prates_ref, mate, far, edges, i)
        rhs = rhs + feed_ref[8 * i : 8 * i + 8, :]
        y = pa_ref[i : i + 1, :] * rhs + pb_ref[i : i + 1, :] * y
        psolved_ref[i] = y
    parent_up(y, pc_ref, psolved_ref, mate_rows, far_rows, 0, cols_ref, 0)


def parent_last(psolved_in, prates_ref, mate_in, far_in, mate_cols, far_cols, out_ref):
    half, vectors = psolved_in.shape[0], psolved_in.shape[1]
    edges = parent_edges(mate_cols, far_cols, 0)
    mate = lambda j: mate_in[8 * j : 8 * j + 8, :]
    far = lambda j: far_in[8 * j : 8 * j + 8, :]
    for i in range(half):
        x = parent_transport(psolved_in, prates_ref, mate, far, edges, i)
        for h in range(2):
            for r in range(2):
                lo = 64 * h + 32 * r
                k = 2 * half - 1 - i if h else i
                out_ref[pl.ds(2 * vectors * k + r, vectors, stride=2), :] = x[:, lo : lo + 32]


def passed_along(value, axis, steps):
    count = lax.axis_size(axis)
    return lax.ppermute(value, axis, [(i, (i + steps) % count) for i in range(count)])


def swapped(value, axis, offset):
    count = lax.axis_size(axis)
    pairs = []
    for i in range(offset, count, 2):
        j = (i + 1) % count
        pairs += [(i, j), (j, i)]
    return lax.ppermute(value, axis, pairs)


def halos_of(mate, far, cols):
    return [swapped(mate, "gy", 0), swapped(far, "gy", 1), swapped(cols, "gx", 0), swapped(cols, "gx", 1)]


def local(
    child_adjoint,
    parent_adjoint,
    child_rates,
    child_mixing,
    child_land,
    parent_rates,
    parent_mixing,
    parent_land,
    relaxation,
):
    depth, vectors, lines, columns = child_adjoint.shape
    half = depth // 2
    quarter = lax.axis_size("gy") // 4
    field = shape(depth, vectors, lines, columns)
    factor = shape(depth, lines, columns)
    tiles = shape(half, vectors, LANES)
    sums = shape(half * vectors, LANES)
    count = depth * vectors
    edge = depth // LEVELS * 8
    sum_scratch = pltpu.VMEM((half * vectors, 4 * LANES), F32)
    edge_scratch = [pltpu.VMEM((edge, LANES), F32)]
    narrow = parent_adjoint.shape[-1]

    sums1, x, a, b, c, relax, land, parent_land, rates = call(
        begin,
        [sums, field, factor, factor, factor, shape(lines, columns), shape(lines, columns), shape(*parent_land.shape)]
        + [shape(*child_rates.shape)],
        [
            pltpu.VMEM(factor.shape, F32),
            pltpu.VMEM(child_land.shape, jnp.int32),
            pltpu.VMEM(parent_land.shape, jnp.int32),
            sum_scratch,
            pltpu.SemaphoreType.DMA((5 + half // 2,)),
        ],
        [child_adjoint, child_mixing, relaxation, child_land, parent_land, child_rates],
        4_000_000,
        3_000_000,
        far_in=range(6),
    )
    feed = passed_along(sums1, "gy", quarter)
    solved, mate, far, cols = call(
        child_first,
        [field, shape(count, LANES), shape(count, LANES), shape(edge, LANES)],
        [],
        [x, a, b, c],
        4_000_000,
        3_000_000,
    )
    halos = halos_of(mate, far, cols)
    inner, row_rates, column_rates = call(
        child_inner,
        [field, factor, factor],
        [],
        [solved, rates, land, cols],
        INNER,
        4_000_000,
    )
    fed, mixed = call(
        parent_fed,
        [tiles, shape(half, LANES)],
        [],
        [parent_adjoint.reshape(-1, narrow), parent_mixing.reshape(-1, narrow), feed, inner],
        LONG,
        1_000_000,
    )
    raw_sums, x = call(
        child_columns,
        [shape(half * vectors, 4 * LANES), field],
        edge_scratch,
        [inner, column_rates, relax, mixed, *halos[2:]],
        INNER,
        3_000_000,
    )
    pa, pb, pc = call(
        parent_factors,
        [shape(half, LANES)] * 3,
        [],
        [mixed, halos[1], x, raw_sums],
        LONG,
        1_000_000,
    )
    sums2 = call(
        child_rows,
        sums,
        [sum_scratch],
        [raw_sums, row_rates, relax, pa, *halos[:2]],
        INNER,
        1_000_000,
    )
    feed = passed_along(sums2, "gy", quarter)
    rows = count + half // 2 * vectors
    solved, psolved, mate, far, cols = call(
        child_second,
        [field, tiles, shape(rows, LANES), shape(rows, LANES), shape(edge + 8, LANES)],
        [],
        [x, row_rates, *halos[:2], a, b, c, fed, pa, pb, pc],
        8_000_000,
        3_000_000,
    )
    halos = halos_of(mate, far, cols)
    inner, row_rates, column_rates = call(
        child_inner,
        [field, factor, factor],
        [],
        [solved, rates, land, cols],
        INNER,
        4_000_000,
    )
    packed_rates = call(
        parent_rates_packed,
        shape(4, half, LANES),
        [],
        [parent_rates.reshape(-1, narrow), feed, inner],
        1_450_000_000,
        1_000_000,
    )
    prates = call(
        parent_rates_masked,
        shape(5, half, LANES),
        [],
        [packed_rates, parent_land, *halos[1:]],
        LONG,
        1_000_000,
    )
    few = half // 2 * vectors
    psolved, mate, far, cols = call(
        parent_second,
        [tiles, shape(few, LANES), shape(few, LANES), shape(8, LANES)],
        [],
        [psolved, prates, pa, pb, pc, *halos, feed],
        1_000_000,
        500_000,
    )
    last_halos = halos_of(mate, far, cols)
    child_out = call(
        child_last,
        field,
        [pltpu.VMEM(field.shape, F32)] + edge_scratch + [pltpu.SemaphoreType.DMA((depth // LEVELS,))],
        [inner, row_rates, column_rates, *halos],
        4_000_000,
        3_000_000,
        far_out=True,
    )
    parent_out = call(
        parent_last,
        shape(depth * vectors * 2, narrow),
        [],
        [psolved, prates, *last_halos],
        500_000,
        500_000,
    )
    return (child_out, parent_out.reshape(parent_adjoint.shape))


def solution(mesh):
    wide = P(None, None, "gy", "gx")
    level = P(None, "gy", "gx")
    flat = P("gy", "gx")
    in_specs = (wide, wide, wide, level, flat, wide, level, flat, flat)
    return jax.shard_map(local, mesh=mesh, in_specs=in_specs, out_specs=(wide, wide), check_vma=False)
```

```python
import jax
import jax.numpy as jnp
from jax import lax
from jax.experimental import pallas as pl
from jax.experimental.pallas import tpu as pltpu
from jax.sharding import PartitionSpec as P

F32 = jnp.float32
VMEM = pl.BlockSpec(memory_space=pltpu.VMEM)
FAR = pl.BlockSpec(memory_space=pltpu.HBM)
LIMIT = 40 * 1024 * 1024
LANES = 128
LONG = 1_000_000_000
INNER = 10_000_000
LEVELS = 8


def shape(*dims):
    return jax.ShapeDtypeStruct(dims, F32)


def call(body, outs, scratch, operands, flops, touched, far_in=(), far_out=False):
    operands = [pltpu.with_memory_space_constraint(x, pltpu.HBM) if i in far_in else x for i, x in enumerate(operands)]
    return pl.pallas_call(
        body,
        out_shape=outs,
        in_specs=[FAR if i in far_in else VMEM for i in range(len(operands))],
        out_specs=jax.tree.map(lambda _: FAR if far_out else VMEM, outs),
        scratch_shapes=scratch,
        compiler_params=pltpu.CompilerParams(vmem_limit_bytes=LIMIT),
        cost_estimate=pl.CostEstimate(flops=flops, bytes_accessed=touched, transcendentals=0),
        name=body.__name__,
    )(*operands)


def lane_index(rows=8):
    return lax.broadcasted_iota(jnp.int32, (rows, LANES), 1)


def row_index():
    return lax.broadcasted_iota(jnp.int32, (8, LANES), 0)


def minors(inner, outer):
    theta = delta = jnp.ones_like(inner[0])
    inverse = []
    for i in range(len(inner)):
        delta = theta + outer[i] * delta
        theta_next = delta + inner[i] * theta
        inverse.append(theta / theta_next)
        theta = theta_next
    return inverse


def parity(axis):
    return lax.rem(lax.axis_index(axis), 2)


def child_factors(mix_ref, keep, a_ref, b_ref, c_ref):
    depth = mix_ref.shape[0]
    half = depth // 2
    zero = jnp.zeros_like(keep)
    top_inner = [mix_ref[i] for i in range(half)]
    top_outer = [zero] + top_inner[:-1]
    low_outer = [mix_ref[depth - 1 - i] for i in range(half)]
    low_inner = [mix_ref[depth - 2 - i] for i in range(half)]
    for levels, inner, outer in (
        (range(half), top_inner, top_outer),
        (range(depth - 1, half - 1, -1), low_inner, low_outer),
    ):
        inverse = minors(inner, outer)
        for i, k in enumerate(levels):
            a_ref[k] = inverse[i] * keep
            b_ref[k] = inverse[i] * outer[i]
            c_ref[k] = inverse[i] * inner[i]


def block_rows(source_ref, k, weights, sums_ref, i, place):
    vectors = source_ref.shape[1]
    for r in range(2):
        total = source_ref[k, :, 4 * r, :] * weights[4 * r]
        for j in range(4 * r + 1, 4 * r + 4):
            total = total + source_ref[k, :, j, :] * weights[j]
        column = (2 * place + r) * LANES
        sums_ref[pl.ds(i * vectors, vectors), column : column + LANES] = total


def block_columns(sums_ref):
    wide = sums_ref.shape[1]
    p = lax.broadcasted_iota(jnp.int32, (wide, LANES), 0)
    q = lax.broadcasted_iota(jnp.int32, (wide, LANES), 1)
    pick = jnp.where(p // 4 == q, F32(0.0625), F32(0.0)).astype(jnp.bfloat16)
    rest, total = sums_ref[...], None
    for _ in range(3):
        part = rest.astype(jnp.bfloat16)
        rest = rest - part.astype(F32)
        product = jnp.dot(part, pick, preferred_element_type=F32)
        total = product if total is None else total + product
    return total


def child_middle(carry, c_ref, half):
    vectors = len(carry) // 2
    top, low = c_ref[half - 1], c_ref[half]
    scale = 1.0 / (1.0 - top * low)
    first = [(carry[v] + top * carry[vectors + v]) * scale for v in range(vectors)]
    second = [(carry[vectors + v] + low * carry[v]) * scale for v in range(vectors)]
    return first + second


def child_up(carry, c_ref, solved_ref, mate_rows, far_rows, cols_ref):
    depth, vectors = solved_ref.shape[0], solved_ref.shape[1]
    half = depth // 2
    lane = lane_index()
    pair = lane >> 1
    swap = jnp.broadcast_to(parity("gy"), (8, LANES)) == 1

    def emit(i, values, packed):
        k_low = depth - 1 - i
        packed = list(packed)
        inside = i % LEVELS if isinstance(i, int) else lax.rem(i, LEVELS)
        for side, k, base in ((0, i, inside * vectors), (1, k_low, (LEVELS - 1 - inside) * vectors)):
            for v in range(vectors):
                x = values[side * vectors + v]
                solved_ref[k, v] = x
                at = base + v
                packed[side] = jnp.where(pair == at, pltpu.roll(x, 2 * at + 1 & (LANES - 1), 1), packed[side])
            lo, hi = solved_ref[k, :, 0, :], solved_ref[k, :, 7, :]
            mate_rows[pl.ds(k * vectors, vectors), :] = jnp.where(swap, lo, hi)
            far_rows[pl.ds(k * vectors, vectors), :] = jnp.where(swap, hi, lo)
        return packed

    def up(i, state):
        k_low = depth - 1 - i
        top, low = c_ref[i], c_ref[k_low]
        values = []
        for v in range(vectors):
            values.append(solved_ref[i, v] + top * state[v])
        for v in range(vectors):
            values.append(solved_ref[k_low, v] + low * state[vectors + v])
        return tuple(values) + tuple(emit(i, values, state[2 * vectors :]))

    def keep_columns(group, packed):
        for side, g in ((0, group), (1, depth // LEVELS - 1 - group)):
            cols_ref[LEVELS * g : LEVELS * g + 8, :] = packed[side]

    blank = jnp.zeros((8, LANES), F32)
    values = child_middle(carry, c_ref, half)
    state = tuple(values) + tuple(emit(half - 1, values, [blank] * 2))
    for group in range(half // LEVELS - 1, -1, -1):
        last = LEVELS * (group + 1) - 1
        if group == half // LEVELS - 1:
            last -= 1
        count = last - LEVELS * group + 1
        state = lax.fori_loop(0, count, lambda step, state, last=last: up(last - step, state), state, unroll=count)
        keep_columns(group, state[2 * vectors :])
        state = state[: 2 * vectors] + (blank,) * 2


def begin(
    x_hbm, mix_hbm, relax_hbm, land_hbm, parent_land_hbm, rates_hbm,
    sums_out, x_ref, a_ref, b_ref, c_ref, relax_ref, land_ref, parent_land_ref, rates_ref,
    mix_ref, land_in, parent_land_in, sums_ref, sems,
):
    depth = x_ref.shape[0]
    half = depth // 2
    small = []
    for source, target in (
        (mix_hbm, mix_ref), (relax_hbm, relax_ref), (land_hbm, land_in), (parent_land_hbm, parent_land_in),
    ):
        small.append(pltpu.make_async_copy(source, target, sems.at[len(small)]))
        small[-1].start()
    size, large = 4, []
    for start in range(0, half, size):
        for first in (start, depth - size - start):
            part = pl.ds(first, size)
            large.append(pltpu.make_async_copy(x_hbm.at[part], x_ref.at[part], sems.at[len(large) + len(small)]))
            large[-1].start()
    rates_copy = pltpu.make_async_copy(rates_hbm, rates_ref, sems.at[len(large) + len(small)])
    rates_copy.start()
    for copy in small:
        copy.wait()
    land_ref[...] = land_in[...].astype(F32)
    parent_land_ref[...] = parent_land_in[...].astype(F32)
    child_factors(mix_ref, 1.0 - relax_ref[...], a_ref, b_ref, c_ref)
    weights = [relax_ref[j : j + 1, :] for j in range(8)]

    def level(i, _):
        for side, k in ((0, i), (1, depth - 1 - i)):
            block_rows(x_ref, k, weights, sums_ref, i, side)
        return 0

    for part, start in enumerate(range(0, half, size)):
        large[2 * part].wait()
        large[2 * part + 1].wait()
        lax.fori_loop(start, start + size, level, 0, unroll=size)
    sums_out[...] = block_columns(sums_ref)
    rates_copy.wait()


def child_first(x_ref, a_ref, b_ref, c_ref, solved_ref, mate_rows, far_rows, cols_ref):
    child_solve(x_ref, a_ref, b_ref, c_ref, solved_ref, mate_rows, far_rows, cols_ref, lambda k, v, _: x_ref[k, v])


def child_solve(x_ref, a_ref, b_ref, c_ref, solved_ref, mate_rows, far_rows, cols_ref, load, row_ref=None):
    depth, vectors = x_ref.shape[0], x_ref.shape[1]
    half = depth // 2

    def down(i, carry):
        values = []
        for side, k in ((0, i), (1, depth - 1 - i)):
            a, b = a_ref[k], b_ref[k]
            row_rates = None if row_ref is None else row_ref[k]
            for v in range(vectors):
                y = a * load(k, v, row_rates) + b * carry[side * vectors + v]
                solved_ref[k, v] = y
                values.append(y)
        return tuple(values)

    carry = lax.fori_loop(0, half, down, (jnp.zeros((8, LANES), F32),) * (2 * vectors), unroll=8)
    child_up(carry, c_ref, solved_ref, mate_rows, far_rows, cols_ref)


def combine(sides, land):
    east, west, north, south = sides
    return [land * part for part in (1.0 - (east + west + north + south), east, west, north, south)]


def merge_edges(mate, far, turn):
    swap = jnp.broadcast_to(parity("gx"), (8, LANES)) == 1
    east, west = jnp.where(swap, far, mate), jnp.where(swap, mate, far)
    return jnp.where((lane_index() & 1) == 0, west, pltpu.roll(east, turn, 1))


def child_inner(solved_ref, rates_ref, land_ref, after_ref, inner_ref, row_ref, column_ref):
    depth, vectors = solved_ref.shape[0], solved_ref.shape[1]
    lane, row = lane_index(), row_index()
    land = land_ref[...]

    def level(k, _):
        centre, east, west, north, south = combine([rates_ref[d, k] for d in range(4)], land)
        column_ref[k] = jnp.where(lane == 0, west, jnp.where(lane == LANES - 1, east, 0.0))
        row_ref[k] = jnp.where(row == 0, south, jnp.where(row == 7, north, 0.0))
        east, west = jnp.where(lane == LANES - 1, 0.0, east), jnp.where(lane == 0, 0.0, west)
        north, south = jnp.where(row == 7, 0.0, north), jnp.where(row == 0, 0.0, south)
        for v in range(vectors):
            s = solved_ref[k, v]
            across = east * pltpu.roll(s, LANES - 1, 1) + west * pltpu.roll(s, 1, 1)
            along = north * pltpu.roll(s, 7, 0) + south * pltpu.roll(s, 1, 0)
            inner_ref[k, v] = centre * s + across + along
        return 0

    lax.fori_loop(0, depth, level, 0, unroll=16)


def edge_merger(mate_cols, far_cols, merged_ref):
    for g in range(merged_ref.shape[0] // 8):
        part = slice(8 * g, 8 * g + 8)
        merged_ref[part, :] = merge_edges(mate_cols[part, :], far_cols[part, :], LANES - 2)


def column_edged(inner_ref, column_rates, edges, k, v, at):
    return inner_ref[k, v] + column_rates * pltpu.roll(edges, (LANES - 2 * at) & (LANES - 1), 1)


def row_halo(mate_ref, far_ref, k, v, vectors, mates):
    line = pl.ds(k * vectors + v, 1)
    mate = jnp.broadcast_to(mate_ref[line, :], (8, LANES))
    far = jnp.broadcast_to(far_ref[line, :], (8, LANES))
    return jnp.where(mates, mate, far)


def mate_rows_mask():
    return row_index() == 7 * (1 - parity("gy"))


def child_columns(inner_ref, column_ref, relax_ref, after_ref, mate_cols, far_cols, sums_ref, x_ref, merged_ref):
    depth, vectors = inner_ref.shape[0], inner_ref.shape[1]
    half, groups = depth // 2, depth // LEVELS
    weights = [relax_ref[j : j + 1, :] for j in range(8)]
    edge_merger(mate_cols, far_cols, merged_ref)

    def level(i, _, edges):
        inside = lax.rem(i, LEVELS)
        for side, k, base in ((0, i, inside * vectors), (1, depth - 1 - i, (LEVELS - 1 - inside) * vectors)):
            column_rates = column_ref[k]
            for v in range(vectors):
                x_ref[k, v] = column_edged(inner_ref, column_rates, edges[side], k, v, base + v)
        return 0

    def add(i, _):
        for side, k in ((0, i), (1, depth - 1 - i)):
            block_rows(x_ref, k, weights, sums_ref, i, side)
        return 0

    for group in range(half // LEVELS):
        edges = [merged_ref[8 * g : 8 * g + 8, :] for g in (group, groups - 1 - group)]
        lax.fori_loop(
            LEVELS * group, LEVELS * (group + 1), lambda i, _, edges=edges: level(i, _, edges), 0, unroll=LEVELS
        )
        lax.fori_loop(LEVELS * group, LEVELS * (group + 1), add, 0, unroll=LEVELS)


def child_rows(sums_in, row_ref, relax_ref, after_ref, mate_in, far_in, sums_out, sums_ref):
    depth = row_ref.shape[0]
    vectors = 2 * sums_in.shape[0] // depth
    swap = jnp.broadcast_to(parity("gy"), (vectors, LANES)) == 1
    for k in range(depth):
        place, i = (0, k) if k < depth // 2 else (1, depth - 1 - k)
        lines = slice(k * vectors, (k + 1) * vectors)
        mate, far = mate_in[lines, :], far_in[lines, :]
        for r, at, halo in ((0, 0, jnp.where(swap, mate, far)), (1, 7, jnp.where(swap, far, mate))):
            share = (row_ref[k, at : at + 1, :] * relax_ref[at : at + 1, :]) * halo
            part = slice(i * vectors, (i + 1) * vectors), slice((2 * place + r) * LANES, (2 * place + r + 1) * LANES)
            sums_ref[part] = sums_in[part] + share
    sums_out[...] = block_columns(sums_ref)


def child_second(
    x_ref, row_ref, mate_in, far_in, a_ref, b_ref, c_ref, parent_ref, pa_ref, pb_ref, pc_ref,
    solved_ref, psolved_ref, mate_rows, far_rows, cols_ref,
):
    depth, vectors = x_ref.shape[0], x_ref.shape[1]
    y = jnp.zeros((8, LANES), F32)
    for i in range(depth // 2):
        y = pa_ref[i : i + 1, :] * parent_ref[i] + pb_ref[i : i + 1, :] * y
        psolved_ref[i] = y
    lines, at = depth * vectors, depth // LEVELS * 8
    parent_up(y, pc_ref, psolved_ref, mate_rows, far_rows, lines, cols_ref, at)
    mates = mate_rows_mask()

    def load(k, v, row_rates):
        return x_ref[k, v] + row_rates * row_halo(mate_in, far_in, k, v, vectors, mates)

    child_solve(x_ref, a_ref, b_ref, c_ref, solved_ref, mate_rows, far_rows, cols_ref, load, row_ref)


def child_last(
    inner_ref, row_ref, column_ref, mate_in, far_in, mate_cols, far_cols, out_hbm, out_ref, merged_ref, sems
):
    depth, vectors = inner_ref.shape[0], inner_ref.shape[1]
    mates = mate_rows_mask()
    edge_merger(mate_cols, far_cols, merged_ref)
    copies = []
    for group in range(depth // LEVELS):
        edges = merged_ref[8 * group : 8 * group + 8, :]

        def level(inside, _):
            k = LEVELS * group + inside
            row_rates, column_rates = row_ref[k], column_ref[k]
            for v in range(vectors):
                out_ref[k, v] = column_edged(
                    inner_ref, column_rates, edges, k, v, inside * vectors + v
                ) + row_rates * row_halo(mate_in, far_in, k, v, vectors, mates)
            return 0

        lax.fori_loop(0, LEVELS, level, 0, unroll=LEVELS)
        part = pl.ds(LEVELS * group, LEVELS)
        copies.append(pltpu.make_async_copy(out_ref.at[part], out_hbm.at[part], sems.at[group]))
        copies[-1].start()
    for copy in copies:
        copy.wait()


PLACES = [(h, r, 64 * h + 32 * r) for h in range(2) for r in range(2)]


def parent_fed(parent_ref, mix_ref, feed_ref, after_ref, packed_ref, mixed):
    half, vectors = packed_ref.shape[0], packed_ref.shape[1]
    for i in range(half):
        for h, r, lo in PLACES:
            k = 2 * half - 1 - i if h else i
            packed_ref[i, :, lo : lo + 32] = parent_ref[pl.ds(2 * vectors * k + r, vectors, stride=2), :]
            mixed[i : i + 1, lo : lo + 32] = mix_ref[2 * k + r : 2 * k + r + 1, :]
        packed_ref[i] = packed_ref[i] + feed_ref[vectors * i : vectors * (i + 1), :]


def parent_factors(mixed, far_ref, x_ref, sums_ref, pa_ref, pb_ref, pc_ref):
    half = pa_ref.shape[0]
    upper = lane_index(1) < 64
    rows = [mixed[i : i + 1, :] for i in range(half)]
    inner, outer = [], []
    for i in range(half):
        nearer = rows[i + 1] if i + 1 < half else pltpu.roll(rows[i], 64, 1)
        inner.append(jnp.where(upper, rows[i], nearer))
        outer.append(jnp.where(upper, rows[i - 1] if i else jnp.zeros_like(rows[0]), rows[i]))
    inverse = minors(inner, outer)
    for i in range(half):
        pa_ref[i : i + 1, :] = inverse[i]
        pb_ref[i : i + 1, :] = inverse[i] * outer[i]
        pc_ref[i : i + 1, :] = inverse[i] * inner[i]


def parent_rates_packed(rates_ref, feed_ref, after_ref, packed_ref):
    half = packed_ref.shape[1]
    depth = 2 * half
    for i in range(half):
        for h, r, lo in PLACES:
            k = depth - 1 - i if h else i
            for d in range(4):
                at = 2 * (d * depth + k) + r
                packed_ref[d, i : i + 1, lo : lo + 32] = rates_ref[at : at + 1, :]


def parent_rates_masked(packed_ref, land_ref, far_ref, mate_cols, far_cols, prates_ref):
    half = packed_ref.shape[1]
    land = jnp.concatenate([land_ref[r : r + 1, :] for _, r, _ in PLACES], axis=1)
    land = jnp.broadcast_to(land, (half, LANES))
    for d, part in enumerate(combine([packed_ref[d] for d in range(4)], land)):
        prates_ref[d] = part


def parent_up(carry, pc_ref, psolved_ref, mate_rows, far_rows, lines, cols_ref, cols_at):
    half = psolved_ref.shape[0]
    lane = lane_index()
    middle = pc_ref[half - 1 : half, :]
    scale = 1.0 / (1.0 - middle * pltpu.roll(middle, 64, 1))
    x = (carry + middle * pltpu.roll(carry, 64, 1)) * scale
    tiles = [None] * half
    tiles[half - 1] = x
    for i in range(half - 2, -1, -1):
        x = psolved_ref[i] + pc_ref[i : i + 1, :] * x
        tiles[i] = x
    packed = jnp.zeros((8, LANES), F32)
    for i in range(half):
        psolved_ref[i] = tiles[i]
        packed = jnp.where(((lane & 31) >> 1) == i, pltpu.roll(tiles[i], 2 * i + 1, 1), packed)
    cols_ref[cols_at : cols_at + 8, :] = packed
    first = (lane & 32) == 0
    swap = jnp.broadcast_to(parity("gy"), (8, LANES)) == 1
    for j in range(half // 2):
        one, two = tiles[j], tiles[j + half // 2]
        lo = jnp.where(first, one, pltpu.roll(two, 32, 1))
        hi = jnp.where(first, pltpu.roll(one, 96, 1), two)
        part = slice(lines + 8 * j, lines + 8 * j + 8)
        mate_rows[part, :] = jnp.where(swap, lo, hi)
        far_rows[part, :] = jnp.where(swap, hi, lo)


def parent_edges(mate_cols, far_cols, at):
    return merge_edges(mate_cols[at : at + 8, :], far_cols[at : at + 8, :], 62)


def parent_transport(psolved_ref, prates_ref, mate_row, far_row, edges, i):
    half = psolved_ref.shape[0]
    lane = lane_index()
    swap = jnp.broadcast_to(parity("gy"), (8, LANES)) == 1
    x = psolved_ref[i]
    mate, far = mate_row(i % (half // 2)), far_row(i % (half // 2))
    lo, hi = jnp.where(swap, far, mate), jnp.where(swap, mate, far)
    if i < half // 2:
        lo = pltpu.roll(lo, 32, 1)
    else:
        hi = pltpu.roll(hi, 96, 1)
    first = (lane & 32) == 0
    to_north = jnp.where(first, pltpu.roll(x, 96, 1), lo)
    to_south = jnp.where(first, hi, pltpu.roll(x, 32, 1))
    edge = pltpu.roll(edges, (LANES - 2 * i - 32) & (LANES - 1), 1)
    column = lane & 31
    to_east = jnp.where(column == 31, edge, pltpu.roll(x, 127, 1))
    to_west = jnp.where(column == 0, edge, pltpu.roll(x, 1, 1))
    parts = [prates_ref[d, i : i + 1, :] for d in range(5)]
    return (parts[0] * x + parts[1] * to_east) + (parts[2] * to_west + parts[3] * to_north) + parts[4] * to_south


def parent_second(
    psolved_in, prates_ref, pa_ref, pb_ref, pc_ref, mate_in, far_in, mate_cols, far_cols, feed_ref,
    psolved_ref, mate_rows, far_rows, cols_ref,
):
    half = psolved_in.shape[0]
    lines = mate_in.shape[0] - mate_rows.shape[0]
    edges = parent_edges(mate_cols, far_cols, mate_cols.shape[0] - 8)
    mate = lambda j: mate_in[lines + 8 * j : lines + 8 * j + 8, :]
    far = lambda j: far_in[lines + 8 * j : lines + 8 * j + 8, :]
    y = jnp.zeros((8, LANES), F32)
    for i in range(half):
        rhs = parent_transport(psolved_in, prates_ref, mate, far, edges, i)
        rhs = rhs + feed_ref[8 * i : 8 * i + 8, :]
        y = pa_ref[i : i + 1, :] * rhs + pb_ref[i : i + 1, :] * y
        psolved_ref[i] = y
    parent_up(y, pc_ref, psolved_ref, mate_rows, far_rows, 0, cols_ref, 0)


def parent_last(psolved_in, prates_ref, mate_in, far_in, mate_cols, far_cols, out_ref):
    half, vectors = psolved_in.shape[0], psolved_in.shape[1]
    edges = parent_edges(mate_cols, far_cols, 0)
    mate = lambda j: mate_in[8 * j : 8 * j + 8, :]
    far = lambda j: far_in[8 * j : 8 * j + 8, :]
    for i in range(half):
        x = parent_transport(psolved_in, prates_ref, mate, far, edges, i)
        for h in range(2):
            for r in range(2):
                lo = 64 * h + 32 * r
                k = 2 * half - 1 - i if h else i
                out_ref[pl.ds(2 * vectors * k + r, vectors, stride=2), :] = x[:, lo : lo + 32]


def passed_along(value, axis, steps):
    count = lax.axis_size(axis)
    return lax.ppermute(value, axis, [(i, (i + steps) % count) for i in range(count)])


def swapped(value, axis, offset):
    count = lax.axis_size(axis)
    pairs = []
    for i in range(offset, count, 2):
        j = (i + 1) % count
        pairs += [(i, j), (j, i)]
    return lax.ppermute(value, axis, pairs)


def halos_of(mate, far, cols):
    return [swapped(mate, "gy", 0), swapped(far, "gy", 1), swapped(cols, "gx", 0), swapped(cols, "gx", 1)]


def local(
    child_adjoint,
    parent_adjoint,
    child_rates,
    child_mixing,
    child_land,
    parent_rates,
    parent_mixing,
    parent_land,
    relaxation,
):
    depth, vectors, lines, columns = child_adjoint.shape
    half = depth // 2
    quarter = lax.axis_size("gy") // 4
    field = shape(depth, vectors, lines, columns)
    factor = shape(depth, lines, columns)
    tiles = shape(half, vectors, LANES)
    sums = shape(half * vectors, LANES)
    count = depth * vectors
    edge = depth // LEVELS * 8
    sum_scratch = pltpu.VMEM((half * vectors, 4 * LANES), F32)
    edge_scratch = [pltpu.VMEM((edge, LANES), F32)]
    narrow = parent_adjoint.shape[-1]

    sums1, x, a, b, c, relax, land, parent_land, rates = call(
        begin,
        [sums, field, factor, factor, factor, shape(lines, columns), shape(lines, columns), shape(*parent_land.shape)]
        + [shape(*child_rates.shape)],
        [
            pltpu.VMEM(factor.shape, F32),
            pltpu.VMEM(child_land.shape, jnp.int32),
            pltpu.VMEM(parent_land.shape, jnp.int32),
            sum_scratch,
            pltpu.SemaphoreType.DMA((5 + half // 2,)),
        ],
        [child_adjoint, child_mixing, relaxation, child_land, parent_land, child_rates],
        4_000_000,
        3_000_000,
        far_in=range(6),
    )
    feed = passed_along(sums1, "gy", quarter)
    solved, mate, far, cols = call(
        child_first,
        [field, shape(count, LANES), shape(count, LANES), shape(edge, LANES)],
        [],
        [x, a, b, c],
        4_000_000,
        3_000_000,
    )
    halos = halos_of(mate, far, cols)
    inner, row_rates, column_rates = call(
        child_inner,
        [field, factor, factor],
        [],
        [solved, rates, land, cols],
        INNER,
        4_000_000,
    )
    fed, mixed = call(
        parent_fed,
        [tiles, shape(half, LANES)],
        [],
        [parent_adjoint.reshape(-1, narrow), parent_mixing.reshape(-1, narrow), feed, inner],
        LONG,
        1_000_000,
    )
    raw_sums, x = call(
        child_columns,
        [shape(half * vectors, 4 * LANES), field],
        edge_scratch,
        [inner, column_rates, relax, mixed, *halos[2:]],
        INNER,
        3_000_000,
    )
    pa, pb, pc = call(
        parent_factors,
        [shape(half, LANES)] * 3,
        [],
        [mixed, halos[1], x, raw_sums],
        LONG,
        1_000_000,
    )
    sums2 = call(
        child_rows,
        sums,
        [sum_scratch],
        [raw_sums, row_rates, relax, pa, *halos[:2]],
        INNER,
        1_000_000,
    )
    feed = passed_along(sums2, "gy", quarter)
    rows = count + half // 2 * vectors
    solved, psolved, mate, far, cols = call(
        child_second,
        [field, tiles, shape(rows, LANES), shape(rows, LANES), shape(edge + 8, LANES)],
        [],
        [x, row_rates, *halos[:2], a, b, c, fed, pa, pb, pc],
        8_000_000,
        3_000_000,
    )
    halos = halos_of(mate, far, cols)
    inner, row_rates, column_rates = call(
        child_inner,
        [field, factor, factor],
        [],
        [solved, rates, land, cols],
        INNER,
        4_000_000,
    )
    packed_rates = call(
        parent_rates_packed,
        shape(4, half, LANES),
        [],
        [parent_rates.reshape(-1, narrow), feed, inner],
        1_450_000_000,
        1_000_000,
    )
    prates = call(
        parent_rates_masked,
        shape(5, half, LANES),
        [],
        [packed_rates, parent_land, *halos[1:]],
        LONG,
        1_000_000,
    )
    few = half // 2 * vectors
    psolved, mate, far, cols = call(
        parent_second,
        [tiles, shape(few, LANES), shape(few, LANES), shape(8, LANES)],
        [],
        [psolved, prates, pa, pb, pc, *halos, feed],
        1_000_000,
        500_000,
    )
    last_halos = halos_of(mate, far, cols)
    child_out = call(
        child_last,
        field,
        [pltpu.VMEM(field.shape, F32)] + edge_scratch + [pltpu.SemaphoreType.DMA((depth // LEVELS,))],
        [inner, row_rates, column_rates, *halos],
        4_000_000,
        3_000_000,
        far_out=True,
    )
    parent_out = call(
        parent_last,
        shape(depth * vectors * 2, narrow),
        [],
        [psolved, prates, *last_halos],
        500_000,
        500_000,
    )
    return (child_out, parent_out.reshape(parent_adjoint.shape))


def solution(mesh):
    wide = P(None, None, "gy", "gx")
    level = P(None, "gy", "gx")
    flat = P("gy", "gx")
    in_specs = (wide, wide, wide, level, flat, wide, level, flat, flat)
    return jax.shard_map(local, mesh=mesh, in_specs=in_specs, out_specs=(wide, wide), check_vma=False)
```

```python
import jax
import jax.numpy as jnp
from jax import lax
from jax.experimental import pallas as pl
from jax.experimental.pallas import tpu as pltpu
from jax.sharding import PartitionSpec as P

F32 = jnp.float32
VMEM = pl.BlockSpec(memory_space=pltpu.VMEM)
FAR = pl.BlockSpec(memory_space=pltpu.HBM)
LIMIT = 40 * 1024 * 1024
LANES = 128
LONG = 1_000_000_000
INNER = 10_000_000
LEVELS = 8


def shape(*dims):
    return jax.ShapeDtypeStruct(dims, F32)


def call(body, outs, scratch, operands, flops, touched, far_in=(), far_out=False):
    operands = [pltpu.with_memory_space_constraint(x, pltpu.HBM) if i in far_in else x for i, x in enumerate(operands)]
    return pl.pallas_call(
        body,
        out_shape=outs,
        in_specs=[FAR if i in far_in else VMEM for i in range(len(operands))],
        out_specs=jax.tree.map(lambda _: FAR if far_out else VMEM, outs),
        scratch_shapes=scratch,
        compiler_params=pltpu.CompilerParams(vmem_limit_bytes=LIMIT),
        cost_estimate=pl.CostEstimate(flops=flops, bytes_accessed=touched, transcendentals=0),
        name=body.__name__,
    )(*operands)


def lane_index(rows=8):
    return lax.broadcasted_iota(jnp.int32, (rows, LANES), 1)


def row_index():
    return lax.broadcasted_iota(jnp.int32, (8, LANES), 0)


def minors(inner, outer):
    theta = delta = jnp.ones_like(inner[0])
    inverse = []
    for i in range(len(inner)):
        delta = theta + outer[i] * delta
        theta_next = delta + inner[i] * theta
        inverse.append(theta / theta_next)
        theta = theta_next
    return inverse


def parity(axis):
    return lax.rem(lax.axis_index(axis), 2)


def child_factors(mix_ref, keep, a_ref, b_ref, c_ref):
    depth = mix_ref.shape[0]
    half = depth // 2
    zero = jnp.zeros_like(keep)
    top_inner = [mix_ref[i] for i in range(half)]
    top_outer = [zero] + top_inner[:-1]
    low_outer = [mix_ref[depth - 1 - i] for i in range(half)]
    low_inner = [mix_ref[depth - 2 - i] for i in range(half)]
    for levels, inner, outer in (
        (range(half), top_inner, top_outer),
        (range(depth - 1, half - 1, -1), low_inner, low_outer),
    ):
        inverse = minors(inner, outer)
        for i, k in enumerate(levels):
            a_ref[k] = inverse[i] * keep
            b_ref[k] = inverse[i] * outer[i]
            c_ref[k] = inverse[i] * inner[i]


def block_rows(source_ref, k, weights, sums_ref, i, place):
    vectors = source_ref.shape[1]
    for r in range(2):
        total = source_ref[k, :, 4 * r, :] * weights[4 * r]
        for j in range(4 * r + 1, 4 * r + 4):
            total = total + source_ref[k, :, j, :] * weights[j]
        column = (2 * place + r) * LANES
        sums_ref[pl.ds(i * vectors, vectors), column : column + LANES] = total


def block_columns(sums_ref):
    wide = sums_ref.shape[1]
    p = lax.broadcasted_iota(jnp.int32, (wide, LANES), 0)
    q = lax.broadcasted_iota(jnp.int32, (wide, LANES), 1)
    pick = jnp.where(p // 4 == q, F32(0.0625), F32(0.0)).astype(jnp.bfloat16)
    rest, total = sums_ref[...], None
    for _ in range(3):
        part = rest.astype(jnp.bfloat16)
        rest = rest - part.astype(F32)
        product = jnp.dot(part, pick, preferred_element_type=F32)
        total = product if total is None else total + product
    return total


def child_middle(carry, c_ref, half):
    vectors = len(carry) // 2
    top, low = c_ref[half - 1], c_ref[half]
    scale = 1.0 / (1.0 - top * low)
    first = [(carry[v] + top * carry[vectors + v]) * scale for v in range(vectors)]
    second = [(carry[vectors + v] + low * carry[v]) * scale for v in range(vectors)]
    return first + second


def child_up(carry, c_ref, solved_ref, mate_rows, far_rows, cols_ref):
    depth, vectors = solved_ref.shape[0], solved_ref.shape[1]
    half = depth // 2
    lane = lane_index()
    pair = lane >> 1
    swap = jnp.broadcast_to(parity("gy"), (8, LANES)) == 1

    def emit(i, values, packed):
        k_low = depth - 1 - i
        packed = list(packed)
        inside = i % LEVELS if isinstance(i, int) else lax.rem(i, LEVELS)
        for side, k, base in ((0, i, inside * vectors), (1, k_low, (LEVELS - 1 - inside) * vectors)):
            for v in range(vectors):
                x = values[side * vectors + v]
                solved_ref[k, v] = x
                at = base + v
                packed[side] = jnp.where(pair == at, pltpu.roll(x, 2 * at + 1 & (LANES - 1), 1), packed[side])
            lo, hi = solved_ref[k, :, 0, :], solved_ref[k, :, 7, :]
            mate_rows[pl.ds(k * vectors, vectors), :] = jnp.where(swap, lo, hi)
            far_rows[pl.ds(k * vectors, vectors), :] = jnp.where(swap, hi, lo)
        return packed

    def up(i, state):
        k_low = depth - 1 - i
        top, low = c_ref[i], c_ref[k_low]
        values = []
        for v in range(vectors):
            values.append(solved_ref[i, v] + top * state[v])
        for v in range(vectors):
            values.append(solved_ref[k_low, v] + low * state[vectors + v])
        return tuple(values) + tuple(emit(i, values, state[2 * vectors :]))

    def keep_columns(group, packed):
        for side, g in ((0, group), (1, depth // LEVELS - 1 - group)):
            cols_ref[LEVELS * g : LEVELS * g + 8, :] = packed[side]

    blank = jnp.zeros((8, LANES), F32)
    values = child_middle(carry, c_ref, half)
    state = tuple(values) + tuple(emit(half - 1, values, [blank] * 2))
    for group in range(half // LEVELS - 1, -1, -1):
        last = LEVELS * (group + 1) - 1
        if group == half // LEVELS - 1:
            last -= 1
        count = last - LEVELS * group + 1
        state = lax.fori_loop(0, count, lambda step, state, last=last: up(last - step, state), state, unroll=count)
        keep_columns(group, state[2 * vectors :])
        state = state[: 2 * vectors] + (blank,) * 2


def begin(
    x_hbm, mix_hbm, relax_hbm, land_hbm, parent_land_hbm, rates_hbm,
    sums_out, x_ref, a_ref, b_ref, c_ref, relax_ref, land_ref, parent_land_ref, rates_ref,
    mix_ref, land_in, parent_land_in, sums_ref, sems,
):
    depth = x_ref.shape[0]
    half = depth // 2
    small = []
    for source, target in (
        (mix_hbm, mix_ref), (relax_hbm, relax_ref), (land_hbm, land_in), (parent_land_hbm, parent_land_in),
    ):
        small.append(pltpu.make_async_copy(source, target, sems.at[len(small)]))
        small[-1].start()
    size, large = 4, []
    for start in range(0, half, size):
        for first in (start, depth - size - start):
            part = pl.ds(first, size)
            large.append(pltpu.make_async_copy(x_hbm.at[part], x_ref.at[part], sems.at[len(large) + len(small)]))
            large[-1].start()
    rates_copy = pltpu.make_async_copy(rates_hbm, rates_ref, sems.at[len(large) + len(small)])
    rates_copy.start()
    for copy in small:
        copy.wait()
    land_ref[...] = land_in[...].astype(F32)
    parent_land_ref[...] = parent_land_in[...].astype(F32)
    child_factors(mix_ref, 1.0 - relax_ref[...], a_ref, b_ref, c_ref)
    weights = [relax_ref[j : j + 1, :] for j in range(8)]

    def level(i, _):
        for side, k in ((0, i), (1, depth - 1 - i)):
            block_rows(x_ref, k, weights, sums_ref, i, side)
        return 0

    for part, start in enumerate(range(0, half, size)):
        large[2 * part].wait()
        large[2 * part + 1].wait()
        lax.fori_loop(start, start + size, level, 0, unroll=size)
    sums_out[...] = block_columns(sums_ref)
    rates_copy.wait()


def child_first(x_ref, a_ref, b_ref, c_ref, solved_ref, mate_rows, far_rows, cols_ref):
    child_solve(x_ref, a_ref, b_ref, c_ref, solved_ref, mate_rows, far_rows, cols_ref, lambda k, v, _: x_ref[k, v])


def child_solve(x_ref, a_ref, b_ref, c_ref, solved_ref, mate_rows, far_rows, cols_ref, load, row_ref=None):
    depth, vectors = x_ref.shape[0], x_ref.shape[1]
    half = depth // 2

    def down(i, carry):
        values = []
        for side, k in ((0, i), (1, depth - 1 - i)):
            a, b = a_ref[k], b_ref[k]
            row_rates = None if row_ref is None else row_ref[k]
            for v in range(vectors):
                y = a * load(k, v, row_rates) + b * carry[side * vectors + v]
                solved_ref[k, v] = y
                values.append(y)
        return tuple(values)

    carry = lax.fori_loop(0, half, down, (jnp.zeros((8, LANES), F32),) * (2 * vectors), unroll=half)
    child_up(carry, c_ref, solved_ref, mate_rows, far_rows, cols_ref)


def combine(sides, land):
    east, west, north, south = sides
    return [land * part for part in (1.0 - (east + west + north + south), east, west, north, south)]


def merge_edges(mate, far, turn):
    swap = jnp.broadcast_to(parity("gx"), (8, LANES)) == 1
    east, west = jnp.where(swap, far, mate), jnp.where(swap, mate, far)
    return jnp.where((lane_index() & 1) == 0, west, pltpu.roll(east, turn, 1))


def child_inner(solved_ref, rates_ref, land_ref, after_ref, inner_ref, row_ref, column_ref):
    depth, vectors = solved_ref.shape[0], solved_ref.shape[1]
    lane, row = lane_index(), row_index()
    land = land_ref[...]

    def level(k, _):
        centre, east, west, north, south = combine([rates_ref[d, k] for d in range(4)], land)
        column_ref[k] = jnp.where(lane == 0, west, jnp.where(lane == LANES - 1, east, 0.0))
        row_ref[k] = jnp.where(row == 0, south, jnp.where(row == 7, north, 0.0))
        east, west = jnp.where(lane == LANES - 1, 0.0, east), jnp.where(lane == 0, 0.0, west)
        north, south = jnp.where(row == 7, 0.0, north), jnp.where(row == 0, 0.0, south)
        for v in range(vectors):
            s = solved_ref[k, v]
            across = east * pltpu.roll(s, LANES - 1, 1) + west * pltpu.roll(s, 1, 1)
            along = north * pltpu.roll(s, 7, 0) + south * pltpu.roll(s, 1, 0)
            inner_ref[k, v] = centre * s + across + along
        return 0

    lax.fori_loop(0, depth, level, 0, unroll=16)


def edge_merger(mate_cols, far_cols, merged_ref):
    for g in range(merged_ref.shape[0] // 8):
        part = slice(8 * g, 8 * g + 8)
        merged_ref[part, :] = merge_edges(mate_cols[part, :], far_cols[part, :], LANES - 2)


def column_edged(inner_ref, column_rates, edges, k, v, at):
    return inner_ref[k, v] + column_rates * pltpu.roll(edges, (LANES - 2 * at) & (LANES - 1), 1)


def row_halo(mate_ref, far_ref, k, v, vectors, mates):
    line = pl.ds(k * vectors + v, 1)
    mate = jnp.broadcast_to(mate_ref[line, :], (8, LANES))
    far = jnp.broadcast_to(far_ref[line, :], (8, LANES))
    return jnp.where(mates, mate, far)


def mate_rows_mask():
    return row_index() == 7 * (1 - parity("gy"))


def child_columns(inner_ref, column_ref, relax_ref, after_ref, mate_cols, far_cols, sums_ref, x_ref, merged_ref):
    depth, vectors = inner_ref.shape[0], inner_ref.shape[1]
    half, groups = depth // 2, depth // LEVELS
    weights = [relax_ref[j : j + 1, :] for j in range(8)]
    edge_merger(mate_cols, far_cols, merged_ref)

    def level(i, _, edges):
        inside = lax.rem(i, LEVELS)
        for side, k, base in ((0, i, inside * vectors), (1, depth - 1 - i, (LEVELS - 1 - inside) * vectors)):
            column_rates = column_ref[k]
            for v in range(vectors):
                x_ref[k, v] = column_edged(inner_ref, column_rates, edges[side], k, v, base + v)
        return 0

    def add(i, _):
        for side, k in ((0, i), (1, depth - 1 - i)):
            block_rows(x_ref, k, weights, sums_ref, i, side)
        return 0

    for group in range(half // LEVELS):
        edges = [merged_ref[8 * g : 8 * g + 8, :] for g in (group, groups - 1 - group)]
        lax.fori_loop(
            LEVELS * group, LEVELS * (group + 1), lambda i, _, edges=edges: level(i, _, edges), 0, unroll=LEVELS
        )
        lax.fori_loop(LEVELS * group, LEVELS * (group + 1), add, 0, unroll=LEVELS)


def child_rows(sums_in, row_ref, relax_ref, after_ref, mate_in, far_in, sums_out, sums_ref):
    depth = row_ref.shape[0]
    vectors = 2 * sums_in.shape[0] // depth
    swap = jnp.broadcast_to(parity("gy"), (vectors, LANES)) == 1
    for k in range(depth):
        place, i = (0, k) if k < depth // 2 else (1, depth - 1 - k)
        lines = slice(k * vectors, (k + 1) * vectors)
        mate, far = mate_in[lines, :], far_in[lines, :]
        for r, at, halo in ((0, 0, jnp.where(swap, mate, far)), (1, 7, jnp.where(swap, far, mate))):
            share = (row_ref[k, at : at + 1, :] * relax_ref[at : at + 1, :]) * halo
            part = slice(i * vectors, (i + 1) * vectors), slice((2 * place + r) * LANES, (2 * place + r + 1) * LANES)
            sums_ref[part] = sums_in[part] + share
    sums_out[...] = block_columns(sums_ref)


def child_second(
    x_ref, row_ref, mate_in, far_in, a_ref, b_ref, c_ref, parent_ref, pa_ref, pb_ref, pc_ref,
    solved_ref, psolved_ref, mate_rows, far_rows, cols_ref,
):
    depth, vectors = x_ref.shape[0], x_ref.shape[1]
    y = jnp.zeros((8, LANES), F32)
    for i in range(depth // 2):
        y = pa_ref[i : i + 1, :] * parent_ref[i] + pb_ref[i : i + 1, :] * y
        psolved_ref[i] = y
    lines, at = depth * vectors, depth // LEVELS * 8
    parent_up(y, pc_ref, psolved_ref, mate_rows, far_rows, lines, cols_ref, at)
    mates = mate_rows_mask()

    def load(k, v, row_rates):
        return x_ref[k, v] + row_rates * row_halo(mate_in, far_in, k, v, vectors, mates)

    child_solve(x_ref, a_ref, b_ref, c_ref, solved_ref, mate_rows, far_rows, cols_ref, load, row_ref)


def child_last(
    inner_ref, row_ref, column_ref, mate_in, far_in, mate_cols, far_cols, out_hbm, out_ref, merged_ref, sems
):
    depth, vectors = inner_ref.shape[0], inner_ref.shape[1]
    mates = mate_rows_mask()
    edge_merger(mate_cols, far_cols, merged_ref)
    copies = []
    for group in range(depth // LEVELS):
        edges = merged_ref[8 * group : 8 * group + 8, :]

        def level(inside, _):
            k = LEVELS * group + inside
            row_rates, column_rates = row_ref[k], column_ref[k]
            for v in range(vectors):
                out_ref[k, v] = column_edged(
                    inner_ref, column_rates, edges, k, v, inside * vectors + v
                ) + row_rates * row_halo(mate_in, far_in, k, v, vectors, mates)
            return 0

        lax.fori_loop(0, LEVELS, level, 0, unroll=LEVELS)
        part = pl.ds(LEVELS * group, LEVELS)
        copies.append(pltpu.make_async_copy(out_ref.at[part], out_hbm.at[part], sems.at[group]))
        copies[-1].start()
    for copy in copies:
        copy.wait()


PLACES = [(h, r, 64 * h + 32 * r) for h in range(2) for r in range(2)]


def parent_fed(parent_ref, mix_ref, feed_ref, after_ref, packed_ref, mixed):
    half, vectors = packed_ref.shape[0], packed_ref.shape[1]
    for i in range(half):
        for h, r, lo in PLACES:
            k = 2 * half - 1 - i if h else i
            packed_ref[i, :, lo : lo + 32] = parent_ref[pl.ds(2 * vectors * k + r, vectors, stride=2), :]
            mixed[i : i + 1, lo : lo + 32] = mix_ref[2 * k + r : 2 * k + r + 1, :]
        packed_ref[i] = packed_ref[i] + feed_ref[vectors * i : vectors * (i + 1), :]


def parent_factors(mixed, far_ref, x_ref, sums_ref, pa_ref, pb_ref, pc_ref):
    half = pa_ref.shape[0]
    upper = lane_index(1) < 64
    rows = [mixed[i : i + 1, :] for i in range(half)]
    inner, outer = [], []
    for i in range(half):
        nearer = rows[i + 1] if i + 1 < half else pltpu.roll(rows[i], 64, 1)
        inner.append(jnp.where(upper, rows[i], nearer))
        outer.append(jnp.where(upper, rows[i - 1] if i else jnp.zeros_like(rows[0]), rows[i]))
    inverse = minors(inner, outer)
    for i in range(half):
        pa_ref[i : i + 1, :] = inverse[i]
        pb_ref[i : i + 1, :] = inverse[i] * outer[i]
        pc_ref[i : i + 1, :] = inverse[i] * inner[i]


def parent_rates_packed(rates_ref, feed_ref, after_ref, packed_ref):
    half = packed_ref.shape[1]
    depth = 2 * half
    for i in range(half):
        for h, r, lo in PLACES:
            k = depth - 1 - i if h else i
            for d in range(4):
                at = 2 * (d * depth + k) + r
                packed_ref[d, i : i + 1, lo : lo + 32] = rates_ref[at : at + 1, :]


def parent_rates_masked(packed_ref, land_ref, far_ref, mate_cols, far_cols, prates_ref):
    half = packed_ref.shape[1]
    land = jnp.concatenate([land_ref[r : r + 1, :] for _, r, _ in PLACES], axis=1)
    land = jnp.broadcast_to(land, (half, LANES))
    for d, part in enumerate(combine([packed_ref[d] for d in range(4)], land)):
        prates_ref[d] = part


def parent_up(carry, pc_ref, psolved_ref, mate_rows, far_rows, lines, cols_ref, cols_at):
    half = psolved_ref.shape[0]
    lane = lane_index()
    middle = pc_ref[half - 1 : half, :]
    scale = 1.0 / (1.0 - middle * pltpu.roll(middle, 64, 1))
    x = (carry + middle * pltpu.roll(carry, 64, 1)) * scale
    tiles = [None] * half
    tiles[half - 1] = x
    for i in range(half - 2, -1, -1):
        x = psolved_ref[i] + pc_ref[i : i + 1, :] * x
        tiles[i] = x
    packed = jnp.zeros((8, LANES), F32)
    for i in range(half):
        psolved_ref[i] = tiles[i]
        packed = jnp.where(((lane & 31) >> 1) == i, pltpu.roll(tiles[i], 2 * i + 1, 1), packed)
    cols_ref[cols_at : cols_at + 8, :] = packed
    first = (lane & 32) == 0
    swap = jnp.broadcast_to(parity("gy"), (8, LANES)) == 1
    for j in range(half // 2):
        one, two = tiles[j], tiles[j + half // 2]
        lo = jnp.where(first, one, pltpu.roll(two, 32, 1))
        hi = jnp.where(first, pltpu.roll(one, 96, 1), two)
        part = slice(lines + 8 * j, lines + 8 * j + 8)
        mate_rows[part, :] = jnp.where(swap, lo, hi)
        far_rows[part, :] = jnp.where(swap, hi, lo)


def parent_edges(mate_cols, far_cols, at):
    return merge_edges(mate_cols[at : at + 8, :], far_cols[at : at + 8, :], 62)


def parent_transport(psolved_ref, prates_ref, mate_row, far_row, edges, i):
    half = psolved_ref.shape[0]
    lane = lane_index()
    swap = jnp.broadcast_to(parity("gy"), (8, LANES)) == 1
    x = psolved_ref[i]
    mate, far = mate_row(i % (half // 2)), far_row(i % (half // 2))
    lo, hi = jnp.where(swap, far, mate), jnp.where(swap, mate, far)
    if i < half // 2:
        lo = pltpu.roll(lo, 32, 1)
    else:
        hi = pltpu.roll(hi, 96, 1)
    first = (lane & 32) == 0
    to_north = jnp.where(first, pltpu.roll(x, 96, 1), lo)
    to_south = jnp.where(first, hi, pltpu.roll(x, 32, 1))
    edge = pltpu.roll(edges, (LANES - 2 * i - 32) & (LANES - 1), 1)
    column = lane & 31
    to_east = jnp.where(column == 31, edge, pltpu.roll(x, 127, 1))
    to_west = jnp.where(column == 0, edge, pltpu.roll(x, 1, 1))
    parts = [prates_ref[d, i : i + 1, :] for d in range(5)]
    return (parts[0] * x + parts[1] * to_east) + (parts[2] * to_west + parts[3] * to_north) + parts[4] * to_south


def parent_second(
    psolved_in, prates_ref, pa_ref, pb_ref, pc_ref, mate_in, far_in, mate_cols, far_cols, feed_ref,
    psolved_ref, mate_rows, far_rows, cols_ref,
):
    half = psolved_in.shape[0]
    lines = mate_in.shape[0] - mate_rows.shape[0]
    edges = parent_edges(mate_cols, far_cols, mate_cols.shape[0] - 8)
    mate = lambda j: mate_in[lines + 8 * j : lines + 8 * j + 8, :]
    far = lambda j: far_in[lines + 8 * j : lines + 8 * j + 8, :]
    y = jnp.zeros((8, LANES), F32)
    for i in range(half):
        rhs = parent_transport(psolved_in, prates_ref, mate, far, edges, i)
        rhs = rhs + feed_ref[8 * i : 8 * i + 8, :]
        y = pa_ref[i : i + 1, :] * rhs + pb_ref[i : i + 1, :] * y
        psolved_ref[i] = y
    parent_up(y, pc_ref, psolved_ref, mate_rows, far_rows, 0, cols_ref, 0)


def parent_last(psolved_in, prates_ref, mate_in, far_in, mate_cols, far_cols, out_hbm, out_ref, sems):
    half, vectors = psolved_in.shape[0], psolved_in.shape[1]
    edges = parent_edges(mate_cols, far_cols, 0)
    mate = lambda j: mate_in[8 * j : 8 * j + 8, :]
    far = lambda j: far_in[8 * j : 8 * j + 8, :]
    size, copies = 4, []
    for i in range(half):
        x = parent_transport(psolved_in, prates_ref, mate, far, edges, i)
        for h in range(2):
            for r in range(2):
                lo = 64 * h + 32 * r
                k = 2 * half - 1 - i if h else i
                out_ref[pl.ds(2 * vectors * k + r, vectors, stride=2), :] = x[:, lo : lo + 32]
        if i % size == size - 1:
            for first in (i + 1 - size, 2 * half - 1 - i):
                part = pl.ds(2 * vectors * first, 2 * vectors * size)
                copies.append(pltpu.make_async_copy(out_ref.at[part], out_hbm.at[part], sems.at[len(copies)]))
                copies[-1].start()
    for copy in copies:
        copy.wait()


def passed_along(value, axis, steps):
    count = lax.axis_size(axis)
    return lax.ppermute(value, axis, [(i, (i + steps) % count) for i in range(count)])


def swapped(value, axis, offset):
    count = lax.axis_size(axis)
    pairs = []
    for i in range(offset, count, 2):
        j = (i + 1) % count
        pairs += [(i, j), (j, i)]
    return lax.ppermute(value, axis, pairs)


def halos_of(mate, far, cols):
    return [swapped(mate, "gy", 0), swapped(far, "gy", 1), swapped(cols, "gx", 0), swapped(cols, "gx", 1)]


def local(
    child_adjoint,
    parent_adjoint,
    child_rates,
    child_mixing,
    child_land,
    parent_rates,
    parent_mixing,
    parent_land,
    relaxation,
):
    depth, vectors, lines, columns = child_adjoint.shape
    half = depth // 2
    quarter = lax.axis_size("gy") // 4
    field = shape(depth, vectors, lines, columns)
    factor = shape(depth, lines, columns)
    tiles = shape(half, vectors, LANES)
    sums = shape(half * vectors, LANES)
    count = depth * vectors
    edge = depth // LEVELS * 8
    sum_scratch = pltpu.VMEM((half * vectors, 4 * LANES), F32)
    edge_scratch = [pltpu.VMEM((edge, LANES), F32)]
    narrow = parent_adjoint.shape[-1]

    sums1, x, a, b, c, relax, land, parent_land, rates = call(
        begin,
        [sums, field, factor, factor, factor, shape(lines, columns), shape(lines, columns), shape(*parent_land.shape)]
        + [shape(*child_rates.shape)],
        [
            pltpu.VMEM(factor.shape, F32),
            pltpu.VMEM(child_land.shape, jnp.int32),
            pltpu.VMEM(parent_land.shape, jnp.int32),
            sum_scratch,
            pltpu.SemaphoreType.DMA((5 + half // 2,)),
        ],
        [child_adjoint, child_mixing, relaxation, child_land, parent_land, child_rates],
        4_000_000,
        3_000_000,
        far_in=range(6),
    )
    feed = passed_along(sums1, "gy", quarter)
    solved, mate, far, cols = call(
        child_first,
        [field, shape(count, LANES), shape(count, LANES), shape(edge, LANES)],
        [],
        [x, a, b, c],
        4_000_000,
        3_000_000,
    )
    halos = halos_of(mate, far, cols)
    inner, row_rates, column_rates = call(
        child_inner,
        [field, factor, factor],
        [],
        [solved, rates, land, cols],
        INNER,
        4_000_000,
    )
    fed, mixed = call(
        parent_fed,
        [tiles, shape(half, LANES)],
        [],
        [parent_adjoint.reshape(-1, narrow), parent_mixing.reshape(-1, narrow), feed, inner],
        LONG,
        1_000_000,
    )
    raw_sums, x = call(
        child_columns,
        [shape(half * vectors, 4 * LANES), field],
        edge_scratch,
        [inner, column_rates, relax, mixed, *halos[2:]],
        INNER,
        3_000_000,
    )
    pa, pb, pc = call(
        parent_factors,
        [shape(half, LANES)] * 3,
        [],
        [mixed, halos[1], x, raw_sums],
        LONG,
        1_000_000,
    )
    sums2 = call(
        child_rows,
        sums,
        [sum_scratch],
        [raw_sums, row_rates, relax, pa, *halos[:2]],
        INNER,
        1_000_000,
    )
    feed = passed_along(sums2, "gy", quarter)
    rows = count + half // 2 * vectors
    solved, psolved, mate, far, cols = call(
        child_second,
        [field, tiles, shape(rows, LANES), shape(rows, LANES), shape(edge + 8, LANES)],
        [],
        [x, row_rates, *halos[:2], a, b, c, fed, pa, pb, pc],
        8_000_000,
        3_000_000,
    )
    halos = halos_of(mate, far, cols)
    inner, row_rates, column_rates = call(
        child_inner,
        [field, factor, factor],
        [],
        [solved, rates, land, cols],
        INNER,
        4_000_000,
    )
    packed_rates = call(
        parent_rates_packed,
        shape(4, half, LANES),
        [],
        [parent_rates.reshape(-1, narrow), feed, inner],
        1_450_000_000,
        1_000_000,
    )
    prates = call(
        parent_rates_masked,
        shape(5, half, LANES),
        [],
        [packed_rates, parent_land, *halos[1:]],
        LONG,
        1_000_000,
    )
    few = half // 2 * vectors
    psolved, mate, far, cols = call(
        parent_second,
        [tiles, shape(few, LANES), shape(few, LANES), shape(8, LANES)],
        [],
        [psolved, prates, pa, pb, pc, *halos, feed],
        1_000_000,
        500_000,
    )
    last_halos = halos_of(mate, far, cols)
    child_out = call(
        child_last,
        field,
        [pltpu.VMEM(field.shape, F32)] + edge_scratch + [pltpu.SemaphoreType.DMA((depth // LEVELS,))],
        [inner, row_rates, column_rates, *halos],
        4_000_000,
        3_000_000,
        far_out=True,
    )
    parent_out = call(
        parent_last,
        shape(depth * vectors * 2, narrow),
        [pltpu.VMEM((depth * vectors * 2, narrow), F32), pltpu.SemaphoreType.DMA((half // 2,))],
        [psolved, prates, *last_halos],
        500_000,
        500_000,
        far_out=True,
    )
    return (child_out, parent_out.reshape(parent_adjoint.shape))


def solution(mesh):
    wide = P(None, None, "gy", "gx")
    level = P(None, "gy", "gx")
    flat = P("gy", "gx")
    in_specs = (wide, wide, wide, level, flat, wide, level, flat, flat)
    return jax.shard_map(local, mesh=mesh, in_specs=in_specs, out_specs=(wide, wide), check_vma=False)
```

```python
import jax
import jax.numpy as jnp
from jax import lax
from jax.experimental import pallas as pl
from jax.experimental.pallas import tpu as pltpu
from jax.sharding import PartitionSpec as P

F32 = jnp.float32
VMEM = pl.BlockSpec(memory_space=pltpu.VMEM)
FAR = pl.BlockSpec(memory_space=pltpu.HBM)
LIMIT = 40 * 1024 * 1024
LANES = 128
LONG = 1_000_000_000
INNER = 10_000_000
LEVELS = 8


def shape(*dims):
    return jax.ShapeDtypeStruct(dims, F32)


def call(body, outs, scratch, operands, flops, touched, far_in=(), far_out=False):
    operands = [pltpu.with_memory_space_constraint(x, pltpu.HBM) if i in far_in else x for i, x in enumerate(operands)]
    return pl.pallas_call(
        body,
        out_shape=outs,
        in_specs=[FAR if i in far_in else VMEM for i in range(len(operands))],
        out_specs=jax.tree.map(lambda _: FAR if far_out else VMEM, outs),
        scratch_shapes=scratch,
        compiler_params=pltpu.CompilerParams(vmem_limit_bytes=LIMIT),
        cost_estimate=pl.CostEstimate(flops=flops, bytes_accessed=touched, transcendentals=0),
        name=body.__name__,
    )(*operands)


def lane_index(rows=8):
    return lax.broadcasted_iota(jnp.int32, (rows, LANES), 1)


def row_index():
    return lax.broadcasted_iota(jnp.int32, (8, LANES), 0)


def minors(inner, outer):
    theta = delta = jnp.ones_like(inner[0])
    inverse = []
    for i in range(len(inner)):
        delta = theta + outer[i] * delta
        theta_next = delta + inner[i] * theta
        inverse.append(theta / theta_next)
        theta = theta_next
    return inverse


def parity(axis):
    return lax.rem(lax.axis_index(axis), 2)


def child_factors(mix_ref, keep, a_ref, b_ref, c_ref):
    depth = mix_ref.shape[0]
    half = depth // 2
    zero = jnp.zeros_like(keep)
    top_inner = [mix_ref[i] for i in range(half)]
    top_outer = [zero] + top_inner[:-1]
    low_outer = [mix_ref[depth - 1 - i] for i in range(half)]
    low_inner = [mix_ref[depth - 2 - i] for i in range(half)]
    for levels, inner, outer in (
        (range(half), top_inner, top_outer),
        (range(depth - 1, half - 1, -1), low_inner, low_outer),
    ):
        inverse = minors(inner, outer)
        for i, k in enumerate(levels):
            a_ref[k] = inverse[i] * keep
            b_ref[k] = inverse[i] * outer[i]
            c_ref[k] = inverse[i] * inner[i]


def block_rows(source_ref, k, weights, sums_ref, i, place):
    vectors = source_ref.shape[1]
    for r in range(2):
        total = source_ref[k, :, 4 * r, :] * weights[4 * r]
        for j in range(4 * r + 1, 4 * r + 4):
            total = total + source_ref[k, :, j, :] * weights[j]
        column = (2 * place + r) * LANES
        sums_ref[pl.ds(i * vectors, vectors), column : column + LANES] = total


def block_columns(sums_ref):
    wide = sums_ref.shape[1]
    p = lax.broadcasted_iota(jnp.int32, (wide, LANES), 0)
    q = lax.broadcasted_iota(jnp.int32, (wide, LANES), 1)
    pick = jnp.where(p // 4 == q, F32(0.0625), F32(0.0)).astype(jnp.bfloat16)
    rest, total = sums_ref[...], None
    for _ in range(3):
        part = rest.astype(jnp.bfloat16)
        rest = rest - part.astype(F32)
        product = jnp.dot(part, pick, preferred_element_type=F32)
        total = product if total is None else total + product
    return total


def child_middle(carry, c_ref, half):
    vectors = len(carry) // 2
    top, low = c_ref[half - 1], c_ref[half]
    scale = 1.0 / (1.0 - top * low)
    first = [(carry[v] + top * carry[vectors + v]) * scale for v in range(vectors)]
    second = [(carry[vectors + v] + low * carry[v]) * scale for v in range(vectors)]
    return first + second


def child_up(carry, c_ref, solved_ref, mate_rows, far_rows, cols_ref):
    depth, vectors = solved_ref.shape[0], solved_ref.shape[1]
    half = depth // 2
    lane = lane_index()
    pair = lane >> 1
    swap = jnp.broadcast_to(parity("gy"), (8, LANES)) == 1

    def emit(i, values, packed):
        k_low = depth - 1 - i
        packed = list(packed)
        inside = i % LEVELS if isinstance(i, int) else lax.rem(i, LEVELS)
        for side, k, base in ((0, i, inside * vectors), (1, k_low, (LEVELS - 1 - inside) * vectors)):
            for v in range(vectors):
                x = values[side * vectors + v]
                solved_ref[k, v] = x
                at = base + v
                packed[side] = jnp.where(pair == at, pltpu.roll(x, 2 * at + 1 & (LANES - 1), 1), packed[side])
            lo, hi = solved_ref[k, :, 0, :], solved_ref[k, :, 7, :]
            mate_rows[pl.ds(k * vectors, vectors), :] = jnp.where(swap, lo, hi)
            far_rows[pl.ds(k * vectors, vectors), :] = jnp.where(swap, hi, lo)
        return packed

    def up(i, state):
        k_low = depth - 1 - i
        top, low = c_ref[i], c_ref[k_low]
        values = []
        for v in range(vectors):
            values.append(solved_ref[i, v] + top * state[v])
        for v in range(vectors):
            values.append(solved_ref[k_low, v] + low * state[vectors + v])
        return tuple(values) + tuple(emit(i, values, state[2 * vectors :]))

    def keep_columns(group, packed):
        for side, g in ((0, group), (1, depth // LEVELS - 1 - group)):
            cols_ref[LEVELS * g : LEVELS * g + 8, :] = packed[side]

    blank = jnp.zeros((8, LANES), F32)
    values = child_middle(carry, c_ref, half)
    state = tuple(values) + tuple(emit(half - 1, values, [blank] * 2))
    for group in range(half // LEVELS - 1, -1, -1):
        last = LEVELS * (group + 1) - 1
        if group == half // LEVELS - 1:
            last -= 1
        count = last - LEVELS * group + 1
        state = lax.fori_loop(0, count, lambda step, state, last=last: up(last - step, state), state, unroll=count)
        keep_columns(group, state[2 * vectors :])
        state = state[: 2 * vectors] + (blank,) * 2


def begin(
    x_hbm, mix_hbm, relax_hbm, land_hbm, parent_land_hbm, rates_hbm,
    sums_out, x_ref, a_ref, b_ref, c_ref, relax_ref, land_ref, parent_land_ref, rates_ref,
    mix_ref, land_in, parent_land_in, sums_ref, sems,
):
    depth = x_ref.shape[0]
    half = depth // 2
    small = []
    for source, target in (
        (mix_hbm, mix_ref), (relax_hbm, relax_ref), (land_hbm, land_in), (parent_land_hbm, parent_land_in),
    ):
        small.append(pltpu.make_async_copy(source, target, sems.at[len(small)]))
        small[-1].start()
    size, large = 4, []
    for start in range(0, half, size):
        for first in (start, depth - size - start):
            part = pl.ds(first, size)
            large.append(pltpu.make_async_copy(x_hbm.at[part], x_ref.at[part], sems.at[len(large) + len(small)]))
            large[-1].start()
    rates_copy = pltpu.make_async_copy(rates_hbm, rates_ref, sems.at[len(large) + len(small)])
    rates_copy.start()
    for copy in small:
        copy.wait()
    land_ref[...] = land_in[...].astype(F32)
    parent_land_ref[...] = parent_land_in[...].astype(F32)
    child_factors(mix_ref, 1.0 - relax_ref[...], a_ref, b_ref, c_ref)
    weights = [relax_ref[j : j + 1, :] for j in range(8)]

    def level(i, _):
        for side, k in ((0, i), (1, depth - 1 - i)):
            block_rows(x_ref, k, weights, sums_ref, i, side)
        return 0

    for part, start in enumerate(range(0, half, size)):
        large[2 * part].wait()
        large[2 * part + 1].wait()
        lax.fori_loop(start, start + size, level, 0, unroll=size)
    sums_out[...] = block_columns(sums_ref)
    rates_copy.wait()


def child_first(x_ref, a_ref, b_ref, c_ref, solved_ref, mate_rows, far_rows, cols_ref):
    child_solve(x_ref, a_ref, b_ref, c_ref, solved_ref, mate_rows, far_rows, cols_ref, lambda k, v, _: x_ref[k, v])


def child_solve(x_ref, a_ref, b_ref, c_ref, solved_ref, mate_rows, far_rows, cols_ref, load, row_ref=None):
    depth, vectors = x_ref.shape[0], x_ref.shape[1]
    half = depth // 2

    def down(i, carry):
        values = []
        for side, k in ((0, i), (1, depth - 1 - i)):
            a, b = a_ref[k], b_ref[k]
            row_rates = None if row_ref is None else row_ref[k]
            for v in range(vectors):
                y = a * load(k, v, row_rates) + b * carry[side * vectors + v]
                solved_ref[k, v] = y
                values.append(y)
        return tuple(values)

    carry = lax.fori_loop(0, half, down, (jnp.zeros((8, LANES), F32),) * (2 * vectors), unroll=8)
    child_up(carry, c_ref, solved_ref, mate_rows, far_rows, cols_ref)


def combine(sides, land):
    east, west, north, south = sides
    return [land * part for part in (1.0 - (east + west + north + south), east, west, north, south)]


def merge_edges(mate, far, turn):
    swap = jnp.broadcast_to(parity("gx"), (8, LANES)) == 1
    east, west = jnp.where(swap, far, mate), jnp.where(swap, mate, far)
    return jnp.where((lane_index() & 1) == 0, west, pltpu.roll(east, turn, 1))


def child_inner(solved_ref, rates_ref, land_ref, after_ref, inner_ref, row_ref, column_ref):
    depth, vectors = solved_ref.shape[0], solved_ref.shape[1]
    lane, row = lane_index(), row_index()
    land = land_ref[...]

    def level(k, _):
        centre, east, west, north, south = combine([rates_ref[d, k] for d in range(4)], land)
        column_ref[k] = jnp.where(lane == 0, west, jnp.where(lane == LANES - 1, east, 0.0))
        row_ref[k] = jnp.where(row == 0, south, jnp.where(row == 7, north, 0.0))
        east, west = jnp.where(lane == LANES - 1, 0.0, east), jnp.where(lane == 0, 0.0, west)
        north, south = jnp.where(row == 7, 0.0, north), jnp.where(row == 0, 0.0, south)
        for v in range(vectors):
            s = solved_ref[k, v]
            across = east * pltpu.roll(s, LANES - 1, 1) + west * pltpu.roll(s, 1, 1)
            along = north * pltpu.roll(s, 7, 0) + south * pltpu.roll(s, 1, 0)
            inner_ref[k, v] = centre * s + across + along
        return 0

    lax.fori_loop(0, depth, level, 0, unroll=16)


def edge_merger(mate_cols, far_cols, merged_ref):
    for g in range(merged_ref.shape[0] // 8):
        part = slice(8 * g, 8 * g + 8)
        merged_ref[part, :] = merge_edges(mate_cols[part, :], far_cols[part, :], LANES - 2)


def column_edged(inner_ref, column_rates, edges, k, v, at):
    return inner_ref[k, v] + column_rates * pltpu.roll(edges, (LANES - 2 * at) & (LANES - 1), 1)


def row_halo(mate_ref, far_ref, k, v, vectors, mates):
    line = pl.ds(k * vectors + v, 1)
    mate = jnp.broadcast_to(mate_ref[line, :], (8, LANES))
    far = jnp.broadcast_to(far_ref[line, :], (8, LANES))
    return jnp.where(mates, mate, far)


def mate_rows_mask():
    return row_index() == 7 * (1 - parity("gy"))


def child_columns(inner_ref, column_ref, relax_ref, after_ref, mate_cols, far_cols, sums_ref, x_ref, merged_ref):
    depth, vectors = inner_ref.shape[0], inner_ref.shape[1]
    half, groups = depth // 2, depth // LEVELS
    weights = [relax_ref[j : j + 1, :] for j in range(8)]
    edge_merger(mate_cols, far_cols, merged_ref)

    def level(i, _, edges):
        inside = lax.rem(i, LEVELS)
        for side, k, base in ((0, i, inside * vectors), (1, depth - 1 - i, (LEVELS - 1 - inside) * vectors)):
            column_rates = column_ref[k]
            for v in range(vectors):
                x_ref[k, v] = column_edged(inner_ref, column_rates, edges[side], k, v, base + v)
        return 0

    def add(i, _):
        for side, k in ((0, i), (1, depth - 1 - i)):
            block_rows(x_ref, k, weights, sums_ref, i, side)
        return 0

    for group in range(half // LEVELS):
        edges = [merged_ref[8 * g : 8 * g + 8, :] for g in (group, groups - 1 - group)]
        lax.fori_loop(
            LEVELS * group, LEVELS * (group + 1), lambda i, _, edges=edges: level(i, _, edges), 0, unroll=LEVELS
        )
        lax.fori_loop(LEVELS * group, LEVELS * (group + 1), add, 0, unroll=LEVELS)


def child_rows(sums_in, row_ref, relax_ref, after_ref, mate_in, far_in, sums_out, sums_ref):
    depth = row_ref.shape[0]
    vectors = 2 * sums_in.shape[0] // depth
    swap = jnp.broadcast_to(parity("gy"), (vectors, LANES)) == 1
    for k in range(depth):
        place, i = (0, k) if k < depth // 2 else (1, depth - 1 - k)
        lines = slice(k * vectors, (k + 1) * vectors)
        mate, far = mate_in[lines, :], far_in[lines, :]
        for r, at, halo in ((0, 0, jnp.where(swap, mate, far)), (1, 7, jnp.where(swap, far, mate))):
            share = (row_ref[k, at : at + 1, :] * relax_ref[at : at + 1, :]) * halo
            part = slice(i * vectors, (i + 1) * vectors), slice((2 * place + r) * LANES, (2 * place + r + 1) * LANES)
            sums_ref[part] = sums_in[part] + share
    sums_out[...] = block_columns(sums_ref)


def child_second(
    x_ref, row_ref, mate_in, far_in, a_ref, b_ref, c_ref, parent_ref, pa_ref, pb_ref, pc_ref,
    solved_ref, psolved_ref, mate_rows, far_rows, cols_ref,
):
    depth, vectors = x_ref.shape[0], x_ref.shape[1]
    y = jnp.zeros((8, LANES), F32)
    for i in range(depth // 2):
        y = pa_ref[i : i + 1, :] * parent_ref[i] + pb_ref[i : i + 1, :] * y
        psolved_ref[i] = y
    lines, at = depth * vectors, depth // LEVELS * 8
    parent_up(y, pc_ref, psolved_ref, mate_rows, far_rows, lines, cols_ref, at)
    mates = mate_rows_mask()

    def load(k, v, row_rates):
        return x_ref[k, v] + row_rates * row_halo(mate_in, far_in, k, v, vectors, mates)

    child_solve(x_ref, a_ref, b_ref, c_ref, solved_ref, mate_rows, far_rows, cols_ref, load, row_ref)


def child_last(
    inner_ref, row_ref, column_ref, mate_in, far_in, mate_cols, far_cols, out_hbm, out_ref, merged_ref, sems
):
    depth, vectors = inner_ref.shape[0], inner_ref.shape[1]
    mates = mate_rows_mask()
    edge_merger(mate_cols, far_cols, merged_ref)
    copies = []
    for group in range(depth // LEVELS):
        edges = merged_ref[8 * group : 8 * group + 8, :]

        def level(inside, _):
            k = LEVELS * group + inside
            row_rates, column_rates = row_ref[k], column_ref[k]
            for v in range(vectors):
                out_ref[k, v] = column_edged(
                    inner_ref, column_rates, edges, k, v, inside * vectors + v
                ) + row_rates * row_halo(mate_in, far_in, k, v, vectors, mates)
            return 0

        lax.fori_loop(0, LEVELS, level, 0, unroll=LEVELS)
        part = pl.ds(LEVELS * group, LEVELS)
        copies.append(pltpu.make_async_copy(out_ref.at[part], out_hbm.at[part], sems.at[group]))
        copies[-1].start()
    for copy in copies:
        copy.wait()


PLACES = [(h, r, 64 * h + 32 * r) for h in range(2) for r in range(2)]


def parent_fed(parent_ref, mix_ref, feed_ref, after_ref, packed_ref, mixed):
    half, vectors = packed_ref.shape[0], packed_ref.shape[1]
    for i in range(half):
        for h, r, lo in PLACES:
            k = 2 * half - 1 - i if h else i
            packed_ref[i, :, lo : lo + 32] = parent_ref[pl.ds(2 * vectors * k + r, vectors, stride=2), :]
            mixed[i : i + 1, lo : lo + 32] = mix_ref[2 * k + r : 2 * k + r + 1, :]
        packed_ref[i] = packed_ref[i] + feed_ref[vectors * i : vectors * (i + 1), :]


def parent_factors(mixed, far_ref, x_ref, sums_ref, pa_ref, pb_ref, pc_ref):
    half = pa_ref.shape[0]
    upper = lane_index(1) < 64
    rows = [mixed[i : i + 1, :] for i in range(half)]
    inner, outer = [], []
    for i in range(half):
        nearer = rows[i + 1] if i + 1 < half else pltpu.roll(rows[i], 64, 1)
        inner.append(jnp.where(upper, rows[i], nearer))
        outer.append(jnp.where(upper, rows[i - 1] if i else jnp.zeros_like(rows[0]), rows[i]))
    inverse = minors(inner, outer)
    for i in range(half):
        pa_ref[i : i + 1, :] = inverse[i]
        pb_ref[i : i + 1, :] = inverse[i] * outer[i]
        pc_ref[i : i + 1, :] = inverse[i] * inner[i]


def parent_rates_packed(rates_ref, feed_ref, after_ref, packed_ref):
    half = packed_ref.shape[1]
    depth = 2 * half
    for i in range(half):
        for h, r, lo in PLACES:
            k = depth - 1 - i if h else i
            for d in range(4):
                at = 2 * (d * depth + k) + r
                packed_ref[d, i : i + 1, lo : lo + 32] = rates_ref[at : at + 1, :]


def parent_rates_masked(packed_ref, land_ref, far_ref, mate_cols, far_cols, prates_ref):
    half = packed_ref.shape[1]
    land = jnp.concatenate([land_ref[r : r + 1, :] for _, r, _ in PLACES], axis=1)
    land = jnp.broadcast_to(land, (half, LANES))
    for d, part in enumerate(combine([packed_ref[d] for d in range(4)], land)):
        prates_ref[d] = part


def parent_up(carry, pc_ref, psolved_ref, mate_rows, far_rows, lines, cols_ref, cols_at):
    half = psolved_ref.shape[0]
    lane = lane_index()
    middle = pc_ref[half - 1 : half, :]
    scale = 1.0 / (1.0 - middle * pltpu.roll(middle, 64, 1))
    x = (carry + middle * pltpu.roll(carry, 64, 1)) * scale
    tiles = [None] * half
    tiles[half - 1] = x
    for i in range(half - 2, -1, -1):
        x = psolved_ref[i] + pc_ref[i : i + 1, :] * x
        tiles[i] = x
    packed = jnp.zeros((8, LANES), F32)
    for i in range(half):
        psolved_ref[i] = tiles[i]
        packed = jnp.where(((lane & 31) >> 1) == i, pltpu.roll(tiles[i], 2 * i + 1, 1), packed)
    cols_ref[cols_at : cols_at + 8, :] = packed
    first = (lane & 32) == 0
    swap = jnp.broadcast_to(parity("gy"), (8, LANES)) == 1
    for j in range(half // 2):
        one, two = tiles[j], tiles[j + half // 2]
        lo = jnp.where(first, one, pltpu.roll(two, 32, 1))
        hi = jnp.where(first, pltpu.roll(one, 96, 1), two)
        part = slice(lines + 8 * j, lines + 8 * j + 8)
        mate_rows[part, :] = jnp.where(swap, lo, hi)
        far_rows[part, :] = jnp.where(swap, hi, lo)


def parent_edges(mate_cols, far_cols, at):
    return merge_edges(mate_cols[at : at + 8, :], far_cols[at : at + 8, :], 62)


def parent_transport(psolved_ref, prates_ref, mate_row, far_row, edges, i):
    half = psolved_ref.shape[0]
    lane = lane_index()
    swap = jnp.broadcast_to(parity("gy"), (8, LANES)) == 1
    x = psolved_ref[i]
    mate, far = mate_row(i % (half // 2)), far_row(i % (half // 2))
    lo, hi = jnp.where(swap, far, mate), jnp.where(swap, mate, far)
    if i < half // 2:
        lo = pltpu.roll(lo, 32, 1)
    else:
        hi = pltpu.roll(hi, 96, 1)
    first = (lane & 32) == 0
    to_north = jnp.where(first, pltpu.roll(x, 96, 1), lo)
    to_south = jnp.where(first, hi, pltpu.roll(x, 32, 1))
    edge = pltpu.roll(edges, (LANES - 2 * i - 32) & (LANES - 1), 1)
    column = lane & 31
    to_east = jnp.where(column == 31, edge, pltpu.roll(x, 127, 1))
    to_west = jnp.where(column == 0, edge, pltpu.roll(x, 1, 1))
    parts = [prates_ref[d, i : i + 1, :] for d in range(5)]
    return (parts[0] * x + parts[1] * to_east) + (parts[2] * to_west + parts[3] * to_north) + parts[4] * to_south


def parent_second(
    psolved_in, prates_ref, pa_ref, pb_ref, pc_ref, mate_in, far_in, mate_cols, far_cols, feed_ref,
    psolved_ref, mate_rows, far_rows, cols_ref,
):
    half = psolved_in.shape[0]
    lines = mate_in.shape[0] - mate_rows.shape[0]
    edges = parent_edges(mate_cols, far_cols, mate_cols.shape[0] - 8)
    mate = lambda j: mate_in[lines + 8 * j : lines + 8 * j + 8, :]
    far = lambda j: far_in[lines + 8 * j : lines + 8 * j + 8, :]
    y = jnp.zeros((8, LANES), F32)
    for i in range(half):
        rhs = parent_transport(psolved_in, prates_ref, mate, far, edges, i)
        rhs = rhs + feed_ref[8 * i : 8 * i + 8, :]
        y = pa_ref[i : i + 1, :] * rhs + pb_ref[i : i + 1, :] * y
        psolved_ref[i] = y
    parent_up(y, pc_ref, psolved_ref, mate_rows, far_rows, 0, cols_ref, 0)


def parent_merged(mate_cols, far_cols, far_ref, after_ref, edges_ref):
    edges_ref[...] = parent_edges(mate_cols, far_cols, 0)


def parent_last(psolved_in, prates_ref, edges_ref, mate_in, far_in, out_ref):
    half, vectors = psolved_in.shape[0], psolved_in.shape[1]
    edges = edges_ref[...]
    mate = lambda j: mate_in[8 * j : 8 * j + 8, :]
    far = lambda j: far_in[8 * j : 8 * j + 8, :]
    for i in range(half):
        x = parent_transport(psolved_in, prates_ref, mate, far, edges, i)
        for h in range(2):
            for r in range(2):
                lo = 64 * h + 32 * r
                k = 2 * half - 1 - i if h else i
                out_ref[pl.ds(2 * vectors * k + r, vectors, stride=2), :] = x[:, lo : lo + 32]


def passed_along(value, axis, steps):
    count = lax.axis_size(axis)
    return lax.ppermute(value, axis, [(i, (i + steps) % count) for i in range(count)])


def swapped(value, axis, offset):
    count = lax.axis_size(axis)
    pairs = []
    for i in range(offset, count, 2):
        j = (i + 1) % count
        pairs += [(i, j), (j, i)]
    return lax.ppermute(value, axis, pairs)


def halos_of(mate, far, cols):
    return [swapped(mate, "gy", 0), swapped(far, "gy", 1), swapped(cols, "gx", 0), swapped(cols, "gx", 1)]


def local(
    child_adjoint,
    parent_adjoint,
    child_rates,
    child_mixing,
    child_land,
    parent_rates,
    parent_mixing,
    parent_land,
    relaxation,
):
    depth, vectors, lines, columns = child_adjoint.shape
    half = depth // 2
    quarter = lax.axis_size("gy") // 4
    field = shape(depth, vectors, lines, columns)
    factor = shape(depth, lines, columns)
    tiles = shape(half, vectors, LANES)
    sums = shape(half * vectors, LANES)
    count = depth * vectors
    edge = depth // LEVELS * 8
    sum_scratch = pltpu.VMEM((half * vectors, 4 * LANES), F32)
    edge_scratch = [pltpu.VMEM((edge, LANES), F32)]
    narrow = parent_adjoint.shape[-1]

    sums1, x, a, b, c, relax, land, parent_land, rates = call(
        begin,
        [sums, field, factor, factor, factor, shape(lines, columns), shape(lines, columns), shape(*parent_land.shape)]
        + [shape(*child_rates.shape)],
        [
            pltpu.VMEM(factor.shape, F32),
            pltpu.VMEM(child_land.shape, jnp.int32),
            pltpu.VMEM(parent_land.shape, jnp.int32),
            sum_scratch,
            pltpu.SemaphoreType.DMA((5 + half // 2,)),
        ],
        [child_adjoint, child_mixing, relaxation, child_land, parent_land, child_rates],
        4_000_000,
        3_000_000,
        far_in=range(6),
    )
    feed = passed_along(sums1, "gy", quarter)
    solved, mate, far, cols = call(
        child_first,
        [field, shape(count, LANES), shape(count, LANES), shape(edge, LANES)],
        [],
        [x, a, b, c],
        4_000_000,
        3_000_000,
    )
    halos = halos_of(mate, far, cols)
    inner, row_rates, column_rates = call(
        child_inner,
        [field, factor, factor],
        [],
        [solved, rates, land, cols],
        INNER,
        4_000_000,
    )
    fed, mixed = call(
        parent_fed,
        [tiles, shape(half, LANES)],
        [],
        [parent_adjoint.reshape(-1, narrow), parent_mixing.reshape(-1, narrow), feed, inner],
        LONG,
        1_000_000,
    )
    raw_sums, x = call(
        child_columns,
        [shape(half * vectors, 4 * LANES), field],
        edge_scratch,
        [inner, column_rates, relax, mixed, *halos[2:]],
        INNER,
        3_000_000,
    )
    pa, pb, pc = call(
        parent_factors,
        [shape(half, LANES)] * 3,
        [],
        [mixed, halos[1], x, raw_sums],
        LONG,
        1_000_000,
    )
    sums2 = call(
        child_rows,
        sums,
        [sum_scratch],
        [raw_sums, row_rates, relax, pa, *halos[:2]],
        INNER,
        1_000_000,
    )
    feed = passed_along(sums2, "gy", quarter)
    rows = count + half // 2 * vectors
    solved, psolved, mate, far, cols = call(
        child_second,
        [field, tiles, shape(rows, LANES), shape(rows, LANES), shape(edge + 8, LANES)],
        [],
        [x, row_rates, *halos[:2], a, b, c, fed, pa, pb, pc],
        8_000_000,
        3_000_000,
    )
    halos = halos_of(mate, far, cols)
    inner, row_rates, column_rates = call(
        child_inner,
        [field, factor, factor],
        [],
        [solved, rates, land, cols],
        INNER,
        4_000_000,
    )
    packed_rates = call(
        parent_rates_packed,
        shape(4, half, LANES),
        [],
        [parent_rates.reshape(-1, narrow), feed, inner],
        1_450_000_000,
        1_000_000,
    )
    prates = call(
        parent_rates_masked,
        shape(5, half, LANES),
        [],
        [packed_rates, parent_land, *halos[1:]],
        LONG,
        1_000_000,
    )
    few = half // 2 * vectors
    psolved, mate, far, cols = call(
        parent_second,
        [tiles, shape(few, LANES), shape(few, LANES), shape(8, LANES)],
        [],
        [psolved, prates, pa, pb, pc, *halos, feed],
        1_000_000,
        500_000,
    )
    last_halos = halos_of(mate, far, cols)
    child_out = call(
        child_last,
        field,
        [pltpu.VMEM(field.shape, F32)] + edge_scratch + [pltpu.SemaphoreType.DMA((depth // LEVELS,))],
        [inner, row_rates, column_rates, *halos],
        4_000_000,
        3_000_000,
        far_out=True,
    )
    edges = call(
        parent_merged,
        shape(8, LANES),
        [],
        [*last_halos[2:], last_halos[1], child_out],
        LONG,
        100_000,
        far_in=(3,),
    )
    parent_out = call(
        parent_last,
        shape(depth * vectors * 2, narrow),
        [],
        [psolved, prates, edges, *last_halos[:2]],
        500_000,
        500_000,
    )
    return (child_out, parent_out.reshape(parent_adjoint.shape))


def solution(mesh):
    wide = P(None, None, "gy", "gx")
    level = P(None, "gy", "gx")
    flat = P("gy", "gx")
    in_specs = (wide, wide, wide, level, flat, wide, level, flat, flat)
    return jax.shard_map(local, mesh=mesh, in_specs=in_specs, out_specs=(wide, wide), check_vma=False)
```
